32 devices in a mesh: seq: 8 (over z, x), wt: 4 (over y, core).
Axes of the slice: x: 2, y: 2, z: 4, core: 2. Of those that a mesh axis runs over, the one named last changes fastest.
Arguments:
- tokens: bfloat16 [4096, 2560], P(('seq', 'wt'))
- norm1_gain: bfloat16 [2560], P(('seq', 'wt')), may hold values from 0.5 to 1.5
- x_weight: bfloat16 [2560, 2560], P('seq', 'wt'), may hold values from -0.125 to 0.125
- y_weight: bfloat16 [2560, 2560], P('seq', 'wt'), may hold values from -0.125 to 0.125
- conv_weight: bfloat16 [2560, 4], P(('seq', 'wt')), may hold values from -3 to 3
- conv_bias: bfloat16 [2560], P(('seq', 'wt')), may hold values from -2 to 2
- decay_gate_weight: bfloat16 [2560, 256], P(('seq', 'wt')), may hold values from -0.375 to 0.375
- decay_bias: bfloat16 [2560], P(('seq', 'wt')), may hold values from -4 to 4
- input_gate_weight: bfloat16 [2560, 256], P(('seq', 'wt')), may hold values from -0.375 to 0.375
- input_bias: bfloat16 [2560], P(('seq', 'wt')), may hold values from -4 to 4
- decay_param: float32 [2560], P(('seq', 'wt'))
- out_weight: bfloat16 [2560, 2560], P('seq', 'wt'), may hold values from -0.125 to 0.125
- norm2_gain: bfloat16 [2560], P(('seq', 'wt')), may hold values from 0.5 to 1.5
- gate_weight: bfloat16 [2560, 7680], P('seq', 'wt'), may hold values from -0.125 to 0.125
- up_weight: bfloat16 [2560, 7680], P('seq', 'wt'), may hold values from -0.125 to 0.125
- down_weight: bfloat16 [2560, 7680], P('seq', 'wt'), may hold values from -0.0625 to 0.0625
- out_grad: bfloat16 [4096, 2560], P(('seq', 'wt')), may hold values from -6 to 6
Outputs:
- block_out: bfloat16 [4096, 2560], P(('seq', 'wt'))
- tokens_grad: bfloat16 [4096, 2560], P(('seq', 'wt'))
- norm1_gain_grad: float32 [2560], P(('seq', 'wt'))
- x_weight_grad: float32 [2560, 2560], P('seq', 'wt')
- y_weight_grad: float32 [2560, 2560], P('seq', 'wt')
- conv_weight_grad: float32 [2560, 4], P(('seq', 'wt'))
- conv_bias_grad: float32 [2560], P(('seq', 'wt'))
- decay_gate_weight_grad: float32 [2560, 256], P(('seq', 'wt'))
- decay_bias_grad: float32 [2560], P(('seq', 'wt'))
- input_gate_weight_grad: float32 [2560, 256], P(('seq', 'wt'))
- input_bias_grad: float32 [2560], P(('seq', 'wt'))
- decay_param_grad: float32 [2560], P(('seq', 'wt'))
- out_weight_grad: float32 [2560, 2560], P('seq', 'wt')
- norm2_gain_grad: float32 [2560], P(('seq', 'wt'))
- gate_weight_grad: float32 [2560, 7680], P('seq', 'wt')
- up_weight_grad: float32 [2560, 7680], P('seq', 'wt')
- down_weight_grad: float32 [2560, 7680], P('seq', 'wt')
The draws below stay inside these ranges and needn't reach their ends.
All inputs are finite; a program needn't handle non-finite values.
Results may differ from the reference program's by a relative error of at most 0.0109.
Values may be sent and summed in bfloat16 or wider, within the bound.
A program may use at most 256 MiB of HBM per device.

```python
import math
import jax
import jax.numpy as jnp
from jax import lax

D = 2560
L = 2560
F = 7680
HEADS = 10
CONV = 4
BLOCK = 256
TOKENS = 4096


def draw_tokens(key, part):
    key = jax.random.fold_in(key, 11)
    first_key = jax.random.fold_in(key, 0)
    position = jnp.arange(TOKENS, dtype=jnp.float32) / max(TOKENS - 1, 1)
    rising = 3.0 ** position
    values = jax.random.normal(first_key, (TOKENS, D), jnp.float32)
    return (values * rising[:, None]).astype(jnp.bfloat16)


def draw_decay_param(key, part):
    key = jax.random.fold_in(key, 23)
    pick_key, slow_key, fast_key = jax.random.split(key, 3)
    share = 0.5
    slow_rate = jnp.exp(jax.random.uniform(slow_key, (L,), jnp.float32, math.log(0.02 / TOKENS), math.log(0.5 / TOKENS)))
    fast_rate = jnp.exp(jax.random.uniform(fast_key, (L,), jnp.float32, math.log(0.003), math.log(0.03)))
    chosen = jnp.where(jax.random.uniform(pick_key, (L,), jnp.float32) < share, slow_rate, fast_rate)
    return (-jnp.log(jnp.expm1(chosen))).astype(jnp.float32)


def levels(stream_key, extent, cuts, least, top_value):
    level = 1.0
    for axis_at, parts in cuts:
        heights = jax.random.uniform(jax.random.fold_in(jax.random.fold_in(stream_key, 6), axis_at), (parts,), jnp.float32, least / len(cuts), top_value / len(cuts))
        level = level * jnp.repeat(jnp.exp(heights), extent[axis_at] // parts).reshape((-1,) + (1,) * (len(extent) - 1 - axis_at))
    return level


def noise(stream_key, shape, scale, most, cuts=(), held_as=jnp.bfloat16):
    drawn = scale * jax.random.normal(stream_key, shape, jnp.float32)
    if cuts:
        drawn = drawn * levels(stream_key, shape, cuts, -0.22, 0.18)
    return jnp.clip(drawn, -most, most).astype(held_as)


def setup_inputs(seed: int = 0) -> dict:
    seeds = jax.random.split(jax.random.key(seed), 18)
    tokens = draw_tokens(jax.random.fold_in(seeds[17], 71), 0)
    norm1_gain = jnp.clip(1.0 + 0.1 * jax.random.normal(seeds[1], (D,), jnp.float32), 0.5, 1.5).astype(jnp.bfloat16)
    x_weight = noise(seeds[2], (D, L), D ** -0.5, 0.125, ((0, 8), (1, 4)))
    y_weight = noise(seeds[3], (D, L), D ** -0.5, 0.125, ((0, 8), (1, 4)))
    conv_weight = noise(seeds[4], (L, CONV), 0.5, 3.0, ((0, 32),))
    conv_bias = noise(seeds[5], (L,), 0.3, 2.0, ((0, 32),))
    decay_gate_weight = noise(seeds[6], (L, BLOCK), BLOCK ** -0.5, 0.375, ((0, 32),))
    decay_bias = noise(seeds[7], (L,), 1.0, 4.0, ((0, 32),))
    input_gate_weight = noise(seeds[8], (L, BLOCK), BLOCK ** -0.5, 0.375, ((0, 32),))
    input_bias = noise(seeds[9], (L,), 1.0, 4.0, ((0, 32),))
    decay_param = draw_decay_param(jax.random.fold_in(seeds[17], 71), 0)
    out_weight = noise(seeds[11], (D, L), L ** -0.5, 0.125, ((0, 8), (1, 4)))
    norm2_gain = jnp.clip(1.0 + 0.1 * jax.random.normal(seeds[12], (D,), jnp.float32), 0.5, 1.5).astype(jnp.bfloat16)
    gate_weight = noise(seeds[13], (D, F), D ** -0.5, 0.125, ((0, 8), (1, 4)))
    up_weight = noise(seeds[14], (D, F), D ** -0.5, 0.125, ((0, 8), (1, 4)))
    down_weight = noise(seeds[15], (D, F), F ** -0.5, 0.0625, ((0, 8), (1, 4)))
    out_grad = noise(seeds[16], (TOKENS, D), 1.0, 6.0, ((0, 32),))
    return dict(tokens=tokens, norm1_gain=norm1_gain, x_weight=x_weight, y_weight=y_weight, conv_weight=conv_weight, conv_bias=conv_bias, decay_gate_weight=decay_gate_weight, decay_bias=decay_bias, input_gate_weight=input_gate_weight, input_bias=input_bias, decay_param=decay_param, out_weight=out_weight, norm2_gain=norm2_gain, gate_weight=gate_weight, up_weight=up_weight, down_weight=down_weight, out_grad=out_grad)


@jax.custom_vjp
def low(v):
    return lax.optimization_barrier(v.astype(jnp.bfloat16)).astype(jnp.float32)

@jax.custom_vjp
def low_back(v):
    return v

def low_keep(v):
    return (low(v), None)

def low_pass(kept, grad):
    return (grad,)

def back_keep(v):
    return (v, None)

def back_low(kept, grad):
    return (low(grad),)
low.defvjp(low_keep, low_pass)
low_back.defvjp(back_keep, back_low)
EPSILON = 1e-06
DECAY_SCALE = 8.0
PRECISE = lax.Precision.HIGHEST

def gelu_tanh(values):
    return jax.nn.gelu(values, approximate=True)

def rms_scaled(values, gain_row):
    return values * lax.rsqrt(lax.optimization_barrier(jnp.mean(values * values, axis=1, keepdims=True)) + EPSILON) * gain_row

def product(left_side, right_side):
    return jnp.dot(left_side, right_side, precision=PRECISE)

def compose(earlier, following):
    return (earlier[0] * following[0], following[0] * earlier[1] + following[1])

def scan_block(carried, pieces):
    running = lax.associative_scan(compose, pieces, axis=0)
    states = running[1] + running[0] * carried[None, :]
    return (states[-1], states)

def block_diagonal(values, weight_rows):
    head_view = values.reshape(values.shape[0], HEADS, L // HEADS)
    blocks = weight_rows.reshape(HEADS, L // HEADS, L // HEADS)
    return jnp.einsum('thi,hij->thj', head_view, blocks, precision=PRECISE).reshape(values.shape[0], L)

def forward(stream, norm1_gain, x_weight, y_weight, conv_weight, conv_bias, decay_gate_weight, decay_bias, input_gate_weight, input_bias, decay_param, out_weight, norm2_gain, gate_weight, up_weight, down_weight):
    h_one = low(rms_scaled(stream, norm1_gain))
    x_branch = low_back(low(product(h_one, x_weight)))
    y_gated = gelu_tanh(low_back(product(h_one, y_weight)))
    padded = jnp.concatenate([jnp.zeros((CONV - 1, L), jnp.float32), x_branch], axis=0)
    conv_out = conv_bias
    for offset in range(CONV):
        conv_out = conv_out + conv_weight[:, offset] * padded[CONV - 1 - offset:CONV - 1 - offset + TOKENS]
    conv_low = low(conv_out)
    decay_pre = low_back(block_diagonal(conv_low, decay_gate_weight)) + decay_bias
    input_pre = low_back(block_diagonal(conv_low, input_gate_weight)) + input_bias
    log_decay = -DECAY_SCALE * jax.nn.softplus(-decay_param) * jax.nn.sigmoid(decay_pre)
    retain = jnp.exp(log_decay)
    inflow = jnp.sqrt(-jnp.expm1(2.0 * log_decay)) * jax.nn.sigmoid(input_pre) * conv_low
    block_rows = math.gcd(TOKENS, 512)
    block_count = TOKENS // block_rows
    final_state, states = lax.scan(jax.checkpoint(scan_block), jnp.zeros((L,), jnp.float32), (retain.reshape(block_count, block_rows, L), inflow.reshape(block_count, block_rows, L)))
    lru_out = low_back(low(states.reshape(TOKENS, L)))
    mixed_rows = low(lru_out * y_gated)
    middle = stream + low_back(product(mixed_rows, out_weight.T))
    h_two = low(rms_scaled(middle, norm2_gain))
    gate_pre = low_back(product(h_two, gate_weight))
    up_pre = low_back(product(h_two, up_weight))
    hidden = low(gelu_tanh(gate_pre) * up_pre)
    return middle + product(hidden, down_weight.T)

def as_float(values):
    return values.astype(jnp.float32)

def reference(tokens, norm1_gain, x_weight, y_weight, conv_weight, conv_bias, decay_gate_weight, decay_bias, input_gate_weight, input_bias, decay_param, out_weight, norm2_gain, gate_weight, up_weight, down_weight, out_grad):
    block_out, pullback = jax.vjp(forward, as_float(tokens), as_float(norm1_gain), as_float(x_weight), as_float(y_weight), as_float(conv_weight), as_float(conv_bias), as_float(decay_gate_weight), as_float(decay_bias), as_float(input_gate_weight), as_float(input_bias), as_float(decay_param), as_float(out_weight), as_float(norm2_gain), as_float(gate_weight), as_float(up_weight), as_float(down_weight))
    grads = pullback(as_float(out_grad))
    return (block_out.astype(jnp.bfloat16), grads[0].astype(jnp.bfloat16), grads[1], grads[2], grads[3], grads[4], grads[5], grads[6], grads[7], grads[8], grads[9], grads[10], grads[11], grads[12], grads[13], grads[14], grads[15])
```

```python
import functools

import jax
import jax.numpy as jnp
from jax import lax
from jax.experimental import pallas as pl
from jax.experimental.pallas import tpu as pltpu
from jax.sharding import PartitionSpec as P

EPSILON = 1e-06
DECAY_SCALE = 8.0
Z = 4
C = 2
LANES = 128
F32 = jnp.float32
BF16 = jnp.bfloat16


def gelu_tanh(values):
    return jax.nn.gelu(values, approximate=True)


def sizes():
    return lax.axis_size("seq") // Z, lax.axis_size("wt") // C


def places():
    inner, outer = sizes()
    s, w = lax.axis_index("seq"), lax.axis_index("wt")
    return s // inner, s % inner, w // C, w % C


def after(value, *earlier):
    return lax.optimization_barrier((value, *earlier))[0]


def z_move(value, by, senders):
    inner, _ = sizes()
    pairs = [(z * inner + x, (z + by) % Z * inner + x) for z in senders for x in range(inner)]
    return lax.ppermute(value, "seq", pairs)


def x_move(value, by):
    inner, _ = sizes()
    pairs = [(z * inner + x, z * inner + (x + by) % inner) for z in range(Z) for x in range(inner)]
    return lax.ppermute(value, "seq", pairs)


def y_move(value, by):
    _, outer = sizes()
    pairs = [(y * C + c, (y + by) % outer * C + c) for y in range(outer) for c in range(C)]
    return lax.ppermute(value, "wt", pairs)


def c_swap(value):
    _, outer = sizes()
    pairs = [(y * C + c, y * C + 1 - c) for y in range(outer) for c in range(C)]
    return lax.ppermute(value, "wt", pairs)


def line_gather(value):
    z = places()[0]
    up, down = [value], [value]
    for k in range(1, Z):
        up.append(z_move(up[-1], 1, range(k - 1, Z - 1)))
        down.append(z_move(down[-1], -1, range(1, Z - k + 1)))
    return [value] + [jnp.where(z >= k, up[k], down[Z - k]) for k in range(1, Z)]


def line_scatter(parts):
    up = down = None
    for step in range(1, Z):
        rising = parts[step] if up is None else parts[step] + up
        falling = parts[Z - step] if down is None else parts[Z - step] + down
        up = z_move(rising.astype(BF16), 1, range(0, step)).astype(F32)
        down = z_move(falling.astype(BF16), -1, range(Z - step, Z)).astype(F32)
    return parts[0] + up + down


def pick(value, index, axis):
    return lax.dynamic_index_in_dim(value, index, axis, keepdims=False)


def put(buffer, value, starts):
    return lax.dynamic_update_slice(buffer, value, starts)


def contract_last(left_side, right_side):
    return lax.dot_general(
        left_side, right_side, (((1,), (1,)), ((), ())), preferred_element_type=F32
    )


def contract_rows(left_side, right_side):
    return lax.dot_general(
        left_side, right_side, (((0,), (0,)), ((), ())), preferred_element_type=F32
    )


def multiply(left_side, right_side):
    return jnp.dot(left_side, right_side, preferred_element_type=F32)


def seq_gather(unit):
    inner, _ = sizes()
    z, x = places()[:2]
    blocks = []
    for k, block in enumerate(line_gather(unit)):
        blocks.append(((z - k) % Z, x, block))
        for j in range(1, inner):
            blocks.append(((z - k) % Z, (x - j) % inner, x_move(block, j)))
    return blocks


def assembled(blocks, rows):
    inner, _ = sizes()
    width = blocks[0][2].shape[1]
    buffer = jnp.zeros((Z, inner, rows.stop - rows.start, width), blocks[0][2].dtype)
    for z_at, x_at, block in blocks:
        buffer = put(buffer, block[rows][None, None], (z_at, x_at, 0, 0))
    return buffer


def seq_scatter(total):
    inner, _ = sizes()
    z, x = places()[:2]
    total = total.reshape(Z, inner, -1, total.shape[1])
    kept = pick(total, x, 1)
    for j in range(1, inner):
        kept = kept + x_move(pick(total, (x + j) % inner, 1).astype(BF16), j).astype(F32)
    return line_scatter([pick(kept, (z - k) % Z, 0) for k in range(Z)])


def z_exchange(weight):
    z = places()[0]
    rows, width = weight.shape
    share = -(-width // (Z * LANES)) * LANES
    padded = jnp.pad(weight, ((0, 0), (0, Z * share - width)))

    def cut(at):
        return lax.dynamic_slice(padded, (0, at * share), (rows, share))

    buffer = put(jnp.zeros((Z, rows, share), weight.dtype), cut(z)[None], (z, 0, 0))
    for k in range(1, Z):
        moved = z_move(cut((z + k) % Z), k, range(Z))
        buffer = put(buffer, moved[None], ((z - k) % Z, 0, 0))
    return buffer


def plane_gather(unit, x_first):
    inner, outer = sizes()
    x = places()[1]
    _, rows, share = unit.shape
    grid = {(0, 0): unit}
    if x_first:
        for j in range(1, inner):
            grid[j, 0] = x_move(unit, j)
        for j in range(inner):
            for i in range(1, outer):
                grid[j, i] = y_move(grid[j, 0], i)
    else:
        for i in range(1, outer):
            grid[0, i] = y_move(unit, i)
        for i in range(outer):
            for j in range(1, inner):
                grid[j, i] = x_move(grid[0, i], j)
    buffer = jnp.zeros((Z, inner, rows, outer * share), unit.dtype)
    for (j, i), block in grid.items():
        buffer = put(buffer, block[:, None], (0, (x - j) % inner, 0, i * share))
    return buffer.reshape(Z * inner * rows, outer * share)


def plane_scatter(total, width, x_first):
    inner, outer = sizes()
    z, x = places()[:2]
    share = total.shape[1] // outer
    total = total.reshape(Z, inner, -1, outer * share)
    rows = total.shape[2]

    def over_x(value):
        kept = pick(value, x, 1)
        for j in range(1, inner):
            kept = kept + x_move(pick(value, (x + j) % inner, 1).astype(BF16), j).astype(F32)
        return kept

    def over_y(value):
        kept = value[..., :share]
        for i in range(1, outer):
            sent = value[..., i * share : (i + 1) * share].astype(BF16)
            kept = kept + y_move(sent, -i).astype(F32)
        return kept

    kept = over_y(over_x(total)) if x_first else over_x(over_y(total))
    kept = kept.astype(BF16)
    buffer = put(jnp.zeros((rows, Z * share), BF16), pick(kept, z, 0), (0, z * share))
    for k in range(1, Z):
        moved = z_move(pick(kept, (z + k) % Z, 0), k, range(Z))
        buffer = put(buffer, moved, (0, (z - k) % Z * share))
    return buffer[:, :width].astype(F32)


def wt_gather(value):
    _, outer = sizes()
    _, _, y, c = places()
    rows, width = value.shape
    other = c_swap(value)
    pair = jnp.where(
        c == 0, jnp.concatenate([value, other]), jnp.concatenate([other, value])
    )
    buffer = put(jnp.zeros((outer, C * rows, width), value.dtype), pair[None], (y, 0, 0))
    for i in range(1, outer):
        buffer = put(buffer, y_move(pair, i)[None], ((y - i) % outer, 0, 0))
    return buffer.reshape(outer * C * rows, width)


def wt_scatter(product_of, *sides):
    _, outer = sizes()
    _, _, y, c = places()

    def chosen(at):
        cut = [side.reshape(outer, C, -1, side.shape[1]) for side in sides]
        return [pick(side, at, 1).reshape(-1, side.shape[3]) for side in cut]

    sent = c_swap(product_of(*chosen(1 - c)))
    kept = product_of(*chosen(c)) + sent
    kept = kept.reshape(outer, -1, kept.shape[1])
    total = pick(kept, y, 0)
    for i in range(1, outer):
        total = total + y_move(pick(kept, (y + i) % outer, 0).astype(BF16), i).astype(F32)
    return total


def group_gather(value):
    blocks = line_gather(value)
    return jnp.concatenate(blocks + [c_swap(block) for block in blocks])


def group_scatter(product_of, *sides):
    half = sides[0].shape[0] // 2
    sent = c_swap(product_of(*[side[half:] for side in sides]).astype(BF16))
    kept = product_of(*[side[:half] for side in sides]) + sent.astype(F32)
    rows = half // Z
    return line_scatter([kept[k * rows : (k + 1) * rows] for k in range(Z)])


def scan_kernel(backward, a_ref, b_ref, h_ref, p_ref):
    rows, width = a_ref.shape
    segments = 8
    length = rows // segments

    def step(i, carried):
        held, product = carried
        at = length - 1 - i if backward else i
        where = pl.ds(at, segments, stride=length)
        factor = a_ref[where, :]
        held = factor * held + b_ref[where, :]
        product = factor * product
        h_ref[where, :] = held
        p_ref[where, :] = product
        return held, product

    held, product = lax.fori_loop(
        0, length, step, (jnp.zeros((segments, width), F32), jnp.ones((segments, width), F32)),
        unroll=4,
    )
    carry = jnp.zeros((1, width), F32)
    scale = jnp.ones((1, width), F32)
    order = range(segments - 1, -1, -1) if backward else range(segments)
    for at in order:
        if at != order[0]:
            part = pl.ds(at * length, length)
            local = p_ref[part, :]
            h_ref[part, :] = h_ref[part, :] + local * carry
            p_ref[part, :] = local * scale
        carry = held[at : at + 1] + product[at : at + 1] * carry
        scale = product[at : at + 1] * scale


def local_scan(factor, inflow, backward):
    shape = jax.ShapeDtypeStruct(factor.shape, F32)
    column = pl.BlockSpec((factor.shape[0], LANES), lambda i: (0, i))
    return pl.pallas_call(
        functools.partial(scan_kernel, backward),
        out_shape=(shape, shape),
        grid=(factor.shape[1] // LANES,),
        in_specs=[column] * 2,
        out_specs=(column,) * 2,
        name="scan_back" if backward else "scan_ahead",
    )(factor, inflow)


def full_scan(factor, inflow, backward):
    count = lax.axis_size("seq")
    held, product = local_scan(factor, inflow, backward)
    end = slice(0, 1) if backward else slice(held.shape[0] - 1, None)
    ends = jnp.concatenate([product[end], held[end]])
    sign = -1 if backward else 1
    carry = jnp.zeros_like(held[:1])
    for k in range(count - 1, 0, -1):
        pairs = [(s, s + sign * k) for s in range(count) if 0 <= s + sign * k < count]
        moved = lax.ppermute(ends, "seq", pairs)
        carry = moved[:1] * carry + moved[1:]
    return held + product * carry, carry


def recurrence_terms(decay_pre, input_pre, decay_log, conv_float):
    log_decay = -DECAY_SCALE * jax.nn.softplus(-decay_log) * jax.nn.sigmoid(decay_pre)
    return (
        jnp.exp(log_decay),
        jnp.sqrt(-jnp.expm1(2.0 * log_decay)) * jax.nn.sigmoid(input_pre) * conv_float,
    )


def norm_back(d_normed, normed, inverse, gain_row):
    scaled = d_normed * gain_row
    return inverse * (scaled - normed * jnp.mean(scaled * normed, axis=1, keepdims=True))


def normed_rows(stream):
    inverse = lax.rsqrt(jnp.mean(stream * stream, axis=1, keepdims=True) + EPSILON)
    return stream * inverse, inverse


def per_device(
    tokens,
    norm1_gain,
    x_weight,
    y_weight,
    conv_weight,
    conv_bias,
    decay_gate_weight,
    decay_bias,
    input_gate_weight,
    input_bias,
    decay_param,
    out_weight,
    norm2_gain,
    gate_weight,
    up_weight,
    down_weight,
    out_grad,
):
    seq, wt = lax.axis_size("seq"), lax.axis_size("wt")
    inner, outer = sizes()
    z, x, y, c = places()
    w = lax.axis_index("wt")
    rows_dev, width = tokens.shape
    weight_rows, lru_cols = x_weight.shape
    chunk, block = decay_gate_weight.shape
    half = block // 2
    full = lru_cols - half
    taps_count = conv_weight.shape[1]
    reach = taps_count - 1
    hidden_cols = gate_weight.shape[1]

    def turned(value, axis):
        return jnp.where(c == 0, value, jnp.roll(value, -half, axis))

    def turned_back(value, axis):
        return jnp.where(c == 0, value, jnp.roll(value, half, axis))

    def in_order(own, partner, axis):
        return jnp.where(
            c == 0,
            jnp.concatenate([own, partner], axis),
            jnp.concatenate([partner, own], axis),
        )

    vectors = jnp.stack(
        [v.astype(F32) for v in (norm1_gain, norm2_gain, conv_bias, decay_bias, input_bias)]
        + [decay_param]
        + [conv_weight[:, k].astype(F32) for k in range(taps_count)]
    )
    vectors = lax.all_gather(vectors, ("seq", "wt"), axis=1, tiled=True)
    gain_one, gain_two = vectors[0], vectors[1]
    own_vectors = turned(
        lax.dynamic_slice(vectors[2:], (0, w * lru_cols), (taps_count + 4, lru_cols)), 1
    )
    tap_bias, decay_shift, input_shift, decay_log = (own_vectors[i] for i in range(4))
    taps = own_vectors[4:]

    across = [(i, i % seq * wt + i // seq) for i in range(seq * wt)]
    gates = jnp.concatenate([decay_gate_weight, input_gate_weight], axis=1)
    gates = lax.ppermute(gates, ("seq", "wt"), across)

    group_tokens = wt_gather(tokens)
    xy_unit = jnp.concatenate([turned(x_weight, 1), turned(y_weight, 1)], axis=1)
    gate_rows = chunk * 2 * block // xy_unit.shape[1]
    xy_unit = jnp.concatenate([xy_unit, gates.reshape(gate_rows, xy_unit.shape[1])])
    xy_blocks = seq_gather(xy_unit)
    xy_kernel = assembled(xy_blocks, slice(0, weight_rows)).reshape(width, 2 * lru_cols)
    gate_all = assembled(xy_blocks, slice(weight_rows, weight_rows + gate_rows))
    gate_all = turned(gate_all.reshape(lru_cols, 2 * block), 0)
    partner_rows = c_swap(gate_all[full:])
    shared_rows = in_order(gate_all[full:], partner_rows, 0)

    gate_unit = z_exchange(gate_weight)
    gate_kernel = plane_gather(gate_unit, True)
    up_unit = z_exchange(up_weight)
    up_kernel = plane_gather(up_unit, False)
    out_kernel = assembled(seq_gather(turned(out_weight, 1)), slice(0, weight_rows))
    out_kernel = out_kernel.reshape(width, lru_cols)
    down_unit = z_exchange(down_weight)
    down_kernel = plane_gather(down_unit, True)
    grad_group = group_gather(out_grad)

    stream = tokens.astype(F32)
    group_normed, _ = normed_rows(group_tokens.astype(F32))
    group_one = (group_normed * gain_one).astype(BF16)
    rows = group_one.shape[0]
    xy = multiply(group_one, xy_kernel)
    x_branch = xy[:, :lru_cols].astype(BF16)
    y_before = xy[:, lru_cols:]
    y_gated, gelu_y_back = jax.vjp(gelu_tanh, y_before)
    rim = lax.ppermute(x_branch[rows - reach :], "seq", [(i, i + 1) for i in range(seq - 1)])
    extended = jnp.concatenate([rim, x_branch], axis=0).astype(F32)
    conv_low = (
        tap_bias
        + sum(taps[k] * extended[reach - k : reach - k + rows] for k in range(taps_count))
    ).astype(BF16)
    shared_conv = in_order(conv_low[:, full:], c_swap(conv_low[:, full:]), 1)
    heads = full // block

    def of_head(value, i):
        return value[:, i * block : (i + 1) * block]

    pre_parts = [
        multiply(of_head(conv_low, i), gate_all[i * block : (i + 1) * block]) for i in range(heads)
    ]
    shared_pre = multiply(shared_conv, shared_rows).reshape(rows, 2, C, half)
    shared_pre = pick(shared_pre, c, 2)
    decay_pre = decay_shift + jnp.concatenate(
        [part[:, :block] for part in pre_parts] + [shared_pre[:, 0]], axis=1
    )
    input_pre = input_shift + jnp.concatenate(
        [part[:, block:] for part in pre_parts] + [shared_pre[:, 1]], axis=1
    )
    (retain, inflow), terms_back = jax.vjp(
        recurrence_terms, decay_pre, input_pre, decay_log, conv_low.astype(F32)
    )
    states, state_in = full_scan(retain, inflow, False)
    before = jnp.concatenate([state_in, states[:-1]])
    lru_low = states.astype(BF16).astype(F32)
    mixed_rows = (lru_low * y_gated).astype(BF16)
    branch = wt_scatter(lambda rows_: contract_last(rows_, out_kernel), mixed_rows)
    middle = stream + branch

    normed_two, inverse_two = normed_rows(middle)
    group_two = group_gather((normed_two * gain_two).astype(BF16))
    gate_pre = multiply(group_two, gate_kernel)
    up_pre = multiply(group_two, up_kernel)
    active, gelu_gate_back = jax.vjp(gelu_tanh, gate_pre)
    hidden = (active * up_pre).astype(BF16)

    d_hidden = multiply(grad_group, down_kernel)
    d_up = (d_hidden * active).astype(BF16)
    d_gate = gelu_gate_back(d_hidden * up_pre)[0].astype(BF16)
    d_normed_two = group_scatter(
        lambda g, u: contract_last(g, gate_kernel) + contract_last(u, up_kernel), d_gate, d_up
    )
    feed = group_scatter(lambda rows_: contract_last(rows_, down_kernel), hidden)
    block_out = (middle + feed).astype(BF16)
    down_grad = plane_scatter(contract_rows(grad_group, hidden), hidden_cols, True)
    gate_grad = plane_scatter(contract_rows(group_two, d_gate), hidden_cols, False)
    up_grad = plane_scatter(contract_rows(group_two, d_up), hidden_cols, True)
    gain_two_grad = jnp.sum(d_normed_two * normed_two, axis=0)
    d_middle = out_grad.astype(F32) + norm_back(d_normed_two, normed_two, inverse_two, gain_two)

    branch_rows = wt_gather(d_middle.astype(BF16))
    d_mixed = multiply(branch_rows, out_kernel)
    d_lru = (d_mixed * y_gated).astype(BF16).astype(F32)
    d_y = gelu_y_back(d_mixed * lru_low)[0].astype(BF16)
    passed, passed_in = full_scan(retain, retain * d_lru, True)
    d_total = d_lru + jnp.concatenate([passed[1:], passed_in])
    d_decay_pre, d_input_pre, decay_log_grad, d_conv_direct = terms_back(
        (d_total * before, d_total)
    )
    d_decay_low, d_input_low = d_decay_pre.astype(BF16), d_input_pre.astype(BF16)
    own_low = jnp.concatenate([d_decay_low[:, full:], d_input_low[:, full:]], axis=1)
    partner_low = c_swap(own_low)
    shared_low = jnp.concatenate(
        [
            in_order(own_low[:, :half], partner_low[:, :half], 1),
            in_order(own_low[:, half:], partner_low[:, half:], 1),
        ],
        axis=1,
    )
    lows = [
        jnp.concatenate([of_head(d_decay_low, i), of_head(d_input_low, i)], axis=1)
        for i in range(heads)
    ]
    d_conv = d_conv_direct + jnp.concatenate(
        [contract_last(lows[i], gate_all[i * block : (i + 1) * block]) for i in range(heads)]
        + [contract_last(shared_low, gate_all[full:])],
        axis=1,
    )
    gates_grad = jnp.concatenate(
        [contract_rows(of_head(conv_low, i), lows[i]) for i in range(heads)]
        + [contract_rows(conv_low[:, full:], shared_low)]
    )
    ahead = lax.ppermute(d_conv[:reach], "seq", [(i + 1, i) for i in range(seq - 1)])
    d_extended = jnp.concatenate([d_conv, ahead], axis=0)
    d_x_branch = sum(taps[k] * d_extended[k : k + rows] for k in range(taps_count)).astype(BF16)
    d_normed_one = wt_scatter(
        lambda dx, dy: contract_last(dx, xy_kernel[:, :lru_cols])
        + contract_last(dy, xy_kernel[:, lru_cols:]),
        d_x_branch,
        d_y,
    )
    normed_one, inverse_one = normed_rows(stream)
    gain_one_grad = jnp.sum(d_normed_one * normed_one, axis=0)
    tokens_grad = (d_middle + norm_back(d_normed_one, normed_one, inverse_one, gain_one)).astype(
        BF16
    )

    out_weight_grad = turned_back(seq_scatter(contract_rows(branch_rows, mixed_rows)), 1)
    y_weight_grad = turned_back(seq_scatter(contract_rows(group_one, d_y)), 1)
    x_weight_grad = turned_back(seq_scatter(contract_rows(group_one, d_x_branch)), 1)
    own_sums = jnp.stack(
        [jnp.sum(d_conv, axis=0), jnp.sum(d_decay_pre, axis=0), jnp.sum(d_input_pre, axis=0)]
        + [decay_log_grad]
        + [jnp.sum(d_conv * extended[reach - k : reach - k + rows], axis=0) for k in range(taps_count)],
        axis=1,
    )
    own_sums = jnp.concatenate([turned_back(gates_grad, 0), turned_back(own_sums, 0)], axis=1)
    own_sums = lax.psum_scatter(own_sums, "seq", scatter_dimension=0, tiled=True)
    own_sums = lax.ppermute(own_sums, ("seq", "wt"), [(to, at) for at, to in across])
    gains = lax.psum_scatter(
        jnp.stack([gain_one_grad, gain_two_grad], axis=1),
        ("seq", "wt"),
        scatter_dimension=0,
        tiled=True,
    )
    sums = own_sums[:, 2 * block :]
    return (
        block_out,
        tokens_grad,
        gains[:, 0],
        x_weight_grad,
        y_weight_grad,
        sums[:, 4:],
        sums[:, 0],
        own_sums[:, :block],
        sums[:, 1],
        own_sums[:, block : 2 * block],
        sums[:, 2],
        sums[:, 3],
        out_weight_grad,
        gains[:, 1],
        gate_grad,
        up_grad,
        down_grad,
    )


def solution(mesh):
    rows, both, lone = P(("seq", "wt"), None), P("seq", "wt"), P(("seq", "wt"))
    in_specs = (
        rows, lone, both, both, rows, lone, rows, lone, rows, lone, lone,
        both, lone, both, both, both, rows,
    )
    out_specs = (
        rows, rows, lone, both, both, rows, lone, rows, lone, rows, lone, lone,
        both, lone, both, both, both,
    )
    return jax.shard_map(
        per_device, mesh=mesh, in_specs=in_specs, out_specs=out_specs, check_vma=False
    )
```

```python
import functools

import jax
import jax.numpy as jnp
from jax import lax
from jax.experimental import pallas as pl
from jax.experimental.pallas import tpu as pltpu
from jax.sharding import PartitionSpec as P

EPSILON = 1e-06
DECAY_SCALE = 8.0
Z = 4
C = 2
LANES = 128
F32 = jnp.float32
BF16 = jnp.bfloat16
MESH = pl.DeviceIdType.MESH


def gelu_tanh(values):
    return jax.nn.gelu(values, approximate=True)


def sizes():
    return lax.axis_size("seq") // Z, lax.axis_size("wt") // C


def places():
    inner, outer = sizes()
    s, w = lax.axis_index("seq"), lax.axis_index("wt")
    return s // inner, s % inner, w // C, w % C


def after(value, *earlier):
    return lax.optimization_barrier((value, *earlier))[0]


def z_move(value, by, senders):
    inner, _ = sizes()
    pairs = [(z * inner + x, (z + by) % Z * inner + x) for z in senders for x in range(inner)]
    return lax.ppermute(value, "seq", pairs)


def z_turn(value, by):
    return z_move(value, by, range(Z))


def x_move(value, by):
    inner, _ = sizes()
    pairs = [(z * inner + x, z * inner + (x + by) % inner) for z in range(Z) for x in range(inner)]
    return lax.ppermute(value, "seq", pairs)


def y_move(value, by):
    _, outer = sizes()
    pairs = [(y * C + c, (y + by) % outer * C + c) for y in range(outer) for c in range(C)]
    return lax.ppermute(value, "wt", pairs)


def c_swap(value):
    _, outer = sizes()
    pairs = [(y * C + c, y * C + 1 - c) for y in range(outer) for c in range(C)]
    return lax.ppermute(value, "wt", pairs)


def line_gather(value):
    z = places()[0]
    up, down = [value], [value]
    for k in range(1, Z):
        up.append(z_move(up[-1], 1, range(k - 1, Z - 1)))
        down.append(z_move(down[-1], -1, range(1, Z - k + 1)))
    return [value] + [jnp.where(z >= k, up[k], down[Z - k]) for k in range(1, Z)]


def line_scatter(parts):
    up = down = None
    for step in range(1, Z):
        rising = parts[step] if up is None else parts[step] + up
        falling = parts[Z - step] if down is None else parts[Z - step] + down
        up = z_move(rising.astype(BF16), 1, range(0, step)).astype(F32)
        down = z_move(falling.astype(BF16), -1, range(Z - step, Z)).astype(F32)
    return parts[0] + up + down


def pick(value, index, axis):
    return lax.dynamic_index_in_dim(value, index, axis, keepdims=False)


def put(buffer, value, starts):
    return lax.dynamic_update_slice(buffer, value, starts)


def contract_last(left_side, right_side):
    return lax.dot_general(
        left_side, right_side, (((1,), (1,)), ((), ())), preferred_element_type=F32
    )


def contract_rows(left_side, right_side):
    return lax.dot_general(
        left_side, right_side, (((0,), (0,)), ((), ())), preferred_element_type=F32
    )


def multiply(left_side, right_side):
    return jnp.dot(left_side, right_side, preferred_element_type=F32)


def seq_scatter(total):
    inner, _ = sizes()
    z, x = places()[:2]
    total = total.reshape(Z, inner, -1, total.shape[1])
    kept = pick(total, x, 1)
    for j in range(1, inner):
        kept = kept + x_move(pick(total, (x + j) % inner, 1).astype(BF16), j).astype(F32)
    return line_scatter([pick(kept, (z - k) % Z, 0) for k in range(Z)])


def plane_scatter(total, width, x_first):
    inner, outer = sizes()
    z, x = places()[:2]
    share = total.shape[1] // outer
    total = total.reshape(Z, inner, -1, outer * share)
    rows = total.shape[2]

    def over_x(value):
        kept = pick(value, x, 1)
        for j in range(1, inner):
            kept = kept + x_move(pick(value, (x + j) % inner, 1).astype(BF16), j).astype(F32)
        return kept

    def over_y(value):
        kept = value[..., :share]
        for i in range(1, outer):
            sent = value[..., i * share : (i + 1) * share].astype(BF16)
            kept = kept + y_move(sent, -i).astype(F32)
        return kept

    kept = over_y(over_x(total)) if x_first else over_x(over_y(total))
    kept = kept.astype(BF16)
    buffer = put(jnp.zeros((rows, Z * share), BF16), pick(kept, z, 0), (0, z * share))
    for k in range(1, Z):
        moved = z_move(pick(kept, (z + k) % Z, 0), k, range(Z))
        buffer = put(buffer, moved, (0, (z - k) % Z * share))
    return buffer[:, :width].astype(F32)


def wt_gather(value):
    _, outer = sizes()
    _, _, y, c = places()
    rows, width = value.shape
    other = c_swap(value)
    pair = jnp.where(
        c == 0, jnp.concatenate([value, other]), jnp.concatenate([other, value])
    )
    buffer = put(jnp.zeros((outer, C * rows, width), value.dtype), pair[None], (y, 0, 0))
    for i in range(1, outer):
        buffer = put(buffer, y_move(pair, i)[None], ((y - i) % outer, 0, 0))
    return buffer.reshape(outer * C * rows, width)


def wt_scatter(product_of, *sides):
    _, outer = sizes()
    _, _, y, c = places()

    def chosen(at):
        cut = [side.reshape(outer, C, -1, side.shape[1]) for side in sides]
        return [pick(side, at, 1).reshape(-1, side.shape[3]) for side in cut]

    sent = c_swap(product_of(*chosen(1 - c)))
    kept = product_of(*chosen(c)) + sent
    kept = kept.reshape(outer, -1, kept.shape[1])
    total = pick(kept, y, 0)
    for i in range(1, outer):
        total = total + y_move(pick(kept, (y + i) % outer, 0).astype(BF16), i).astype(F32)
    return total


def group_gather(value):
    blocks = line_gather(value)
    return jnp.concatenate(blocks + [c_swap(block) for block in blocks])


def group_scatter(product_of, *sides):
    half = sides[0].shape[0] // 2
    sent = c_swap(product_of(*[side[half:] for side in sides]).astype(BF16))
    kept = product_of(*[side[:half] for side in sides]) + sent.astype(F32)
    rows = half // Z
    return line_scatter([kept[k * rows : (k + 1) * rows] for k in range(Z)])


class Sends:
    def __init__(self, sems):
        self.sems, self.started = sems, []

    def start(self, when, source, target, arrival, device):
        copy = pltpu.make_async_remote_copy(
            src_ref=source,
            dst_ref=target,
            send_sem=self.sems.at[len(self.started)],
            recv_sem=arrival,
            device_id=device,
            device_id_type=MESH,
        )
        if when is True:
            copy.start()
        else:
            pl.when(when)(copy.start)
        self.started.append((when, copy))

    def finish(self):
        for when, copy in self.started:
            if when is True:
                copy.wait_send()
            else:
                pl.when(when)(copy.wait_send)


def arrived(target, arrival, device):
    pltpu.make_async_remote_copy(
        src_ref=target, dst_ref=target, send_sem=arrival, recv_sem=arrival,
        device_id=device, device_id_type=MESH,
    ).wait_recv()


def gather_kernel(shape, *refs):
    inner, outer = shape
    (tokens, grads, vectors, gates, xy, out, gate, up, down) = refs[:9]
    (tokens_to, grads_to, vectors_to, gates_to, xy_to, out_to, gate_to, up_to, down_to) = refs[9:18]
    send_sems, local_sems, line_sems, plane_sems, rows_sems, grads_sems, vector_sems = refs[18:]
    seq, wt = Z * inner, outer * C
    s, w = lax.axis_index("seq"), lax.axis_index("wt")
    z, x, y, c = s // inner, s % inner, w // C, w % C
    sends = Sends(send_sems)
    here = []

    def at_z(to):
        return {"seq": to * inner + x, "wt": w}

    def at_x(by):
        return {"seq": z * inner + (x + by) % inner, "wt": w}

    def at_y(by):
        return {"seq": s, "wt": (y + by) % outer * C + c}

    at_c = {"seq": s, "wt": y * C + 1 - c}

    def keep(source, target, waited=False):
        copy = pltpu.make_async_copy(source, target, local_sems.at[len(here)])
        copy.start()
        here.append((waited, copy))
        return copy

    barrier = pltpu.get_barrier_semaphore()

    def greet(i, carried):
        @pl.when(i != s * wt + w)
        def _():
            pl.semaphore_signal(
                barrier, inc=1, device_id={"seq": i // wt, "wt": i % wt}, device_id_type=MESH
            )

        return carried

    lax.fori_loop(0, seq * wt, greet, 0)
    pl.semaphore_wait(barrier, seq * wt - 1)

    class Line:
        def __init__(self, index, source, target):
            self.source, self.target = source, target
            self.sems = line_sems.at[index]

        def forward(self, block, at, up_when, down_when):
            place = self.target.at[at, x]
            arrival = self.sems.at[at, x]
            sends.start(up_when, block, place, arrival, at_z(jnp.minimum(z + 1, Z - 1)))
            sends.start(down_when, block, place, arrival, at_z(jnp.maximum(z - 1, 0)))
            return place, arrival

        def across(self, when, block, at):
            for j in range(1, inner):
                sends.start(when, block, self.target.at[at, x], self.sems.at[at, x], at_x(j))

        def begin(self):
            keep(self.source, self.target.at[z, x])
            self.forward(self.source, z, z < Z - 1, z > 0)
            self.across(True, self.source, z)

        def step(self, k):
            for at, there, up_when, down_when in (
                (jnp.maximum(z - k, 0), z - k >= 0, (z - k >= 0) & (z < Z - 1), None),
                (jnp.minimum(z + k, Z - 1), z + k < Z, None, (z + k < Z) & (z > 0)),
            ):
                place, arrival = self.target.at[at, x], self.sems.at[at, x]

                @pl.when(there)
                def _(place=place, arrival=arrival):
                    arrived(place, arrival, at_c)

                if up_when is not None:
                    sends.start(up_when, place, place, arrival, at_z(jnp.minimum(z + 1, Z - 1)))
                else:
                    sends.start(down_when, place, place, arrival, at_z(jnp.maximum(z - 1, 0)))
                self.across(there, place, at)

        def finish(self):
            for at in range(Z):
                for j in range(1, inner):
                    from_x = (x + inner - j) % inner
                    arrived(self.target.at[at, from_x], self.sems.at[at, from_x], at_c)

    class Plane:
        def __init__(self, index, source, target, x_first):
            self.source, self.target, self.x_first = source, target, x_first
            self.share = source.shape[1] // Z
            self.sems = plane_sems.at[index]

        def cut(self, at):
            return self.source.at[:, pl.ds(pl.multiple_of(at * self.share, LANES), self.share)]

        def place(self, at, x_at, i):
            return self.target.at[at, x_at, :, i * self.share : (i + 1) * self.share]

        def begin(self):
            self.own = keep(self.cut(z), self.place(z, x, 0), True)
            for k in range(1, Z):
                to = (z + k) % Z
                sends.start(True, self.cut(to), self.place(z, x, 0), self.sems.at[z, 0, 0], at_z(to))

        def over_x(self, at, i):
            place = self.place(at, x, i)
            for j in range(1, inner):
                sends.start(True, place, place, self.sems.at[at, j, i], at_x(j))

        def over_y(self, at, j):
            x_at = (x + inner - j) % inner
            for i in range(1, outer):
                sends.start(
                    True, self.place(at, x_at, 0), self.place(at, x_at, i),
                    self.sems.at[at, j, i], at_y(i),
                )

        def got(self, at, j, i):
            arrived(self.place(at, (x + inner - j) % inner, i), self.sems.at[at, j, i], at_c)

        def first(self, k):
            at = (z + Z - k) % Z
            if k == 0:
                self.own.wait()
            else:
                self.got(at, 0, 0)
            if self.x_first[k]:
                self.over_x(at, 0)
                self.over_y(at, 0)
            else:
                self.over_y(at, 0)
                self.over_x(at, 0)

        def second(self, k):
            at = (z + Z - k) % Z
            if self.x_first[k]:
                for j in range(1, inner):
                    self.got(at, j, 0)
                    self.over_y(at, j)
            else:
                for i in range(1, outer):
                    self.got(at, 0, i)
                    self.over_x(at, i)

        def finish(self, k):
            at = (z + Z - k) % Z
            for j in range(inner):
                for i in range(outer):
                    done = i == 0 if self.x_first[k] else j == 0
                    if not done:
                        self.got(at, j, i)

    lines = [Line(0, xy, xy_to), Line(1, gates, gates_to), Line(2, out, out_to)]
    order_xy, order_yx = [True] * Z, [False] * Z
    planes = [
        Plane(0, gate, gate_to, order_xy),
        Plane(1, up, up_to, order_yx),
        Plane(2, down, down_to, [k % 2 == 0 for k in range(Z)]),
    ]

    me = s * wt + w
    keep(vectors, vectors_to.at[me])

    def vector_copy(i):
        return pltpu.make_async_remote_copy(
            src_ref=vectors, dst_ref=vectors_to.at[me],
            send_sem=vector_sems.at[0, i], recv_sem=vector_sems.at[1, me],
            device_id={"seq": i // wt, "wt": i % wt}, device_id_type=MESH,
        )

    def vector_send(i, carried):
        pl.when(i != me)(lambda: vector_copy(i).start())
        return carried

    def tokens_begin():
        keep(tokens, tokens_to.at[w])
        sends.start(True, tokens, tokens_to.at[w], rows_sems.at[w], at_c)
        for i in range(1, outer):
            sends.start(True, tokens, tokens_to.at[w], rows_sems.at[w], at_y(i))

    def tokens_step():
        for i in range(1, outer):
            at = (y + outer - i) % outer * C + c
            arrived(tokens_to.at[at], rows_sems.at[at], at_c)
            sends.start(True, tokens_to.at[at], tokens_to.at[at], rows_sems.at[at], at_c)

    def tokens_finish():
        for i in range(outer):
            at = (y + outer - i) % outer * C + 1 - c
            arrived(tokens_to.at[at], rows_sems.at[at], at_c)

    def grads_place(own, at, z_to):
        return grads_to.at[own, (z_to - at + Z) % Z]

    def grads_forward(at, source, there, way):
        z_to = jnp.minimum(z + 1, Z - 1) if way > 0 else jnp.maximum(z - 1, 0)
        room = z < Z - 1 if way > 0 else z > 0
        when = room if there is None else there & room
        sends.start(when, source, grads_place(0, at, z_to), grads_sems.at[0, at], at_z(z_to))

    def grads_begin():
        keep(grads, grads_place(0, z, z))
        grads_forward(z, grads, None, 1)
        grads_forward(z, grads, None, -1)
        sends.start(True, grads, grads_place(1, z, z), grads_sems.at[1, z], at_c)

    def grads_step(k):
        for at, there, way in (
            (jnp.maximum(z - k, 0), z - k >= 0, 1),
            (jnp.minimum(z + k, Z - 1), z + k < Z, -1),
        ):
            place = grads_place(0, at, z)

            @pl.when(there)
            def _(place=place, at=at):
                arrived(place, grads_sems.at[0, at], at_c)

            grads_forward(at, place, there, way)
            sends.start(there, place, grads_place(1, at, z), grads_sems.at[1, at], at_c)

    def grads_finish():
        for at in range(Z):
            arrived(grads_place(1, at, z), grads_sems.at[1, at], at_c)

    lines[0].begin()
    tokens_begin()
    lines[1].begin()
    lax.fori_loop(0, seq * wt, vector_send, 0)
    for k in range(1, Z):
        lines[1].step(k)
        lines[0].step(k)
        if k == 1:
            tokens_step()
    planes[0].begin()
    lines[2].begin()
    planes[0].first(0)
    for k in range(1, Z):
        lines[2].step(k)
        planes[0].first(k)
    planes[1].begin()
    for k in range(Z):
        planes[1].first(k)
        planes[0].second(k)
    planes[2].begin()
    for k in range(Z):
        planes[2].first(k)
        planes[1].second(k)
    grads_begin()
    for k in range(Z):
        planes[2].second(k)
    for k in range(1, Z):
        grads_step(k)

    for line in lines:
        line.finish()
    tokens_finish()
    grads_finish()
    for plane in planes:
        for k in range(Z):
            plane.finish(k)

    def vector_wait(i, carried):
        @pl.when(i != me)
        def _():
            vector_copy(i).wait_send()
            arrived(vectors_to.at[i], vector_sems.at[1, i], at_c)

        return carried

    lax.fori_loop(0, seq * wt, vector_wait, 0)
    sends.finish()
    for waited, copy in here:
        if not waited:
            copy.wait()


def gather_all(tokens, grads, vectors, gates, xy, out, gate, up, down):
    inner, outer = sizes()
    seq, wt = Z * inner, outer * C

    def buffer(*shape, like):
        return jax.ShapeDtypeStruct(shape, like.dtype)

    def plane(weight):
        rows, columns = weight.shape
        return buffer(Z, inner, rows, outer * columns // Z, like=weight)

    shapes = (
        buffer(wt, *tokens.shape, like=tokens),
        buffer(C, Z, *grads.shape, like=grads),
        buffer(seq * wt, *vectors.shape, like=vectors),
        buffer(Z, inner, *gates.shape, like=gates),
        buffer(Z, inner, *xy.shape, like=xy),
        buffer(Z, inner, *out.shape, like=out),
        plane(gate),
        plane(up),
        plane(down),
    )
    copies = 3 * (2 + inner + (Z - 1) * 2 * inner) + 3 * (Z - 1 + Z * (inner + 2 * outer + inner * outer))
    copies += 2 * outer + 3 + 4 * Z
    dma = pltpu.SemaphoreType.DMA
    return pl.pallas_call(
        functools.partial(gather_kernel, (inner, outer)),
        out_shape=shapes,
        in_specs=[pl.BlockSpec(memory_space=pl.ANY)] * 9,
        out_specs=[pl.BlockSpec(memory_space=pl.ANY)] * 9,
        scratch_shapes=[
            dma((copies,)),
            dma((16,)),
            dma((3, Z, inner)),
            dma((3, Z, inner, outer)),
            dma((wt,)),
            dma((C, Z)),
            dma((2, seq * wt)),
        ],
        compiler_params=pltpu.CompilerParams(collective_id=0, has_side_effects=True),
        name="gather_all",
    )(tokens, grads, vectors, gates, xy, out, gate, up, down)


def scan_kernel(backward, a_ref, b_ref, h_ref, p_ref):
    rows, width = a_ref.shape
    segments = 8
    length = rows // segments

    def step(i, carried):
        held, product = carried
        at = length - 1 - i if backward else i
        where = pl.ds(at, segments, stride=length)
        factor = a_ref[where, :]
        held = factor * held + b_ref[where, :]
        product = factor * product
        h_ref[where, :] = held
        p_ref[where, :] = product
        return held, product

    held, product = lax.fori_loop(
        0, length, step, (jnp.zeros((segments, width), F32), jnp.ones((segments, width), F32)),
        unroll=4,
    )
    carry = jnp.zeros((1, width), F32)
    scale = jnp.ones((1, width), F32)
    order = range(segments - 1, -1, -1) if backward else range(segments)
    for at in order:
        if at != order[0]:
            part = pl.ds(at * length, length)
            local = p_ref[part, :]
            h_ref[part, :] = h_ref[part, :] + local * carry
            p_ref[part, :] = local * scale
        carry = held[at : at + 1] + product[at : at + 1] * carry
        scale = product[at : at + 1] * scale


def local_scan(factor, inflow, backward):
    shape = jax.ShapeDtypeStruct(factor.shape, F32)
    column = pl.BlockSpec((factor.shape[0], LANES), lambda i: (0, i))
    return pl.pallas_call(
        functools.partial(scan_kernel, backward),
        out_shape=(shape, shape),
        grid=(factor.shape[1] // LANES,),
        in_specs=[column] * 2,
        out_specs=(column,) * 2,
        name="scan_back" if backward else "scan_ahead",
    )(factor, inflow)


def full_scan(factor, inflow, backward):
    count = lax.axis_size("seq")
    held, product = local_scan(factor, inflow, backward)
    end = slice(0, 1) if backward else slice(held.shape[0] - 1, None)
    ends = jnp.concatenate([product[end], held[end]])
    sign = -1 if backward else 1
    carry = jnp.zeros_like(held[:1])
    for k in range(count - 1, 0, -1):
        pairs = [(s, s + sign * k) for s in range(count) if 0 <= s + sign * k < count]
        moved = lax.ppermute(ends, "seq", pairs)
        carry = moved[:1] * carry + moved[1:]
    return held + product * carry, carry


def recurrence_terms(decay_pre, input_pre, decay_log, conv_float):
    log_decay = -DECAY_SCALE * jax.nn.softplus(-decay_log) * jax.nn.sigmoid(decay_pre)
    return (
        jnp.exp(log_decay),
        jnp.sqrt(-jnp.expm1(2.0 * log_decay)) * jax.nn.sigmoid(input_pre) * conv_float,
    )


def norm_back(d_normed, normed, inverse, gain_row):
    scaled = d_normed * gain_row
    return inverse * (scaled - normed * jnp.mean(scaled * normed, axis=1, keepdims=True))


def normed_rows(stream):
    inverse = lax.rsqrt(jnp.mean(stream * stream, axis=1, keepdims=True) + EPSILON)
    return stream * inverse, inverse


def per_device(
    tokens,
    norm1_gain,
    x_weight,
    y_weight,
    conv_weight,
    conv_bias,
    decay_gate_weight,
    decay_bias,
    input_gate_weight,
    input_bias,
    decay_param,
    out_weight,
    norm2_gain,
    gate_weight,
    up_weight,
    down_weight,
    out_grad,
):
    seq, wt = lax.axis_size("seq"), lax.axis_size("wt")
    inner, outer = sizes()
    z, x, y, c = places()
    w = lax.axis_index("wt")
    rows_dev, width = tokens.shape
    weight_rows, lru_cols = x_weight.shape
    chunk, block = decay_gate_weight.shape
    half = block // 2
    full = lru_cols - half
    taps_count = conv_weight.shape[1]
    reach = taps_count - 1
    hidden_cols = gate_weight.shape[1]

    def turned(value, axis):
        return jnp.where(c == 0, value, jnp.roll(value, -half, axis))

    def turned_back(value, axis):
        return jnp.where(c == 0, value, jnp.roll(value, half, axis))

    def in_order(own, partner, axis):
        return jnp.where(
            c == 0,
            jnp.concatenate([own, partner], axis),
            jnp.concatenate([partner, own], axis),
        )

    vectors = jnp.stack(
        [v.astype(F32) for v in (norm1_gain, norm2_gain, conv_bias, decay_bias, input_bias)]
        + [decay_param]
        + [conv_weight[:, k].astype(F32) for k in range(taps_count)]
    )
    vectors = jnp.pad(vectors, ((0, -vectors.shape[0] % 8), (0, -chunk % LANES)))

    across = [(i, i % seq * wt + i // seq) for i in range(seq * wt)]
    gates = jnp.concatenate([decay_gate_weight, input_gate_weight], axis=1)
    gates = lax.ppermute(gates, ("seq", "wt"), across)

    def padded(weight):
        share = -(-hidden_cols // (Z * LANES)) * LANES
        return jnp.pad(weight, ((0, 0), (0, Z * share - hidden_cols)))

    xy_unit = jnp.concatenate([turned(x_weight, 1), turned(y_weight, 1)], axis=1)
    (
        group_tokens, grad_group, vectors, gate_all, xy_kernel, out_kernel,
        gate_kernel, up_kernel, down_kernel,
    ) = gather_all(
        tokens, out_grad, vectors, gates, xy_unit, turned(out_weight, 1),
        padded(gate_weight), padded(up_weight), padded(down_weight),
    )
    group_tokens = group_tokens.reshape(-1, width)
    grad_group = grad_group.reshape(-1, width)
    vectors = jnp.moveaxis(vectors[:, : 6 + taps_count, :chunk], 0, 1).reshape(6 + taps_count, -1)
    gain_one, gain_two = vectors[0], vectors[1]
    own_vectors = turned(
        lax.dynamic_slice(vectors[2:], (0, w * lru_cols), (taps_count + 4, lru_cols)), 1
    )
    tap_bias, decay_shift, input_shift, decay_log = (own_vectors[i] for i in range(4))
    taps = own_vectors[4:]
    xy_kernel = xy_kernel.reshape(width, -1)
    out_kernel = out_kernel.reshape(width, -1)
    gate_kernel = gate_kernel.reshape(width, -1)
    up_kernel = up_kernel.reshape(width, -1)
    down_kernel = down_kernel.reshape(width, -1)
    gate_all = turned(gate_all.reshape(lru_cols, 2 * block), 0)
    partner_rows = c_swap(gate_all[full:])
    shared_rows = in_order(gate_all[full:], partner_rows, 0)

    stream = tokens.astype(F32)
    group_normed, _ = normed_rows(group_tokens.astype(F32))
    group_one = (group_normed * gain_one).astype(BF16)
    rows = group_one.shape[0]
    xy = multiply(group_one, xy_kernel)
    x_branch = xy[:, :lru_cols].astype(BF16)
    y_before = xy[:, lru_cols:]
    y_gated, gelu_y_back = jax.vjp(gelu_tanh, y_before)
    rim = lax.ppermute(x_branch[rows - reach :], "seq", [(i, i + 1) for i in range(seq - 1)])
    extended = jnp.concatenate([rim, x_branch], axis=0).astype(F32)
    conv_low = (
        tap_bias
        + sum(taps[k] * extended[reach - k : reach - k + rows] for k in range(taps_count))
    ).astype(BF16)
    shared_conv = in_order(conv_low[:, full:], c_swap(conv_low[:, full:]), 1)
    heads = full // block

    def of_head(value, i):
        return value[:, i * block : (i + 1) * block]

    pre_parts = [
        multiply(of_head(conv_low, i), gate_all[i * block : (i + 1) * block]) for i in range(heads)
    ]
    shared_pre = multiply(shared_conv, shared_rows).reshape(rows, 2, C, half)
    shared_pre = pick(shared_pre, c, 2)
    decay_pre = decay_shift + jnp.concatenate(
        [part[:, :block] for part in pre_parts] + [shared_pre[:, 0]], axis=1
    )
    input_pre = input_shift + jnp.concatenate(
        [part[:, block:] for part in pre_parts] + [shared_pre[:, 1]], axis=1
    )
    (retain, inflow), terms_back = jax.vjp(
        recurrence_terms, decay_pre, input_pre, decay_log, conv_low.astype(F32)
    )
    states, state_in = full_scan(retain, inflow, False)
    before = jnp.concatenate([state_in, states[:-1]])
    lru_low = states.astype(BF16).astype(F32)
    mixed_rows = (lru_low * y_gated).astype(BF16)
    branch = wt_scatter(lambda rows_: contract_last(rows_, out_kernel), mixed_rows)
    middle = stream + branch

    normed_two, inverse_two = normed_rows(middle)
    group_two = group_gather((normed_two * gain_two).astype(BF16))
    gate_pre = multiply(group_two, gate_kernel)
    up_pre = multiply(group_two, up_kernel)
    active, gelu_gate_back = jax.vjp(gelu_tanh, gate_pre)
    hidden = (active * up_pre).astype(BF16)

    d_hidden = multiply(grad_group, down_kernel)
    d_up = (d_hidden * active).astype(BF16)
    d_gate = gelu_gate_back(d_hidden * up_pre)[0].astype(BF16)
    d_normed_two = group_scatter(
        lambda g, u: contract_last(g, gate_kernel) + contract_last(u, up_kernel), d_gate, d_up
    )
    feed = group_scatter(lambda rows_: contract_last(rows_, down_kernel), hidden)
    block_out = (middle + feed).astype(BF16)
    down_grad = plane_scatter(contract_rows(grad_group, hidden), hidden_cols, True)
    gate_grad = plane_scatter(contract_rows(group_two, d_gate), hidden_cols, False)
    up_grad = plane_scatter(contract_rows(group_two, d_up), hidden_cols, True)
    gain_two_grad = jnp.sum(d_normed_two * normed_two, axis=0)
    d_middle = out_grad.astype(F32) + norm_back(d_normed_two, normed_two, inverse_two, gain_two)

    branch_rows = wt_gather(d_middle.astype(BF16))
    d_mixed = multiply(branch_rows, out_kernel)
    d_lru = (d_mixed * y_gated).astype(BF16).astype(F32)
    d_y = gelu_y_back(d_mixed * lru_low)[0].astype(BF16)
    passed, passed_in = full_scan(retain, retain * d_lru, True)
    d_total = d_lru + jnp.concatenate([passed[1:], passed_in])
    d_decay_pre, d_input_pre, decay_log_grad, d_conv_direct = terms_back(
        (d_total * before, d_total)
    )
    d_decay_low, d_input_low = d_decay_pre.astype(BF16), d_input_pre.astype(BF16)
    own_low = jnp.concatenate([d_decay_low[:, full:], d_input_low[:, full:]], axis=1)
    partner_low = c_swap(own_low)
    shared_low = jnp.concatenate(
        [
            in_order(own_low[:, :half], partner_low[:, :half], 1),
            in_order(own_low[:, half:], partner_low[:, half:], 1),
        ],
        axis=1,
    )
    lows = [
        jnp.concatenate([of_head(d_decay_low, i), of_head(d_input_low, i)], axis=1)
        for i in range(heads)
    ]
    d_conv = d_conv_direct + jnp.concatenate(
        [contract_last(lows[i], gate_all[i * block : (i + 1) * block]) for i in range(heads)]
        + [contract_last(shared_low, gate_all[full:])],
        axis=1,
    )
    gates_grad = jnp.concatenate(
        [contract_rows(of_head(conv_low, i), lows[i]) for i in range(heads)]
        + [contract_rows(conv_low[:, full:], shared_low)]
    )
    ahead = lax.ppermute(d_conv[:reach], "seq", [(i + 1, i) for i in range(seq - 1)])
    d_extended = jnp.concatenate([d_conv, ahead], axis=0)
    d_x_branch = sum(taps[k] * d_extended[k : k + rows] for k in range(taps_count)).astype(BF16)
    d_normed_one = wt_scatter(
        lambda dx, dy: contract_last(dx, xy_kernel[:, :lru_cols])
        + contract_last(dy, xy_kernel[:, lru_cols:]),
        d_x_branch,
        d_y,
    )
    normed_one, inverse_one = normed_rows(stream)
    gain_one_grad = jnp.sum(d_normed_one * normed_one, axis=0)
    tokens_grad = (d_middle + norm_back(d_normed_one, normed_one, inverse_one, gain_one)).astype(
        BF16
    )

    out_weight_grad = turned_back(seq_scatter(contract_rows(branch_rows, mixed_rows)), 1)
    y_weight_grad = turned_back(seq_scatter(contract_rows(group_one, d_y)), 1)
    x_weight_grad = turned_back(seq_scatter(contract_rows(group_one, d_x_branch)), 1)
    own_sums = jnp.stack(
        [jnp.sum(d_conv, axis=0), jnp.sum(d_decay_pre, axis=0), jnp.sum(d_input_pre, axis=0)]
        + [decay_log_grad]
        + [jnp.sum(d_conv * extended[reach - k : reach - k + rows], axis=0) for k in range(taps_count)],
        axis=1,
    )
    own_sums = jnp.concatenate([turned_back(gates_grad, 0), turned_back(own_sums, 0)], axis=1)
    own_sums = lax.psum_scatter(own_sums, "seq", scatter_dimension=0, tiled=True)
    own_sums = lax.ppermute(own_sums, ("seq", "wt"), [(to, at) for at, to in across])
    gains = jnp.stack([gain_one_grad, gain_two_grad])
    for move, count in ((c_swap, None), (y_move, outer), (x_move, inner), (z_turn, Z)):
        if count is None:
            gains = gains + move(gains)
        else:
            gains = gains + sum(move(gains, j) for j in range(1, count))
    gains = lax.dynamic_slice(gains, (0, (lax.axis_index("seq") * wt + w) * chunk), (2, chunk))
    sums = own_sums[:, 2 * block :]
    return (
        block_out,
        tokens_grad,
        gains[0],
        x_weight_grad,
        y_weight_grad,
        sums[:, 4:],
        sums[:, 0],
        own_sums[:, :block],
        sums[:, 1],
        own_sums[:, block : 2 * block],
        sums[:, 2],
        sums[:, 3],
        out_weight_grad,
        gains[1],
        gate_grad,
        up_grad,
        down_grad,
    )


def solution(mesh):
    rows, both, lone = P(("seq", "wt"), None), P("seq", "wt"), P(("seq", "wt"))
    in_specs = (
        rows, lone, both, both, rows, lone, rows, lone, rows, lone, lone,
        both, lone, both, both, both, rows,
    )
    out_specs = (
        rows, rows, lone, both, both, rows, lone, rows, lone, rows, lone, lone,
        both, lone, both, both, both,
    )
    return jax.shard_map(
        per_device, mesh=mesh, in_specs=in_specs, out_specs=out_specs, check_vma=False
    )
```

```python
import functools

import jax
import jax.numpy as jnp
from jax import lax
from jax.experimental import pallas as pl
from jax.experimental.pallas import tpu as pltpu
from jax.sharding import PartitionSpec as P

EPSILON = 1e-06
DECAY_SCALE = 8.0
Z = 4
C = 2
LANES = 128
F32 = jnp.float32
BF16 = jnp.bfloat16
MESH = pl.DeviceIdType.MESH


def gelu_tanh(values):
    return jax.nn.gelu(values, approximate=True)


def sizes():
    return lax.axis_size("seq") // Z, lax.axis_size("wt") // C


def places():
    inner, outer = sizes()
    s, w = lax.axis_index("seq"), lax.axis_index("wt")
    return s // inner, s % inner, w // C, w % C


def after(value, *earlier):
    return lax.optimization_barrier((value, *earlier))[0]


def z_move(value, by, senders):
    inner, _ = sizes()
    pairs = [(z * inner + x, (z + by) % Z * inner + x) for z in senders for x in range(inner)]
    return lax.ppermute(value, "seq", pairs)


def z_turn(value, by):
    return z_move(value, by, range(Z))


def x_move(value, by):
    inner, _ = sizes()
    pairs = [(z * inner + x, z * inner + (x + by) % inner) for z in range(Z) for x in range(inner)]
    return lax.ppermute(value, "seq", pairs)


def y_move(value, by):
    _, outer = sizes()
    pairs = [(y * C + c, (y + by) % outer * C + c) for y in range(outer) for c in range(C)]
    return lax.ppermute(value, "wt", pairs)


def c_swap(value):
    _, outer = sizes()
    pairs = [(y * C + c, y * C + 1 - c) for y in range(outer) for c in range(C)]
    return lax.ppermute(value, "wt", pairs)


def line_gather(value):
    z = places()[0]
    up, down = [value], [value]
    for k in range(1, Z):
        up.append(z_move(up[-1], 1, range(k - 1, Z - 1)))
        down.append(z_move(down[-1], -1, range(1, Z - k + 1)))
    return [value] + [jnp.where(z >= k, up[k], down[Z - k]) for k in range(1, Z)]


def line_scatter(parts):
    up = down = None
    for step in range(1, Z):
        rising = parts[step] if up is None else parts[step] + up
        falling = parts[Z - step] if down is None else parts[Z - step] + down
        up = z_move(rising.astype(BF16), 1, range(0, step)).astype(F32)
        down = z_move(falling.astype(BF16), -1, range(Z - step, Z)).astype(F32)
    return parts[0] + up + down


def pick(value, index, axis):
    return lax.dynamic_index_in_dim(value, index, axis, keepdims=False)


def put(buffer, value, starts):
    return lax.dynamic_update_slice(buffer, value, starts)


def contract_last(left_side, right_side):
    return lax.dot_general(
        left_side, right_side, (((1,), (1,)), ((), ())), preferred_element_type=F32
    )


def contract_rows(left_side, right_side):
    return lax.dot_general(
        left_side, right_side, (((0,), (0,)), ((), ())), preferred_element_type=F32
    )


def multiply(left_side, right_side):
    return jnp.dot(left_side, right_side, preferred_element_type=F32)


def seq_scatter(total):
    inner, _ = sizes()
    z, x = places()[:2]
    total = total.reshape(Z, inner, -1, total.shape[1])
    kept = pick(total, x, 1)
    for j in range(1, inner):
        kept = kept + x_move(pick(total, (x + j) % inner, 1).astype(BF16), j).astype(F32)
    return line_scatter([pick(kept, (z - k) % Z, 0) for k in range(Z)])


def plane_scatter(left_side, right_side, width, x_first, gate):
    inner, outer = sizes()
    z, x = places()[:2]
    share = right_side.shape[1] // outer

    def over_x(value):
        total = pick(value, x, 1).astype(F32)
        for j in range(1, inner):
            total = total + x_move(pick(value, (x + j) % inner, 1), j).astype(F32)
        return total.astype(BF16)

    def over_y(parts):
        total = parts[0].astype(F32)
        for i in range(1, outer):
            total = total + y_move(parts[i], -i).astype(F32)
        return total.astype(BF16)

    parts = []
    for i in range(outer):
        part = contract_rows(left_side, right_side[:, i * share : (i + 1) * share]).astype(BF16)
        parts.append(part.reshape(Z, inner, -1, share))
    rows = parts[0].shape[2]
    kept = over_y([over_x(part) for part in parts]) if x_first else over_x(over_y(parts))
    kept = after(kept, gate)
    buffer = put(jnp.zeros((rows, Z * share), BF16), pick(kept, z, 0), (0, z * share))
    for k in range(1, Z):
        moved = z_move(pick(kept, (z + k) % Z, 0), k, range(Z))
        buffer = put(buffer, moved, (0, (z - k) % Z * share))
    return buffer[:, :width].astype(F32)


def wt_scatter(product_of, *sides):
    _, outer = sizes()
    _, _, y, c = places()

    def chosen(at):
        cut = [side.reshape(outer, C, -1, side.shape[1]) for side in sides]
        return [pick(side, at, 1).reshape(-1, side.shape[3]) for side in cut]

    sent = c_swap(product_of(*chosen(1 - c)))
    kept = product_of(*chosen(c)) + sent
    kept = kept.reshape(outer, -1, kept.shape[1])
    total = pick(kept, y, 0)
    for i in range(1, outer):
        total = total + y_move(pick(kept, (y + i) % outer, 0).astype(BF16), i).astype(F32)
    return total


def group_scatter(product_of, *sides):
    half = sides[0].shape[0] // 2
    sent = c_swap(product_of(*[side[half:] for side in sides]).astype(BF16))
    kept = product_of(*[side[:half] for side in sides]) + sent.astype(F32)
    rows = half // Z
    return line_scatter([kept[k * rows : (k + 1) * rows] for k in range(Z)])


class Sends:
    def __init__(self, sems):
        self.sems, self.started = sems, []

    def start(self, when, source, target, arrival, device):
        copy = pltpu.make_async_remote_copy(
            src_ref=source,
            dst_ref=target,
            send_sem=self.sems.at[len(self.started)],
            recv_sem=arrival,
            device_id=device,
            device_id_type=MESH,
        )
        if when is True:
            copy.start()
        else:
            pl.when(when)(copy.start)
        self.started.append((when, copy))

    def finish(self):
        for when, copy in self.started:
            if when is True:
                copy.wait_send()
            else:
                pl.when(when)(copy.wait_send)


def arrived(target, arrival, device):
    pltpu.make_async_remote_copy(
        src_ref=target, dst_ref=target, send_sem=arrival, recv_sem=arrival,
        device_id=device, device_id_type=MESH,
    ).wait_recv()


def gather_kernel(shape, *refs):
    inner, outer = shape
    (tokens, grads, vectors, gates, xy, out, gate, up, down) = refs[:9]
    (tokens_to, grads_to, vectors_to, gates_to, xy_to, out_to, gate_to, up_to, down_to) = refs[9:18]
    send_sems, local_sems, line_sems, plane_sems, rows_sems, grads_sems, vector_sems = refs[18:]
    seq, wt = Z * inner, outer * C
    s, w = lax.axis_index("seq"), lax.axis_index("wt")
    z, x, y, c = s // inner, s % inner, w // C, w % C
    sends = Sends(send_sems)
    here = []

    def at_z(to):
        return {"seq": to * inner + x, "wt": w}

    def at_x(by):
        return {"seq": z * inner + (x + by) % inner, "wt": w}

    def at_y(by):
        return {"seq": s, "wt": (y + by) % outer * C + c}

    at_c = {"seq": s, "wt": y * C + 1 - c}

    def keep(source, target, waited=False):
        copy = pltpu.make_async_copy(source, target, local_sems.at[len(here)])
        copy.start()
        here.append((waited, copy))
        return copy

    barrier = pltpu.get_barrier_semaphore()

    def greet(i, carried):
        @pl.when(i != s * wt + w)
        def _():
            pl.semaphore_signal(
                barrier, inc=1, device_id={"seq": i // wt, "wt": i % wt}, device_id_type=MESH
            )

        return carried

    lax.fori_loop(0, seq * wt, greet, 0)
    pl.semaphore_wait(barrier, seq * wt - 1)

    class Line:
        def __init__(self, index, source, target):
            self.source, self.target = source, target
            self.sems = line_sems.at[index]

        def forward(self, block, at, up_when, down_when):
            place = self.target.at[at, x]
            arrival = self.sems.at[at, x]
            sends.start(up_when, block, place, arrival, at_z(jnp.minimum(z + 1, Z - 1)))
            sends.start(down_when, block, place, arrival, at_z(jnp.maximum(z - 1, 0)))
            return place, arrival

        def across(self, when, block, at):
            for j in range(1, inner):
                sends.start(when, block, self.target.at[at, x], self.sems.at[at, x], at_x(j))

        def begin(self):
            keep(self.source, self.target.at[z, x])
            self.forward(self.source, z, z < Z - 1, z > 0)
            self.across(True, self.source, z)

        def step(self, k):
            for at, there, up_when, down_when in (
                (jnp.maximum(z - k, 0), z - k >= 0, (z - k >= 0) & (z < Z - 1), None),
                (jnp.minimum(z + k, Z - 1), z + k < Z, None, (z + k < Z) & (z > 0)),
            ):
                place, arrival = self.target.at[at, x], self.sems.at[at, x]

                @pl.when(there)
                def _(place=place, arrival=arrival):
                    arrived(place, arrival, at_c)

                if up_when is not None:
                    sends.start(up_when, place, place, arrival, at_z(jnp.minimum(z + 1, Z - 1)))
                else:
                    sends.start(down_when, place, place, arrival, at_z(jnp.maximum(z - 1, 0)))
                self.across(there, place, at)

        def finish(self):
            for at in range(Z):
                for j in range(1, inner):
                    from_x = (x + inner - j) % inner
                    arrived(self.target.at[at, from_x], self.sems.at[at, from_x], at_c)

    class Plane:
        def __init__(self, index, source, target, x_first):
            self.source, self.target, self.x_first = source, target, x_first
            self.share = source.shape[1] // Z
            self.sems = plane_sems.at[index]

        def cut(self, at):
            return self.source.at[:, pl.ds(pl.multiple_of(at * self.share, LANES), self.share)]

        def place(self, at, x_at, i):
            return self.target.at[at, x_at, :, i * self.share : (i + 1) * self.share]

        def begin(self):
            self.own = keep(self.cut(z), self.place(z, x, 0), True)
            for k in range(1, Z):
                to = (z + k) % Z
                sends.start(True, self.cut(to), self.place(z, x, 0), self.sems.at[z, 0, 0], at_z(to))

        def over_x(self, at, i):
            place = self.place(at, x, i)
            for j in range(1, inner):
                sends.start(True, place, place, self.sems.at[at, j, i], at_x(j))

        def over_y(self, at, j):
            x_at = (x + inner - j) % inner
            for i in range(1, outer):
                sends.start(
                    True, self.place(at, x_at, 0), self.place(at, x_at, i),
                    self.sems.at[at, j, i], at_y(i),
                )

        def got(self, at, j, i):
            arrived(self.place(at, (x + inner - j) % inner, i), self.sems.at[at, j, i], at_c)

        def first(self, k):
            at = (z + Z - k) % Z
            if k == 0:
                self.own.wait()
            else:
                self.got(at, 0, 0)
            if self.x_first[k]:
                self.over_x(at, 0)
                self.over_y(at, 0)
            else:
                self.over_y(at, 0)
                self.over_x(at, 0)

        def second(self, k):
            at = (z + Z - k) % Z
            if self.x_first[k]:
                for j in range(1, inner):
                    self.got(at, j, 0)
                    self.over_y(at, j)
            else:
                for i in range(1, outer):
                    self.got(at, 0, i)
                    self.over_x(at, i)

        def finish(self, k):
            at = (z + Z - k) % Z
            for j in range(inner):
                for i in range(outer):
                    done = i == 0 if self.x_first[k] else j == 0
                    if not done:
                        self.got(at, j, i)

    lines = [Line(0, xy, xy_to), Line(1, gates, gates_to), Line(2, out, out_to)]
    order_xy, order_yx = [True] * Z, [False] * Z
    planes = [
        Plane(0, gate, gate_to, order_xy),
        Plane(1, up, up_to, order_yx),
        Plane(2, down, down_to, [k % 2 == 0 for k in range(Z)]),
    ]

    me = s * wt + w
    keep(vectors, vectors_to.at[me])

    def vector_copy(i):
        return pltpu.make_async_remote_copy(
            src_ref=vectors, dst_ref=vectors_to.at[me],
            send_sem=vector_sems.at[0, i], recv_sem=vector_sems.at[1, me],
            device_id={"seq": i // wt, "wt": i % wt}, device_id_type=MESH,
        )

    def vector_send(i, carried):
        pl.when(i != me)(lambda: vector_copy(i).start())
        return carried

    def tokens_begin():
        keep(tokens, tokens_to.at[w])
        sends.start(True, tokens, tokens_to.at[w], rows_sems.at[w], at_c)
        for i in range(1, outer):
            sends.start(True, tokens, tokens_to.at[w], rows_sems.at[w], at_y(i))

    def tokens_step():
        for i in range(1, outer):
            at = (y + outer - i) % outer * C + c
            arrived(tokens_to.at[at], rows_sems.at[at], at_c)
            sends.start(True, tokens_to.at[at], tokens_to.at[at], rows_sems.at[at], at_c)

    def tokens_finish():
        for i in range(outer):
            at = (y + outer - i) % outer * C + 1 - c
            arrived(tokens_to.at[at], rows_sems.at[at], at_c)

    def grads_place(own, at, z_to):
        return grads_to.at[own, (z_to - at + Z) % Z]

    def grads_forward(at, source, there, way):
        z_to = jnp.minimum(z + 1, Z - 1) if way > 0 else jnp.maximum(z - 1, 0)
        room = z < Z - 1 if way > 0 else z > 0
        when = room if there is None else there & room
        sends.start(when, source, grads_place(0, at, z_to), grads_sems.at[0, at], at_z(z_to))

    def grads_begin():
        keep(grads, grads_place(0, z, z))
        grads_forward(z, grads, None, 1)
        grads_forward(z, grads, None, -1)
        sends.start(True, grads, grads_place(1, z, z), grads_sems.at[1, z], at_c)

    def grads_step(k):
        for at, there, way in (
            (jnp.maximum(z - k, 0), z - k >= 0, 1),
            (jnp.minimum(z + k, Z - 1), z + k < Z, -1),
        ):
            place = grads_place(0, at, z)

            @pl.when(there)
            def _(place=place, at=at):
                arrived(place, grads_sems.at[0, at], at_c)

            grads_forward(at, place, there, way)
            sends.start(there, place, grads_place(1, at, z), grads_sems.at[1, at], at_c)

    def grads_finish():
        for at in range(Z):
            arrived(grads_place(1, at, z), grads_sems.at[1, at], at_c)

    lines[0].begin()
    tokens_begin()
    lines[1].begin()
    lax.fori_loop(0, seq * wt, vector_send, 0)
    for k in range(1, Z):
        lines[1].step(k)
        lines[0].step(k)
        if k == 1:
            tokens_step()
    planes[0].begin()
    lines[2].begin()
    planes[0].first(0)
    for k in range(1, Z):
        lines[2].step(k)
        planes[0].first(k)
    planes[1].begin()
    for k in range(Z):
        planes[1].first(k)
        planes[0].second(k)
    planes[2].begin()
    for k in range(Z):
        planes[2].first(k)
        planes[1].second(k)
    grads_begin()
    for k in range(Z):
        planes[2].second(k)
    for k in range(1, Z):
        grads_step(k)

    for line in lines:
        line.finish()
    tokens_finish()
    grads_finish()
    for plane in planes:
        for k in range(Z):
            plane.finish(k)

    def vector_wait(i, carried):
        @pl.when(i != me)
        def _():
            vector_copy(i).wait_send()
            arrived(vectors_to.at[i], vector_sems.at[1, i], at_c)

        return carried

    lax.fori_loop(0, seq * wt, vector_wait, 0)
    sends.finish()
    for waited, copy in here:
        if not waited:
            copy.wait()


def gather_all(tokens, grads, vectors, gates, xy, out, gate, up, down):
    inner, outer = sizes()
    seq, wt = Z * inner, outer * C

    def buffer(*shape, like):
        return jax.ShapeDtypeStruct(shape, like.dtype)

    def plane(weight):
        rows, columns = weight.shape
        return buffer(Z, inner, rows, outer * columns // Z, like=weight)

    shapes = (
        buffer(wt, *tokens.shape, like=tokens),
        buffer(C, Z, *grads.shape, like=grads),
        buffer(seq * wt, *vectors.shape, like=vectors),
        buffer(Z, inner, *gates.shape, like=gates),
        buffer(Z, inner, *xy.shape, like=xy),
        buffer(Z, inner, *out.shape, like=out),
        plane(gate),
        plane(up),
        plane(down),
    )
    copies = 3 * (2 + inner + (Z - 1) * 2 * inner) + 3 * (Z - 1 + Z * (inner + 2 * outer + inner * outer))
    copies += 2 * outer + 3 + 4 * Z
    dma = pltpu.SemaphoreType.DMA
    return pl.pallas_call(
        functools.partial(gather_kernel, (inner, outer)),
        out_shape=shapes,
        in_specs=[pl.BlockSpec(memory_space=pl.ANY)] * 9,
        out_specs=[pl.BlockSpec(memory_space=pl.ANY)] * 9,
        scratch_shapes=[
            dma((copies,)),
            dma((16,)),
            dma((3, Z, inner)),
            dma((3, Z, inner, outer)),
            dma((wt,)),
            dma((C, Z)),
            dma((2, seq * wt)),
        ],
        compiler_params=pltpu.CompilerParams(collective_id=0, has_side_effects=True),
        name="gather_all",
    )(tokens, grads, vectors, gates, xy, out, gate, up, down)


class Place:
    def __init__(self, shape):
        self.inner, self.outer = shape
        self.s, self.w = lax.axis_index("seq"), lax.axis_index("wt")
        self.z, self.x = self.s // self.inner, self.s % self.inner
        self.y, self.c = self.w // C, self.w % C
        self.at_c = {"seq": self.s, "wt": self.y * C + 1 - self.c}
        self.z_up, self.z_down = jnp.minimum(self.z + 1, Z - 1), jnp.maximum(self.z - 1, 0)

    def at_z(self, to):
        return {"seq": to * self.inner + self.x, "wt": self.w}

    def at_x(self, by):
        return {"seq": self.z * self.inner + (self.x + by) % self.inner, "wt": self.w}

    def at_y(self, by):
        return {"seq": self.s, "wt": (self.y + self.outer + by) % self.outer * C + self.c}

    def greet(self):
        barrier = pltpu.get_barrier_semaphore()
        devices = [self.at_c]
        devices += [self.at_z((self.z + k) % Z) for k in range(1, Z)]
        devices += [self.at_x(j) for j in range(1, self.inner)]
        devices += [self.at_y(i) for i in range(1, self.outer)]
        for device in devices:
            pl.semaphore_signal(barrier, inc=1, device_id=device, device_id_type=MESH)
        pl.semaphore_wait(barrier, len(devices))


def each_rows(count, step, body):
    def run(i, carried):
        body(pl.ds(pl.multiple_of(i * step, step), step))
        return carried

    lax.fori_loop(0, count // step, run, 0)


class WtRows:
    def __init__(self, me, sends, source, target, sems):
        self.me, self.sends, self.source, self.target, self.sems = me, sends, source, target, sems

    def begin(self):
        me = self.me
        for device in [me.at_y(i) for i in range(1, me.outer)] + [me.at_c]:
            self.sends.start(True, self.source, self.target.at[me.w], self.sems.at[me.w], device)

    def step(self):
        me = self.me
        for i in range(1, me.outer):
            at = (me.y + me.outer - i) % me.outer * C + me.c
            arrived(self.target.at[at], self.sems.at[at], me.at_c)
            self.sends.start(True, self.target.at[at], self.target.at[at], self.sems.at[at], me.at_c)

    def finish(self):
        me = self.me
        for i in range(me.outer):
            at = (me.y + me.outer - i) % me.outer * C + 1 - me.c
            arrived(self.target.at[at], self.sems.at[at], me.at_c)


class GroupRows:
    def __init__(self, me, sends, source, target, sems):
        self.me, self.sends, self.source, self.target, self.sems = me, sends, source, target, sems

    def place(self, own, at, z_to):
        return self.target.at[own, (z_to - at + Z) % Z]

    def forward(self, at, source, there, way):
        me = self.me
        z_to = me.z_up if way > 0 else me.z_down
        room = me.z < Z - 1 if way > 0 else me.z > 0
        when = room if there is None else there & room
        self.sends.start(
            when, source, self.place(0, at, z_to), self.sems.at[0, at], me.at_z(z_to)
        )

    def begin(self):
        me = self.me
        self.forward(me.z, self.source, None, 1)
        self.forward(me.z, self.source, None, -1)
        self.sends.start(
            True, self.source, self.place(1, me.z, me.z), self.sems.at[1, me.z], me.at_c
        )

    def step(self, k):
        me = self.me
        for at, there, way in (
            (jnp.maximum(me.z - k, 0), me.z - k >= 0, 1),
            (jnp.minimum(me.z + k, Z - 1), me.z + k < Z, -1),
        ):
            place = self.place(0, at, me.z)

            @pl.when(there)
            def _(place=place, at=at):
                arrived(place, self.sems.at[0, at], me.at_c)

            self.forward(at, place, there, way)
            self.sends.start(there, place, self.place(1, at, me.z), self.sems.at[1, at], me.at_c)

    def finish(self):
        me = self.me
        for at in range(Z):
            arrived(self.place(1, at, me.z), self.sems.at[1, at], me.at_c)


def branch_kernel(
    shape, sent, own, tokens, gain, group_to, middle, own_v, c_in, y_out, y_in, low,
    send_sems, local_sems, c_sems, y_sems, group_sems,
):
    me = Place(shape)
    outer = me.outer
    rows = tokens.shape[0]
    sends = Sends(send_sems)
    load = pltpu.make_async_copy(own, own_v, local_sems.at[0])
    load.start()
    me.greet()
    order = [(me.y + i) % outer for i in list(range(1, outer)) + [0]]
    for at in order:
        sends.start(True, sent.at[at], c_in.at[at], c_sems.at[at], me.at_c)
    load.wait()
    for i, at in enumerate(order):
        arrived(c_in.at[at], c_sems.at[at], me.at_c)
        if i < outer - 1:
            each_rows(rows, 16, lambda r, i=i, at=at: y_out.__setitem__(
                (i, r), (own_v[at, r] + c_in[at, r]).astype(BF16)))
            sends.start(True, y_out.at[i], y_in.at[i], y_sems.at[i], me.at_y(i + 1))
    for i in range(outer - 1):
        arrived(y_in.at[i], y_sems.at[i], me.at_c)

    def work(r):
        total = tokens[r].astype(F32) + own_v[me.y, r] + c_in[me.y, r]
        for i in range(outer - 1):
            total = total + y_in[i, r].astype(F32)
        inverse = lax.rsqrt(jnp.mean(total * total, axis=1, keepdims=True) + EPSILON)
        middle[r] = total
        low[r] = (total * inverse * gain[...]).astype(BF16)

    each_rows(rows, 16, work)
    keep = pltpu.make_async_copy(low, group_to.at[0, 0], local_sems.at[1])
    keep.start()
    group = GroupRows(me, sends, low, group_to, group_sems)
    group.begin()
    for k in range(1, Z):
        group.step(k)
    group.finish()
    sends.finish()
    keep.wait()


def branch_and_group(sent, own, tokens, gain):
    inner, outer = sizes()
    rows, width = tokens.shape
    dma = pltpu.SemaphoreType.DMA
    vmem, anywhere = pl.BlockSpec(memory_space=pltpu.VMEM), pl.BlockSpec(memory_space=pl.ANY)
    return pl.pallas_call(
        functools.partial(branch_kernel, (inner, outer)),
        out_shape=(
            jax.ShapeDtypeStruct((C, Z, rows, width), BF16),
            jax.ShapeDtypeStruct((rows, width), F32),
        ),
        in_specs=[anywhere, anywhere, vmem, vmem],
        out_specs=(anywhere, vmem),
        scratch_shapes=[
            pltpu.VMEM((outer, rows, width), F32),
            pltpu.VMEM((outer, rows, width), F32),
            pltpu.VMEM((outer - 1, rows, width), BF16),
            pltpu.VMEM((outer - 1, rows, width), BF16),
            pltpu.VMEM((rows, width), BF16),
            dma((2 * outer + 3 + 4 * (Z - 1),)),
            dma((2,)),
            dma((outer,)),
            dma((outer - 1,)),
            dma((C, Z)),
        ],
        compiler_params=pltpu.CompilerParams(
            collective_id=1, has_side_effects=True, vmem_limit_bytes=40 * 1024 * 1024
        ),
        name="branch_and_group",
    )(sent, own, tokens, gain)


def line_order():
    order = []
    for k in [n for t in range(1, Z) for n in (t, Z - t)] + [0]:
        if k not in order:
            order.append(k)
    return order


def line_sum(me, sends, rows, term, ready, store, held, up, down, between=None):
    z = me.z
    waited = set()

    def wait_for(k):
        if k not in waited:
            ready(k)
            waited.add(k)

    def add(when, target, slot, k, received=None):
        def body(r):
            value = term(k, r)
            if received is not None:
                value = value + received[slot - 1, r].astype(F32)
            target[slot, r] = value.astype(BF16)

        pl.when(when)(lambda: each_rows(rows, 16, body))

    for t in range(1, Z):
        slot = t - 1
        for k, (out, into, sems), has, when, to in (
            (t, up, z > 0, (z <= t - 1) & (z < Z - 1), me.z_up),
            (Z - t, down, z < Z - 1, (z >= Z - t) & (z > 0), me.z_down),
        ):
            wait_for(k)
            if t == 1:
                add(when, out, slot, k)
            else:
                pl.when(when & has)(
                    lambda into=into, sems=sems, slot=slot: arrived(
                        into.at[slot - 1], sems.at[slot - 1], me.at_c
                    )
                )
                add(when & has, out, slot, k, into)
                add(when & jnp.logical_not(has), out, slot, k)
            sends.start(when, out.at[slot], into.at[slot], sems.at[slot], me.at_z(to))
        if between is not None:
            between(t)
    wait_for(0)
    each_rows(rows, 16, lambda r: store(r, term(0, r)))
    for (_, into, sems), has in ((up, z > 0), (down, z < Z - 1)):

        @pl.when(has)
        def _(into=into, sems=sems):
            arrived(into.at[Z - 2], sems.at[Z - 2], me.at_c)
            each_rows(rows, 16, lambda r: store(r, held(r) + into[Z - 2, r].astype(F32)))


class PlaneTerms:
    def __init__(self, me, sends, parts, target, sems, over_x, blocks):
        self.me, self.sends, self.parts, self.target, self.sems = me, sends, parts, target, sems
        self.over_x, self.blocks = over_x, blocks

    def begin(self):
        me = self.me
        if self.over_x:
            for j in range(1, me.inner):
                for i, part in enumerate(self.parts):
                    self.sends.start(
                        True, part.at[self.blocks, (me.x + j) % me.inner],
                        self.target.at[j - 1, i], self.sems.at[j - 1, i], me.at_x(j),
                    )
        else:
            for i in range(1, me.outer):
                self.sends.start(
                    True, self.parts[i].at[self.blocks], self.target.at[i - 1],
                    self.sems.at[0, i - 1], me.at_y(-i),
                )

    def finish(self):
        me = self.me
        if self.over_x:
            for j in range(1, me.inner):
                for i in range(me.outer):
                    arrived(self.target.at[j - 1, i], self.sems.at[j - 1, i], me.at_c)
        else:
            for i in range(1, me.outer):
                arrived(self.target.at[i - 1], self.sems.at[0, i - 1], me.at_c)


def middle_kernel(shape, *refs):
    outer = shape[1]
    sent, own, middle, grads, gain = refs[:5]
    parts = refs[5 : 5 + 3 * outer]
    rows_to, d_middle, gain_grad = refs[5 + 3 * outer : 8 + 3 * outer]
    targets = refs[8 + 3 * outer : 12 + 3 * outer]
    middle_body(
        shape, sent, own, middle, grads, gain, parts, targets, rows_to, d_middle, gain_grad,
        *refs[12 + 3 * outer :],
    )


def plane_units(me, sends, parts, targets, sems):
    outer = me.outer
    gate, up, down = (parts[n * outer : (n + 1) * outer] for n in range(3))
    every, low, high = slice(0, Z), slice(0, Z // 2), slice(Z // 2, Z)
    return [
        PlaneTerms(me, sends, down, targets[0], sems.at[0], True, every),
        PlaneTerms(me, sends, gate, targets[1], sems.at[1], False, every),
        PlaneTerms(me, sends, up, targets[2], sems.at[2], True, low),
        PlaneTerms(me, sends, up, targets[3], sems.at[3], False, high),
    ]


def middle_body(
    shape, sent, own, middle, grads, gain, parts, targets, rows_to, d_middle, gain_grad,
    own_v, c_in, up_out, up_in, down_out, down_in, low,
    send_sems, local_sems, c_sems, up_sems, down_sems, rows_sems, unit_sems,
):
    me = Place(shape)
    rows = middle.shape[0]
    sends = Sends(send_sems)
    load = pltpu.make_async_copy(own, own_v, local_sems.at[0])
    load.start()
    me.greet()
    for k in line_order():
        sends.start(True, sent.at[k], c_in.at[k], c_sems.at[k], me.at_c)
    units = plane_units(me, sends, parts, targets, unit_sems)
    for unit in units:
        unit.begin()
    load.wait()

    def ready(k):
        arrived(c_in.at[k], c_sems.at[k], me.at_c)

    def term(k, r):
        return own_v[k, r] + c_in[k, r].astype(F32)

    def store(r, value):
        own_v[0, r] = value

    line_sum(
        me, sends, rows, term, ready, store, lambda r: own_v[0, r],
        (up_out, up_in, up_sems), (down_out, down_in, down_sems),
    )
    gain_grad[...] = jnp.zeros_like(gain_grad)

    def work(r):
        values = middle[r]
        inverse = lax.rsqrt(jnp.mean(values * values, axis=1, keepdims=True) + EPSILON)
        normed = values * inverse
        d_normed = own_v[0, r]
        gain_grad[...] += d_normed * normed
        scaled = d_normed * gain[...]
        passed = inverse * (scaled - normed * jnp.mean(scaled * normed, axis=1, keepdims=True))
        total = grads[r].astype(F32) + passed
        d_middle[r] = total
        low[r] = total.astype(BF16)

    each_rows(rows, 16, work)
    keep = pltpu.make_async_copy(low, rows_to.at[me.w], local_sems.at[1])
    keep.start()
    gather = WtRows(me, sends, low, rows_to, rows_sems)
    gather.begin()
    gather.step()
    gather.finish()
    for unit in units:
        unit.finish()
    sends.finish()
    keep.wait()


def middle_and_rows(sent, own, middle, grads, gain, parts):
    inner, outer = sizes()
    rows, width = middle.shape
    unit_rows, share = parts[0].shape[2:]
    over_x, over_y = (inner - 1, outer), (outer - 1,)
    targets = [
        jax.ShapeDtypeStruct(shape, BF16)
        for shape in (
            (*over_x, Z, unit_rows, share),
            (*over_y, Z, inner, unit_rows, share),
            (*over_x, Z // 2, unit_rows, share),
            (*over_y, Z // 2, inner, unit_rows, share),
        )
    ]
    unit_copies = 2 * (inner - 1) * outer + 2 * (outer - 1)
    dma = pltpu.SemaphoreType.DMA
    vmem, anywhere = pl.BlockSpec(memory_space=pltpu.VMEM), pl.BlockSpec(memory_space=pl.ANY)
    return pl.pallas_call(
        functools.partial(middle_kernel, (inner, outer)),
        out_shape=(
            jax.ShapeDtypeStruct((outer * C, rows, width), BF16),
            jax.ShapeDtypeStruct((rows, width), F32),
            jax.ShapeDtypeStruct((16, width), F32),
            *targets,
        ),
        in_specs=[anywhere, anywhere, vmem, vmem, vmem] + [anywhere] * (3 * outer),
        out_specs=(anywhere, vmem, vmem) + (anywhere,) * 4,
        scratch_shapes=[
            pltpu.VMEM((Z, rows, width), F32),
            pltpu.VMEM((Z, rows, width), BF16),
        ]
        + [pltpu.VMEM((Z - 1, rows, width), BF16)] * 4
        + [
            pltpu.VMEM((rows, width), BF16),
            dma((Z + 2 * (Z - 1) + 2 * outer + unit_copies,)),
            dma((2,)),
            dma((Z,)),
            dma((Z - 1,)),
            dma((Z - 1,)),
            dma((outer * C,)),
            dma((4, max(inner - 1, 1), outer)),
        ],
        compiler_params=pltpu.CompilerParams(
            collective_id=2, has_side_effects=True, vmem_limit_bytes=48 * 1024 * 1024
        ),
        name="middle_and_rows",
    )(sent, own, middle, grads, gain, *parts)


class RowsSum:
    def __init__(self, me, sends, terms, total, scratch, sems):
        self.me, self.sends, self.terms, self.total = me, sends, terms, total
        self.own, self.x_in, *ways = scratch
        self.own_sems, self.x_sems, up_sems, down_sems = sems
        self.up, self.down = (*ways[:2], up_sems), (*ways[2:], down_sems)

    def begin(self):
        me = self.me
        self.loads = {}
        for k in line_order():
            at = (me.z + Z - k) % Z
            for j in range(1, me.inner):
                self.sends.start(
                    True, self.terms.at[at, (me.x + j) % me.inner], self.x_in.at[j - 1, k],
                    self.x_sems.at[j - 1, k], me.at_x(j),
                )
            self.loads[k] = pltpu.make_async_copy(
                self.terms.at[at, me.x], self.own.at[k], self.own_sems.at[k]
            )
            self.loads[k].start()

    def run(self, between=None):
        me = self.me

        def ready(k):
            self.loads[k].wait()
            for j in range(1, me.inner):
                arrived(self.x_in.at[j - 1, k], self.x_sems.at[j - 1, k], me.at_c)

        def term(k, r):
            value = self.own[k, r].astype(F32)
            for j in range(1, me.inner):
                value = value + self.x_in[j - 1, k, r].astype(F32)
            return value

        def store(r, value):
            self.total[r] = value

        line_sum(
            me, self.sends, self.total.shape[0], term, ready, store, lambda r: self.total[r],
            self.up, self.down, between,
        )


def sums_kernel(shape, *refs):
    inner, outer = shape
    (units, wide, narrow, sent, own, tokens, gain, d_middle, gain_two_grad, vectors) = refs[:10]
    (units_to, wide_to, narrow_to, tokens_grad, gains, vectors_to) = refs[10:16]
    wide_scratch, narrow_scratch = refs[16:22], refs[22:28]
    (own_v, c_in, y_out, y_in, all_in, vec_in) = refs[28:34]
    (send_sems, local_sems, unit_sems, c_sems, y_sems, all_sems, vec_sems) = refs[34:41]
    wide_sems, narrow_sems = refs[41:45], refs[45:49]
    me = Place(shape)
    rows = tokens.shape[0]
    share = units.shape[3]
    count = units.shape[0]
    sends = Sends(send_sems)
    loads = [pltpu.make_async_copy(own, own_v, local_sems.at[0])]
    loads[0].start()
    me.greet()

    order = [(me.y + i) % outer for i in list(range(1, outer)) + [0]]
    for at in order:
        sends.start(True, sent.at[at], c_in.at[at], c_sems.at[at], me.at_c)
    narrow_sum = RowsSum(me, sends, narrow, narrow_to, narrow_scratch, narrow_sems)
    wide_sum = RowsSum(me, sends, wide, wide_to, wide_scratch, wide_sems)
    narrow_sum.begin()
    wide_sum.begin()

    def columns(n, at):
        return units_to.at[n, :, pl.ds(pl.multiple_of(at * share, LANES), share)]

    def units_begin():
        for n in range(count):
            copy = pltpu.make_async_copy(units.at[n, me.z], columns(n, me.z), local_sems.at[1 + n])
            copy.start()
            loads.append(copy)
            for k in range(1, Z):
                to = (me.z + k) % Z
                sends.start(
                    True, units.at[n, to], columns(n, me.z), unit_sems.at[n, me.z], me.at_z(to)
                )

    def units_finish():
        for n in range(count):
            for k in range(1, Z):
                at = (me.z + Z - k) % Z
                arrived(columns(n, at), unit_sems.at[n, at], me.at_c)

    units_begin()

    def exchange(held, into, sems, first, devices):
        for n, device in enumerate(devices):
            sends.start(True, held, into.at[first + n], sems.at[first + n], device)

    def gathered(held, into, sems, first, devices):
        for n, _ in enumerate(devices):
            arrived(into.at[first + n], sems.at[first + n], me.at_c)
        total = into[first]
        for n in range(1, len(devices)):
            total = total + into[first + n]
        return held[...] + total

    stages = [
        [me.at_c],
        [me.at_y(i) for i in range(1, outer)],
        [me.at_x(j) for j in range(1, inner)],
        [me.at_z((me.z + k) % Z) for k in range(1, Z)],
    ]
    at_stage = [0]
    for stage in stages:
        at_stage.append(at_stage[-1] + len(stage))

    loads[0].wait()
    for i, at in enumerate(order):
        arrived(c_in.at[at], c_sems.at[at], me.at_c)
        if i < outer - 1:
            each_rows(rows, 16, lambda r, i=i, at=at: y_out.__setitem__(
                (i, r), (own_v[at, r] + c_in[at, r]).astype(BF16)))
            sends.start(True, y_out.at[i], y_in.at[i], y_sems.at[i], me.at_y(i + 1))
    x_stage, z_stage = stages[2], stages[3]
    exchange(vectors, vec_in, vec_sems, 0, x_stage)
    narrow_sum.run()
    vectors_to[0] = gathered(vectors, vec_in, vec_sems, 0, x_stage)
    exchange(vectors_to.at[0], vec_in, vec_sems, len(x_stage), z_stage)
    for i in range(outer - 1):
        arrived(y_in.at[i], y_sems.at[i], me.at_c)
    gains[0] = jnp.zeros_like(gains[0])

    def work(r):
        d_normed = own_v[me.y, r] + c_in[me.y, r]
        for i in range(outer - 1):
            d_normed = d_normed + y_in[i, r].astype(F32)
        stream = tokens[r].astype(F32)
        inverse = lax.rsqrt(jnp.mean(stream * stream, axis=1, keepdims=True) + EPSILON)
        normed = stream * inverse
        part = d_normed * normed
        gains[0, 0:8] += part[0:8] + part[8:16]
        scaled = d_normed * gain[...]
        passed = inverse * (scaled - normed * jnp.mean(scaled * normed, axis=1, keepdims=True))
        tokens_grad[r] = (d_middle[r] + passed).astype(BF16)

    each_rows(rows, 16, work)
    gains[0, 8:16] = gain_two_grad[0:8] + gain_two_grad[8:16]
    exchange(gains.at[0], all_in, all_sems, 0, stages[0])

    def between(t):
        if t <= 3:
            held, into = gains.at[t - 1], gains.at[t]
            into[...] = gathered(held, all_in, all_sems, at_stage[t - 1], stages[t - 1])
            exchange(into, all_in, all_sems, at_stage[t], stages[t])

    wide_sum.run(between)
    gains[4] = gathered(gains.at[3], all_in, all_sems, at_stage[3], stages[3])
    vectors_to[1] = gathered(vectors_to.at[0], vec_in, vec_sems, len(x_stage), z_stage)
    units_finish()
    sends.finish()
    for copy in loads[1:]:
        copy.wait()


def last_sums(units, wide, narrow, sent, own, tokens, gain, d_middle, gain_two_grad, vectors):
    inner, outer = sizes()
    rows, width = tokens.shape
    dma = pltpu.SemaphoreType.DMA
    vmem, anywhere = pl.BlockSpec(memory_space=pltpu.VMEM), pl.BlockSpec(memory_space=pl.ANY)

    def scratch(terms):
        one = terms.shape[2:]
        return [pltpu.VMEM((Z, *one), BF16), pltpu.VMEM((inner - 1, Z, *one), BF16)] + [
            pltpu.VMEM((Z - 1, *one), BF16)
        ] * 4

    peers = 1 + (outer - 1) + (inner - 1) + (Z - 1)
    count, _, unit_rows, share = units.shape
    copies = 2 * outer - 1 + 2 * (Z * (inner - 1) + 2 * (Z - 1)) + count * (Z - 1)
    copies += peers + (inner - 1) + (Z - 1)
    line_sems = [dma((Z,)), dma((inner - 1, Z)), dma((Z - 1,)), dma((Z - 1,))]
    return pl.pallas_call(
        functools.partial(sums_kernel, (inner, outer)),
        out_shape=(
            jax.ShapeDtypeStruct((count, unit_rows, Z * share), BF16),
            jax.ShapeDtypeStruct(wide.shape[2:], F32),
            jax.ShapeDtypeStruct(narrow.shape[2:], F32),
            jax.ShapeDtypeStruct((rows, width), BF16),
            jax.ShapeDtypeStruct((5, 16, width), F32),
            jax.ShapeDtypeStruct((2, *vectors.shape), F32),
        ),
        in_specs=[anywhere] * 5 + [vmem] * 5,
        out_specs=(anywhere,) + (vmem,) * 5,
        scratch_shapes=scratch(wide)
        + scratch(narrow)
        + [
            pltpu.VMEM((outer, rows, width), F32),
            pltpu.VMEM((outer, rows, width), F32),
            pltpu.VMEM((outer - 1, rows, width), BF16),
            pltpu.VMEM((outer - 1, rows, width), BF16),
            pltpu.VMEM((peers, 16, width), F32),
            pltpu.VMEM((inner - 1 + Z - 1, *vectors.shape), F32),
            dma((copies,)),
            dma((1 + count,)),
            dma((count, Z)),
            dma((outer,)),
            dma((outer - 1,)),
            dma((peers,)),
            dma((inner - 1 + Z - 1,)),
        ]
        + line_sems * 2,
        compiler_params=pltpu.CompilerParams(
            collective_id=5, has_side_effects=True, vmem_limit_bytes=58 * 1024 * 1024
        ),
        name="last_sums",
    )(units, wide, narrow, sent, own, tokens, gain, d_middle, gain_two_grad, vectors)


def scan_kernel(backward, factors, inflows, states, entered, products, ends, ends_in, carry, send_sems, arrivals):
    seq = ends_in.shape[0]
    s = lax.axis_index("seq")
    rows, width = factors.shape
    barrier = pltpu.get_barrier_semaphore()

    def device(at):
        return {"seq": at, "wt": lax.axis_index("wt")}

    def greet(i, carried):
        @pl.when(i != s)
        def _():
            pl.semaphore_signal(barrier, inc=1, device_id=device(i), device_id_type=MESH)

        return carried

    lax.fori_loop(0, seq, greet, 0)
    group = 8
    at_row = lax.broadcasted_iota(jnp.int32, (group, width), 0)

    def step(i, carried):
        held, product = carried
        i = rows // group - 1 - i if backward else i
        where = pl.ds(pl.multiple_of(i * group, group), group)
        factor, inflow = factors[where, :], inflows[where, :]
        for by in (1, 2, 4):
            inside = at_row < group - by if backward else at_row >= by
            turn = group - by if backward else by
            inflow = factor * jnp.where(inside, pltpu.roll(inflow, turn, 0), 0.0) + inflow
            factor = factor * jnp.where(inside, pltpu.roll(factor, turn, 0), 1.0)
        inflow = inflow + factor * held
        factor = factor * product
        states[where, :] = inflow
        products[where, :] = factor
        last = slice(0, 1) if backward else slice(group - 1, group)
        return inflow[last], factor[last]

    held, product = lax.fori_loop(
        0, rows // group, step, (jnp.zeros((1, width), F32), jnp.ones((1, width), F32))
    )
    ends[0:1] = product
    ends[1:2] = held
    pl.semaphore_wait(barrier, seq - 1)

    def copy_to(i):
        return pltpu.make_async_remote_copy(
            src_ref=ends, dst_ref=ends_in.at[s], send_sem=send_sems.at[i], recv_sem=arrivals.at[s],
            device_id=device(i), device_id_type=MESH,
        )

    def later(i):
        return i < s if backward else i > s

    def send(i, carried):
        pl.when(later(i))(lambda: copy_to(i).start())
        return carried

    lax.fori_loop(0, seq, send, 0)
    carry[...] = jnp.zeros_like(carry)

    def receive(n, carried):
        i = seq - 1 - n if backward else n

        @pl.when(jnp.logical_not(later(i)) & (i != s))
        def _():
            arrived(ends_in.at[i], arrivals.at[i], device((s + 1) % seq))
            carry[0:1] = ends_in[i, 0:1] * carry[0:1] + ends_in[i, 1:2]

        return carried

    lax.fori_loop(0, seq, receive, 0)
    entering = carry[0:1]
    entered[...] = entering

    def spread(i, carried):
        where = pl.ds(pl.multiple_of(i * group, group), group)
        states[where, :] += products[where, :] * entering
        return carried

    lax.fori_loop(0, rows // group, spread, 0)

    def sent(i, carried):
        pl.when(later(i))(lambda: copy_to(i).wait_send())
        return carried

    lax.fori_loop(0, seq, sent, 0)


def full_scan(factor, inflow, backward):
    seq = lax.axis_size("seq")
    rows, width = factor.shape
    vmem = pl.BlockSpec(memory_space=pltpu.VMEM)
    return pl.pallas_call(
        functools.partial(scan_kernel, backward),
        out_shape=(
            jax.ShapeDtypeStruct((rows, width), F32),
            jax.ShapeDtypeStruct((1, width), F32),
        ),
        in_specs=[vmem, vmem],
        out_specs=(vmem, vmem),
        scratch_shapes=[
            pltpu.VMEM((rows, width), F32),
            pltpu.VMEM((8, width), F32),
            pltpu.VMEM((seq, 8, width), F32),
            pltpu.VMEM((8, width), F32),
            pltpu.SemaphoreType.DMA((seq,)),
            pltpu.SemaphoreType.DMA((seq,)),
        ],
        compiler_params=pltpu.CompilerParams(
            collective_id=4 if backward else 3,
            has_side_effects=True,
            vmem_limit_bytes=32 * 1024 * 1024,
        ),
        name="scan_back" if backward else "scan_ahead",
    )(factor, inflow)


def recurrence_terms(decay_pre, input_pre, decay_log, conv_float):
    log_decay = -DECAY_SCALE * jax.nn.softplus(-decay_log) * jax.nn.sigmoid(decay_pre)
    return (
        jnp.exp(log_decay),
        jnp.sqrt(-jnp.expm1(2.0 * log_decay)) * jax.nn.sigmoid(input_pre) * conv_float,
    )


def norm_back(d_normed, normed, inverse, gain_row):
    scaled = d_normed * gain_row
    return inverse * (scaled - normed * jnp.mean(scaled * normed, axis=1, keepdims=True))


def normed_rows(stream):
    inverse = lax.rsqrt(jnp.mean(stream * stream, axis=1, keepdims=True) + EPSILON)
    return stream * inverse, inverse


def per_device(
    tokens,
    norm1_gain,
    x_weight,
    y_weight,
    conv_weight,
    conv_bias,
    decay_gate_weight,
    decay_bias,
    input_gate_weight,
    input_bias,
    decay_param,
    out_weight,
    norm2_gain,
    gate_weight,
    up_weight,
    down_weight,
    out_grad,
):
    seq, wt = lax.axis_size("seq"), lax.axis_size("wt")
    inner, outer = sizes()
    z, x, y, c = places()
    w = lax.axis_index("wt")
    rows_dev, width = tokens.shape
    weight_rows, lru_cols = x_weight.shape
    chunk, block = decay_gate_weight.shape
    half = block // 2
    full = lru_cols - half
    taps_count = conv_weight.shape[1]
    reach = taps_count - 1
    hidden_cols = gate_weight.shape[1]

    def turned(value, axis):
        return jnp.where(c == 0, value, jnp.roll(value, -half, axis))

    def turned_back(value, axis):
        return jnp.where(c == 0, value, jnp.roll(value, half, axis))

    def in_order(own, partner, axis):
        return jnp.where(
            c == 0,
            jnp.concatenate([own, partner], axis),
            jnp.concatenate([partner, own], axis),
        )

    vectors = jnp.stack(
        [v.astype(F32) for v in (norm1_gain, norm2_gain, conv_bias, decay_bias, input_bias)]
        + [decay_param]
        + [conv_weight[:, k].astype(F32) for k in range(taps_count)]
    )
    vectors = jnp.pad(vectors, ((0, -vectors.shape[0] % 8), (0, -chunk % LANES)))

    across = [(i, i % seq * wt + i // seq) for i in range(seq * wt)]
    gates = jnp.concatenate([decay_gate_weight, input_gate_weight], axis=1)
    gates = lax.ppermute(gates, ("seq", "wt"), across)

    def padded(weight):
        share = -(-hidden_cols // (Z * LANES)) * LANES
        return jnp.pad(weight, ((0, 0), (0, Z * share - hidden_cols)))

    xy_unit = jnp.concatenate([turned(x_weight, 1), turned(y_weight, 1)], axis=1)
    (
        group_tokens, grad_group, vectors, gate_all, xy_kernel, out_kernel,
        gate_kernel, up_kernel, down_kernel,
    ) = gather_all(
        tokens, out_grad, vectors, gates, xy_unit, turned(out_weight, 1),
        padded(gate_weight), padded(up_weight), padded(down_weight),
    )
    group_tokens = group_tokens.reshape(-1, width)
    grad_group = grad_group.reshape(-1, width)
    vectors = jnp.moveaxis(vectors[:, : 6 + taps_count, :chunk], 0, 1).reshape(6 + taps_count, -1)
    gain_one, gain_two = vectors[0], vectors[1]
    own_vectors = turned(
        lax.dynamic_slice(vectors[2:], (0, w * lru_cols), (taps_count + 4, lru_cols)), 1
    )
    tap_bias, decay_shift, input_shift, decay_log = (own_vectors[i] for i in range(4))
    taps = own_vectors[4:]
    xy_kernel = xy_kernel.reshape(width, -1)
    out_kernel = out_kernel.reshape(width, -1)
    gate_kernel = gate_kernel.reshape(width, -1)
    up_kernel = up_kernel.reshape(width, -1)
    down_kernel = down_kernel.reshape(width, -1)
    gate_all = turned(gate_all.reshape(lru_cols, 2 * block), 0)
    partner_rows = c_swap(gate_all[full:])
    shared_rows = in_order(gate_all[full:], partner_rows, 0)

    stream = tokens.astype(F32)
    group_normed, _ = normed_rows(group_tokens.astype(F32))
    group_one = (group_normed * gain_one).astype(BF16)
    rows = group_one.shape[0]
    xy = multiply(group_one, xy_kernel)
    x_branch = xy[:, :lru_cols].astype(BF16)
    y_before = xy[:, lru_cols:]
    y_gated, gelu_y_back = jax.vjp(gelu_tanh, y_before)
    rim = lax.ppermute(x_branch[rows - reach :], "seq", [(i, i + 1) for i in range(seq - 1)])
    extended = jnp.concatenate([rim, x_branch], axis=0).astype(F32)
    conv_low = (
        tap_bias
        + sum(taps[k] * extended[reach - k : reach - k + rows] for k in range(taps_count))
    ).astype(BF16)
    shared_conv = in_order(conv_low[:, full:], c_swap(conv_low[:, full:]), 1)
    heads = full // block

    def of_head(value, i):
        return value[:, i * block : (i + 1) * block]

    pre_parts = [
        multiply(of_head(conv_low, i), gate_all[i * block : (i + 1) * block]) for i in range(heads)
    ]
    shared_pre = multiply(shared_conv, shared_rows).reshape(rows, 2, C, half)
    shared_pre = pick(shared_pre, c, 2)
    decay_pre = decay_shift + jnp.concatenate(
        [part[:, :block] for part in pre_parts] + [shared_pre[:, 0]], axis=1
    )
    input_pre = input_shift + jnp.concatenate(
        [part[:, block:] for part in pre_parts] + [shared_pre[:, 1]], axis=1
    )
    (retain, inflow), terms_back = jax.vjp(
        recurrence_terms, decay_pre, input_pre, decay_log, conv_low.astype(F32)
    )
    states, state_in = full_scan(retain, inflow, False)
    before = jnp.concatenate([state_in, states[:-1]])
    lru_low = states.astype(BF16).astype(F32)
    mixed_rows = (lru_low * y_gated).astype(BF16)
    mixed_parts = mixed_rows.reshape(outer, C, rows_dev, lru_cols)

    def branch_of(at):
        part = pick(mixed_parts, at, 1).reshape(outer * rows_dev, lru_cols)
        return contract_last(part, out_kernel).reshape(outer, rows_dev, width)

    group_two, middle = branch_and_group(
        branch_of(1 - c), branch_of(c), tokens, gain_two[None]
    )
    group_two = group_two.reshape(C * Z * rows_dev, width)

    gate_pre = multiply(group_two, gate_kernel)
    up_pre = multiply(group_two, up_kernel)
    active, gelu_gate_back = jax.vjp(gelu_tanh, gate_pre)
    hidden = (active * up_pre).astype(BF16)

    d_hidden = multiply(grad_group, down_kernel)
    d_up = (d_hidden * active).astype(BF16)
    d_gate = gelu_gate_back(d_hidden * up_pre)[0].astype(BF16)
    half_rows = Z * rows_dev

    def d_normed_of(part):
        total = contract_last(d_gate[part], gate_kernel) + contract_last(d_up[part], up_kernel)
        return total.reshape(Z, rows_dev, width)

    def terms_of(left_side, right_side):
        share = right_side.shape[1] // outer
        return [
            contract_rows(left_side, right_side[:, i * share : (i + 1) * share])
            .astype(BF16)
            .reshape(Z, inner, weight_rows, share)
            for i in range(outer)
        ]

    gate_terms = terms_of(group_two, d_gate)
    up_terms = terms_of(group_two, d_up)
    down_terms = terms_of(grad_group, hidden)
    branch_rows, d_middle, gain_two_grad, *came = middle_and_rows(
        d_normed_of(slice(half_rows, None)).astype(BF16),
        d_normed_of(slice(0, half_rows)),
        middle,
        out_grad,
        gain_two[None],
        gate_terms + up_terms + down_terms,
    )
    branch_rows = branch_rows.reshape(-1, width)

    def added_over_x(terms, moved):
        return [
            sum((moved[j - 1, i].astype(F32) for j in range(1, inner)), pick(term, x, 1).astype(F32))
            for i, term in enumerate(terms)
        ]

    def added_over_y(term, moved):
        return sum((moved[i - 1].astype(F32) for i in range(1, outer)), term.astype(F32))

    half_z = Z // 2
    down_x = added_over_x(down_terms, came[0])
    gate_y = added_over_y(gate_terms[0], came[1])
    up_x = added_over_x([term[:half_z] for term in up_terms], came[2])
    up_y = added_over_y(up_terms[0][half_z:], came[3])
    by_y = [jnp.concatenate([down_x[i], up_x[i]]).astype(BF16) for i in range(outer)]
    by_y = sum(
        (y_move(by_y[i], -i).astype(F32) for i in range(1, outer)),
        jnp.concatenate([down_x[0], up_x[0]]),
    )
    by_x_all = jnp.concatenate([gate_y, up_y])
    by_x = sum(
        (
            x_move(pick(by_x_all, (x + j) % inner, 1).astype(BF16), j).astype(F32)
            for j in range(1, inner)
        ),
        pick(by_x_all, x, 1),
    )
    units = jnp.stack([by_x[:Z], jnp.concatenate([by_y[Z:], by_x[Z:]]), by_y[:Z]]).astype(BF16)

    feed = group_scatter(lambda rows_: contract_last(rows_, down_kernel), after(hidden, d_middle))
    block_out = (middle + feed).astype(BF16)

    d_mixed = multiply(branch_rows, out_kernel)
    d_lru = (d_mixed * y_gated).astype(BF16).astype(F32)
    d_y = gelu_y_back(d_mixed * lru_low)[0].astype(BF16)
    passed, passed_in = full_scan(retain, retain * d_lru, True)
    d_total = d_lru + jnp.concatenate([passed[1:], passed_in])
    d_decay_pre, d_input_pre, decay_log_grad, d_conv_direct = terms_back(
        (d_total * before, d_total)
    )
    d_decay_low, d_input_low = d_decay_pre.astype(BF16), d_input_pre.astype(BF16)
    own_low = jnp.concatenate([d_decay_low[:, full:], d_input_low[:, full:]], axis=1)
    partner_low = c_swap(own_low)
    shared_low = jnp.concatenate(
        [
            in_order(own_low[:, :half], partner_low[:, :half], 1),
            in_order(own_low[:, half:], partner_low[:, half:], 1),
        ],
        axis=1,
    )
    lows = [
        jnp.concatenate([of_head(d_decay_low, i), of_head(d_input_low, i)], axis=1)
        for i in range(heads)
    ]
    d_conv = d_conv_direct + jnp.concatenate(
        [contract_last(lows[i], gate_all[i * block : (i + 1) * block]) for i in range(heads)]
        + [contract_last(shared_low, gate_all[full:])],
        axis=1,
    )
    gates_grad = jnp.concatenate(
        [contract_rows(of_head(conv_low, i), lows[i]) for i in range(heads)]
        + [contract_rows(conv_low[:, full:], shared_low)]
    )
    ahead = lax.ppermute(d_conv[:reach], "seq", [(i + 1, i) for i in range(seq - 1)])
    d_extended = jnp.concatenate([d_conv, ahead], axis=0)
    d_x_branch = sum(taps[k] * d_extended[k : k + rows] for k in range(taps_count)).astype(BF16)
    dx_parts = d_x_branch.reshape(outer, C, rows_dev, lru_cols)
    dy_parts = d_y.reshape(outer, C, rows_dev, lru_cols)

    def d_normed_one_of(at):
        dx, dy = (
            pick(parts, at, 1).reshape(outer * rows_dev, lru_cols) for parts in (dx_parts, dy_parts)
        )
        total = contract_last(dx, xy_kernel[:, :lru_cols]) + contract_last(
            dy, xy_kernel[:, lru_cols:]
        )
        return total.reshape(outer, rows_dev, width)

    wide = jnp.concatenate(
        [
            contract_rows(group_one, d_x_branch),
            contract_rows(group_one, d_y),
            contract_rows(branch_rows, mixed_rows),
        ],
        axis=1,
    )
    wide = wide.astype(BF16).reshape(Z, inner, weight_rows, 3 * lru_cols)
    narrow = turned_back(gates_grad, 0).astype(BF16).reshape(Z, inner, chunk, 2 * block)
    narrow = jnp.pad(narrow, ((0, 0), (0, 0), (0, -chunk % 16), (0, 0)))
    own_sums = jnp.stack(
        [jnp.sum(d_conv, axis=0), jnp.sum(d_decay_pre, axis=0), jnp.sum(d_input_pre, axis=0)]
        + [decay_log_grad]
        + [jnp.sum(d_conv * extended[reach - k : reach - k + rows], axis=0) for k in range(taps_count)],
    )
    own_sums = turned_back(own_sums, 1)
    units, wide, narrow, tokens_grad, gains, own_sums = last_sums(
        units, wide, narrow, d_normed_one_of(1 - c), d_normed_one_of(c), tokens, gain_one[None],
        d_middle, gain_two_grad, own_sums,
    )
    weight_grads = [
        turned_back(wide[:, n * lru_cols : (n + 1) * lru_cols], 1) for n in range(3)
    ]
    gate_grad, up_grad, down_grad = (units[n, :, :hidden_cols].astype(F32) for n in range(3))
    gains = gains[4].reshape(2, 8, width).sum(axis=1)
    gains = lax.dynamic_slice(gains, (0, (lax.axis_index("seq") * wt + w) * chunk), (2, chunk))
    sums = lax.dynamic_slice(own_sums[1], (0, lax.axis_index("seq") * chunk), (taps_count + 4, chunk))
    own_sums = jnp.concatenate([narrow[:chunk], sums.T], axis=1)
    own_sums = lax.ppermute(own_sums, ("seq", "wt"), [(to, at) for at, to in across])
    sums = own_sums[:, 2 * block :]
    return (
        block_out,
        tokens_grad,
        gains[0],
        weight_grads[0],
        weight_grads[1],
        sums[:, 4:],
        sums[:, 0],
        own_sums[:, :block],
        sums[:, 1],
        own_sums[:, block : 2 * block],
        sums[:, 2],
        sums[:, 3],
        weight_grads[2],
        gains[1],
        gate_grad,
        up_grad,
        down_grad,
    )


def solution(mesh):
    rows, both, lone = P(("seq", "wt"), None), P("seq", "wt"), P(("seq", "wt"))
    in_specs = (
        rows, lone, both, both, rows, lone, rows, lone, rows, lone, lone,
        both, lone, both, both, both, rows,
    )
    out_specs = (
        rows, rows, lone, both, both, rows, lone, rows, lone, rows, lone, lone,
        both, lone, both, both, both,
    )
    return jax.shard_map(
        per_device, mesh=mesh, in_specs=in_specs, out_specs=out_specs, check_vma=False
    )
```

```python
import functools

import jax
import jax.numpy as jnp
from jax import lax
from jax.experimental import pallas as pl
from jax.experimental.pallas import tpu as pltpu
from jax.sharding import PartitionSpec as P

EPSILON = 1e-06
DECAY_SCALE = 8.0
Z = 4
C = 2
LANES = 128
F32 = jnp.float32
BF16 = jnp.bfloat16
MESH = pl.DeviceIdType.MESH


def gelu_tanh(values):
    return jax.nn.gelu(values, approximate=True)


def sizes():
    return lax.axis_size("seq") // Z, lax.axis_size("wt") // C


def places():
    inner, outer = sizes()
    s, w = lax.axis_index("seq"), lax.axis_index("wt")
    return s // inner, s % inner, w // C, w % C


def after(value, *earlier):
    return lax.optimization_barrier((value, *earlier))[0]


def z_move(value, by, senders):
    inner, _ = sizes()
    pairs = [(z * inner + x, (z + by) % Z * inner + x) for z in senders for x in range(inner)]
    return lax.ppermute(value, "seq", pairs)


def z_turn(value, by):
    return z_move(value, by, range(Z))


def x_move(value, by):
    inner, _ = sizes()
    pairs = [(z * inner + x, z * inner + (x + by) % inner) for z in range(Z) for x in range(inner)]
    return lax.ppermute(value, "seq", pairs)


def y_move(value, by):
    _, outer = sizes()
    pairs = [(y * C + c, (y + by) % outer * C + c) for y in range(outer) for c in range(C)]
    return lax.ppermute(value, "wt", pairs)


def c_swap(value):
    _, outer = sizes()
    pairs = [(y * C + c, y * C + 1 - c) for y in range(outer) for c in range(C)]
    return lax.ppermute(value, "wt", pairs)


def line_gather(value):
    z = places()[0]
    up, down = [value], [value]
    for k in range(1, Z):
        up.append(z_move(up[-1], 1, range(k - 1, Z - 1)))
        down.append(z_move(down[-1], -1, range(1, Z - k + 1)))
    return [value] + [jnp.where(z >= k, up[k], down[Z - k]) for k in range(1, Z)]


def line_scatter(parts):
    up = down = None
    for step in range(1, Z):
        rising = parts[step] if up is None else parts[step] + up
        falling = parts[Z - step] if down is None else parts[Z - step] + down
        up = z_move(rising.astype(BF16), 1, range(0, step)).astype(F32)
        down = z_move(falling.astype(BF16), -1, range(Z - step, Z)).astype(F32)
    return parts[0] + up + down


def pick(value, index, axis):
    return lax.dynamic_index_in_dim(value, index, axis, keepdims=False)


def put(buffer, value, starts):
    return lax.dynamic_update_slice(buffer, value, starts)


def contract_last(left_side, right_side):
    return lax.dot_general(
        left_side, right_side, (((1,), (1,)), ((), ())), preferred_element_type=F32
    )


def contract_rows(left_side, right_side):
    return lax.dot_general(
        left_side, right_side, (((0,), (0,)), ((), ())), preferred_element_type=F32
    )


def multiply(left_side, right_side):
    return jnp.dot(left_side, right_side, preferred_element_type=F32)


def seq_scatter(total):
    inner, _ = sizes()
    z, x = places()[:2]
    total = total.reshape(Z, inner, -1, total.shape[1])
    kept = pick(total, x, 1)
    for j in range(1, inner):
        kept = kept + x_move(pick(total, (x + j) % inner, 1).astype(BF16), j).astype(F32)
    return line_scatter([pick(kept, (z - k) % Z, 0) for k in range(Z)])


def plane_scatter(left_side, right_side, width, x_first, gate):
    inner, outer = sizes()
    z, x = places()[:2]
    share = right_side.shape[1] // outer

    def over_x(value):
        total = pick(value, x, 1).astype(F32)
        for j in range(1, inner):
            total = total + x_move(pick(value, (x + j) % inner, 1), j).astype(F32)
        return total.astype(BF16)

    def over_y(parts):
        total = parts[0].astype(F32)
        for i in range(1, outer):
            total = total + y_move(parts[i], -i).astype(F32)
        return total.astype(BF16)

    parts = []
    for i in range(outer):
        part = contract_rows(left_side, right_side[:, i * share : (i + 1) * share]).astype(BF16)
        parts.append(part.reshape(Z, inner, -1, share))
    rows = parts[0].shape[2]
    kept = over_y([over_x(part) for part in parts]) if x_first else over_x(over_y(parts))
    kept = after(kept, gate)
    buffer = put(jnp.zeros((rows, Z * share), BF16), pick(kept, z, 0), (0, z * share))
    for k in range(1, Z):
        moved = z_move(pick(kept, (z + k) % Z, 0), k, range(Z))
        buffer = put(buffer, moved, (0, (z - k) % Z * share))
    return buffer[:, :width].astype(F32)


def wt_scatter(product_of, *sides):
    _, outer = sizes()
    _, _, y, c = places()

    def chosen(at):
        cut = [side.reshape(outer, C, -1, side.shape[1]) for side in sides]
        return [pick(side, at, 1).reshape(-1, side.shape[3]) for side in cut]

    sent = c_swap(product_of(*chosen(1 - c)))
    kept = product_of(*chosen(c)) + sent
    kept = kept.reshape(outer, -1, kept.shape[1])
    total = pick(kept, y, 0)
    for i in range(1, outer):
        total = total + y_move(pick(kept, (y + i) % outer, 0).astype(BF16), i).astype(F32)
    return total


def group_gather(value):
    blocks = line_gather(value)
    return jnp.concatenate(blocks + [c_swap(block) for block in blocks])


def group_scatter(product_of, *sides):
    half = sides[0].shape[0] // 2
    sent = c_swap(product_of(*[side[half:] for side in sides]).astype(BF16))
    kept = product_of(*[side[:half] for side in sides]) + sent.astype(F32)
    rows = half // Z
    return line_scatter([kept[k * rows : (k + 1) * rows] for k in range(Z)])


class Sends:
    def __init__(self, sems):
        self.sems, self.started = sems, []

    def start(self, when, source, target, arrival, device):
        copy = pltpu.make_async_remote_copy(
            src_ref=source,
            dst_ref=target,
            send_sem=self.sems.at[len(self.started)],
            recv_sem=arrival,
            device_id=device,
            device_id_type=MESH,
        )
        if when is True:
            copy.start()
        else:
            pl.when(when)(copy.start)
        self.started.append((when, copy))

    def finish(self):
        for when, copy in self.started:
            if when is True:
                copy.wait_send()
            else:
                pl.when(when)(copy.wait_send)


def arrived(target, arrival, device):
    pltpu.make_async_remote_copy(
        src_ref=target, dst_ref=target, send_sem=arrival, recv_sem=arrival,
        device_id=device, device_id_type=MESH,
    ).wait_recv()


def gather_kernel(shape, *refs):
    inner, outer = shape
    (tokens, vectors, gates, xy, out, gate, up, down) = refs[:8]
    (tokens_to, vectors_to, gates_to, xy_to, out_to, gate_to, up_to, down_to) = refs[8:16]
    (gates_own, send_sems, local_sems, line_sems, plane_sems, rows_sems, vector_sems, turn_sems) = refs[16:]
    seq, wt = Z * inner, outer * C
    s, w = lax.axis_index("seq"), lax.axis_index("wt")
    z, x, y, c = s // inner, s % inner, w // C, w % C
    sends = Sends(send_sems)
    here = []

    def at_z(to):
        return {"seq": to * inner + x, "wt": w}

    def at_x(by):
        return {"seq": z * inner + (x + by) % inner, "wt": w}

    def at_y(by):
        return {"seq": s, "wt": (y + by) % outer * C + c}

    at_c = {"seq": s, "wt": y * C + 1 - c}

    def keep(source, target, waited=False):
        copy = pltpu.make_async_copy(source, target, local_sems.at[len(here)])
        copy.start()
        here.append((waited, copy))
        return copy

    barrier = pltpu.get_barrier_semaphore()

    def greet(i, carried):
        @pl.when(i != s * wt + w)
        def _():
            pl.semaphore_signal(
                barrier, inc=1, device_id={"seq": i // wt, "wt": i % wt}, device_id_type=MESH
            )

        return carried

    lax.fori_loop(0, seq * wt, greet, 0)
    pl.semaphore_wait(barrier, seq * wt - 1)

    class Line:
        def __init__(self, index, source, target):
            self.source, self.target = source, target
            self.sems = line_sems.at[index]

        def forward(self, block, at, up_when, down_when):
            place = self.target.at[at, x]
            arrival = self.sems.at[at, x]
            sends.start(up_when, block, place, arrival, at_z(jnp.minimum(z + 1, Z - 1)))
            sends.start(down_when, block, place, arrival, at_z(jnp.maximum(z - 1, 0)))
            return place, arrival

        def across(self, when, block, at):
            for j in range(1, inner):
                sends.start(when, block, self.target.at[at, x], self.sems.at[at, x], at_x(j))

        def begin(self):
            keep(self.source, self.target.at[z, x])
            self.forward(self.source, z, z < Z - 1, z > 0)
            self.across(True, self.source, z)

        def step(self, k):
            for at, there, up_when, down_when in (
                (jnp.maximum(z - k, 0), z - k >= 0, (z - k >= 0) & (z < Z - 1), None),
                (jnp.minimum(z + k, Z - 1), z + k < Z, None, (z + k < Z) & (z > 0)),
            ):
                place, arrival = self.target.at[at, x], self.sems.at[at, x]

                @pl.when(there)
                def _(place=place, arrival=arrival):
                    arrived(place, arrival, at_c)

                if up_when is not None:
                    sends.start(up_when, place, place, arrival, at_z(jnp.minimum(z + 1, Z - 1)))
                else:
                    sends.start(down_when, place, place, arrival, at_z(jnp.maximum(z - 1, 0)))
                self.across(there, place, at)

        def finish(self):
            for at in range(Z):
                for j in range(1, inner):
                    from_x = (x + inner - j) % inner
                    arrived(self.target.at[at, from_x], self.sems.at[at, from_x], at_c)

    class Plane:
        def __init__(self, index, source, target, x_first, whole):
            self.source, self.target, self.x_first, self.whole = source, target, x_first, whole
            self.share = source.shape[1] // Z
            self.sems = plane_sems.at[index]

        def cut(self, at):
            return self.source.at[:, pl.ds(pl.multiple_of(at * self.share, LANES), self.share)]

        def place(self, at, x_at, i):
            return self.target.at[at, x_at, :, i * self.share : (i + 1) * self.share]

        def begin(self):
            self.own = keep(self.cut(z), self.place(z, x, 0), True)
            for k in range(1, Z):
                to = (z + k) % Z
                sends.start(True, self.cut(to), self.place(z, x, 0), self.sems.at[z, 0, 0], at_z(to))

        def over_x(self, at, i):
            place = self.place(at, x, i)
            for j in range(1, inner):
                sends.start(True, place, place, self.sems.at[at, j, i], at_x(j))

        def over_y(self, at, j):
            x_at = (x + inner - j) % inner
            for i in range(1, outer):
                sends.start(
                    True, self.place(at, x_at, 0), self.place(at, x_at, i),
                    self.sems.at[at, j, i], at_y(i),
                )

        def got(self, at, j, i):
            arrived(self.place(at, (x + inner - j) % inner, i), self.sems.at[at, j, i], at_c)

        def first(self, k):
            at = (z + Z - k) % Z
            if k == 0:
                self.own.wait()
            else:
                self.got(at, 0, 0)
            if self.x_first or self.whole:
                self.over_x(at, 0)
            if self.whole or not self.x_first:
                self.over_y(at, 0)

        def second(self, k):
            at = (z + Z - k) % Z
            if self.x_first:
                for j in range(1, inner):
                    self.got(at, j, 0)
                    if self.whole:
                        self.over_y(at, j)
            else:
                for i in range(1, outer):
                    self.got(at, 0, i)

        def finish(self, k):
            if self.whole:
                at = (z + Z - k) % Z
                for j in range(inner):
                    for i in range(1, outer):
                        self.got(at, j, i)

    lines = [Line(0, xy, xy_to), Line(1, gates_own, gates_to), Line(2, out, out_to)]
    planes = [
        Plane(0, gate, gate_to, True, True),
        Plane(1, up, up_to, False, False),
        Plane(2, down, down_to, True, False),
    ]

    me = s * wt + w
    keep(vectors, vectors_to.at[me])

    def vector_copy(i):
        return pltpu.make_async_remote_copy(
            src_ref=vectors, dst_ref=vectors_to.at[me],
            send_sem=vector_sems.at[0, i], recv_sem=vector_sems.at[1, me],
            device_id={"seq": i // wt, "wt": i % wt}, device_id_type=MESH,
        )

    def vector_send(i, carried):
        pl.when(i != me)(lambda: vector_copy(i).start())
        return carried

    def tokens_begin():
        keep(tokens, tokens_to.at[w])
        sends.start(True, tokens, tokens_to.at[w], rows_sems.at[w], at_c)
        for i in range(1, outer):
            sends.start(True, tokens, tokens_to.at[w], rows_sems.at[w], at_y(i))

    def tokens_step():
        for i in range(1, outer):
            at = (y + outer - i) % outer * C + c
            arrived(tokens_to.at[at], rows_sems.at[at], at_c)
            sends.start(True, tokens_to.at[at], tokens_to.at[at], rows_sems.at[at], at_c)

    def tokens_finish():
        for i in range(outer):
            at = (y + outer - i) % outer * C + 1 - c
            arrived(tokens_to.at[at], rows_sems.at[at], at_c)

    to_seq, to_wt = me % seq, me // seq
    from_me = w * seq + s
    turn = pltpu.make_async_remote_copy(
        src_ref=gates, dst_ref=gates_own, send_sem=turn_sems.at[0], recv_sem=turn_sems.at[1],
        device_id={"seq": to_seq, "wt": to_wt}, device_id_type=MESH,
    )
    stay = pltpu.make_async_copy(gates, gates_own, turn_sems.at[2])
    here_too = from_me == me

    pl.when(jnp.logical_not(here_too))(turn.start)
    pl.when(here_too)(stay.start)
    lines[0].begin()
    tokens_begin()

    @pl.when(jnp.logical_not(here_too))
    def _():
        arrived(gates_own, turn_sems.at[1], at_c)

    pl.when(here_too)(stay.wait)
    lines[1].begin()
    lax.fori_loop(0, seq * wt, vector_send, 0)
    for k in range(1, Z):
        lines[1].step(k)
        lines[0].step(k)
        if k == 1:
            tokens_step()
            planes[1].begin()
    for k in range(Z):
        planes[1].first(k)
    planes[0].begin()
    lines[2].begin()
    planes[0].first(0)
    for k in range(1, Z):
        lines[2].step(k)
        planes[0].first(k)
    planes[2].begin()
    for k in range(Z):
        planes[2].first(k)
        planes[0].second(k)

    for line in lines:
        line.finish()
    tokens_finish()
    for k in range(Z):
        planes[1].second(k)
        planes[2].second(k)
        planes[0].finish(k)

    def vector_wait(i, carried):
        @pl.when(i != me)
        def _():
            vector_copy(i).wait_send()
            arrived(vectors_to.at[i], vector_sems.at[1, i], at_c)

        return carried

    pl.when(jnp.logical_not(here_too))(turn.wait_send)
    lax.fori_loop(0, seq * wt, vector_wait, 0)
    sends.finish()
    for waited, copy in here:
        if not waited:
            copy.wait()


def gather_all(tokens, vectors, gates, xy, out, gate, up, down):
    inner, outer = sizes()
    seq, wt = Z * inner, outer * C

    def buffer(*shape, like):
        return jax.ShapeDtypeStruct(shape, like.dtype)

    def plane(weight):
        rows, columns = weight.shape
        return buffer(Z, inner, rows, outer * columns // Z, like=weight)

    shapes = (
        buffer(wt, *tokens.shape, like=tokens),
        buffer(seq * wt, *vectors.shape, like=vectors),
        buffer(Z, inner, *gates.shape, like=gates),
        buffer(Z, inner, *xy.shape, like=xy),
        buffer(Z, inner, *out.shape, like=out),
        plane(gate),
        plane(up),
        plane(down),
    )
    copies = 3 * (2 + inner + (Z - 1) * 2 * inner) + 3 * (Z - 1 + Z * (inner + 2 * outer + inner * outer))
    copies += 2 * outer + 3 + 4 * Z
    dma = pltpu.SemaphoreType.DMA
    return pl.pallas_call(
        functools.partial(gather_kernel, (inner, outer)),
        out_shape=shapes,
        in_specs=[pl.BlockSpec(memory_space=pl.ANY)] * 8,
        out_specs=[pl.BlockSpec(memory_space=pl.ANY)] * 8,
        scratch_shapes=[
            pltpu.VMEM(gates.shape, gates.dtype),
            dma((copies,)),
            dma((16,)),
            dma((3, Z, inner)),
            dma((3, Z, inner, outer)),
            dma((wt,)),
            dma((2, seq * wt)),
            dma((3,)),
        ],
        compiler_params=pltpu.CompilerParams(collective_id=0, has_side_effects=True),
        name="gather_all",
    )(tokens, vectors, gates, xy, out, gate, up, down)


class Place:
    def __init__(self, shape):
        self.inner, self.outer = shape
        self.s, self.w = lax.axis_index("seq"), lax.axis_index("wt")
        self.z, self.x = self.s // self.inner, self.s % self.inner
        self.y, self.c = self.w // C, self.w % C
        self.at_c = {"seq": self.s, "wt": self.y * C + 1 - self.c}
        self.z_up, self.z_down = jnp.minimum(self.z + 1, Z - 1), jnp.maximum(self.z - 1, 0)

    def at_z(self, to):
        return {"seq": to * self.inner + self.x, "wt": self.w}

    def at_x(self, by):
        return {"seq": self.z * self.inner + (self.x + by) % self.inner, "wt": self.w}

    def at_y(self, by):
        return {"seq": self.s, "wt": (self.y + self.outer + by) % self.outer * C + self.c}

    def greet(self):
        barrier = pltpu.get_barrier_semaphore()
        devices = [self.at_c]
        devices += [self.at_z((self.z + k) % Z) for k in range(1, Z)]
        devices += [self.at_x(j) for j in range(1, self.inner)]
        devices += [self.at_y(i) for i in range(1, self.outer)]
        for device in devices:
            pl.semaphore_signal(barrier, inc=1, device_id=device, device_id_type=MESH)
        pl.semaphore_wait(barrier, len(devices))


def each_rows(count, step, body):
    def run(i, carried):
        body(pl.ds(pl.multiple_of(i * step, step), step))
        return carried

    lax.fori_loop(0, count // step, run, 0)


class WtRows:
    def __init__(self, me, sends, source, target, sems):
        self.me, self.sends, self.source, self.target, self.sems = me, sends, source, target, sems

    def begin(self):
        me = self.me
        for device in [me.at_y(i) for i in range(1, me.outer)] + [me.at_c]:
            self.sends.start(True, self.source, self.target.at[me.w], self.sems.at[me.w], device)

    def step(self):
        me = self.me
        for i in range(1, me.outer):
            at = (me.y + me.outer - i) % me.outer * C + me.c
            arrived(self.target.at[at], self.sems.at[at], me.at_c)
            self.sends.start(True, self.target.at[at], self.target.at[at], self.sems.at[at], me.at_c)

    def finish(self):
        me = self.me
        for i in range(me.outer):
            at = (me.y + me.outer - i) % me.outer * C + 1 - me.c
            arrived(self.target.at[at], self.sems.at[at], me.at_c)


class GroupRows:
    def __init__(self, me, sends, source, target, sems):
        self.me, self.sends, self.source, self.target, self.sems = me, sends, source, target, sems

    def place(self, own, at, z_to):
        return self.target.at[own, (z_to - at + Z) % Z]

    def forward(self, at, source, there, way):
        me = self.me
        z_to = me.z_up if way > 0 else me.z_down
        room = me.z < Z - 1 if way > 0 else me.z > 0
        when = room if there is None else there & room
        self.sends.start(
            when, source, self.place(0, at, z_to), self.sems.at[0, at], me.at_z(z_to)
        )

    def begin(self):
        me = self.me
        self.forward(me.z, self.source, None, 1)
        self.forward(me.z, self.source, None, -1)
        self.sends.start(
            True, self.source, self.place(1, me.z, me.z), self.sems.at[1, me.z], me.at_c
        )

    def step(self, k):
        me = self.me
        for at, there, way in (
            (jnp.maximum(me.z - k, 0), me.z - k >= 0, 1),
            (jnp.minimum(me.z + k, Z - 1), me.z + k < Z, -1),
        ):
            place = self.place(0, at, me.z)

            @pl.when(there)
            def _(place=place, at=at):
                arrived(place, self.sems.at[0, at], me.at_c)

            self.forward(at, place, there, way)
            self.sends.start(there, place, self.place(1, at, me.z), self.sems.at[1, at], me.at_c)

    def finish(self):
        me = self.me
        for at in range(Z):
            arrived(self.place(1, at, me.z), self.sems.at[1, at], me.at_c)


def branch_kernel(
    shape, sent, own, tokens, gain, up_held, down_held, group_to, middle, up_to, down_to,
    own_v, c_in, y_out, y_in, low,
    send_sems, local_sems, c_sems, y_sems, group_sems, up_sems, down_sems,
):
    del up_held, down_held
    me = Place(shape)
    inner, outer = shape
    share = up_to.shape[3] // outer
    rows = tokens.shape[0]
    sends = Sends(send_sems)
    load = pltpu.make_async_copy(own, own_v, local_sems.at[0])
    load.start()
    me.greet()
    order = [(me.y + i) % outer for i in list(range(1, outer)) + [0]]
    for at in order:
        sends.start(True, sent.at[at], c_in.at[at], c_sems.at[at], me.at_c)

    def columns(held, x_at, i):
        return held.at[:, x_at, :, i * share : (i + 1) * share]

    for j in range(1, inner):
        for i in range(outer):
            place = columns(up_to, me.x, i)
            sends.start(True, place, place, up_sems.at[j - 1, i], me.at_x(j))
    load.wait()
    for i, at in enumerate(order):
        arrived(c_in.at[at], c_sems.at[at], me.at_c)
        if i < outer - 1:
            each_rows(rows, 16, lambda r, i=i, at=at: y_out.__setitem__(
                (i, r), (own_v[at, r] + c_in[at, r]).astype(BF16)))
            sends.start(True, y_out.at[i], y_in.at[i], y_sems.at[i], me.at_y(i + 1))
    for i in range(outer - 1):
        arrived(y_in.at[i], y_sems.at[i], me.at_c)
    for i in range(1, outer):
        for j in range(inner):
            x_at = (me.x + inner - j) % inner
            sends.start(
                True, columns(down_to, x_at, 0), columns(down_to, x_at, i),
                down_sems.at[i - 1, j], me.at_y(i),
            )

    def work(r):
        total = tokens[r].astype(F32) + own_v[me.y, r] + c_in[me.y, r]
        for i in range(outer - 1):
            total = total + y_in[i, r].astype(F32)
        inverse = lax.rsqrt(jnp.mean(total * total, axis=1, keepdims=True) + EPSILON)
        middle[r] = total
        low[r] = (total * inverse * gain[...]).astype(BF16)

    each_rows(rows, 16, work)
    keep = pltpu.make_async_copy(low, group_to.at[0, 0], local_sems.at[1])
    keep.start()
    group = GroupRows(me, sends, low, group_to, group_sems)
    group.begin()
    for k in range(1, Z):
        group.step(k)
    group.finish()
    for j in range(1, inner):
        for i in range(outer):
            x_at = (me.x + inner - j) % inner
            arrived(columns(up_to, x_at, i), up_sems.at[j - 1, i], me.at_c)
    for i in range(1, outer):
        for j in range(inner):
            x_at = (me.x + inner - j) % inner
            arrived(columns(down_to, x_at, i), down_sems.at[i - 1, j], me.at_c)
    sends.finish()
    keep.wait()


def branch_and_group(sent, own, tokens, gain, up, down):
    inner, outer = sizes()
    rows, width = tokens.shape
    dma = pltpu.SemaphoreType.DMA
    vmem, anywhere = pl.BlockSpec(memory_space=pltpu.VMEM), pl.BlockSpec(memory_space=pl.ANY)
    return pl.pallas_call(
        functools.partial(branch_kernel, (inner, outer)),
        out_shape=(
            jax.ShapeDtypeStruct((C, Z, rows, width), BF16),
            jax.ShapeDtypeStruct((rows, width), F32),
            jax.ShapeDtypeStruct(up.shape, up.dtype),
            jax.ShapeDtypeStruct(down.shape, down.dtype),
        ),
        in_specs=[anywhere, anywhere, vmem, vmem, anywhere, anywhere],
        out_specs=(anywhere, vmem, anywhere, anywhere),
        input_output_aliases={4: 2, 5: 3},
        scratch_shapes=[
            pltpu.VMEM((outer, rows, width), F32),
            pltpu.VMEM((outer, rows, width), F32),
            pltpu.VMEM((outer - 1, rows, width), BF16),
            pltpu.VMEM((outer - 1, rows, width), BF16),
            pltpu.VMEM((rows, width), BF16),
            dma((2 * outer + 3 + 4 * (Z - 1) + (inner - 1) * outer + inner * (outer - 1),)),
            dma((2,)),
            dma((outer,)),
            dma((outer - 1,)),
            dma((C, Z)),
            dma((inner - 1, outer)),
            dma((outer - 1, inner)),
        ],
        compiler_params=pltpu.CompilerParams(
            collective_id=1, has_side_effects=True, vmem_limit_bytes=40 * 1024 * 1024
        ),
        name="branch_and_group",
    )(sent, own, tokens, gain, up, down)


def line_order():
    order = []
    for k in [n for t in range(1, Z) for n in (t, Z - t)] + [0]:
        if k not in order:
            order.append(k)
    return order


def line_sum(me, sends, rows, term, ready, store, held, up, down, between=None):
    z = me.z

    def add(when, target, slot, k, received=None):
        def body(r):
            value = term(k, r)
            if received is not None:
                value = value + received[slot - 1, r].astype(F32)
            target[slot, r] = value.astype(BF16)

        pl.when(when)(lambda: each_rows(rows, 16, body))

    for t in range(1, Z):
        slot = t - 1
        for k, (out, into, sems), has, when, to in (
            (t, up, z > 0, (z <= t - 1) & (z < Z - 1), me.z_up),
            (Z - t, down, z < Z - 1, (z >= Z - t) & (z > 0), me.z_down),
        ):
            pl.when(when)(lambda k=k: ready(k))
            if t == 1:
                add(when, out, slot, k)
            else:
                pl.when(when & has)(
                    lambda into=into, sems=sems, slot=slot: arrived(
                        into.at[slot - 1], sems.at[slot - 1], me.at_c
                    )
                )
                add(when & has, out, slot, k, into)
                add(when & jnp.logical_not(has), out, slot, k)
            sends.start(when, out.at[slot], into.at[slot], sems.at[slot], me.at_z(to))
        if between is not None:
            between(t)
    ready(0)
    each_rows(rows, 16, lambda r: store(r, term(0, r)))
    for (_, into, sems), has in ((up, z > 0), (down, z < Z - 1)):

        @pl.when(has)
        def _(into=into, sems=sems):
            arrived(into.at[Z - 2], sems.at[Z - 2], me.at_c)
            each_rows(rows, 16, lambda r: store(r, held(r) + into[Z - 2, r].astype(F32)))


class PlaneTerms:
    def __init__(self, me, sends, parts, target, sems, over_x):
        self.me, self.sends, self.parts, self.target, self.sems = me, sends, parts, target, sems
        self.over_x = over_x

    def begin(self):
        me = self.me
        if self.over_x:
            for j in range(1, me.inner):
                for i, part in enumerate(self.parts):
                    self.sends.start(
                        True, part.at[:, (me.x + j) % me.inner],
                        self.target.at[j - 1, i], self.sems.at[j - 1, i], me.at_x(j),
                    )
        else:
            for i in range(1, me.outer):
                self.sends.start(
                    True, self.parts[i], self.target.at[i - 1],
                    self.sems.at[0, i - 1], me.at_y(-i),
                )

    def finish(self):
        me = self.me
        if self.over_x:
            for j in range(1, me.inner):
                for i in range(me.outer):
                    arrived(self.target.at[j - 1, i], self.sems.at[j - 1, i], me.at_c)
        else:
            for i in range(1, me.outer):
                arrived(self.target.at[i - 1], self.sems.at[0, i - 1], me.at_c)


def middle_kernel(shape, *refs):
    outer = shape[1]
    sent, own, middle, grads, gain, feed_sent, feed_own = refs[:7]
    parts = refs[7 : 7 + 3 * outer]
    rows_to, d_middle, gain_grad, block_out = refs[7 + 3 * outer : 11 + 3 * outer]
    targets = refs[11 + 3 * outer : 14 + 3 * outer]
    scratch = refs[14 + 3 * outer :]
    middle_body(
        shape, sent, own, middle, grads, gain, feed_sent, feed_own, parts, targets,
        rows_to, d_middle, gain_grad, block_out, scratch[:9], scratch[9:18], *scratch[18:],
    )


class PairSum:
    def __init__(self, me, sends, sent, own, scratch):
        self.me, self.sends, self.sent = me, sends, sent
        (
            self.held, self.c_in, up_out, up_in, down_out, down_in,
            self.c_sems, up_sems, down_sems,
        ) = scratch
        self.up, self.down = (up_out, up_in, up_sems), (down_out, down_in, down_sems)

    def begin(self):
        for k in line_order():
            self.sends.start(
                True, self.sent.at[k], self.c_in.at[k], self.c_sems.at[k], self.me.at_c
            )

    def run(self):
        def ready(k):
            arrived(self.c_in.at[k], self.c_sems.at[k], self.me.at_c)

        def term(k, r):
            return self.held[k, r] + self.c_in[k, r].astype(F32)

        def store(r, value):
            self.held[0, r] = value

        line_sum(
            self.me, self.sends, self.held.shape[1], term, ready, store,
            lambda r: self.held[0, r], self.up, self.down,
        )


def plane_units(me, sends, parts, targets, sems):
    outer = me.outer
    return [
        PlaneTerms(me, sends, parts[n * outer : (n + 1) * outer], targets[n], sems.at[n], n != 1)
        for n in (1, 2, 0)
    ]


def middle_body(
    shape, sent, own, middle, grads, gain, feed_sent, feed_own, parts, targets,
    rows_to, d_middle, gain_grad, block_out, sum_scratch, feed_scratch, low,
    send_sems, local_sems, rows_sems, unit_sems,
):
    me = Place(shape)
    rows = middle.shape[0]
    sends = Sends(send_sems)
    total = PairSum(me, sends, sent, own, sum_scratch)
    feed = PairSum(me, sends, feed_sent, feed_own, feed_scratch)
    load = pltpu.make_async_copy(own, total.held, local_sems.at[0])
    feed_load = pltpu.make_async_copy(feed_own, feed.held, local_sems.at[2])
    load.start()
    me.greet()
    total.begin()
    units = plane_units(me, sends, parts, targets, unit_sems)
    for unit in units:
        unit.begin()
    feed_load.start()
    load.wait()
    total.run()
    own_v = total.held
    gain_grad[...] = jnp.zeros_like(gain_grad)

    def work(r):
        values = middle[r]
        inverse = lax.rsqrt(jnp.mean(values * values, axis=1, keepdims=True) + EPSILON)
        normed = values * inverse
        d_normed = own_v[0, r]
        gain_grad[...] += d_normed * normed
        scaled = d_normed * gain[...]
        passed = inverse * (scaled - normed * jnp.mean(scaled * normed, axis=1, keepdims=True))
        total = grads[r].astype(F32) + passed
        d_middle[r] = total
        low[r] = total.astype(BF16)

    each_rows(rows, 16, work)
    keep = pltpu.make_async_copy(low, rows_to.at[me.w], local_sems.at[1])
    keep.start()
    gather = WtRows(me, sends, low, rows_to, rows_sems)
    gather.begin()
    feed.begin()
    feed_load.wait()
    feed.run()
    each_rows(rows, 16, lambda r: block_out.__setitem__(
        r, (middle[r] + feed.held[0, r]).astype(BF16)))
    gather.step()
    gather.finish()
    for unit in units:
        unit.finish()
    sends.finish()
    keep.wait()


def middle_and_rows(sent, own, middle, grads, gain, feed_sent, feed_own, parts):
    inner, outer = sizes()
    rows, width = middle.shape
    unit_rows, share = parts[0].shape[2:]
    over_x, over_y = (inner - 1, outer), (outer - 1,)
    targets = [
        jax.ShapeDtypeStruct(shape, BF16)
        for shape in (
            (*over_x, Z, unit_rows, share),
            (*over_y, Z, inner, unit_rows, share),
            (*over_x, Z, unit_rows, share),
        )
    ]
    unit_copies = 2 * (inner - 1) * outer + (outer - 1)
    pair_scratch = [pltpu.VMEM((Z, rows, width), F32), pltpu.VMEM((Z, rows, width), BF16)]
    pair_scratch += [pltpu.VMEM((Z - 1, rows, width), BF16)] * 4
    dma = pltpu.SemaphoreType.DMA
    pair_scratch += [dma((Z,)), dma((Z - 1,)), dma((Z - 1,))]
    vmem, anywhere = pl.BlockSpec(memory_space=pltpu.VMEM), pl.BlockSpec(memory_space=pl.ANY)
    return pl.pallas_call(
        functools.partial(middle_kernel, (inner, outer)),
        out_shape=(
            jax.ShapeDtypeStruct((outer * C, rows, width), BF16),
            jax.ShapeDtypeStruct((rows, width), F32),
            jax.ShapeDtypeStruct((16, width), F32),
            jax.ShapeDtypeStruct((rows, width), BF16),
            *targets,
        ),
        in_specs=[anywhere, anywhere, vmem, vmem, vmem] + [anywhere] * (2 + 3 * outer),
        out_specs=(anywhere, vmem, vmem, vmem) + (anywhere,) * 3,
        scratch_shapes=pair_scratch * 2
        + [
            pltpu.VMEM((rows, width), BF16),
            dma((2 * (Z + 2 * (Z - 1)) + 2 * outer + unit_copies,)),
            dma((3,)),
            dma((outer * C,)),
            dma((3, inner - 1, outer)),
        ],
        compiler_params=pltpu.CompilerParams(
            collective_id=2, has_side_effects=True, vmem_limit_bytes=56 * 1024 * 1024
        ),
        name="middle_and_rows",
    )(sent, own, middle, grads, gain, feed_sent, feed_own, *parts)


class RowsSum:
    def __init__(self, me, sends, terms, total, scratch, sems):
        self.me, self.sends, self.terms, self.total = me, sends, terms, total
        self.own, self.x_in, *ways = scratch
        self.own_sems, self.x_sems, up_sems, down_sems = sems
        self.up, self.down = (*ways[:2], up_sems), (*ways[2:], down_sems)

    def load(self):
        me = self.me
        self.loads = []
        for k in range(Z):
            self.loads.append(
                pltpu.make_async_copy(
                    self.terms.at[(me.z + Z - k) % Z, me.x], self.own.at[k], self.own_sems.at[k]
                )
            )
            self.loads[k].start()

    def begin(self, turns):
        me = self.me
        for turn in turns:
            if turn == Z - 1:
                k = 0
            else:
                k = (jnp.minimum(me.z, Z - 1 - me.z) + turn) % (Z - 1) + 1
                k = jnp.where(me.z < Z // 2, k, Z - k)
            at = (me.z + Z - k) % Z
            for j in range(1, me.inner):
                self.sends.start(
                    True, self.terms.at[at, (me.x + j) % me.inner], self.x_in.at[j - 1, k],
                    self.x_sems.at[j - 1, k], me.at_x(j),
                )

    def run(self, between=None):
        me = self.me

        def ready(k):
            self.loads[k].wait()
            for j in range(1, me.inner):
                arrived(self.x_in.at[j - 1, k], self.x_sems.at[j - 1, k], me.at_c)

        def term(k, r):
            value = self.own[k, r].astype(F32)
            for j in range(1, me.inner):
                value = value + self.x_in[j - 1, k, r].astype(F32)
            return value

        def store(r, value):
            self.total[r] = value

        line_sum(
            me, self.sends, self.total.shape[0], term, ready, store, lambda r: self.total[r],
            self.up, self.down, between,
        )


def sums_kernel(shape, *refs):
    inner, outer = shape
    units, units_y, units_x = refs[:3]
    refs = refs[3:]
    (wide, narrow, sent, own, tokens, gain, d_middle, gain_two_grad, vectors, units_to) = refs[:10]
    refs = refs[1:]
    (wide_to, narrow_to, tokens_grad, gains, vectors_to) = refs[9:14]
    wide_scratch, narrow_scratch = refs[14:20], refs[20:26]
    (own_v, c_in, y_out, y_in, all_in, vec_in) = refs[26:32]
    (send_sems, local_sems, c_sems, y_sems, all_sems, vec_sems) = refs[32:38]
    wide_sems, narrow_sems = refs[38:42], refs[42:46]
    units_v, units_y_in, units_x_in, unit_sems, units_y_sems, units_x_sems = refs[46:]
    share = units.shape[3]
    me = Place(shape)
    rows = tokens.shape[0]
    sends = Sends(send_sems)
    load = pltpu.make_async_copy(own, own_v, local_sems.at[0])
    load.start()
    units_load = pltpu.make_async_copy(units, units_v, local_sems.at[1])
    units_load.start()
    me.greet()

    order = [(me.y + i) % outer for i in list(range(1, outer)) + [0]]
    for at in order:
        sends.start(True, sent.at[at], c_in.at[at], c_sems.at[at], me.at_c)
    narrow_sum = RowsSum(me, sends, narrow, narrow_to, narrow_scratch, narrow_sems)
    wide_sum = RowsSum(me, sends, wide, wide_to, wide_scratch, wide_sems)
    narrow_sum.load()
    wide_sum.load()
    narrow_sum.begin(range(Z))

    def columns(n, at):
        return units_to.at[n, :, pl.ds(pl.multiple_of(at * share, LANES), share)]

    def units_begin_y():
        for n in range(2):
            for i in range(1, outer):
                sends.start(
                    True, units_y.at[i - 1, n], units_y_in.at[i - 1, n],
                    units_y_sems.at[i - 1, n], me.at_y(-i),
                )

    def units_begin_x():
        for j in range(1, inner):
            sends.start(
                True, units_x.at[j - 1], units_x_in.at[j - 1], units_x_sems.at[j - 1], me.at_x(j)
            )

    kept = []

    def unit_pass_on(n, came):
        def body(r):
            for at in range(Z):
                total = units_v[n, at, r].astype(F32)
                for part in came:
                    total = total + part[at, r].astype(F32)
                units_v[n, at, r] = total.astype(BF16)

        each_rows(units_v.shape[2], 16, body)
        copy = pltpu.make_async_copy(units_v.at[n, me.z], columns(n, me.z), local_sems.at[2 + n])
        copy.start()
        kept.append(copy)
        for k in range(1, Z):
            to = (me.z + k) % Z
            sends.start(
                True, units_v.at[n, to], columns(n, me.z), unit_sems.at[n, me.z], me.at_z(to)
            )

    def unit_over_y(n):
        for i in range(1, outer):
            arrived(units_y_in.at[i - 1, n], units_y_sems.at[i - 1, n], me.at_c)
        unit_pass_on(2 * n, [units_y_in.at[i - 1, n] for i in range(1, outer)])

    def unit_over_x():
        for j in range(1, inner):
            arrived(units_x_in.at[j - 1], units_x_sems.at[j - 1], me.at_c)
        unit_pass_on(1, [units_x_in.at[j - 1] for j in range(1, inner)])

    def units_finish():
        for n in range(3):
            for k in range(1, Z):
                at = (me.z + Z - k) % Z
                arrived(columns(n, at), unit_sems.at[n, at], me.at_c)
        for copy in kept:
            copy.wait()

    def exchange(held, into, sems, first, devices):
        for n, device in enumerate(devices):
            sends.start(True, held, into.at[first + n], sems.at[first + n], device)

    def gathered(held, into, sems, first, devices):
        for n, _ in enumerate(devices):
            arrived(into.at[first + n], sems.at[first + n], me.at_c)
        total = into[first]
        for n in range(1, len(devices)):
            total = total + into[first + n]
        return held[...] + total

    stages = [
        [me.at_c],
        [me.at_y(i) for i in range(1, outer)],
        [me.at_z((me.z + k) % Z) for k in range(1, Z)],
        [me.at_x(j) for j in range(1, inner)],
    ]
    at_stage = [0]
    for stage in stages:
        at_stage.append(at_stage[-1] + len(stage))

    z_stage, x_stage = stages[2], stages[3]
    exchange(vectors, vec_in, vec_sems, 0, x_stage)
    wide_sum.begin(range(2))
    units_begin_x()
    wide_sum.begin(range(2, Z))

    load.wait()
    for i, at in enumerate(order):
        arrived(c_in.at[at], c_sems.at[at], me.at_c)
        if i < outer - 1:
            each_rows(rows, 16, lambda r, i=i, at=at: y_out.__setitem__(
                (i, r), (own_v[at, r] + c_in[at, r]).astype(BF16)))
            sends.start(True, y_out.at[i], y_in.at[i], y_sems.at[i], me.at_y(i + 1))
    units_begin_y()
    vectors_to[0] = gathered(vectors, vec_in, vec_sems, 0, x_stage)
    exchange(vectors_to.at[0], vec_in, vec_sems, len(x_stage), z_stage)
    narrow_sum.run()
    for i in range(outer - 1):
        arrived(y_in.at[i], y_sems.at[i], me.at_c)
    gains[0] = jnp.zeros_like(gains[0])

    def work(r):
        d_normed = own_v[me.y, r] + c_in[me.y, r]
        for i in range(outer - 1):
            d_normed = d_normed + y_in[i, r].astype(F32)
        stream = tokens[r].astype(F32)
        inverse = lax.rsqrt(jnp.mean(stream * stream, axis=1, keepdims=True) + EPSILON)
        normed = stream * inverse
        part = d_normed * normed
        gains[0, 0:8] += part[0:8] + part[8:16]
        scaled = d_normed * gain[...]
        passed = inverse * (scaled - normed * jnp.mean(scaled * normed, axis=1, keepdims=True))
        tokens_grad[r] = (d_middle[r] + passed).astype(BF16)

    each_rows(rows, 16, work)
    gains[0, 8:16] = gain_two_grad[0:8] + gain_two_grad[8:16]
    exchange(gains.at[0], all_in, all_sems, 0, stages[0])

    units_load.wait()

    def between(t):
        if t == 1:
            unit_over_y(0)
        if t == 2:
            unit_over_y(1)
            unit_over_x()
        if t <= 3:
            held, into = gains.at[t - 1], gains.at[t]
            into[...] = gathered(held, all_in, all_sems, at_stage[t - 1], stages[t - 1])
            exchange(into, all_in, all_sems, at_stage[t], stages[t])

    wide_sum.run(between)
    gains[4] = gathered(gains.at[3], all_in, all_sems, at_stage[3], stages[3])
    vectors_to[1] = gathered(vectors_to.at[0], vec_in, vec_sems, len(x_stage), z_stage)
    units_finish()
    sends.finish()


def last_sums(units, units_y, units_x, wide, narrow, sent, own, tokens, gain, d_middle, gain_two_grad, vectors):
    inner, outer = sizes()
    rows, width = tokens.shape
    dma = pltpu.SemaphoreType.DMA
    vmem, anywhere = pl.BlockSpec(memory_space=pltpu.VMEM), pl.BlockSpec(memory_space=pl.ANY)

    def scratch(terms):
        one = terms.shape[2:]
        return [pltpu.VMEM((Z, *one), BF16), pltpu.VMEM((inner - 1, Z, *one), BF16)] + [
            pltpu.VMEM((Z - 1, *one), BF16)
        ] * 4

    peers = 1 + (outer - 1) + (inner - 1) + (Z - 1)
    copies = 2 * outer - 1 + 2 * (Z * (inner - 1) + 2 * (Z - 1))
    copies += peers + (inner - 1) + (Z - 1) + 2 * (outer - 1) + (inner - 1) + 3 * (Z - 1)
    _, _, unit_rows, share = units.shape
    line_sems = [dma((Z,)), dma((inner - 1, Z)), dma((Z - 1,)), dma((Z - 1,))]
    return pl.pallas_call(
        functools.partial(sums_kernel, (inner, outer)),
        out_shape=(
            jax.ShapeDtypeStruct((3, unit_rows, Z * share), BF16),
            jax.ShapeDtypeStruct(wide.shape[2:], F32),
            jax.ShapeDtypeStruct(narrow.shape[2:], F32),
            jax.ShapeDtypeStruct((rows, width), BF16),
            jax.ShapeDtypeStruct((5, 16, width), F32),
            jax.ShapeDtypeStruct((2, *vectors.shape), F32),
        ),
        in_specs=[anywhere] * 7 + [vmem] * 5,
        out_specs=(anywhere,) + (vmem,) * 5,
        scratch_shapes=scratch(wide)
        + scratch(narrow)
        + [
            pltpu.VMEM((outer, rows, width), F32),
            pltpu.VMEM((outer, rows, width), F32),
            pltpu.VMEM((outer - 1, rows, width), BF16),
            pltpu.VMEM((outer - 1, rows, width), BF16),
            pltpu.VMEM((peers, 16, width), F32),
            pltpu.VMEM((inner - 1 + Z - 1, *vectors.shape), F32),
            dma((copies,)),
            dma((5,)),
            dma((outer,)),
            dma((outer - 1,)),
            dma((peers,)),
            dma((inner - 1 + Z - 1,)),
        ]
        + line_sems * 2
        + [
            pltpu.VMEM(units.shape, BF16),
            pltpu.VMEM(units_y.shape, BF16),
            pltpu.VMEM(units_x.shape, BF16),
            dma((3, Z)),
            dma((outer - 1, 2)),
            dma((inner - 1,)),
        ],
        compiler_params=pltpu.CompilerParams(
            collective_id=5, has_side_effects=True, vmem_limit_bytes=58 * 1024 * 1024
        ),
        name="last_sums",
    )(units, units_y, units_x, wide, narrow, sent, own, tokens, gain, d_middle, gain_two_grad, vectors)


def scan_kernel(backward, factors, inflows, states, entered, products, ends, ends_in, carry, send_sems, arrivals):
    seq = ends_in.shape[0]
    s = lax.axis_index("seq")
    rows, width = factors.shape
    barrier = pltpu.get_barrier_semaphore()

    def device(at):
        return {"seq": at, "wt": lax.axis_index("wt")}

    def greet(i, carried):
        @pl.when(i != s)
        def _():
            pl.semaphore_signal(barrier, inc=1, device_id=device(i), device_id_type=MESH)

        return carried

    lax.fori_loop(0, seq, greet, 0)
    group = 8
    at_row = lax.broadcasted_iota(jnp.int32, (group, width), 0)

    def step(i, carried):
        held, product = carried
        i = rows // group - 1 - i if backward else i
        where = pl.ds(pl.multiple_of(i * group, group), group)
        factor, inflow = factors[where, :], inflows[where, :]
        for by in (1, 2, 4):
            inside = at_row < group - by if backward else at_row >= by
            turn = group - by if backward else by
            inflow = factor * jnp.where(inside, pltpu.roll(inflow, turn, 0), 0.0) + inflow
            factor = factor * jnp.where(inside, pltpu.roll(factor, turn, 0), 1.0)
        inflow = inflow + factor * held
        factor = factor * product
        states[where, :] = inflow
        products[where, :] = factor
        last = slice(0, 1) if backward else slice(group - 1, group)
        return inflow[last], factor[last]

    held, product = lax.fori_loop(
        0, rows // group, step, (jnp.zeros((1, width), F32), jnp.ones((1, width), F32))
    )
    ends[0:1] = product
    ends[1:2] = held
    pl.semaphore_wait(barrier, seq - 1)

    def copy_to(i):
        return pltpu.make_async_remote_copy(
            src_ref=ends, dst_ref=ends_in.at[s], send_sem=send_sems.at[i], recv_sem=arrivals.at[s],
            device_id=device(i), device_id_type=MESH,
        )

    def later(i):
        return i < s if backward else i > s

    def send(i, carried):
        pl.when(later(i))(lambda: copy_to(i).start())
        return carried

    lax.fori_loop(0, seq, send, 0)
    carry[...] = jnp.zeros_like(carry)

    def receive(n, carried):
        i = seq - 1 - n if backward else n

        @pl.when(jnp.logical_not(later(i)) & (i != s))
        def _():
            arrived(ends_in.at[i], arrivals.at[i], device((s + 1) % seq))
            carry[0:1] = ends_in[i, 0:1] * carry[0:1] + ends_in[i, 1:2]

        return carried

    lax.fori_loop(0, seq, receive, 0)
    entering = carry[0:1]
    entered[...] = entering

    def spread(i, carried):
        where = pl.ds(pl.multiple_of(i * group, group), group)
        states[where, :] += products[where, :] * entering
        return carried

    lax.fori_loop(0, rows // group, spread, 0)

    def sent(i, carried):
        pl.when(later(i))(lambda: copy_to(i).wait_send())
        return carried

    lax.fori_loop(0, seq, sent, 0)


def full_scan(factor, inflow, backward):
    seq = lax.axis_size("seq")
    rows, width = factor.shape
    vmem = pl.BlockSpec(memory_space=pltpu.VMEM)
    return pl.pallas_call(
        functools.partial(scan_kernel, backward),
        out_shape=(
            jax.ShapeDtypeStruct((rows, width), F32),
            jax.ShapeDtypeStruct((1, width), F32),
        ),
        in_specs=[vmem, vmem],
        out_specs=(vmem, vmem),
        scratch_shapes=[
            pltpu.VMEM((rows, width), F32),
            pltpu.VMEM((8, width), F32),
            pltpu.VMEM((seq, 8, width), F32),
            pltpu.VMEM((8, width), F32),
            pltpu.SemaphoreType.DMA((seq,)),
            pltpu.SemaphoreType.DMA((seq,)),
        ],
        compiler_params=pltpu.CompilerParams(
            collective_id=4 if backward else 3,
            has_side_effects=True,
            vmem_limit_bytes=32 * 1024 * 1024,
        ),
        name="scan_back" if backward else "scan_ahead",
    )(factor, inflow)


def recurrence_terms(decay_pre, input_pre, decay_log, conv_float):
    log_decay = -DECAY_SCALE * jax.nn.softplus(-decay_log) * jax.nn.sigmoid(decay_pre)
    return (
        jnp.exp(log_decay),
        jnp.sqrt(-jnp.expm1(2.0 * log_decay)) * jax.nn.sigmoid(input_pre) * conv_float,
    )


def norm_back(d_normed, normed, inverse, gain_row):
    scaled = d_normed * gain_row
    return inverse * (scaled - normed * jnp.mean(scaled * normed, axis=1, keepdims=True))


def normed_rows(stream):
    inverse = lax.rsqrt(jnp.mean(stream * stream, axis=1, keepdims=True) + EPSILON)
    return stream * inverse, inverse


def per_device(
    tokens,
    norm1_gain,
    x_weight,
    y_weight,
    conv_weight,
    conv_bias,
    decay_gate_weight,
    decay_bias,
    input_gate_weight,
    input_bias,
    decay_param,
    out_weight,
    norm2_gain,
    gate_weight,
    up_weight,
    down_weight,
    out_grad,
):
    seq, wt = lax.axis_size("seq"), lax.axis_size("wt")
    inner, outer = sizes()
    z, x, y, c = places()
    w = lax.axis_index("wt")
    rows_dev, width = tokens.shape
    weight_rows, lru_cols = x_weight.shape
    chunk, block = decay_gate_weight.shape
    half = block // 2
    full = lru_cols - half
    taps_count = conv_weight.shape[1]
    reach = taps_count - 1
    hidden_cols = gate_weight.shape[1]

    def turned(value, axis):
        return jnp.where(c == 0, value, jnp.roll(value, -half, axis))

    def turned_back(value, axis):
        return jnp.where(c == 0, value, jnp.roll(value, half, axis))

    def in_order(own, partner, axis):
        return jnp.where(
            c == 0,
            jnp.concatenate([own, partner], axis),
            jnp.concatenate([partner, own], axis),
        )

    vectors = jnp.stack(
        [v.astype(F32) for v in (norm1_gain, norm2_gain, conv_bias, decay_bias, input_bias)]
        + [decay_param]
        + [conv_weight[:, k].astype(F32) for k in range(taps_count)]
    )
    vectors = jnp.pad(vectors, ((0, -vectors.shape[0] % 8), (0, -chunk % LANES)))

    across = [(i, i % seq * wt + i // seq) for i in range(seq * wt)]
    gates = jnp.concatenate([decay_gate_weight, input_gate_weight], axis=1)

    def padded(weight):
        share = -(-hidden_cols // (Z * LANES)) * LANES
        return jnp.pad(weight, ((0, 0), (0, Z * share - hidden_cols)))

    xy_unit = jnp.concatenate([turned(x_weight, 1), turned(y_weight, 1)], axis=1)
    (
        group_tokens, vectors, gate_all, xy_kernel, out_kernel, gate_kernel, up_kernel, down_kernel,
    ) = gather_all(
        tokens, vectors, gates, xy_unit, turned(out_weight, 1),
        padded(gate_weight), padded(up_weight), padded(down_weight),
    )
    group_tokens = group_tokens.reshape(-1, width)
    grad_group = group_gather(after(out_grad, group_tokens))
    vectors = jnp.moveaxis(vectors[:, : 6 + taps_count, :chunk], 0, 1).reshape(6 + taps_count, -1)
    gain_one, gain_two = vectors[0], vectors[1]
    own_vectors = turned(
        lax.dynamic_slice(vectors[2:], (0, w * lru_cols), (taps_count + 4, lru_cols)), 1
    )
    tap_bias, decay_shift, input_shift, decay_log = (own_vectors[i] for i in range(4))
    taps = own_vectors[4:]
    xy_kernel = xy_kernel.reshape(width, -1)
    out_kernel = out_kernel.reshape(width, -1)
    gate_kernel = gate_kernel.reshape(width, -1)
    gate_all = turned(gate_all.reshape(lru_cols, 2 * block), 0)
    partner_rows = c_swap(gate_all[full:])
    shared_rows = in_order(gate_all[full:], partner_rows, 0)

    stream = tokens.astype(F32)
    group_normed, _ = normed_rows(group_tokens.astype(F32))
    group_one = (group_normed * gain_one).astype(BF16)
    rows = group_one.shape[0]
    xy = multiply(group_one, xy_kernel)
    x_branch = xy[:, :lru_cols].astype(BF16)
    y_before = xy[:, lru_cols:]
    y_gated, gelu_y_back = jax.vjp(gelu_tanh, y_before)
    rim = lax.ppermute(x_branch[rows - reach :], "seq", [(i, i + 1) for i in range(seq - 1)])
    extended = jnp.concatenate([rim, x_branch], axis=0).astype(F32)
    conv_low = (
        tap_bias
        + sum(taps[k] * extended[reach - k : reach - k + rows] for k in range(taps_count))
    ).astype(BF16)
    shared_conv = in_order(conv_low[:, full:], c_swap(conv_low[:, full:]), 1)
    heads = full // block

    def of_head(value, i):
        return value[:, i * block : (i + 1) * block]

    pre_parts = [
        multiply(of_head(conv_low, i), gate_all[i * block : (i + 1) * block]) for i in range(heads)
    ]
    shared_pre = multiply(shared_conv, shared_rows).reshape(rows, 2, C, half)
    shared_pre = pick(shared_pre, c, 2)
    decay_pre = decay_shift + jnp.concatenate(
        [part[:, :block] for part in pre_parts] + [shared_pre[:, 0]], axis=1
    )
    input_pre = input_shift + jnp.concatenate(
        [part[:, block:] for part in pre_parts] + [shared_pre[:, 1]], axis=1
    )
    (retain, inflow), terms_back = jax.vjp(
        recurrence_terms, decay_pre, input_pre, decay_log, conv_low.astype(F32)
    )
    states, state_in = full_scan(retain, inflow, False)
    before = jnp.concatenate([state_in, states[:-1]])
    lru_low = states.astype(BF16).astype(F32)
    mixed_rows = (lru_low * y_gated).astype(BF16)
    mixed_parts = mixed_rows.reshape(outer, C, rows_dev, lru_cols)

    def branch_of(at):
        part = pick(mixed_parts, at, 1).reshape(outer * rows_dev, lru_cols)
        return contract_last(part, out_kernel).reshape(outer, rows_dev, width)

    group_two, middle, up_kernel, down_kernel = branch_and_group(
        branch_of(1 - c), branch_of(c), tokens, gain_two[None], up_kernel, down_kernel
    )
    up_kernel = up_kernel.reshape(width, -1)
    down_kernel = down_kernel.reshape(width, -1)
    group_two = group_two.reshape(C * Z * rows_dev, width)

    gate_pre = multiply(group_two, gate_kernel)
    up_pre = multiply(group_two, up_kernel)
    active, gelu_gate_back = jax.vjp(gelu_tanh, gate_pre)
    hidden = (active * up_pre).astype(BF16)

    d_hidden = multiply(grad_group, down_kernel)
    d_up = (d_hidden * active).astype(BF16)
    d_gate = gelu_gate_back(d_hidden * up_pre)[0].astype(BF16)
    half_rows = Z * rows_dev

    def d_normed_of(part):
        total = contract_last(d_gate[part], gate_kernel) + contract_last(d_up[part], up_kernel)
        return total.reshape(Z, rows_dev, width)

    def terms_of(left_side, right_side):
        share = right_side.shape[1] // outer
        return [
            contract_rows(left_side, right_side[:, i * share : (i + 1) * share])
            .astype(BF16)
            .reshape(Z, inner, weight_rows, share)
            for i in range(outer)
        ]

    gate_terms = terms_of(group_two, d_gate)
    up_terms = terms_of(group_two, d_up)
    down_terms = terms_of(grad_group, hidden)
    def feed_of(part):
        return contract_last(hidden[part], down_kernel).reshape(Z, rows_dev, width)

    branch_rows, d_middle, gain_two_grad, block_out, *came = middle_and_rows(
        d_normed_of(slice(half_rows, None)).astype(BF16),
        d_normed_of(slice(0, half_rows)),
        middle,
        out_grad,
        gain_two[None],
        feed_of(slice(half_rows, None)).astype(BF16),
        feed_of(slice(0, half_rows)),
        gate_terms + up_terms + down_terms,
    )
    branch_rows = branch_rows.reshape(-1, width)

    def added_over_x(terms, moved):
        return [
            sum((moved[j - 1, i].astype(F32) for j in range(1, inner)), pick(term, x, 1).astype(F32))
            for i, term in enumerate(terms)
        ]

    def added_over_y(term, moved):
        return sum((moved[i - 1].astype(F32) for i in range(1, outer)), term.astype(F32))

    gate_x = added_over_x(gate_terms, came[0])
    up_y = added_over_y(up_terms[0], came[1])
    down_x = added_over_x(down_terms, came[2])
    units = jnp.stack([gate_x[0], pick(up_y, x, 1), down_x[0]]).astype(BF16)
    units_y = jnp.stack([jnp.stack([gate_x[i], down_x[i]]) for i in range(1, outer)]).astype(BF16)
    units_x = jnp.stack([pick(up_y, (x + j) % inner, 1) for j in range(1, inner)]).astype(BF16)

    d_mixed = multiply(branch_rows, out_kernel)
    d_lru = (d_mixed * y_gated).astype(BF16).astype(F32)
    d_y = gelu_y_back(d_mixed * lru_low)[0].astype(BF16)
    passed, passed_in = full_scan(retain, retain * d_lru, True)
    d_total = d_lru + jnp.concatenate([passed[1:], passed_in])
    d_decay_pre, d_input_pre, decay_log_grad, d_conv_direct = terms_back(
        (d_total * before, d_total)
    )
    d_decay_low, d_input_low = d_decay_pre.astype(BF16), d_input_pre.astype(BF16)
    own_low = jnp.concatenate([d_decay_low[:, full:], d_input_low[:, full:]], axis=1)
    partner_low = c_swap(own_low)
    shared_low = jnp.concatenate(
        [
            in_order(own_low[:, :half], partner_low[:, :half], 1),
            in_order(own_low[:, half:], partner_low[:, half:], 1),
        ],
        axis=1,
    )
    lows = [
        jnp.concatenate([of_head(d_decay_low, i), of_head(d_input_low, i)], axis=1)
        for i in range(heads)
    ]
    d_conv = d_conv_direct + jnp.concatenate(
        [contract_last(lows[i], gate_all[i * block : (i + 1) * block]) for i in range(heads)]
        + [contract_last(shared_low, gate_all[full:])],
        axis=1,
    )
    gates_grad = jnp.concatenate(
        [contract_rows(of_head(conv_low, i), lows[i]) for i in range(heads)]
        + [contract_rows(conv_low[:, full:], shared_low)]
    )
    ahead = lax.ppermute(d_conv[:reach], "seq", [(i + 1, i) for i in range(seq - 1)])
    d_extended = jnp.concatenate([d_conv, ahead], axis=0)
    d_x_branch = sum(taps[k] * d_extended[k : k + rows] for k in range(taps_count)).astype(BF16)
    dx_parts = d_x_branch.reshape(outer, C, rows_dev, lru_cols)
    dy_parts = d_y.reshape(outer, C, rows_dev, lru_cols)

    def d_normed_one_of(at):
        dx, dy = (
            pick(parts, at, 1).reshape(outer * rows_dev, lru_cols) for parts in (dx_parts, dy_parts)
        )
        total = contract_last(dx, xy_kernel[:, :lru_cols]) + contract_last(
            dy, xy_kernel[:, lru_cols:]
        )
        return total.reshape(outer, rows_dev, width)

    wide = jnp.concatenate(
        [
            contract_rows(group_one, d_x_branch),
            contract_rows(group_one, d_y),
            contract_rows(branch_rows, mixed_rows),
        ],
        axis=1,
    )
    wide = wide.astype(BF16).reshape(Z, inner, weight_rows, 3 * lru_cols)
    narrow = turned_back(gates_grad, 0).astype(BF16).reshape(Z, inner, chunk, 2 * block)
    narrow = jnp.pad(narrow, ((0, 0), (0, 0), (0, -chunk % 16), (0, 0)))
    own_sums = jnp.stack(
        [jnp.sum(d_conv, axis=0), jnp.sum(d_decay_pre, axis=0), jnp.sum(d_input_pre, axis=0)]
        + [decay_log_grad]
        + [jnp.sum(d_conv * extended[reach - k : reach - k + rows], axis=0) for k in range(taps_count)],
    )
    own_sums = turned_back(own_sums, 1)
    placed, wide, narrow, tokens_grad, gains, own_sums = last_sums(
        units, units_y, units_x, wide, narrow, d_normed_one_of(1 - c), d_normed_one_of(c), tokens, gain_one[None],
        d_middle, gain_two_grad, own_sums,
    )
    weight_grads = [
        turned_back(wide[:, n * lru_cols : (n + 1) * lru_cols], 1) for n in range(3)
    ]
    gate_grad, up_grad, down_grad = (placed[n, :, :hidden_cols].astype(F32) for n in range(3))
    gains = gains[4].reshape(2, 8, width).sum(axis=1)
    gains = lax.dynamic_slice(gains, (0, (lax.axis_index("seq") * wt + w) * chunk), (2, chunk))
    sums = lax.dynamic_slice(own_sums[1], (0, lax.axis_index("seq") * chunk), (taps_count + 4, chunk))
    own_sums = jnp.concatenate([narrow[:chunk], sums.T], axis=1)
    own_sums = lax.ppermute(own_sums, ("seq", "wt"), [(to, at) for at, to in across])
    sums = own_sums[:, 2 * block :]
    return (
        block_out,
        tokens_grad,
        gains[0],
        weight_grads[0],
        weight_grads[1],
        sums[:, 4:],
        sums[:, 0],
        own_sums[:, :block],
        sums[:, 1],
        own_sums[:, block : 2 * block],
        sums[:, 2],
        sums[:, 3],
        weight_grads[2],
        gains[1],
        gate_grad,
        up_grad,
        down_grad,
    )


def solution(mesh):
    rows, both, lone = P(("seq", "wt"), None), P("seq", "wt"), P(("seq", "wt"))
    in_specs = (
        rows, lone, both, both, rows, lone, rows, lone, rows, lone, lone,
        both, lone, both, both, both, rows,
    )
    out_specs = (
        rows, rows, lone, both, both, rows, lone, rows, lone, rows, lone, lone,
        both, lone, both, both, both,
    )
    return jax.shard_map(
        per_device, mesh=mesh, in_specs=in_specs, out_specs=out_specs, check_vma=False
    )
```

```python
import functools

import jax
import jax.numpy as jnp
from jax import lax
from jax.experimental import pallas as pl
from jax.experimental.pallas import tpu as pltpu
from jax.sharding import PartitionSpec as P

EPSILON = 1e-06
DECAY_SCALE = 8.0
Z = 4
C = 2
LANES = 128
F32 = jnp.float32
BF16 = jnp.bfloat16
MESH = pl.DeviceIdType.MESH


def gelu_tanh(values):
    return jax.nn.gelu(values, approximate=True)


def sizes():
    return lax.axis_size("seq") // Z, lax.axis_size("wt") // C


def places():
    inner, outer = sizes()
    s, w = lax.axis_index("seq"), lax.axis_index("wt")
    return s // inner, s % inner, w // C, w % C


def z_move(value, by, senders):
    inner, _ = sizes()
    pairs = [(z * inner + x, (z + by) % Z * inner + x) for z in senders for x in range(inner)]
    return lax.ppermute(value, "seq", pairs)


def c_swap(value):
    _, outer = sizes()
    pairs = [(y * C + c, y * C + 1 - c) for y in range(outer) for c in range(C)]
    return lax.ppermute(value, "wt", pairs)


def line_scatter(parts):
    up = down = None
    for step in range(1, Z):
        rising = parts[step] if up is None else parts[step] + up
        falling = parts[Z - step] if down is None else parts[Z - step] + down
        up = z_move(rising.astype(BF16), 1, range(0, step)).astype(F32)
        down = z_move(falling.astype(BF16), -1, range(Z - step, Z)).astype(F32)
    return parts[0] + up + down


def pick(value, index, axis):
    return lax.dynamic_index_in_dim(value, index, axis, keepdims=False)


def contract_last(left_side, right_side):
    return lax.dot_general(
        left_side, right_side, (((1,), (1,)), ((), ())), preferred_element_type=F32
    )


def contract_rows(left_side, right_side):
    return lax.dot_general(
        left_side, right_side, (((0,), (0,)), ((), ())), preferred_element_type=F32
    )


def multiply(left_side, right_side):
    return jnp.dot(left_side, right_side, preferred_element_type=F32)


class Sends:
    def __init__(self, sems):
        self.sems, self.started = sems, []

    def start(self, when, source, target, arrival, device):
        copy = pltpu.make_async_remote_copy(
            src_ref=source,
            dst_ref=target,
            send_sem=self.sems.at[len(self.started)],
            recv_sem=arrival,
            device_id=device,
            device_id_type=MESH,
        )
        if when is True:
            copy.start()
        else:
            pl.when(when)(copy.start)
        self.started.append((when, copy))

    def finish(self):
        for when, copy in self.started:
            if when is True:
                copy.wait_send()
            else:
                pl.when(when)(copy.wait_send)


def arrived(target, arrival, device):
    pltpu.make_async_remote_copy(
        src_ref=target, dst_ref=target, send_sem=arrival, recv_sem=arrival,
        device_id=device, device_id_type=MESH,
    ).wait_recv()


def gather_kernel(shape, *refs):
    inner, outer = shape
    (tokens, grads, vectors, gates, xy, out, gate, up, down) = refs[:9]
    (tokens_to, grads_to, vectors_to, gates_to, xy_to, out_to, gate_to, up_to, down_to) = refs[9:18]
    gates_own, send_sems, local_sems, line_sems, plane_sems, rows_sems = refs[18:24]
    vector_sems, turn_sems, group_sems = refs[24:]
    seq, wt = Z * inner, outer * C
    s, w = lax.axis_index("seq"), lax.axis_index("wt")
    z, x, y, c = s // inner, s % inner, w // C, w % C
    sends = Sends(send_sems)
    group = GroupRows(Place(shape), sends, grads, grads_to, group_sems)
    here = []

    def at_z(to):
        return {"seq": to * inner + x, "wt": w}

    def at_x(by):
        return {"seq": z * inner + (x + by) % inner, "wt": w}

    def at_y(by):
        return {"seq": s, "wt": (y + by) % outer * C + c}

    at_c = {"seq": s, "wt": y * C + 1 - c}

    def keep(source, target, waited=False):
        copy = pltpu.make_async_copy(source, target, local_sems.at[len(here)])
        copy.start()
        here.append((waited, copy))
        return copy

    barrier = pltpu.get_barrier_semaphore()

    def greet(i, carried):
        @pl.when(i != s * wt + w)
        def _():
            pl.semaphore_signal(
                barrier, inc=1, device_id={"seq": i // wt, "wt": i % wt}, device_id_type=MESH
            )

        return carried

    lax.fori_loop(0, seq * wt, greet, 0)
    pl.semaphore_wait(barrier, seq * wt - 1)

    class Line:
        def __init__(self, index, source, target):
            self.source, self.target = source, target
            self.sems = line_sems.at[index]

        def forward(self, block, at, up_when, down_when):
            place = self.target.at[at, x]
            arrival = self.sems.at[at, x]
            sends.start(up_when, block, place, arrival, at_z(jnp.minimum(z + 1, Z - 1)))
            sends.start(down_when, block, place, arrival, at_z(jnp.maximum(z - 1, 0)))
            return place, arrival

        def across(self, when, block, at):
            for j in range(1, inner):
                sends.start(when, block, self.target.at[at, x], self.sems.at[at, x], at_x(j))

        def begin_z(self):
            keep(self.source, self.target.at[z, x])
            self.forward(self.source, z, z < Z - 1, z > 0)

        def begin_x(self):
            self.across(True, self.source, z)

        def begin(self):
            self.begin_z()
            self.begin_x()

        def step(self, k):
            for at, there, up_when, down_when in (
                (jnp.maximum(z - k, 0), z - k >= 0, (z - k >= 0) & (z < Z - 1), None),
                (jnp.minimum(z + k, Z - 1), z + k < Z, None, (z + k < Z) & (z > 0)),
            ):
                place, arrival = self.target.at[at, x], self.sems.at[at, x]

                @pl.when(there)
                def _(place=place, arrival=arrival):
                    arrived(place, arrival, at_c)

                if up_when is not None:
                    sends.start(up_when, place, place, arrival, at_z(jnp.minimum(z + 1, Z - 1)))
                else:
                    sends.start(down_when, place, place, arrival, at_z(jnp.maximum(z - 1, 0)))
                self.across(there, place, at)

        def finish(self):
            for at in range(Z):
                for j in range(1, inner):
                    from_x = (x + inner - j) % inner
                    arrived(self.target.at[at, from_x], self.sems.at[at, from_x], at_c)

    class Plane:
        def __init__(self, index, source, target, x_first, whole):
            self.source, self.target, self.x_first, self.whole = source, target, x_first, whole
            self.share = source.shape[1] // Z
            self.sems = plane_sems.at[index]

        def cut(self, at):
            return self.source.at[:, pl.ds(pl.multiple_of(at * self.share, LANES), self.share)]

        def place(self, at, x_at, i):
            return self.target.at[at, x_at, :, i * self.share : (i + 1) * self.share]

        def begin(self):
            self.own = keep(self.cut(z), self.place(z, x, 0), True)
            for k in range(1, Z):
                to = (z + k) % Z
                sends.start(True, self.cut(to), self.place(z, x, 0), self.sems.at[z, 0, 0], at_z(to))

        def over_x(self, at, i):
            place = self.place(at, x, i)
            for j in range(1, inner):
                sends.start(True, place, place, self.sems.at[at, j, i], at_x(j))

        def over_y(self, at, j):
            x_at = (x + inner - j) % inner
            for i in range(1, outer):
                sends.start(
                    True, self.place(at, x_at, 0), self.place(at, x_at, i),
                    self.sems.at[at, j, i], at_y(i),
                )

        def got(self, at, j, i):
            arrived(self.place(at, (x + inner - j) % inner, i), self.sems.at[at, j, i], at_c)

        def first(self, k):
            at = (z + Z - k) % Z
            if k == 0:
                self.own.wait()
            else:
                self.got(at, 0, 0)
            if self.x_first or self.whole:
                self.over_x(at, 0)
            if self.whole or not self.x_first:
                self.over_y(at, 0)

        def second(self, k):
            at = (z + Z - k) % Z
            if self.x_first:
                for j in range(1, inner):
                    self.got(at, j, 0)
                    if self.whole:
                        self.over_y(at, j)
            else:
                for i in range(1, outer):
                    self.got(at, 0, i)

        def finish(self, k):
            if self.whole:
                at = (z + Z - k) % Z
                for j in range(inner):
                    for i in range(1, outer):
                        self.got(at, j, i)

    lines = [Line(0, xy, xy_to), Line(1, gates_own, gates_to), Line(2, out, out_to)]
    planes = [
        Plane(0, gate, gate_to, True, True),
        Plane(1, up, up_to, False, False),
        Plane(2, down, down_to, True, False),
    ]

    me = s * wt + w
    keep(vectors, vectors_to.at[me])

    def vector_copy(i):
        return pltpu.make_async_remote_copy(
            src_ref=vectors, dst_ref=vectors_to.at[me],
            send_sem=vector_sems.at[0, i], recv_sem=vector_sems.at[1, me],
            device_id={"seq": i // wt, "wt": i % wt}, device_id_type=MESH,
        )

    def vector_send(i, carried):
        pl.when(i != me)(lambda: vector_copy(i).start())
        return carried

    def tokens_begin():
        keep(tokens, tokens_to.at[w])
        sends.start(True, tokens, tokens_to.at[w], rows_sems.at[w], at_c)
        for i in range(1, outer):
            sends.start(True, tokens, tokens_to.at[w], rows_sems.at[w], at_y(i))

    def tokens_step():
        for i in range(1, outer):
            at = (y + outer - i) % outer * C + c
            arrived(tokens_to.at[at], rows_sems.at[at], at_c)
            sends.start(True, tokens_to.at[at], tokens_to.at[at], rows_sems.at[at], at_c)

    def tokens_finish():
        for i in range(outer):
            at = (y + outer - i) % outer * C + 1 - c
            arrived(tokens_to.at[at], rows_sems.at[at], at_c)

    to_seq, to_wt = me % seq, me // seq
    from_me = w * seq + s
    turn = pltpu.make_async_remote_copy(
        src_ref=gates, dst_ref=gates_own, send_sem=turn_sems.at[0], recv_sem=turn_sems.at[1],
        device_id={"seq": to_seq, "wt": to_wt}, device_id_type=MESH,
    )
    stay = pltpu.make_async_copy(gates, gates_own, turn_sems.at[2])
    here_too = from_me == me

    pl.when(jnp.logical_not(here_too))(turn.start)
    pl.when(here_too)(stay.start)
    lines[0].begin()
    tokens_begin()

    @pl.when(jnp.logical_not(here_too))
    def _():
        arrived(gates_own, turn_sems.at[1], at_c)

    pl.when(here_too)(stay.wait)
    lines[1].begin()
    lines[2].begin_z()
    lax.fori_loop(0, seq * wt, vector_send, 0)
    for k in range(1, Z):
        lines[1].step(k)
        lines[0].step(k)
        if k == 1:
            tokens_step()
    lines[2].begin_x()
    for k in range(1, Z):
        lines[2].step(k)
        if k == Z - 2:
            planes[0].begin()
            planes[2].begin()
            planes[1].begin()
    for k in range(Z):
        planes[0].first(k)
    for k in range(Z):
        planes[2].first(k)
    keep(grads, group.place(0, z, z))
    group.begin()
    for k in range(Z):
        planes[1].first(k)
        planes[0].second(k)
    for k in range(1, Z):
        group.step(k)
    group.finish()

    for line in lines:
        line.finish()
    tokens_finish()
    for k in range(Z):
        planes[1].second(k)
        planes[2].second(k)
        planes[0].finish(k)

    def vector_wait(i, carried):
        @pl.when(i != me)
        def _():
            vector_copy(i).wait_send()
            arrived(vectors_to.at[i], vector_sems.at[1, i], at_c)

        return carried

    pl.when(jnp.logical_not(here_too))(turn.wait_send)
    lax.fori_loop(0, seq * wt, vector_wait, 0)
    sends.finish()
    for waited, copy in here:
        if not waited:
            copy.wait()


def gather_all(tokens, grads, vectors, gates, xy, out, gate, up, down):
    inner, outer = sizes()
    seq, wt = Z * inner, outer * C

    def buffer(*shape, like):
        return jax.ShapeDtypeStruct(shape, like.dtype)

    def plane(weight):
        rows, columns = weight.shape
        return buffer(Z, inner, rows, outer * columns // Z, like=weight)

    shapes = (
        buffer(wt, *tokens.shape, like=tokens),
        buffer(C, Z, *grads.shape, like=grads),
        buffer(seq * wt, *vectors.shape, like=vectors),
        buffer(Z, inner, *gates.shape, like=gates),
        buffer(Z, inner, *xy.shape, like=xy),
        buffer(Z, inner, *out.shape, like=out),
        plane(gate),
        plane(up),
        plane(down),
    )
    copies = 3 * (2 + inner + (Z - 1) * 2 * inner) + 3 * (Z - 1 + Z * (inner + 2 * outer + inner * outer))
    copies += 2 * outer + 3 + 4 * Z
    dma = pltpu.SemaphoreType.DMA
    return pl.pallas_call(
        functools.partial(gather_kernel, (inner, outer)),
        out_shape=shapes,
        in_specs=[pl.BlockSpec(memory_space=pl.ANY)] * 9,
        out_specs=[pl.BlockSpec(memory_space=pl.ANY)] * 9,
        scratch_shapes=[
            pltpu.VMEM(gates.shape, gates.dtype),
            dma((copies,)),
            dma((16,)),
            dma((3, Z, inner)),
            dma((3, Z, inner, outer)),
            dma((wt,)),
            dma((2, seq * wt)),
            dma((3,)),
            dma((C, Z)),
        ],
        compiler_params=pltpu.CompilerParams(collective_id=0, has_side_effects=True),
        name="gather_all",
    )(tokens, grads, vectors, gates, xy, out, gate, up, down)


class Place:
    def __init__(self, shape):
        self.inner, self.outer = shape
        self.s, self.w = lax.axis_index("seq"), lax.axis_index("wt")
        self.z, self.x = self.s // self.inner, self.s % self.inner
        self.y, self.c = self.w // C, self.w % C
        self.at_c = {"seq": self.s, "wt": self.y * C + 1 - self.c}
        self.z_up, self.z_down = jnp.minimum(self.z + 1, Z - 1), jnp.maximum(self.z - 1, 0)

    def at_z(self, to):
        return {"seq": to * self.inner + self.x, "wt": self.w}

    def at_x(self, by):
        return {"seq": self.z * self.inner + (self.x + by) % self.inner, "wt": self.w}

    def at_y(self, by):
        return {"seq": self.s, "wt": (self.y + self.outer + by) % self.outer * C + self.c}

    def greet(self):
        barrier = pltpu.get_barrier_semaphore()
        devices = [self.at_c]
        devices += [self.at_z((self.z + k) % Z) for k in range(1, Z)]
        devices += [self.at_x(j) for j in range(1, self.inner)]
        devices += [self.at_y(i) for i in range(1, self.outer)]
        for device in devices:
            pl.semaphore_signal(barrier, inc=1, device_id=device, device_id_type=MESH)
        pl.semaphore_wait(barrier, len(devices))


def each_rows(count, step, body):
    def run(i, carried):
        body(pl.ds(pl.multiple_of(i * step, step), step))
        return carried

    lax.fori_loop(0, count // step, run, 0)


class WtRows:
    def __init__(self, me, sends, source, target, sems):
        self.me, self.sends, self.source, self.target, self.sems = me, sends, source, target, sems

    def begin(self):
        me = self.me
        for device in [me.at_y(i) for i in range(1, me.outer)] + [me.at_c]:
            self.sends.start(True, self.source, self.target.at[me.w], self.sems.at[me.w], device)

    def step(self):
        me = self.me
        for i in range(1, me.outer):
            at = (me.y + me.outer - i) % me.outer * C + me.c
            arrived(self.target.at[at], self.sems.at[at], me.at_c)
            self.sends.start(True, self.target.at[at], self.target.at[at], self.sems.at[at], me.at_c)

    def finish(self):
        me = self.me
        for i in range(me.outer):
            at = (me.y + me.outer - i) % me.outer * C + 1 - me.c
            arrived(self.target.at[at], self.sems.at[at], me.at_c)


class GroupRows:
    def __init__(self, me, sends, source, target, sems):
        self.me, self.sends, self.source, self.target, self.sems = me, sends, source, target, sems

    def place(self, own, at, z_to):
        return self.target.at[own, (z_to - at + Z) % Z]

    def forward(self, at, source, there, way):
        me = self.me
        z_to = me.z_up if way > 0 else me.z_down
        room = me.z < Z - 1 if way > 0 else me.z > 0
        when = room if there is None else there & room
        self.sends.start(
            when, source, self.place(0, at, z_to), self.sems.at[0, at], me.at_z(z_to)
        )

    def begin(self):
        me = self.me
        self.forward(me.z, self.source, None, 1)
        self.forward(me.z, self.source, None, -1)
        self.sends.start(
            True, self.source, self.place(1, me.z, me.z), self.sems.at[1, me.z], me.at_c
        )

    def step(self, k):
        me = self.me
        for at, there, way in (
            (jnp.maximum(me.z - k, 0), me.z - k >= 0, 1),
            (jnp.minimum(me.z + k, Z - 1), me.z + k < Z, -1),
        ):
            place = self.place(0, at, me.z)

            @pl.when(there)
            def _(place=place, at=at):
                arrived(place, self.sems.at[0, at], me.at_c)

            self.forward(at, place, there, way)
            self.sends.start(there, place, self.place(1, at, me.z), self.sems.at[1, at], me.at_c)

    def finish(self):
        me = self.me
        for at in range(Z):
            arrived(self.place(1, at, me.z), self.sems.at[1, at], me.at_c)


def branch_kernel(
    shape, sent, own, tokens, gain, up_held, down_held, group_to, middle, up_to, down_to,
    own_v, c_in, y_out, y_in, low,
    send_sems, local_sems, c_sems, y_sems, group_sems, up_sems, down_sems,
):
    del up_held, down_held
    me = Place(shape)
    inner, outer = shape
    share = up_to.shape[3] // outer
    rows = tokens.shape[0]
    sends = Sends(send_sems)
    load = pltpu.make_async_copy(own, own_v, local_sems.at[0])
    load.start()
    me.greet()
    order = [(me.y + i) % outer for i in list(range(1, outer)) + [0]]
    for at in order:
        sends.start(True, sent.at[at], c_in.at[at], c_sems.at[at], me.at_c)

    def columns(held, x_at, i):
        return held.at[:, x_at, :, i * share : (i + 1) * share]

    for j in range(1, inner):
        for i in range(outer):
            place = columns(up_to, me.x, i)
            sends.start(True, place, place, up_sems.at[j - 1, i], me.at_x(j))
    load.wait()
    for i, at in enumerate(order):
        arrived(c_in.at[at], c_sems.at[at], me.at_c)
        if i < outer - 1:
            each_rows(rows, 16, lambda r, i=i, at=at: y_out.__setitem__(
                (i, r), (own_v[at, r] + c_in[at, r]).astype(BF16)))
            sends.start(True, y_out.at[i], y_in.at[i], y_sems.at[i], me.at_y(i + 1))
    for i in range(outer - 1):
        arrived(y_in.at[i], y_sems.at[i], me.at_c)
    for i in range(1, outer):
        for j in range(inner):
            x_at = (me.x + inner - j) % inner
            sends.start(
                True, columns(down_to, x_at, 0), columns(down_to, x_at, i),
                down_sems.at[i - 1, j], me.at_y(i),
            )

    def work(r):
        total = tokens[r].astype(F32) + own_v[me.y, r] + c_in[me.y, r]
        for i in range(outer - 1):
            total = total + y_in[i, r].astype(F32)
        inverse = lax.rsqrt(jnp.mean(total * total, axis=1, keepdims=True) + EPSILON)
        middle[r] = total
        low[r] = (total * inverse * gain[...]).astype(BF16)

    each_rows(rows, 16, work)
    keep = pltpu.make_async_copy(low, group_to.at[0, 0], local_sems.at[1])
    keep.start()
    group = GroupRows(me, sends, low, group_to, group_sems)
    group.begin()
    for k in range(1, Z):
        group.step(k)
    group.finish()
    for j in range(1, inner):
        for i in range(outer):
            x_at = (me.x + inner - j) % inner
            arrived(columns(up_to, x_at, i), up_sems.at[j - 1, i], me.at_c)
    for i in range(1, outer):
        for j in range(inner):
            x_at = (me.x + inner - j) % inner
            arrived(columns(down_to, x_at, i), down_sems.at[i - 1, j], me.at_c)
    sends.finish()
    keep.wait()


def branch_and_group(sent, own, tokens, gain, up, down):
    inner, outer = sizes()
    rows, width = tokens.shape
    dma = pltpu.SemaphoreType.DMA
    vmem, anywhere = pl.BlockSpec(memory_space=pltpu.VMEM), pl.BlockSpec(memory_space=pl.ANY)
    return pl.pallas_call(
        functools.partial(branch_kernel, (inner, outer)),
        out_shape=(
            jax.ShapeDtypeStruct((C, Z, rows, width), BF16),
            jax.ShapeDtypeStruct((rows, width), F32),
            jax.ShapeDtypeStruct(up.shape, up.dtype),
            jax.ShapeDtypeStruct(down.shape, down.dtype),
        ),
        in_specs=[anywhere, anywhere, vmem, vmem, anywhere, anywhere],
        out_specs=(anywhere, vmem, anywhere, anywhere),
        input_output_aliases={4: 2, 5: 3},
        scratch_shapes=[
            pltpu.VMEM((outer, rows, width), F32),
            pltpu.VMEM((outer, rows, width), F32),
            pltpu.VMEM((outer - 1, rows, width), BF16),
            pltpu.VMEM((outer - 1, rows, width), BF16),
            pltpu.VMEM((rows, width), BF16),
            dma((2 * outer + 3 + 4 * (Z - 1) + (inner - 1) * outer + inner * (outer - 1),)),
            dma((2,)),
            dma((outer,)),
            dma((outer - 1,)),
            dma((C, Z)),
            dma((inner - 1, outer)),
            dma((outer - 1, inner)),
        ],
        compiler_params=pltpu.CompilerParams(
            collective_id=1, has_side_effects=True, vmem_limit_bytes=40 * 1024 * 1024
        ),
        name="branch_and_group",
    )(sent, own, tokens, gain, up, down)


def line_order():
    order = []
    for k in [n for t in range(1, Z) for n in (t, Z - t)] + [0]:
        if k not in order:
            order.append(k)
    return order


def line_sum(me, sends, rows, term, ready, store, held, up, down, between=None):
    z = me.z

    def add(when, target, slot, k, received=None):
        def body(r):
            value = term(k, r)
            if received is not None:
                value = value + received[slot - 1, r].astype(F32)
            target[slot, r] = value.astype(BF16)

        pl.when(when)(lambda: each_rows(rows, 16, body))

    for t in range(1, Z):
        slot = t - 1
        for k, (out, into, sems), has, when, to in (
            (t, up, z > 0, (z <= t - 1) & (z < Z - 1), me.z_up),
            (Z - t, down, z < Z - 1, (z >= Z - t) & (z > 0), me.z_down),
        ):
            pl.when(when)(lambda k=k: ready(k))
            if t == 1:
                add(when, out, slot, k)
            else:
                pl.when(when & has)(
                    lambda into=into, sems=sems, slot=slot: arrived(
                        into.at[slot - 1], sems.at[slot - 1], me.at_c
                    )
                )
                add(when & has, out, slot, k, into)
                add(when & jnp.logical_not(has), out, slot, k)
            sends.start(when, out.at[slot], into.at[slot], sems.at[slot], me.at_z(to))
        if between is not None:
            between(t)
    ready(0)
    each_rows(rows, 16, lambda r: store(r, term(0, r)))
    for (_, into, sems), has in ((up, z > 0), (down, z < Z - 1)):

        @pl.when(has)
        def _(into=into, sems=sems):
            arrived(into.at[Z - 2], sems.at[Z - 2], me.at_c)
            each_rows(rows, 16, lambda r: store(r, held(r) + into[Z - 2, r].astype(F32)))


class PlaneTerms:
    def __init__(self, me, sends, parts, target, sems, over_x, blocks):
        self.me, self.sends, self.parts, self.target, self.sems = me, sends, parts, target, sems
        self.over_x, self.blocks = over_x, blocks

    def begin(self):
        me = self.me
        if self.over_x:
            for j in range(1, me.inner):
                for i, part in enumerate(self.parts):
                    self.sends.start(
                        True, part.at[self.blocks, (me.x + j) % me.inner],
                        self.target.at[j - 1, i], self.sems.at[j - 1, i], me.at_x(j),
                    )
        else:
            for i in range(1, me.outer):
                self.sends.start(
                    True, self.parts[i].at[self.blocks], self.target.at[i - 1],
                    self.sems.at[0, i - 1], me.at_y(-i),
                )

    def finish(self):
        me = self.me
        if self.over_x:
            for j in range(1, me.inner):
                for i in range(me.outer):
                    arrived(self.target.at[j - 1, i], self.sems.at[j - 1, i], me.at_c)
        else:
            for i in range(1, me.outer):
                arrived(self.target.at[i - 1], self.sems.at[0, i - 1], me.at_c)


def middle_kernel(shape, *refs):
    outer = shape[1]
    sent, own, middle, grads, gain, feed_sent, feed_own = refs[:7]
    parts = refs[7 : 7 + 3 * outer]
    rows_to, d_middle, gain_grad, block_out = refs[7 + 3 * outer : 11 + 3 * outer]
    targets = refs[11 + 3 * outer : 15 + 3 * outer]
    scratch = refs[15 + 3 * outer :]
    middle_body(
        shape, sent, own, middle, grads, gain, feed_sent, feed_own, parts, targets,
        rows_to, d_middle, gain_grad, block_out, scratch[:9], scratch[9:18], *scratch[18:],
    )


class PairSum:
    def __init__(self, me, sends, sent, own, scratch):
        self.me, self.sends, self.sent = me, sends, sent
        (
            self.held, self.c_in, up_out, up_in, down_out, down_in,
            self.c_sems, up_sems, down_sems,
        ) = scratch
        self.up, self.down = (up_out, up_in, up_sems), (down_out, down_in, down_sems)

    def begin(self):
        for k in line_order():
            self.sends.start(
                True, self.sent.at[k], self.c_in.at[k], self.c_sems.at[k], self.me.at_c
            )

    def run(self):
        def ready(k):
            arrived(self.c_in.at[k], self.c_sems.at[k], self.me.at_c)

        def term(k, r):
            return self.held[k, r] + self.c_in[k, r].astype(F32)

        def store(r, value):
            self.held[0, r] = value

        line_sum(
            self.me, self.sends, self.held.shape[1], term, ready, store,
            lambda r: self.held[0, r], self.up, self.down,
        )


def plane_units(me, sends, parts, targets, sems):
    outer = me.outer
    gate, up, down = (parts[n * outer : (n + 1) * outer] for n in range(3))
    every, low, high = slice(0, Z), slice(0, Z // 2), slice(Z // 2, Z)
    return [
        PlaneTerms(me, sends, gate, targets[0], sems.at[0], True, every),
        PlaneTerms(me, sends, up, targets[1], sems.at[1], False, every),
        PlaneTerms(me, sends, down, targets[2], sems.at[2], True, low),
        PlaneTerms(me, sends, down, targets[3], sems.at[3], False, high),
    ]


def middle_body(
    shape, sent, own, middle, grads, gain, feed_sent, feed_own, parts, targets,
    rows_to, d_middle, gain_grad, block_out, sum_scratch, feed_scratch, low,
    send_sems, local_sems, rows_sems, unit_sems,
):
    me = Place(shape)
    rows = middle.shape[0]
    sends = Sends(send_sems)
    total = PairSum(me, sends, sent, own, sum_scratch)
    feed = PairSum(me, sends, feed_sent, feed_own, feed_scratch)
    load = pltpu.make_async_copy(own, total.held, local_sems.at[0])
    feed_load = pltpu.make_async_copy(feed_own, feed.held, local_sems.at[2])
    load.start()
    me.greet()
    total.begin()
    units = plane_units(me, sends, parts, targets, unit_sems)
    for unit in units:
        unit.begin()
    feed_load.start()
    load.wait()
    total.run()
    own_v = total.held
    gain_grad[...] = jnp.zeros_like(gain_grad)

    def work(r):
        values = middle[r]
        inverse = lax.rsqrt(jnp.mean(values * values, axis=1, keepdims=True) + EPSILON)
        normed = values * inverse
        d_normed = own_v[0, r]
        gain_grad[...] += d_normed * normed
        scaled = d_normed * gain[...]
        passed = inverse * (scaled - normed * jnp.mean(scaled * normed, axis=1, keepdims=True))
        total = grads[r].astype(F32) + passed
        d_middle[r] = total
        low[r] = total.astype(BF16)

    each_rows(rows, 16, work)
    keep = pltpu.make_async_copy(low, rows_to.at[me.w], local_sems.at[1])
    keep.start()
    gather = WtRows(me, sends, low, rows_to, rows_sems)
    gather.begin()
    feed.begin()
    feed_load.wait()
    feed.run()
    each_rows(rows, 16, lambda r: block_out.__setitem__(
        r, (middle[r] + feed.held[0, r]).astype(BF16)))
    gather.step()
    gather.finish()
    for unit in units:
        unit.finish()
    sends.finish()
    keep.wait()


def middle_and_rows(sent, own, middle, grads, gain, feed_sent, feed_own, parts):
    inner, outer = sizes()
    rows, width = middle.shape
    unit_rows, share = parts[0].shape[2:]
    over_x, over_y = (inner - 1, outer), (outer - 1,)
    targets = [
        jax.ShapeDtypeStruct(shape, BF16)
        for shape in (
            (*over_x, Z, unit_rows, share),
            (*over_y, Z, inner, unit_rows, share),
            (*over_x, Z // 2, unit_rows, share),
            (*over_y, Z // 2, inner, unit_rows, share),
        )
    ]
    unit_copies = 2 * (inner - 1) * outer + 2 * (outer - 1)
    pair_scratch = [pltpu.VMEM((Z, rows, width), F32), pltpu.VMEM((Z, rows, width), BF16)]
    pair_scratch += [pltpu.VMEM((Z - 1, rows, width), BF16)] * 4
    dma = pltpu.SemaphoreType.DMA
    pair_scratch += [dma((Z,)), dma((Z - 1,)), dma((Z - 1,))]
    vmem, anywhere = pl.BlockSpec(memory_space=pltpu.VMEM), pl.BlockSpec(memory_space=pl.ANY)
    return pl.pallas_call(
        functools.partial(middle_kernel, (inner, outer)),
        out_shape=(
            jax.ShapeDtypeStruct((outer * C, rows, width), BF16),
            jax.ShapeDtypeStruct((rows, width), F32),
            jax.ShapeDtypeStruct((16, width), F32),
            jax.ShapeDtypeStruct((rows, width), BF16),
            *targets,
        ),
        in_specs=[anywhere, anywhere, vmem, vmem, vmem] + [anywhere] * (2 + 3 * outer),
        out_specs=(anywhere, vmem, vmem, vmem) + (anywhere,) * 4,
        scratch_shapes=pair_scratch * 2
        + [
            pltpu.VMEM((rows, width), BF16),
            dma((2 * (Z + 2 * (Z - 1)) + 2 * outer + unit_copies,)),
            dma((3,)),
            dma((outer * C,)),
            dma((4, inner - 1, outer)),
        ],
        compiler_params=pltpu.CompilerParams(
            collective_id=2, has_side_effects=True, vmem_limit_bytes=56 * 1024 * 1024
        ),
        name="middle_and_rows",
    )(sent, own, middle, grads, gain, feed_sent, feed_own, *parts)


class RowsSum:
    def __init__(self, me, sends, terms, total, scratch, sems):
        self.me, self.sends, self.terms, self.total = me, sends, terms, total
        self.own, self.x_in, *ways = scratch
        self.own_sems, self.x_sems, up_sems, down_sems = sems
        self.up, self.down = (*ways[:2], up_sems), (*ways[2:], down_sems)

    def load(self):
        me = self.me
        self.loads = []
        for k in range(Z):
            self.loads.append(
                pltpu.make_async_copy(
                    self.terms.at[(me.z + Z - k) % Z, me.x], self.own.at[k], self.own_sems.at[k]
                )
            )
            self.loads[k].start()

    def begin(self, turns):
        me = self.me
        for turn in turns:
            if turn == Z - 1:
                k = 0
            else:
                k = (jnp.minimum(me.z, Z - 1 - me.z) + turn) % (Z - 1) + 1
                k = jnp.where(me.z < Z // 2, k, Z - k)
            at = (me.z + Z - k) % Z
            for j in range(1, me.inner):
                self.sends.start(
                    True, self.terms.at[at, (me.x + j) % me.inner], self.x_in.at[j - 1, k],
                    self.x_sems.at[j - 1, k], me.at_x(j),
                )

    def run(self, between=None):
        me = self.me

        def ready(k):
            self.loads[k].wait()
            for j in range(1, me.inner):
                arrived(self.x_in.at[j - 1, k], self.x_sems.at[j - 1, k], me.at_c)

        def term(k, r):
            value = self.own[k, r].astype(F32)
            for j in range(1, me.inner):
                value = value + self.x_in[j - 1, k, r].astype(F32)
            return value

        def store(r, value):
            self.total[r] = value

        line_sum(
            me, self.sends, self.total.shape[0], term, ready, store, lambda r: self.total[r],
            self.up, self.down, between,
        )


def sums_kernel(shape, *refs):
    inner, outer = shape
    units, units_y, units_x = refs[:3]
    refs = refs[3:]
    (wide, narrow, sent, own, tokens, gain, d_middle, gain_two_grad, vectors, units_to) = refs[:10]
    refs = refs[1:]
    (wide_to, narrow_to, tokens_grad, gains, vectors_to) = refs[9:14]
    wide_scratch, narrow_scratch = refs[14:20], refs[20:26]
    (own_v, c_in, y_out, y_in, all_in, vec_in) = refs[26:32]
    (send_sems, local_sems, c_sems, y_sems, all_sems, vec_sems) = refs[32:38]
    wide_sems, narrow_sems = refs[38:42], refs[42:46]
    units_v, units_y_in, units_x_in, unit_sems, units_y_sems, units_x_sems = refs[46:]
    share = units.shape[3]
    me = Place(shape)
    rows = tokens.shape[0]
    sends = Sends(send_sems)
    load = pltpu.make_async_copy(own, own_v, local_sems.at[0])
    load.start()
    units_load = pltpu.make_async_copy(units, units_v, local_sems.at[1])
    units_load.start()
    me.greet()

    order = [(me.y + i) % outer for i in list(range(1, outer)) + [0]]
    for at in order:
        sends.start(True, sent.at[at], c_in.at[at], c_sems.at[at], me.at_c)
    narrow_sum = RowsSum(me, sends, narrow, narrow_to, narrow_scratch, narrow_sems)
    wide_sum = RowsSum(me, sends, wide, wide_to, wide_scratch, wide_sems)
    narrow_sum.load()
    wide_sum.load()
    narrow_sum.begin(range(Z))

    def columns(n, at):
        return units_to.at[n, :, pl.ds(pl.multiple_of(at * share, LANES), share)]

    low, high, extra = slice(0, Z // 2), slice(Z // 2, Z), slice(Z, Z + Z // 2)
    every = slice(0, Z)

    def units_begin_y():
        for n, blocks in enumerate((every, extra)):
            for i in range(1, outer):
                sends.start(
                    True, units_y.at[i - 1, blocks], units_y_in.at[i - 1, blocks],
                    units_y_sems.at[i - 1, n], me.at_y(-i),
                )

    def units_begin_x():
        for n, blocks in enumerate((every, extra)):
            for j in range(1, inner):
                sends.start(
                    True, units_x.at[j - 1, blocks], units_x_in.at[j - 1, blocks],
                    units_x_sems.at[j - 1, n], me.at_x(j),
                )

    kept = []

    def unit_add(n, blocks, came, came_blocks, sems, count):
        for i in range(count):
            arrived(came.at[i, came_blocks], sems.at[i], me.at_c)

        def body(r):
            for at in range(blocks.stop - blocks.start):
                total = units_v[n, blocks.start + at, r].astype(F32)
                for i in range(count):
                    total = total + came[i, came_blocks.start + at, r].astype(F32)
                units_v[n, blocks.start + at, r] = total.astype(BF16)

        each_rows(units_v.shape[2], 16, body)

    def unit_pass_on(n):
        copy = pltpu.make_async_copy(units_v.at[n, me.z], columns(n, me.z), local_sems.at[2 + n])
        copy.start()
        kept.append(copy)
        for k in range(1, Z):
            to = (me.z + k) % Z
            sends.start(
                True, units_v.at[n, to], columns(n, me.z), unit_sems.at[n, me.z], me.at_z(to)
            )

    def unit_gate():
        unit_add(0, every, units_y_in, every, units_y_sems.at[:, 0], outer - 1)
        unit_pass_on(0)

    def unit_down():
        unit_add(2, low, units_y_in, extra, units_y_sems.at[:, 1], outer - 1)
        unit_add(2, high, units_x_in, extra, units_x_sems.at[:, 1], inner - 1)
        unit_pass_on(2)

    def unit_up():
        unit_add(1, every, units_x_in, every, units_x_sems.at[:, 0], inner - 1)
        unit_pass_on(1)

    def units_finish():
        for n in range(3):
            for k in range(1, Z):
                at = (me.z + Z - k) % Z
                arrived(columns(n, at), unit_sems.at[n, at], me.at_c)
        for copy in kept:
            copy.wait()

    def exchange(held, into, sems, first, devices):
        for n, device in enumerate(devices):
            sends.start(True, held, into.at[first + n], sems.at[first + n], device)

    def gathered(held, into, sems, first, devices):
        for n, _ in enumerate(devices):
            arrived(into.at[first + n], sems.at[first + n], me.at_c)
        total = into[first]
        for n in range(1, len(devices)):
            total = total + into[first + n]
        return held[...] + total

    stages = [
        [me.at_c],
        [me.at_y(i) for i in range(1, outer)],
        [me.at_z((me.z + k) % Z) for k in range(1, Z)],
        [me.at_x(j) for j in range(1, inner)],
    ]
    at_stage = [0]
    for stage in stages:
        at_stage.append(at_stage[-1] + len(stage))

    z_stage, x_stage = stages[2], stages[3]
    exchange(vectors, vec_in, vec_sems, 0, x_stage)
    units_begin_x()
    wide_sum.begin(range(Z))

    units_begin_y()

    load.wait()
    for i, at in enumerate(order):
        arrived(c_in.at[at], c_sems.at[at], me.at_c)
        if i < outer - 1:
            each_rows(rows, 16, lambda r, i=i, at=at: y_out.__setitem__(
                (i, r), (own_v[at, r] + c_in[at, r]).astype(BF16)))
            sends.start(True, y_out.at[i], y_in.at[i], y_sems.at[i], me.at_y(i + 1))
    vectors_to[0] = gathered(vectors, vec_in, vec_sems, 0, x_stage)
    exchange(vectors_to.at[0], vec_in, vec_sems, len(x_stage), z_stage)
    narrow_sum.run()
    vectors_to[1] = gathered(vectors_to.at[0], vec_in, vec_sems, len(x_stage), z_stage)
    units_load.wait()
    unit_gate()
    unit_up()
    unit_down()

    def work(r):
        d_normed = own_v[me.y, r] + c_in[me.y, r]
        for i in range(outer - 1):
            d_normed = d_normed + y_in[i, r].astype(F32)
        stream = tokens[r].astype(F32)
        inverse = lax.rsqrt(jnp.mean(stream * stream, axis=1, keepdims=True) + EPSILON)
        normed = stream * inverse
        part = d_normed * normed
        gains[0, 0:8] += part[0:8] + part[8:16]
        scaled = d_normed * gain[...]
        passed = inverse * (scaled - normed * jnp.mean(scaled * normed, axis=1, keepdims=True))
        tokens_grad[r] = (d_middle[r] + passed).astype(BF16)

    def gains_step(n):
        if n > 0:
            gains[n] = gathered(
                gains.at[n - 1], all_in, all_sems, at_stage[n - 1], stages[n - 1]
            )
        if n < len(stages):
            exchange(gains.at[n], all_in, all_sems, at_stage[n], stages[n])

    def between(t):
        if t == 1:
            for i in range(outer - 1):
                arrived(y_in.at[i], y_sems.at[i], me.at_c)
            gains[0] = jnp.zeros_like(gains[0])
            each_rows(rows, 16, work)
            gains[0, 8:16] = gain_two_grad[0:8] + gain_two_grad[8:16]
        gains_step(t - 1)

    wide_sum.run(between)
    for n in range(Z - 1, len(stages) + 1):
        gains_step(n)
    units_finish()
    sends.finish()


def last_sums(units, units_y, units_x, wide, narrow, sent, own, tokens, gain, d_middle, gain_two_grad, vectors):
    inner, outer = sizes()
    rows, width = tokens.shape
    dma = pltpu.SemaphoreType.DMA
    vmem, anywhere = pl.BlockSpec(memory_space=pltpu.VMEM), pl.BlockSpec(memory_space=pl.ANY)

    def scratch(terms):
        one = terms.shape[2:]
        return [pltpu.VMEM((Z, *one), BF16), pltpu.VMEM((inner - 1, Z, *one), BF16)] + [
            pltpu.VMEM((Z - 1, *one), BF16)
        ] * 4

    peers = 1 + (outer - 1) + (inner - 1) + (Z - 1)
    copies = 2 * outer - 1 + 2 * (Z * (inner - 1) + 2 * (Z - 1))
    copies += peers + (inner - 1) + (Z - 1) + 2 * (outer - 1) + 2 * (inner - 1) + 3 * (Z - 1)
    _, _, unit_rows, share = units.shape
    line_sems = [dma((Z,)), dma((inner - 1, Z)), dma((Z - 1,)), dma((Z - 1,))]
    return pl.pallas_call(
        functools.partial(sums_kernel, (inner, outer)),
        out_shape=(
            jax.ShapeDtypeStruct((3, unit_rows, Z * share), BF16),
            jax.ShapeDtypeStruct(wide.shape[2:], F32),
            jax.ShapeDtypeStruct(narrow.shape[2:], F32),
            jax.ShapeDtypeStruct((rows, width), BF16),
            jax.ShapeDtypeStruct((5, 16, width), F32),
            jax.ShapeDtypeStruct((2, *vectors.shape), F32),
        ),
        in_specs=[anywhere] * 7 + [vmem] * 5,
        out_specs=(anywhere,) + (vmem,) * 5,
        scratch_shapes=scratch(wide)
        + scratch(narrow)
        + [
            pltpu.VMEM((outer, rows, width), F32),
            pltpu.VMEM((outer, rows, width), F32),
            pltpu.VMEM((outer - 1, rows, width), BF16),
            pltpu.VMEM((outer - 1, rows, width), BF16),
            pltpu.VMEM((peers, 16, width), F32),
            pltpu.VMEM((inner - 1 + Z - 1, *vectors.shape), F32),
            dma((copies,)),
            dma((5,)),
            dma((outer,)),
            dma((outer - 1,)),
            dma((peers,)),
            dma((inner - 1 + Z - 1,)),
        ]
        + line_sems * 2
        + [
            pltpu.VMEM(units.shape, BF16),
            pltpu.VMEM(units_y.shape, BF16),
            pltpu.VMEM(units_x.shape, BF16),
            dma((3, Z)),
            dma((outer - 1, 2)),
            dma((inner - 1, 2)),
        ],
        compiler_params=pltpu.CompilerParams(
            collective_id=5, has_side_effects=True, vmem_limit_bytes=58 * 1024 * 1024
        ),
        name="last_sums",
    )(units, units_y, units_x, wide, narrow, sent, own, tokens, gain, d_middle, gain_two_grad, vectors)


def scan_kernel(backward, factors, inflows, states, entered, products, ends, ends_in, carry, send_sems, arrivals):
    seq = ends_in.shape[0]
    s = lax.axis_index("seq")
    rows, width = factors.shape
    barrier = pltpu.get_barrier_semaphore()

    def device(at):
        return {"seq": at, "wt": lax.axis_index("wt")}

    def greet(i, carried):
        @pl.when(i != s)
        def _():
            pl.semaphore_signal(barrier, inc=1, device_id=device(i), device_id_type=MESH)

        return carried

    lax.fori_loop(0, seq, greet, 0)
    group = 8
    at_row = lax.broadcasted_iota(jnp.int32, (group, width), 0)

    def step(i, carried):
        held, product = carried
        i = rows // group - 1 - i if backward else i
        where = pl.ds(pl.multiple_of(i * group, group), group)
        factor, inflow = factors[where, :], inflows[where, :]
        for by in (1, 2, 4):
            inside = at_row < group - by if backward else at_row >= by
            turn = group - by if backward else by
            inflow = factor * jnp.where(inside, pltpu.roll(inflow, turn, 0), 0.0) + inflow
            factor = factor * jnp.where(inside, pltpu.roll(factor, turn, 0), 1.0)
        inflow = inflow + factor * held
        factor = factor * product
        states[where, :] = inflow
        products[where, :] = factor
        last = slice(0, 1) if backward else slice(group - 1, group)
        return inflow[last], factor[last]

    held, product = lax.fori_loop(
        0, rows // group, step, (jnp.zeros((1, width), F32), jnp.ones((1, width), F32))
    )
    ends[0:1] = product
    ends[1:2] = held
    pl.semaphore_wait(barrier, seq - 1)

    def copy_to(i):
        return pltpu.make_async_remote_copy(
            src_ref=ends, dst_ref=ends_in.at[s], send_sem=send_sems.at[i], recv_sem=arrivals.at[s],
            device_id=device(i), device_id_type=MESH,
        )

    def later(i):
        return i < s if backward else i > s

    def send(i, carried):
        pl.when(later(i))(lambda: copy_to(i).start())
        return carried

    lax.fori_loop(0, seq, send, 0)
    carry[...] = jnp.zeros_like(carry)

    def receive(n, carried):
        i = seq - 1 - n if backward else n

        @pl.when(jnp.logical_not(later(i)) & (i != s))
        def _():
            arrived(ends_in.at[i], arrivals.at[i], device((s + 1) % seq))
            carry[0:1] = ends_in[i, 0:1] * carry[0:1] + ends_in[i, 1:2]

        return carried

    lax.fori_loop(0, seq, receive, 0)
    entering = carry[0:1]
    entered[...] = entering

    def spread(i, carried):
        where = pl.ds(pl.multiple_of(i * group, group), group)
        states[where, :] += products[where, :] * entering
        return carried

    lax.fori_loop(0, rows // group, spread, 0)

    def sent(i, carried):
        pl.when(later(i))(lambda: copy_to(i).wait_send())
        return carried

    lax.fori_loop(0, seq, sent, 0)


def full_scan(factor, inflow, backward):
    seq = lax.axis_size("seq")
    rows, width = factor.shape
    vmem = pl.BlockSpec(memory_space=pltpu.VMEM)
    return pl.pallas_call(
        functools.partial(scan_kernel, backward),
        out_shape=(
            jax.ShapeDtypeStruct((rows, width), F32),
            jax.ShapeDtypeStruct((1, width), F32),
        ),
        in_specs=[vmem, vmem],
        out_specs=(vmem, vmem),
        scratch_shapes=[
            pltpu.VMEM((rows, width), F32),
            pltpu.VMEM((8, width), F32),
            pltpu.VMEM((seq, 8, width), F32),
            pltpu.VMEM((8, width), F32),
            pltpu.SemaphoreType.DMA((seq,)),
            pltpu.SemaphoreType.DMA((seq,)),
        ],
        compiler_params=pltpu.CompilerParams(
            collective_id=4 if backward else 3,
            has_side_effects=True,
            vmem_limit_bytes=32 * 1024 * 1024,
        ),
        name="scan_back" if backward else "scan_ahead",
    )(factor, inflow)


def recurrence_terms(decay_pre, input_pre, decay_log, conv_float):
    log_decay = -DECAY_SCALE * jax.nn.softplus(-decay_log) * jax.nn.sigmoid(decay_pre)
    return (
        jnp.exp(log_decay),
        jnp.sqrt(-jnp.expm1(2.0 * log_decay)) * jax.nn.sigmoid(input_pre) * conv_float,
    )


def normed_rows(stream):
    inverse = lax.rsqrt(jnp.mean(stream * stream, axis=1, keepdims=True) + EPSILON)
    return stream * inverse, inverse


def per_device(
    tokens,
    norm1_gain,
    x_weight,
    y_weight,
    conv_weight,
    conv_bias,
    decay_gate_weight,
    decay_bias,
    input_gate_weight,
    input_bias,
    decay_param,
    out_weight,
    norm2_gain,
    gate_weight,
    up_weight,
    down_weight,
    out_grad,
):
    seq, wt = lax.axis_size("seq"), lax.axis_size("wt")
    inner, outer = sizes()
    z, x, y, c = places()
    w = lax.axis_index("wt")
    rows_dev, width = tokens.shape
    weight_rows, lru_cols = x_weight.shape
    chunk, block = decay_gate_weight.shape
    half = block // 2
    full = lru_cols - half
    taps_count = conv_weight.shape[1]
    reach = taps_count - 1
    hidden_cols = gate_weight.shape[1]

    def turned(value, axis):
        return jnp.where(c == 0, value, jnp.roll(value, -half, axis))

    def turned_back(value, axis):
        return jnp.where(c == 0, value, jnp.roll(value, half, axis))

    def in_order(own, partner, axis):
        return jnp.where(
            c == 0,
            jnp.concatenate([own, partner], axis),
            jnp.concatenate([partner, own], axis),
        )

    vectors = jnp.stack(
        [v.astype(F32) for v in (norm1_gain, norm2_gain, conv_bias, decay_bias, input_bias)]
        + [decay_param]
        + [conv_weight[:, k].astype(F32) for k in range(taps_count)]
    )
    vectors = jnp.pad(vectors, ((0, -vectors.shape[0] % 8), (0, -chunk % LANES)))

    across = [(i, i % seq * wt + i // seq) for i in range(seq * wt)]
    gates = jnp.concatenate([decay_gate_weight, input_gate_weight], axis=1)

    def padded(weight):
        share = -(-hidden_cols // (Z * LANES)) * LANES
        return jnp.pad(weight, ((0, 0), (0, Z * share - hidden_cols)))

    xy_unit = jnp.concatenate([turned(x_weight, 1), turned(y_weight, 1)], axis=1)
    (
        group_tokens, grad_group, vectors, gate_all, xy_kernel, out_kernel,
        gate_kernel, up_kernel, down_kernel,
    ) = gather_all(
        tokens, out_grad, vectors, gates, xy_unit, turned(out_weight, 1),
        padded(gate_weight), padded(up_weight), padded(down_weight),
    )
    group_tokens = group_tokens.reshape(-1, width)
    grad_group = grad_group.reshape(-1, width)
    vectors = jnp.moveaxis(vectors[:, : 6 + taps_count, :chunk], 0, 1).reshape(6 + taps_count, -1)
    gain_one, gain_two = vectors[0], vectors[1]
    own_vectors = turned(
        lax.dynamic_slice(vectors[2:], (0, w * lru_cols), (taps_count + 4, lru_cols)), 1
    )
    tap_bias, decay_shift, input_shift, decay_log = (own_vectors[i] for i in range(4))
    taps = own_vectors[4:]
    xy_kernel = xy_kernel.reshape(width, -1)
    out_kernel = out_kernel.reshape(width, -1)
    gate_kernel = gate_kernel.reshape(width, -1)
    gate_all = turned(gate_all.reshape(lru_cols, 2 * block), 0)
    partner_rows = c_swap(gate_all[full:])
    shared_rows = in_order(gate_all[full:], partner_rows, 0)

    stream = tokens.astype(F32)
    group_normed, _ = normed_rows(group_tokens.astype(F32))
    group_one = (group_normed * gain_one).astype(BF16)
    rows = group_one.shape[0]
    xy = multiply(group_one, xy_kernel)
    x_branch = xy[:, :lru_cols].astype(BF16)
    y_before = xy[:, lru_cols:]
    y_gated, gelu_y_back = jax.vjp(gelu_tanh, y_before)
    rim = lax.ppermute(x_branch[rows - reach :], "seq", [(i, i + 1) for i in range(seq - 1)])
    extended = jnp.concatenate([rim, x_branch], axis=0).astype(F32)
    conv_low = (
        tap_bias
        + sum(taps[k] * extended[reach - k : reach - k + rows] for k in range(taps_count))
    ).astype(BF16)
    shared_conv = in_order(conv_low[:, full:], c_swap(conv_low[:, full:]), 1)
    heads = full // block

    def of_head(value, i):
        return value[:, i * block : (i + 1) * block]

    pre_parts = [
        multiply(of_head(conv_low, i), gate_all[i * block : (i + 1) * block]) for i in range(heads)
    ]
    shared_pre = multiply(shared_conv, shared_rows).reshape(rows, 2, C, half)
    shared_pre = pick(shared_pre, c, 2)
    decay_pre = decay_shift + jnp.concatenate(
        [part[:, :block] for part in pre_parts] + [shared_pre[:, 0]], axis=1
    )
    input_pre = input_shift + jnp.concatenate(
        [part[:, block:] for part in pre_parts] + [shared_pre[:, 1]], axis=1
    )
    (retain, inflow), terms_back = jax.vjp(
        recurrence_terms, decay_pre, input_pre, decay_log, conv_low.astype(F32)
    )
    states, state_in = full_scan(retain, inflow, False)
    before = jnp.concatenate([state_in, states[:-1]])
    lru_low = states.astype(BF16).astype(F32)
    mixed_rows = (lru_low * y_gated).astype(BF16)
    mixed_parts = mixed_rows.reshape(outer, C, rows_dev, lru_cols)

    def branch_of(at):
        part = pick(mixed_parts, at, 1).reshape(outer * rows_dev, lru_cols)
        return contract_last(part, out_kernel).reshape(outer, rows_dev, width)

    group_two, middle, up_kernel, down_kernel = branch_and_group(
        branch_of(1 - c), branch_of(c), tokens, gain_two[None], up_kernel, down_kernel
    )
    up_kernel = up_kernel.reshape(width, -1)
    down_kernel = down_kernel.reshape(width, -1)
    group_two = group_two.reshape(C * Z * rows_dev, width)

    gate_pre = multiply(group_two, gate_kernel)
    up_pre = multiply(group_two, up_kernel)
    active, gelu_gate_back = jax.vjp(gelu_tanh, gate_pre)
    hidden = (active * up_pre).astype(BF16)

    d_hidden = multiply(grad_group, down_kernel)
    d_up = (d_hidden * active).astype(BF16)
    d_gate = gelu_gate_back(d_hidden * up_pre)[0].astype(BF16)
    half_rows = Z * rows_dev

    def d_normed_of(part):
        total = contract_last(d_gate[part], gate_kernel) + contract_last(d_up[part], up_kernel)
        return total.reshape(Z, rows_dev, width)

    def terms_of(left_side, right_side):
        share = right_side.shape[1] // outer
        return [
            contract_rows(left_side, right_side[:, i * share : (i + 1) * share])
            .astype(BF16)
            .reshape(Z, inner, weight_rows, share)
            for i in range(outer)
        ]

    gate_terms = terms_of(group_two, d_gate)
    up_terms = terms_of(group_two, d_up)
    down_terms = terms_of(grad_group, hidden)
    def feed_of(part):
        return contract_last(hidden[part], down_kernel).reshape(Z, rows_dev, width)

    branch_rows, d_middle, gain_two_grad, block_out, *came = middle_and_rows(
        d_normed_of(slice(half_rows, None)).astype(BF16),
        d_normed_of(slice(0, half_rows)),
        middle,
        out_grad,
        gain_two[None],
        feed_of(slice(half_rows, None)).astype(BF16),
        feed_of(slice(0, half_rows)),
        gate_terms + up_terms + down_terms,
    )
    branch_rows = branch_rows.reshape(-1, width)

    def added_over_x(terms, moved):
        return [
            sum((moved[j - 1, i].astype(F32) for j in range(1, inner)), pick(term, x, 1).astype(F32))
            for i, term in enumerate(terms)
        ]

    def added_over_y(term, moved):
        return sum((moved[i - 1].astype(F32) for i in range(1, outer)), term.astype(F32))

    half_z = Z // 2
    gate_x = added_over_x(gate_terms, came[0])
    up_y = added_over_y(up_terms[0], came[1])
    down_x = added_over_x([term[:half_z] for term in down_terms], came[2])
    down_y = added_over_y(down_terms[0][half_z:], came[3])
    all_y = jnp.concatenate([up_y, down_y])
    kept_x = pick(all_y, x, 1)
    units = jnp.concatenate([gate_x[0], kept_x[:Z], down_x[0], kept_x[Z:]]).astype(BF16)
    units = units.reshape(3, Z, weight_rows, -1)
    units_y = jnp.stack(
        [jnp.concatenate([gate_x[i], down_x[i]]).astype(BF16) for i in range(1, outer)]
    )
    units_x = jnp.stack(
        [pick(all_y, (x + j) % inner, 1).astype(BF16) for j in range(1, inner)]
    )

    d_mixed = multiply(branch_rows, out_kernel)
    d_lru = (d_mixed * y_gated).astype(BF16).astype(F32)
    d_y = gelu_y_back(d_mixed * lru_low)[0].astype(BF16)
    passed, passed_in = full_scan(retain, retain * d_lru, True)
    d_total = d_lru + jnp.concatenate([passed[1:], passed_in])
    d_decay_pre, d_input_pre, decay_log_grad, d_conv_direct = terms_back(
        (d_total * before, d_total)
    )
    d_decay_low, d_input_low = d_decay_pre.astype(BF16), d_input_pre.astype(BF16)
    own_low = jnp.concatenate([d_decay_low[:, full:], d_input_low[:, full:]], axis=1)
    partner_low = c_swap(own_low)
    shared_low = jnp.concatenate(
        [
            in_order(own_low[:, :half], partner_low[:, :half], 1),
            in_order(own_low[:, half:], partner_low[:, half:], 1),
        ],
        axis=1,
    )
    lows = [
        jnp.concatenate([of_head(d_decay_low, i), of_head(d_input_low, i)], axis=1)
        for i in range(heads)
    ]
    d_conv = d_conv_direct + jnp.concatenate(
        [contract_last(lows[i], gate_all[i * block : (i + 1) * block]) for i in range(heads)]
        + [contract_last(shared_low, gate_all[full:])],
        axis=1,
    )
    gates_grad = jnp.concatenate(
        [contract_rows(of_head(conv_low, i), lows[i]) for i in range(heads)]
        + [contract_rows(conv_low[:, full:], shared_low)]
    )
    ahead = lax.ppermute(d_conv[:reach], "seq", [(i + 1, i) for i in range(seq - 1)])
    d_extended = jnp.concatenate([d_conv, ahead], axis=0)
    d_x_branch = sum(taps[k] * d_extended[k : k + rows] for k in range(taps_count)).astype(BF16)
    dx_parts = d_x_branch.reshape(outer, C, rows_dev, lru_cols)
    dy_parts = d_y.reshape(outer, C, rows_dev, lru_cols)

    def d_normed_one_of(at):
        dx, dy = (
            pick(parts, at, 1).reshape(outer * rows_dev, lru_cols) for parts in (dx_parts, dy_parts)
        )
        total = contract_last(dx, xy_kernel[:, :lru_cols]) + contract_last(
            dy, xy_kernel[:, lru_cols:]
        )
        return total.reshape(outer, rows_dev, width)

    wide = jnp.concatenate(
        [
            contract_rows(group_one, d_x_branch),
            contract_rows(group_one, d_y),
            contract_rows(branch_rows, mixed_rows),
        ],
        axis=1,
    )
    wide = wide.astype(BF16).reshape(Z, inner, weight_rows, 3 * lru_cols)
    narrow = turned_back(gates_grad, 0).astype(BF16).reshape(Z, inner, chunk, 2 * block)
    narrow = jnp.pad(narrow, ((0, 0), (0, 0), (0, -chunk % 16), (0, 0)))
    own_sums = jnp.stack(
        [jnp.sum(d_conv, axis=0), jnp.sum(d_decay_pre, axis=0), jnp.sum(d_input_pre, axis=0)]
        + [decay_log_grad]
        + [jnp.sum(d_conv * extended[reach - k : reach - k + rows], axis=0) for k in range(taps_count)],
    )
    own_sums = turned_back(own_sums, 1)
    placed, wide, narrow, tokens_grad, gains, own_sums = last_sums(
        units, units_y, units_x, wide, narrow, d_normed_one_of(1 - c), d_normed_one_of(c), tokens, gain_one[None],
        d_middle, gain_two_grad, own_sums,
    )
    weight_grads = [
        turned_back(wide[:, n * lru_cols : (n + 1) * lru_cols], 1) for n in range(3)
    ]
    gate_grad, up_grad, down_grad = (placed[n, :, :hidden_cols].astype(F32) for n in range(3))
    gains = gains[4].reshape(2, 8, width).sum(axis=1)
    gains = lax.dynamic_slice(gains, (0, (lax.axis_index("seq") * wt + w) * chunk), (2, chunk))
    sums = lax.dynamic_slice(own_sums[1], (0, lax.axis_index("seq") * chunk), (taps_count + 4, chunk))
    own_sums = jnp.concatenate([narrow[:chunk], sums.T], axis=1)
    own_sums = lax.ppermute(own_sums, ("seq", "wt"), [(to, at) for at, to in across])
    sums = own_sums[:, 2 * block :]
    return (
        block_out,
        tokens_grad,
        gains[0],
        weight_grads[0],
        weight_grads[1],
        sums[:, 4:],
        sums[:, 0],
        own_sums[:, :block],
        sums[:, 1],
        own_sums[:, block : 2 * block],
        sums[:, 2],
        sums[:, 3],
        weight_grads[2],
        gains[1],
        gate_grad,
        up_grad,
        down_grad,
    )


def solution(mesh):
    rows, both, lone = P(("seq", "wt"), None), P("seq", "wt"), P(("seq", "wt"))
    in_specs = (
        rows, lone, both, both, rows, lone, rows, lone, rows, lone, lone,
        both, lone, both, both, both, rows,
    )
    out_specs = (
        rows, rows, lone, both, both, rows, lone, rows, lone, rows, lone, lone,
        both, lone, both, both, both,
    )
    return jax.shard_map(
        per_device, mesh=mesh, in_specs=in_specs, out_specs=out_specs, check_vma=False
    )
```

```python
import functools

import jax
import jax.numpy as jnp
from jax import lax
from jax.experimental import pallas as pl
from jax.experimental.pallas import tpu as pltpu
from jax.sharding import PartitionSpec as P

EPSILON = 1e-06
DECAY_SCALE = 8.0
Z = 4
C = 2
LANES = 128
F32 = jnp.float32
BF16 = jnp.bfloat16
MESH = pl.DeviceIdType.MESH


def gelu_tanh(values):
    return jax.nn.gelu(values, approximate=True)


def sizes():
    return lax.axis_size("seq") // Z, lax.axis_size("wt") // C


def places():
    inner, outer = sizes()
    s, w = lax.axis_index("seq"), lax.axis_index("wt")
    return s // inner, s % inner, w // C, w % C


def z_move(value, by, senders):
    inner, _ = sizes()
    pairs = [(z * inner + x, (z + by) % Z * inner + x) for z in senders for x in range(inner)]
    return lax.ppermute(value, "seq", pairs)


def c_swap(value):
    _, outer = sizes()
    pairs = [(y * C + c, y * C + 1 - c) for y in range(outer) for c in range(C)]
    return lax.ppermute(value, "wt", pairs)


def line_scatter(parts):
    up = down = None
    for step in range(1, Z):
        rising = parts[step] if up is None else parts[step] + up
        falling = parts[Z - step] if down is None else parts[Z - step] + down
        up = z_move(rising.astype(BF16), 1, range(0, step)).astype(F32)
        down = z_move(falling.astype(BF16), -1, range(Z - step, Z)).astype(F32)
    return parts[0] + up + down


def pick(value, index, axis):
    return lax.dynamic_index_in_dim(value, index, axis, keepdims=False)


def contract_last(left_side, right_side):
    return lax.dot_general(
        left_side, right_side, (((1,), (1,)), ((), ())), preferred_element_type=F32
    )


def contract_rows(left_side, right_side):
    return lax.dot_general(
        left_side, right_side, (((0,), (0,)), ((), ())), preferred_element_type=F32
    )


def multiply(left_side, right_side):
    return jnp.dot(left_side, right_side, preferred_element_type=F32)


class Sends:
    def __init__(self, sems):
        self.sems, self.started = sems, []

    def start(self, when, source, target, arrival, device):
        copy = pltpu.make_async_remote_copy(
            src_ref=source,
            dst_ref=target,
            send_sem=self.sems.at[len(self.started)],
            recv_sem=arrival,
            device_id=device,
            device_id_type=MESH,
        )
        if when is True:
            copy.start()
        else:
            pl.when(when)(copy.start)
        self.started.append((when, copy))

    def finish(self):
        for when, copy in self.started:
            if when is True:
                copy.wait_send()
            else:
                pl.when(when)(copy.wait_send)


def arrived(target, arrival, device):
    pltpu.make_async_remote_copy(
        src_ref=target, dst_ref=target, send_sem=arrival, recv_sem=arrival,
        device_id=device, device_id_type=MESH,
    ).wait_recv()


def gather_kernel(shape, *refs):
    inner, outer = shape
    (tokens, grads, vectors, gates, xy, out, gate, up, down) = refs[:9]
    (tokens_to, grads_to, vectors_to, gates_to, xy_to, out_to, gate_to, up_to, down_to) = refs[9:18]
    gates_own, send_sems, local_sems, line_sems, plane_sems, rows_sems = refs[18:24]
    vector_sems, turn_sems, group_sems = refs[24:]
    seq, wt = Z * inner, outer * C
    s, w = lax.axis_index("seq"), lax.axis_index("wt")
    z, x, y, c = s // inner, s % inner, w // C, w % C
    sends = Sends(send_sems)
    group = GroupRows(Place(shape), sends, grads, grads_to, group_sems)
    here = []

    def at_z(to):
        return {"seq": to * inner + x, "wt": w}

    def at_x(by):
        return {"seq": z * inner + (x + by) % inner, "wt": w}

    def at_y(by):
        return {"seq": s, "wt": (y + by) % outer * C + c}

    at_c = {"seq": s, "wt": y * C + 1 - c}

    def keep(source, target, waited=False):
        copy = pltpu.make_async_copy(source, target, local_sems.at[len(here)])
        copy.start()
        here.append((waited, copy))
        return copy

    barrier = pltpu.get_barrier_semaphore()

    def greet(i, carried):
        @pl.when(i != s * wt + w)
        def _():
            pl.semaphore_signal(
                barrier, inc=1, device_id={"seq": i // wt, "wt": i % wt}, device_id_type=MESH
            )

        return carried

    lax.fori_loop(0, seq * wt, greet, 0)
    pl.semaphore_wait(barrier, seq * wt - 1)

    class Line:
        def __init__(self, index, source, target):
            self.source, self.target = source, target
            self.sems = line_sems.at[index]

        def forward(self, block, at, up_when, down_when):
            place = self.target.at[at, x]
            arrival = self.sems.at[at, x]
            sends.start(up_when, block, place, arrival, at_z(jnp.minimum(z + 1, Z - 1)))
            sends.start(down_when, block, place, arrival, at_z(jnp.maximum(z - 1, 0)))
            return place, arrival

        def across(self, when, block, at):
            for j in range(1, inner):
                sends.start(when, block, self.target.at[at, x], self.sems.at[at, x], at_x(j))

        def begin_z(self):
            keep(self.source, self.target.at[z, x])
            self.forward(self.source, z, z < Z - 1, z > 0)

        def begin_x(self):
            self.across(True, self.source, z)

        def begin(self):
            self.begin_z()
            self.begin_x()

        def step(self, k):
            for at, there, up_when, down_when in (
                (jnp.maximum(z - k, 0), z - k >= 0, (z - k >= 0) & (z < Z - 1), None),
                (jnp.minimum(z + k, Z - 1), z + k < Z, None, (z + k < Z) & (z > 0)),
            ):
                place, arrival = self.target.at[at, x], self.sems.at[at, x]

                @pl.when(there)
                def _(place=place, arrival=arrival):
                    arrived(place, arrival, at_c)

                if up_when is not None:
                    sends.start(up_when, place, place, arrival, at_z(jnp.minimum(z + 1, Z - 1)))
                else:
                    sends.start(down_when, place, place, arrival, at_z(jnp.maximum(z - 1, 0)))
                self.across(there, place, at)

        def finish(self):
            for at in range(Z):
                for j in range(1, inner):
                    from_x = (x + inner - j) % inner
                    arrived(self.target.at[at, from_x], self.sems.at[at, from_x], at_c)

    class Plane:
        def __init__(self, index, source, target, x_first, whole):
            self.source, self.target, self.x_first, self.whole = source, target, x_first, whole
            self.share = source.shape[1] // Z
            self.sems = plane_sems.at[index]

        def cut(self, at):
            return self.source.at[:, pl.ds(pl.multiple_of(at * self.share, LANES), self.share)]

        def place(self, at, x_at, i):
            return self.target.at[at, x_at, :, i * self.share : (i + 1) * self.share]

        def begin(self):
            self.own = keep(self.cut(z), self.place(z, x, 0), True)
            for k in range(1, Z):
                to = (z + k) % Z
                sends.start(True, self.cut(to), self.place(z, x, 0), self.sems.at[z, 0, 0], at_z(to))

        def over_x(self, at, i):
            place = self.place(at, x, i)
            for j in range(1, inner):
                sends.start(True, place, place, self.sems.at[at, j, i], at_x(j))

        def over_y(self, at, j):
            x_at = (x + inner - j) % inner
            for i in range(1, outer):
                sends.start(
                    True, self.place(at, x_at, 0), self.place(at, x_at, i),
                    self.sems.at[at, j, i], at_y(i),
                )

        def got(self, at, j, i):
            arrived(self.place(at, (x + inner - j) % inner, i), self.sems.at[at, j, i], at_c)

        def first(self, k):
            at = (z + Z - k) % Z
            if k == 0:
                self.own.wait()
            else:
                self.got(at, 0, 0)
            if self.x_first or self.whole:
                self.over_x(at, 0)
            if self.whole or not self.x_first:
                self.over_y(at, 0)

        def second(self, k):
            at = (z + Z - k) % Z
            if self.x_first:
                for j in range(1, inner):
                    self.got(at, j, 0)
                    if self.whole:
                        self.over_y(at, j)
            else:
                for i in range(1, outer):
                    self.got(at, 0, i)

        def finish(self, k):
            if self.whole:
                at = (z + Z - k) % Z
                for j in range(inner):
                    for i in range(1, outer):
                        self.got(at, j, i)

    lines = [Line(0, xy, xy_to), Line(1, gates_own, gates_to), Line(2, out, out_to)]
    planes = [
        Plane(0, gate, gate_to, True, True),
        Plane(1, up, up_to, False, False),
        Plane(2, down, down_to, True, False),
    ]

    me = s * wt + w
    keep(vectors, vectors_to.at[me])

    def vector_copy(i):
        return pltpu.make_async_remote_copy(
            src_ref=vectors, dst_ref=vectors_to.at[me],
            send_sem=vector_sems.at[0, i], recv_sem=vector_sems.at[1, me],
            device_id={"seq": i // wt, "wt": i % wt}, device_id_type=MESH,
        )

    def vector_send(i, carried):
        pl.when(i != me)(lambda: vector_copy(i).start())
        return carried

    def tokens_begin():
        keep(tokens, tokens_to.at[w])
        sends.start(True, tokens, tokens_to.at[w], rows_sems.at[w], at_c)
        for i in range(1, outer):
            sends.start(True, tokens, tokens_to.at[w], rows_sems.at[w], at_y(i))

    def tokens_step():
        for i in range(1, outer):
            at = (y + outer - i) % outer * C + c
            arrived(tokens_to.at[at], rows_sems.at[at], at_c)
            sends.start(True, tokens_to.at[at], tokens_to.at[at], rows_sems.at[at], at_c)

    def tokens_finish():
        for i in range(outer):
            at = (y + outer - i) % outer * C + 1 - c
            arrived(tokens_to.at[at], rows_sems.at[at], at_c)

    to_seq, to_wt = me % seq, me // seq
    from_me = w * seq + s
    turn = pltpu.make_async_remote_copy(
        src_ref=gates, dst_ref=gates_own, send_sem=turn_sems.at[0], recv_sem=turn_sems.at[1],
        device_id={"seq": to_seq, "wt": to_wt}, device_id_type=MESH,
    )
    stay = pltpu.make_async_copy(gates, gates_own, turn_sems.at[2])
    here_too = from_me == me

    pl.when(jnp.logical_not(here_too))(turn.start)
    pl.when(here_too)(stay.start)
    lines[0].begin()
    tokens_begin()

    @pl.when(jnp.logical_not(here_too))
    def _():
        arrived(gates_own, turn_sems.at[1], at_c)

    pl.when(here_too)(stay.wait)
    lines[1].begin()
    lines[2].begin_z()
    lax.fori_loop(0, seq * wt, vector_send, 0)
    for k in range(1, Z):
        lines[1].step(k)
        lines[0].step(k)
        if k == 1:
            tokens_step()
    lines[2].begin_x()
    for k in range(1, Z):
        lines[2].step(k)
        if k == Z - 2:
            planes[0].begin()
            planes[2].begin()
            planes[1].begin()
    for k in range(Z):
        planes[0].first(k)
    for k in range(Z):
        planes[2].first(k)
    keep(grads, group.place(0, z, z))
    group.begin()
    for k in range(Z):
        planes[1].first(k)
        planes[0].second(k)
    for k in range(1, Z):
        group.step(k)
    group.finish()

    for line in lines:
        line.finish()
    tokens_finish()
    for k in range(Z):
        planes[1].second(k)
        planes[2].second(k)
        planes[0].finish(k)

    def vector_wait(i, carried):
        @pl.when(i != me)
        def _():
            vector_copy(i).wait_send()
            arrived(vectors_to.at[i], vector_sems.at[1, i], at_c)

        return carried

    pl.when(jnp.logical_not(here_too))(turn.wait_send)
    lax.fori_loop(0, seq * wt, vector_wait, 0)
    sends.finish()
    for waited, copy in here:
        if not waited:
            copy.wait()


def gather_all(tokens, grads, vectors, gates, xy, out, gate, up, down):
    inner, outer = sizes()
    seq, wt = Z * inner, outer * C

    def buffer(*shape, like):
        return jax.ShapeDtypeStruct(shape, like.dtype)

    def plane(weight):
        rows, columns = weight.shape
        return buffer(Z, inner, rows, outer * columns // Z, like=weight)

    shapes = (
        buffer(wt, *tokens.shape, like=tokens),
        buffer(C, Z, *grads.shape, like=grads),
        buffer(seq * wt, *vectors.shape, like=vectors),
        buffer(Z, inner, *gates.shape, like=gates),
        buffer(Z, inner, *xy.shape, like=xy),
        buffer(Z, inner, *out.shape, like=out),
        plane(gate),
        plane(up),
        plane(down),
    )
    copies = 3 * (2 + inner + (Z - 1) * 2 * inner) + 3 * (Z - 1 + Z * (inner + 2 * outer + inner * outer))
    copies += 2 * outer + 3 + 4 * Z
    dma = pltpu.SemaphoreType.DMA
    return pl.pallas_call(
        functools.partial(gather_kernel, (inner, outer)),
        out_shape=shapes,
        in_specs=[pl.BlockSpec(memory_space=pl.ANY)] * 9,
        out_specs=[pl.BlockSpec(memory_space=pl.ANY)] * 9,
        scratch_shapes=[
            pltpu.VMEM(gates.shape, gates.dtype),
            dma((copies,)),
            dma((16,)),
            dma((3, Z, inner)),
            dma((3, Z, inner, outer)),
            dma((wt,)),
            dma((2, seq * wt)),
            dma((3,)),
            dma((C, Z)),
        ],
        compiler_params=pltpu.CompilerParams(collective_id=0, has_side_effects=True),
        name="gather_all",
    )(tokens, grads, vectors, gates, xy, out, gate, up, down)


class Place:
    def __init__(self, shape):
        self.inner, self.outer = shape
        self.s, self.w = lax.axis_index("seq"), lax.axis_index("wt")
        self.z, self.x = self.s // self.inner, self.s % self.inner
        self.y, self.c = self.w // C, self.w % C
        self.at_c = {"seq": self.s, "wt": self.y * C + 1 - self.c}
        self.z_up, self.z_down = jnp.minimum(self.z + 1, Z - 1), jnp.maximum(self.z - 1, 0)

    def at_z(self, to):
        return {"seq": to * self.inner + self.x, "wt": self.w}

    def at_x(self, by):
        return {"seq": self.z * self.inner + (self.x + by) % self.inner, "wt": self.w}

    def at_y(self, by):
        return {"seq": self.s, "wt": (self.y + self.outer + by) % self.outer * C + self.c}

    def greet(self):
        barrier = pltpu.get_barrier_semaphore()
        devices = [self.at_c]
        devices += [self.at_z((self.z + k) % Z) for k in range(1, Z)]
        devices += [self.at_x(j) for j in range(1, self.inner)]
        devices += [self.at_y(i) for i in range(1, self.outer)]
        for device in devices:
            pl.semaphore_signal(barrier, inc=1, device_id=device, device_id_type=MESH)
        pl.semaphore_wait(barrier, len(devices))


def each_rows(count, step, body):
    def run(i, carried):
        body(pl.ds(pl.multiple_of(i * step, step), step))
        return carried

    lax.fori_loop(0, count // step, run, 0)


class WtRows:
    def __init__(self, me, sends, source, target, sems):
        self.me, self.sends, self.source, self.target, self.sems = me, sends, source, target, sems

    def begin(self):
        me = self.me
        for device in [me.at_y(i) for i in range(1, me.outer)] + [me.at_c]:
            self.sends.start(True, self.source, self.target.at[me.w], self.sems.at[me.w], device)

    def step(self):
        me = self.me
        for i in range(1, me.outer):
            at = (me.y + me.outer - i) % me.outer * C + me.c
            arrived(self.target.at[at], self.sems.at[at], me.at_c)
            self.sends.start(True, self.target.at[at], self.target.at[at], self.sems.at[at], me.at_c)

    def finish(self):
        me = self.me
        for i in range(me.outer):
            at = (me.y + me.outer - i) % me.outer * C + 1 - me.c
            arrived(self.target.at[at], self.sems.at[at], me.at_c)


class GroupRows:
    def __init__(self, me, sends, source, target, sems):
        self.me, self.sends, self.source, self.target, self.sems = me, sends, source, target, sems

    def place(self, own, at, z_to):
        return self.target.at[own, (z_to - at + Z) % Z]

    def forward(self, at, source, there, way):
        me = self.me
        z_to = me.z_up if way > 0 else me.z_down
        room = me.z < Z - 1 if way > 0 else me.z > 0
        when = room if there is None else there & room
        self.sends.start(
            when, source, self.place(0, at, z_to), self.sems.at[0, at], me.at_z(z_to)
        )

    def begin(self):
        me = self.me
        self.forward(me.z, self.source, None, 1)
        self.forward(me.z, self.source, None, -1)
        self.sends.start(
            True, self.source, self.place(1, me.z, me.z), self.sems.at[1, me.z], me.at_c
        )

    def step(self, k):
        me = self.me
        for at, there, way in (
            (jnp.maximum(me.z - k, 0), me.z - k >= 0, 1),
            (jnp.minimum(me.z + k, Z - 1), me.z + k < Z, -1),
        ):
            place = self.place(0, at, me.z)

            @pl.when(there)
            def _(place=place, at=at):
                arrived(place, self.sems.at[0, at], me.at_c)

            self.forward(at, place, there, way)
            self.sends.start(there, place, self.place(1, at, me.z), self.sems.at[1, at], me.at_c)

    def finish(self):
        me = self.me
        for at in range(Z):
            arrived(self.place(1, at, me.z), self.sems.at[1, at], me.at_c)


def branch_kernel(
    shape, sent, own, tokens, gain, up_held, down_held, group_to, middle, up_to, down_to,
    own_v, c_in, y_out, y_in, low,
    send_sems, local_sems, c_sems, y_sems, group_sems, up_sems, down_sems,
):
    del up_held, down_held
    me = Place(shape)
    inner, outer = shape
    share = up_to.shape[3] // outer
    rows = tokens.shape[0]
    sends = Sends(send_sems)
    load = pltpu.make_async_copy(own, own_v, local_sems.at[0])
    load.start()
    me.greet()
    order = [(me.y + i) % outer for i in list(range(1, outer)) + [0]]
    for at in order:
        sends.start(True, sent.at[at], c_in.at[at], c_sems.at[at], me.at_c)

    def columns(held, x_at, i):
        return held.at[:, x_at, :, i * share : (i + 1) * share]

    for j in range(1, inner):
        for i in range(outer):
            place = columns(up_to, me.x, i)
            sends.start(True, place, place, up_sems.at[j - 1, i], me.at_x(j))
    load.wait()
    for i, at in enumerate(order):
        arrived(c_in.at[at], c_sems.at[at], me.at_c)
        if i < outer - 1:
            each_rows(rows, 16, lambda r, i=i, at=at: y_out.__setitem__(
                (i, r), (own_v[at, r] + c_in[at, r]).astype(BF16)))
            sends.start(True, y_out.at[i], y_in.at[i], y_sems.at[i], me.at_y(i + 1))
    for i in range(outer - 1):
        arrived(y_in.at[i], y_sems.at[i], me.at_c)
    for i in range(1, outer):
        for j in range(inner):
            x_at = (me.x + inner - j) % inner
            sends.start(
                True, columns(down_to, x_at, 0), columns(down_to, x_at, i),
                down_sems.at[i - 1, j], me.at_y(i),
            )

    def work(r):
        total = tokens[r].astype(F32) + own_v[me.y, r] + c_in[me.y, r]
        for i in range(outer - 1):
            total = total + y_in[i, r].astype(F32)
        inverse = lax.rsqrt(jnp.mean(total * total, axis=1, keepdims=True) + EPSILON)
        middle[r] = total
        low[r] = (total * inverse * gain[...]).astype(BF16)

    each_rows(rows, 16, work)
    keep = pltpu.make_async_copy(low, group_to.at[0, 0], local_sems.at[1])
    keep.start()
    group = GroupRows(me, sends, low, group_to, group_sems)
    group.begin()
    for k in range(1, Z):
        group.step(k)
    group.finish()
    for j in range(1, inner):
        for i in range(outer):
            x_at = (me.x + inner - j) % inner
            arrived(columns(up_to, x_at, i), up_sems.at[j - 1, i], me.at_c)
    for i in range(1, outer):
        for j in range(inner):
            x_at = (me.x + inner - j) % inner
            arrived(columns(down_to, x_at, i), down_sems.at[i - 1, j], me.at_c)
    sends.finish()
    keep.wait()


def branch_and_group(sent, own, tokens, gain, up, down):
    inner, outer = sizes()
    rows, width = tokens.shape
    dma = pltpu.SemaphoreType.DMA
    vmem, anywhere = pl.BlockSpec(memory_space=pltpu.VMEM), pl.BlockSpec(memory_space=pl.ANY)
    return pl.pallas_call(
        functools.partial(branch_kernel, (inner, outer)),
        out_shape=(
            jax.ShapeDtypeStruct((C, Z, rows, width), BF16),
            jax.ShapeDtypeStruct((rows, width), F32),
            jax.ShapeDtypeStruct(up.shape, up.dtype),
            jax.ShapeDtypeStruct(down.shape, down.dtype),
        ),
        in_specs=[anywhere, anywhere, vmem, vmem, anywhere, anywhere],
        out_specs=(anywhere, vmem, anywhere, anywhere),
        input_output_aliases={4: 2, 5: 3},
        scratch_shapes=[
            pltpu.VMEM((outer, rows, width), F32),
            pltpu.VMEM((outer, rows, width), F32),
            pltpu.VMEM((outer - 1, rows, width), BF16),
            pltpu.VMEM((outer - 1, rows, width), BF16),
            pltpu.VMEM((rows, width), BF16),
            dma((2 * outer + 3 + 4 * (Z - 1) + (inner - 1) * outer + inner * (outer - 1),)),
            dma((2,)),
            dma((outer,)),
            dma((outer - 1,)),
            dma((C, Z)),
            dma((inner - 1, outer)),
            dma((outer - 1, inner)),
        ],
        compiler_params=pltpu.CompilerParams(
            collective_id=1, has_side_effects=True, vmem_limit_bytes=40 * 1024 * 1024
        ),
        name="branch_and_group",
    )(sent, own, tokens, gain, up, down)


def line_order():
    order = []
    for k in [n for t in range(1, Z) for n in (t, Z - t)] + [0]:
        if k not in order:
            order.append(k)
    return order


def line_sum(me, sends, rows, term, ready, store, held, up, down, between=None):
    z = me.z

    def add(when, target, slot, k, received=None, came=0):
        def body(r):
            value = term(k, r)
            if received is not None:
                value = value + received[came, r].astype(F32)
            target[slot, r] = value.astype(BF16)

        pl.when(when)(lambda: each_rows(rows, 16, body))

    for t in range(1, Z):
        slot = t - 1
        for k, (out, into, sems), out_slot, has, when, to in (
            (t, up, slot, z > 0, (z <= t - 1) & (z < Z - 1), me.z_up),
            (Z - t, down, Z - 1 - t, z < Z - 1, (z >= Z - t) & (z > 0), me.z_down),
        ):
            pl.when(when)(lambda k=k: ready(k))
            if t == 1:
                add(when, out, out_slot, k)
            else:
                pl.when(when & has)(
                    lambda into=into, sems=sems, slot=slot: arrived(
                        into.at[slot - 1], sems.at[slot - 1], me.at_c
                    )
                )
                add(when & has, out, out_slot, k, into, slot - 1)
                add(when & jnp.logical_not(has), out, out_slot, k)
            sends.start(when, out.at[out_slot], into.at[slot], sems.at[slot], me.at_z(to))
        if between is not None:
            between(t)
    ready(0)
    each_rows(rows, 16, lambda r: store(r, term(0, r)))
    for (_, into, sems), has in ((up, z > 0), (down, z < Z - 1)):

        @pl.when(has)
        def _(into=into, sems=sems):
            arrived(into.at[Z - 2], sems.at[Z - 2], me.at_c)
            each_rows(rows, 16, lambda r: store(r, held(r) + into[Z - 2, r].astype(F32)))


class PlaneTerms:
    def __init__(self, me, sends, parts, target, sems, over_x, blocks):
        self.me, self.sends, self.parts, self.target, self.sems = me, sends, parts, target, sems
        self.over_x, self.blocks = over_x, blocks

    def begin(self):
        me = self.me
        if self.over_x:
            for j in range(1, me.inner):
                for i, part in enumerate(self.parts):
                    self.sends.start(
                        True, part.at[self.blocks, (me.x + j) % me.inner],
                        self.target.at[j - 1, i], self.sems.at[j - 1, i], me.at_x(j),
                    )
        else:
            for i in range(1, me.outer):
                self.sends.start(
                    True, self.parts[i].at[self.blocks], self.target.at[i - 1],
                    self.sems.at[0, i - 1], me.at_y(-i),
                )

    def finish(self):
        me = self.me
        if self.over_x:
            for j in range(1, me.inner):
                for i in range(me.outer):
                    arrived(self.target.at[j - 1, i], self.sems.at[j - 1, i], me.at_c)
        else:
            for i in range(1, me.outer):
                arrived(self.target.at[i - 1], self.sems.at[0, i - 1], me.at_c)


def middle_kernel(shape, *refs):
    outer = shape[1]
    sent, own, middle, grads, gain, feed_sent, feed_own = refs[:7]
    parts = refs[7 : 7 + 3 * outer]
    rows_to, d_middle, gain_grad, block_out = refs[7 + 3 * outer : 11 + 3 * outer]
    targets = refs[11 + 3 * outer : 15 + 3 * outer]
    scratch = refs[15 + 3 * outer :]
    middle_body(
        shape, sent, own, middle, grads, gain, feed_sent, feed_own, parts, targets,
        rows_to, d_middle, gain_grad, block_out, scratch[:9], scratch[9:18], *scratch[18:],
    )


class PairSum:
    def __init__(self, me, sends, sent, own, scratch):
        self.me, self.sends, self.sent = me, sends, sent
        (
            self.held, self.c_in, up_out, up_in, down_out, down_in,
            self.c_sems, up_sems, down_sems,
        ) = scratch
        self.up, self.down = (up_out, up_in, up_sems), (down_out, down_in, down_sems)

    def begin(self):
        for k in line_order():
            self.sends.start(
                True, self.sent.at[k], self.c_in.at[k], self.c_sems.at[k], self.me.at_c
            )

    def run(self):
        def ready(k):
            arrived(self.c_in.at[k], self.c_sems.at[k], self.me.at_c)

        def term(k, r):
            return self.held[k, r] + self.c_in[k, r].astype(F32)

        def store(r, value):
            self.held[0, r] = value

        line_sum(
            self.me, self.sends, self.held.shape[1], term, ready, store,
            lambda r: self.held[0, r], self.up, self.down,
        )


def plane_units(me, sends, parts, targets, sems):
    outer = me.outer
    gate, up, down = (parts[n * outer : (n + 1) * outer] for n in range(3))
    every, low, high = slice(0, Z), slice(0, Z // 2), slice(Z // 2, Z)
    return [
        PlaneTerms(me, sends, gate, targets[0], sems.at[0], True, every),
        PlaneTerms(me, sends, up, targets[1], sems.at[1], False, every),
        PlaneTerms(me, sends, down, targets[2], sems.at[2], True, low),
        PlaneTerms(me, sends, down, targets[3], sems.at[3], False, high),
    ]


def middle_body(
    shape, sent, own, middle, grads, gain, feed_sent, feed_own, parts, targets,
    rows_to, d_middle, gain_grad, block_out, sum_scratch, feed_scratch, low,
    send_sems, local_sems, rows_sems, unit_sems,
):
    me = Place(shape)
    rows = middle.shape[0]
    sends = Sends(send_sems)
    total = PairSum(me, sends, sent, own, sum_scratch)
    feed = PairSum(me, sends, feed_sent, feed_own, feed_scratch)
    load = pltpu.make_async_copy(own, total.held, local_sems.at[0])
    feed_load = pltpu.make_async_copy(feed_own, feed.held, local_sems.at[2])
    load.start()
    me.greet()
    total.begin()
    units = plane_units(me, sends, parts, targets, unit_sems)
    for unit in units:
        unit.begin()
    feed_load.start()
    load.wait()
    total.run()
    own_v = total.held
    gain_grad[...] = jnp.zeros_like(gain_grad)

    def work(r):
        values = middle[r]
        inverse = lax.rsqrt(jnp.mean(values * values, axis=1, keepdims=True) + EPSILON)
        normed = values * inverse
        d_normed = own_v[0, r]
        gain_grad[...] += d_normed * normed
        scaled = d_normed * gain[...]
        passed = inverse * (scaled - normed * jnp.mean(scaled * normed, axis=1, keepdims=True))
        total = grads[r].astype(F32) + passed
        d_middle[r] = total
        low[r] = total.astype(BF16)

    each_rows(rows, 16, work)
    keep = pltpu.make_async_copy(low, rows_to.at[me.w], local_sems.at[1])
    keep.start()
    gather = WtRows(me, sends, low, rows_to, rows_sems)
    gather.begin()
    feed.begin()
    feed_load.wait()
    feed.run()
    each_rows(rows, 16, lambda r: block_out.__setitem__(
        r, (middle[r] + feed.held[0, r]).astype(BF16)))
    gather.step()
    gather.finish()
    for unit in units:
        unit.finish()
    sends.finish()
    keep.wait()


def middle_and_rows(sent, own, middle, grads, gain, feed_sent, feed_own, parts):
    inner, outer = sizes()
    rows, width = middle.shape
    unit_rows, share = parts[0].shape[2:]
    over_x, over_y = (inner - 1, outer), (outer - 1,)
    targets = [
        jax.ShapeDtypeStruct(shape, BF16)
        for shape in (
            (*over_x, Z, unit_rows, share),
            (*over_y, Z, inner, unit_rows, share),
            (*over_x, Z // 2, unit_rows, share),
            (*over_y, Z // 2, inner, unit_rows, share),
        )
    ]
    unit_copies = 2 * (inner - 1) * outer + 2 * (outer - 1)
    pair_scratch = [pltpu.VMEM((Z, rows, width), F32), pltpu.VMEM((Z, rows, width), BF16)]
    pair_scratch += [pltpu.VMEM((Z - 1, rows, width), BF16)] * 4
    dma = pltpu.SemaphoreType.DMA
    pair_scratch += [dma((Z,)), dma((Z - 1,)), dma((Z - 1,))]
    vmem, anywhere = pl.BlockSpec(memory_space=pltpu.VMEM), pl.BlockSpec(memory_space=pl.ANY)
    return pl.pallas_call(
        functools.partial(middle_kernel, (inner, outer)),
        out_shape=(
            jax.ShapeDtypeStruct((outer * C, rows, width), BF16),
            jax.ShapeDtypeStruct((rows, width), F32),
            jax.ShapeDtypeStruct((16, width), F32),
            jax.ShapeDtypeStruct((rows, width), BF16),
            *targets,
        ),
        in_specs=[anywhere, anywhere, vmem, vmem, vmem] + [anywhere] * (2 + 3 * outer),
        out_specs=(anywhere, vmem, vmem, vmem) + (anywhere,) * 4,
        scratch_shapes=pair_scratch * 2
        + [
            pltpu.VMEM((rows, width), BF16),
            dma((2 * (Z + 2 * (Z - 1)) + 2 * outer + unit_copies,)),
            dma((3,)),
            dma((outer * C,)),
            dma((4, inner - 1, outer)),
        ],
        compiler_params=pltpu.CompilerParams(
            collective_id=2, has_side_effects=True, vmem_limit_bytes=56 * 1024 * 1024
        ),
        name="middle_and_rows",
    )(sent, own, middle, grads, gain, feed_sent, feed_own, *parts)


class RowsSum:
    def __init__(self, me, sends, terms, total, scratch, sems):
        self.me, self.sends, self.terms, self.total = me, sends, terms, total
        self.own, self.x_in, *ways = scratch
        self.own_sems, self.x_sems, up_sems, down_sems = sems
        self.up, self.down = (*ways[:2], up_sems), (*ways[2:], down_sems)

    def load(self):
        me = self.me
        self.loads = []
        for k in range(Z):
            self.loads.append(
                pltpu.make_async_copy(
                    self.terms.at[(me.z + Z - k) % Z, me.x], self.own.at[k], self.own_sems.at[k]
                )
            )
            self.loads[k].start()

    def begin(self, turns):
        me = self.me
        for turn in turns:
            if turn == Z - 1:
                k = 0
            else:
                k = (jnp.minimum(me.z, Z - 1 - me.z) + turn) % (Z - 1) + 1
                k = jnp.where(me.z < Z // 2, k, Z - k)
            at = (me.z + Z - k) % Z
            for j in range(1, me.inner):
                self.sends.start(
                    True, self.terms.at[at, (me.x + j) % me.inner], self.x_in.at[j - 1, k],
                    self.x_sems.at[j - 1, k], me.at_x(j),
                )

    def run(self, between=None):
        me = self.me

        def ready(k):
            self.loads[k].wait()
            for j in range(1, me.inner):
                arrived(self.x_in.at[j - 1, k], self.x_sems.at[j - 1, k], me.at_c)

        def term(k, r):
            value = self.own[k, r].astype(F32)
            for j in range(1, me.inner):
                value = value + self.x_in[j - 1, k, r].astype(F32)
            return value

        def store(r, value):
            self.total[r] = value

        line_sum(
            me, self.sends, self.total.shape[0], term, ready, store, lambda r: self.total[r],
            self.up, self.down, between,
        )


class ProductsSum(RowsSum):
    def __init__(self, me, sends, factors, total, scratch, sems):
        self.me, self.sends, self.total = me, sends, total
        self.factors = factors
        self.held, self.x_in, out, up_in, down_in, *self.lefts = scratch
        self.own_sems, self.x_sems, up_sems, down_sems = sems
        self.up, self.down = (out, up_in, up_sems), (out, down_in, down_sems)

    def load(self):
        self.loads = []
        for n, (left, _) in enumerate(self.factors):
            copy = pltpu.make_async_copy(left, self.lefts[n], self.own_sems.at[n])
            copy.start()
            self.loads.append(copy)

    def begin(self, turns):
        me = self.me
        while self.loads:
            self.loads.pop().wait()
        rows, span = self.total.shape[0], self.held.shape[1]
        for turn in turns:
            if turn == Z - 1:
                k = 0
            else:
                k = (jnp.minimum(me.z, Z - 1 - me.z) + turn) % (Z - 1) + 1
                k = jnp.where(me.z < Z // 2, k, Z - k)
            at = (me.z + Z - k) % Z

            def tile(i, carried, k=k, at=at):
                first = 0
                down = pl.ds(pl.multiple_of(i * LANES, LANES), LANES)
                across = pl.ds(pl.multiple_of(at * span + i * LANES, LANES), LANES)
                for n, (_, rights) in enumerate(self.factors):
                    left = self.lefts[n][:, across]
                    for right in rights:
                        columns = slice(first, first + right.shape[1])
                        self.held[k, down, columns] = contract_rows(left, right[...]).astype(BF16)
                        first += right.shape[1]
                return carried

            lax.fori_loop(0, span // LANES, tile, 0)
            for j in range(1, me.inner):
                part = pl.ds(pl.multiple_of((me.x + j) % me.inner * rows, 16), rows)
                self.sends.start(
                    True, self.held.at[k, part], self.x_in.at[j - 1, k], self.x_sems.at[j - 1, k],
                    me.at_x(j),
                )

    def run(self, between=None):
        me = self.me
        rows = self.total.shape[0]

        def ready(k):
            for j in range(1, me.inner):
                arrived(self.x_in.at[j - 1, k], self.x_sems.at[j - 1, k], me.at_c)

        def term(k, r):
            mine = pl.ds(pl.multiple_of(me.x * rows + r.start, 16), r.size)
            value = self.held[k, mine].astype(F32)
            for j in range(1, me.inner):
                value = value + self.x_in[j - 1, k, r].astype(F32)
            return value

        def store(r, value):
            self.total[r] = value

        line_sum(
            me, self.sends, rows, term, ready, store, lambda r: self.total[r],
            self.up, self.down, between,
        )


def sums_kernel(shape, *refs):
    inner, outer = shape
    units, units_y, units_x, normed_rows_one, branch_rows, narrow, sent, own = refs[:8]
    d_x, d_y, mixed, tokens, gain, d_middle, gain_two_grad, vectors = refs[8:16]
    units_to, wide_to, narrow_to, tokens_grad, gains, vectors_to = refs[16:22]
    refs = refs[22:]
    wide_scratch, narrow_scratch = refs[:7], refs[7:13]
    (own_v, c_in, y_out, y_in, all_in, vec_in) = refs[13:19]
    (send_sems, local_sems, c_sems, y_sems, all_sems, vec_sems) = refs[19:25]
    wide_sems, narrow_sems = refs[25:29], refs[29:33]
    units_v, units_y_in, units_x_in, unit_sems, units_y_sems, units_x_sems = refs[33:]
    share = units.shape[3]
    me = Place(shape)
    rows = tokens.shape[0]
    sends = Sends(send_sems)
    load = pltpu.make_async_copy(own, own_v, local_sems.at[0])
    load.start()
    units_load = pltpu.make_async_copy(units, units_v, local_sems.at[1])
    units_load.start()
    me.greet()

    order = [(me.y + i) % outer for i in list(range(1, outer)) + [0]]
    for at in order:
        sends.start(True, sent.at[at], c_in.at[at], c_sems.at[at], me.at_c)
    narrow_sum = RowsSum(me, sends, narrow, narrow_to, narrow_scratch, narrow_sems)
    factors = [(normed_rows_one, [d_x, d_y]), (branch_rows, [mixed])]
    wide_sum = ProductsSum(me, sends, factors, wide_to, wide_scratch, wide_sems)
    narrow_sum.load()
    wide_sum.load()
    narrow_sum.begin(range(Z))

    def columns(n, at):
        return units_to.at[n, :, pl.ds(pl.multiple_of(at * share, LANES), share)]

    low, high, extra = slice(0, Z // 2), slice(Z // 2, Z), slice(Z, Z + Z // 2)
    every = slice(0, Z)

    def units_begin_y():
        for n, blocks in enumerate((every, extra)):
            for i in range(1, outer):
                sends.start(
                    True, units_y.at[i - 1, blocks], units_y_in.at[i - 1, blocks],
                    units_y_sems.at[i - 1, n], me.at_y(-i),
                )

    def units_begin_x():
        for n, blocks in enumerate((every, extra)):
            for j in range(1, inner):
                sends.start(
                    True, units_x.at[j - 1, blocks], units_x_in.at[j - 1, blocks],
                    units_x_sems.at[j - 1, n], me.at_x(j),
                )

    kept = []

    def unit_add(n, blocks, came, came_blocks, sems, count):
        for i in range(count):
            arrived(came.at[i, came_blocks], sems.at[i], me.at_c)

        def body(r):
            for at in range(blocks.stop - blocks.start):
                total = units_v[n, blocks.start + at, r].astype(F32)
                for i in range(count):
                    total = total + came[i, came_blocks.start + at, r].astype(F32)
                units_v[n, blocks.start + at, r] = total.astype(BF16)

        each_rows(units_v.shape[2], 16, body)

    def unit_pass_on(n):
        copy = pltpu.make_async_copy(units_v.at[n, me.z], columns(n, me.z), local_sems.at[2 + n])
        copy.start()
        kept.append(copy)
        for k in range(1, Z):
            to = (me.z + k) % Z
            sends.start(
                True, units_v.at[n, to], columns(n, me.z), unit_sems.at[n, me.z], me.at_z(to)
            )

    def unit_gate():
        unit_add(0, every, units_y_in, every, units_y_sems.at[:, 0], outer - 1)
        unit_pass_on(0)

    def unit_down():
        unit_add(2, low, units_y_in, extra, units_y_sems.at[:, 1], outer - 1)
        unit_add(2, high, units_x_in, extra, units_x_sems.at[:, 1], inner - 1)
        unit_pass_on(2)

    def unit_up():
        unit_add(1, every, units_x_in, every, units_x_sems.at[:, 0], inner - 1)
        unit_pass_on(1)

    def units_finish():
        for n in range(3):
            for k in range(1, Z):
                at = (me.z + Z - k) % Z
                arrived(columns(n, at), unit_sems.at[n, at], me.at_c)
        for copy in kept:
            copy.wait()

    def exchange(held, into, sems, first, devices):
        for n, device in enumerate(devices):
            sends.start(True, held, into.at[first + n], sems.at[first + n], device)

    def gathered(held, into, sems, first, devices):
        for n, _ in enumerate(devices):
            arrived(into.at[first + n], sems.at[first + n], me.at_c)
        total = into[first]
        for n in range(1, len(devices)):
            total = total + into[first + n]
        return held[...] + total

    stages = [
        [me.at_c],
        [me.at_y(i) for i in range(1, outer)],
        [me.at_z((me.z + k) % Z) for k in range(1, Z)],
        [me.at_x(j) for j in range(1, inner)],
    ]
    at_stage = [0]
    for stage in stages:
        at_stage.append(at_stage[-1] + len(stage))

    z_stage, x_stage = stages[2], stages[3]
    exchange(vectors, vec_in, vec_sems, 0, x_stage)
    units_begin_x()

    units_begin_y()

    load.wait()
    for i, at in enumerate(order):
        arrived(c_in.at[at], c_sems.at[at], me.at_c)
        if i < outer - 1:
            each_rows(rows, 16, lambda r, i=i, at=at: y_out.__setitem__(
                (i, r), (own_v[at, r] + c_in[at, r].astype(F32)).astype(BF16)))
            sends.start(True, y_out.at[i], y_in.at[i], y_sems.at[i], me.at_y(i + 1))
    vectors_to[0] = gathered(vectors, vec_in, vec_sems, 0, x_stage)
    exchange(vectors_to.at[0], vec_in, vec_sems, len(x_stage), z_stage)
    narrow_sum.run()
    vectors_to[1] = gathered(vectors_to.at[0], vec_in, vec_sems, len(x_stage), z_stage)
    units_load.wait()
    wide_sum.begin(range(1))
    unit_gate()
    wide_sum.begin(range(1, 2))
    unit_up()
    unit_down()
    wide_sum.begin(range(2, Z))

    def work(r):
        d_normed = own_v[me.y, r] + c_in[me.y, r].astype(F32)
        for i in range(outer - 1):
            d_normed = d_normed + y_in[i, r].astype(F32)
        stream = tokens[r].astype(F32)
        inverse = lax.rsqrt(jnp.mean(stream * stream, axis=1, keepdims=True) + EPSILON)
        normed = stream * inverse
        part = d_normed * normed
        gains[0, 0:8] += part[0:8] + part[8:16]
        scaled = d_normed * gain[...]
        passed = inverse * (scaled - normed * jnp.mean(scaled * normed, axis=1, keepdims=True))
        tokens_grad[r] = (d_middle[r] + passed).astype(BF16)

    def gains_step(n):
        if n > 0:
            gains[n] = gathered(
                gains.at[n - 1], all_in, all_sems, at_stage[n - 1], stages[n - 1]
            )
        if n < len(stages):
            exchange(gains.at[n], all_in, all_sems, at_stage[n], stages[n])

    def between(t):
        if t == 1:
            for i in range(outer - 1):
                arrived(y_in.at[i], y_sems.at[i], me.at_c)
            gains[0] = jnp.zeros_like(gains[0])
            each_rows(rows, 16, work)
            gains[0, 8:16] = gain_two_grad[0:8] + gain_two_grad[8:16]
        gains_step(t - 1)

    wide_sum.run(between)
    for n in range(Z - 1, len(stages) + 1):
        gains_step(n)
    units_finish()
    sends.finish()


def last_sums(
    units, units_y, units_x, normed_one, branch_rows, narrow, sent, own,
    d_x, d_y, mixed, tokens, gain, d_middle, gain_two_grad, vectors,
):
    inner, outer = sizes()
    rows, width = tokens.shape
    dma = pltpu.SemaphoreType.DMA
    vmem, anywhere = pl.BlockSpec(memory_space=pltpu.VMEM), pl.BlockSpec(memory_space=pl.ANY)

    def scratch(terms):
        one = terms.shape[2:]
        return [pltpu.VMEM((Z, *one), BF16), pltpu.VMEM((inner - 1, Z, *one), BF16)] + [
            pltpu.VMEM((Z - 1, *one), BF16)
        ] * 4

    peers = 1 + (outer - 1) + (inner - 1) + (Z - 1)
    copies = 2 * outer - 1 + 2 * (Z * (inner - 1) + 2 * (Z - 1))
    copies += peers + (inner - 1) + (Z - 1) + 2 * (outer - 1) + 2 * (inner - 1) + 3 * (Z - 1)
    _, _, unit_rows, share = units.shape
    block = (unit_rows, d_x.shape[1] + d_y.shape[1] + mixed.shape[1])
    line_sems = [dma((Z,)), dma((inner - 1, Z)), dma((Z - 1,)), dma((Z - 1,))]
    return pl.pallas_call(
        functools.partial(sums_kernel, (inner, outer)),
        out_shape=(
            jax.ShapeDtypeStruct((3, unit_rows, Z * share), BF16),
            jax.ShapeDtypeStruct(block, F32),
            jax.ShapeDtypeStruct(narrow.shape[2:], F32),
            jax.ShapeDtypeStruct((rows, width), BF16),
            jax.ShapeDtypeStruct((5, 16, width), F32),
            jax.ShapeDtypeStruct((2, *vectors.shape), F32),
        ),
        in_specs=[anywhere] * 8 + [vmem] * 8,
        out_specs=(anywhere,) + (vmem,) * 5,
        scratch_shapes=[
            pltpu.VMEM((Z, inner * block[0], block[1]), BF16),
            pltpu.VMEM((inner - 1, Z, *block), BF16),
        ]
        + [pltpu.VMEM((Z - 1, *block), BF16)] * 3
        + [pltpu.VMEM(normed_one.shape, BF16), pltpu.VMEM(branch_rows.shape, BF16)]
        + scratch(narrow)
        + [
            pltpu.VMEM((outer, rows, width), F32),
            pltpu.VMEM((outer, rows, width), BF16),
            pltpu.VMEM((outer - 1, rows, width), BF16),
            pltpu.VMEM((outer - 1, rows, width), BF16),
            pltpu.VMEM((peers, 16, width), F32),
            pltpu.VMEM((inner - 1 + Z - 1, *vectors.shape), F32),
            dma((copies,)),
            dma((5,)),
            dma((outer,)),
            dma((outer - 1,)),
            dma((peers,)),
            dma((inner - 1 + Z - 1,)),
        ]
        + line_sems * 2
        + [
            pltpu.VMEM(units.shape, BF16),
            pltpu.VMEM(units_y.shape, BF16),
            pltpu.VMEM(units_x.shape, BF16),
            dma((3, Z)),
            dma((outer - 1, 2)),
            dma((inner - 1, 2)),
        ],
        compiler_params=pltpu.CompilerParams(
            collective_id=5, has_side_effects=True, vmem_limit_bytes=60 * 1024 * 1024
        ),
        name="last_sums",
    )(
        units, units_y, units_x, normed_one, branch_rows, narrow, sent, own,
        d_x, d_y, mixed, tokens, gain, d_middle, gain_two_grad, vectors,
    )


def scan_kernel(backward, factors, inflows, states, entered, products, ends, ends_in, carry, send_sems, arrivals):
    seq = ends_in.shape[0]
    s = lax.axis_index("seq")
    rows, width = factors.shape
    barrier = pltpu.get_barrier_semaphore()

    def device(at):
        return {"seq": at, "wt": lax.axis_index("wt")}

    def greet(i, carried):
        @pl.when(i != s)
        def _():
            pl.semaphore_signal(barrier, inc=1, device_id=device(i), device_id_type=MESH)

        return carried

    lax.fori_loop(0, seq, greet, 0)
    group = 8
    at_row = lax.broadcasted_iota(jnp.int32, (group, width), 0)

    def step(i, carried):
        held, product = carried
        i = rows // group - 1 - i if backward else i
        where = pl.ds(pl.multiple_of(i * group, group), group)
        factor, inflow = factors[where, :], inflows[where, :]
        for by in (1, 2, 4):
            inside = at_row < group - by if backward else at_row >= by
            turn = group - by if backward else by
            inflow = factor * jnp.where(inside, pltpu.roll(inflow, turn, 0), 0.0) + inflow
            factor = factor * jnp.where(inside, pltpu.roll(factor, turn, 0), 1.0)
        inflow = inflow + factor * held
        factor = factor * product
        states[where, :] = inflow
        products[where, :] = factor
        last = slice(0, 1) if backward else slice(group - 1, group)
        return inflow[last], factor[last]

    held, product = lax.fori_loop(
        0, rows // group, step, (jnp.zeros((1, width), F32), jnp.ones((1, width), F32))
    )
    ends[0:1] = product
    ends[1:2] = held
    pl.semaphore_wait(barrier, seq - 1)

    def copy_to(i):
        return pltpu.make_async_remote_copy(
            src_ref=ends, dst_ref=ends_in.at[s], send_sem=send_sems.at[i], recv_sem=arrivals.at[s],
            device_id=device(i), device_id_type=MESH,
        )

    def later(i):
        return i < s if backward else i > s

    def send(i, carried):
        pl.when(later(i))(lambda: copy_to(i).start())
        return carried

    lax.fori_loop(0, seq, send, 0)
    carry[...] = jnp.zeros_like(carry)

    def receive(n, carried):
        i = seq - 1 - n if backward else n

        @pl.when(jnp.logical_not(later(i)) & (i != s))
        def _():
            arrived(ends_in.at[i], arrivals.at[i], device((s + 1) % seq))
            carry[0:1] = ends_in[i, 0:1] * carry[0:1] + ends_in[i, 1:2]

        return carried

    lax.fori_loop(0, seq, receive, 0)
    entering = carry[0:1]
    entered[...] = entering

    def spread(i, carried):
        where = pl.ds(pl.multiple_of(i * group, group), group)
        states[where, :] += products[where, :] * entering
        return carried

    lax.fori_loop(0, rows // group, spread, 0)

    def sent(i, carried):
        pl.when(later(i))(lambda: copy_to(i).wait_send())
        return carried

    lax.fori_loop(0, seq, sent, 0)


def full_scan(factor, inflow, backward):
    seq = lax.axis_size("seq")
    rows, width = factor.shape
    vmem = pl.BlockSpec(memory_space=pltpu.VMEM)
    return pl.pallas_call(
        functools.partial(scan_kernel, backward),
        out_shape=(
            jax.ShapeDtypeStruct((rows, width), F32),
            jax.ShapeDtypeStruct((1, width), F32),
        ),
        in_specs=[vmem, vmem],
        out_specs=(vmem, vmem),
        scratch_shapes=[
            pltpu.VMEM((rows, width), F32),
            pltpu.VMEM((8, width), F32),
            pltpu.VMEM((seq, 8, width), F32),
            pltpu.VMEM((8, width), F32),
            pltpu.SemaphoreType.DMA((seq,)),
            pltpu.SemaphoreType.DMA((seq,)),
        ],
        compiler_params=pltpu.CompilerParams(
            collective_id=4 if backward else 3,
            has_side_effects=True,
            vmem_limit_bytes=32 * 1024 * 1024,
        ),
        name="scan_back" if backward else "scan_ahead",
    )(factor, inflow)


def recurrence_terms(decay_pre, input_pre, decay_log, conv_float):
    log_decay = -DECAY_SCALE * jax.nn.softplus(-decay_log) * jax.nn.sigmoid(decay_pre)
    return (
        jnp.exp(log_decay),
        jnp.sqrt(-jnp.expm1(2.0 * log_decay)) * jax.nn.sigmoid(input_pre) * conv_float,
    )


def normed_rows(stream):
    inverse = lax.rsqrt(jnp.mean(stream * stream, axis=1, keepdims=True) + EPSILON)
    return stream * inverse, inverse


def per_device(
    tokens,
    norm1_gain,
    x_weight,
    y_weight,
    conv_weight,
    conv_bias,
    decay_gate_weight,
    decay_bias,
    input_gate_weight,
    input_bias,
    decay_param,
    out_weight,
    norm2_gain,
    gate_weight,
    up_weight,
    down_weight,
    out_grad,
):
    seq, wt = lax.axis_size("seq"), lax.axis_size("wt")
    inner, outer = sizes()
    z, x, y, c = places()
    w = lax.axis_index("wt")
    rows_dev, width = tokens.shape
    weight_rows, lru_cols = x_weight.shape
    chunk, block = decay_gate_weight.shape
    half = block // 2
    full = lru_cols - half
    taps_count = conv_weight.shape[1]
    reach = taps_count - 1
    hidden_cols = gate_weight.shape[1]

    def turned(value, axis):
        return jnp.where(c == 0, value, jnp.roll(value, -half, axis))

    def turned_back(value, axis):
        return jnp.where(c == 0, value, jnp.roll(value, half, axis))

    def in_order(own, partner, axis):
        return jnp.where(
            c == 0,
            jnp.concatenate([own, partner], axis),
            jnp.concatenate([partner, own], axis),
        )

    vectors = jnp.stack(
        [v.astype(F32) for v in (norm1_gain, norm2_gain, conv_bias, decay_bias, input_bias)]
        + [decay_param]
        + [conv_weight[:, k].astype(F32) for k in range(taps_count)]
    )
    vectors = jnp.pad(vectors, ((0, -vectors.shape[0] % 8), (0, -chunk % LANES)))

    across = [(i, i % seq * wt + i // seq) for i in range(seq * wt)]
    gates = jnp.concatenate([decay_gate_weight, input_gate_weight], axis=1)

    def padded(weight):
        share = -(-hidden_cols // (Z * LANES)) * LANES
        return jnp.pad(weight, ((0, 0), (0, Z * share - hidden_cols)))

    xy_unit = jnp.concatenate([turned(x_weight, 1), turned(y_weight, 1)], axis=1)
    (
        group_tokens, grad_group, vectors, gate_all, xy_kernel, out_kernel,
        gate_kernel, up_kernel, down_kernel,
    ) = gather_all(
        tokens, out_grad, vectors, gates, xy_unit, turned(out_weight, 1),
        padded(gate_weight), padded(up_weight), padded(down_weight),
    )
    group_tokens = group_tokens.reshape(-1, width)
    grad_group = grad_group.reshape(-1, width)
    vectors = jnp.moveaxis(vectors[:, : 6 + taps_count, :chunk], 0, 1).reshape(6 + taps_count, -1)
    gain_one, gain_two = vectors[0], vectors[1]
    own_vectors = turned(
        lax.dynamic_slice(vectors[2:], (0, w * lru_cols), (taps_count + 4, lru_cols)), 1
    )
    tap_bias, decay_shift, input_shift, decay_log = (own_vectors[i] for i in range(4))
    taps = own_vectors[4:]
    xy_kernel = xy_kernel.reshape(width, -1)
    out_kernel = out_kernel.reshape(width, -1)
    gate_kernel = gate_kernel.reshape(width, -1)
    gate_all = turned(gate_all.reshape(lru_cols, 2 * block), 0)
    partner_rows = c_swap(gate_all[full:])
    shared_rows = in_order(gate_all[full:], partner_rows, 0)

    stream = tokens.astype(F32)
    group_normed, _ = normed_rows(group_tokens.astype(F32))
    group_one = (group_normed * gain_one).astype(BF16)
    rows = group_one.shape[0]
    xy = multiply(group_one, xy_kernel)
    x_branch = xy[:, :lru_cols].astype(BF16)
    y_before = xy[:, lru_cols:]
    y_gated, gelu_y_back = jax.vjp(gelu_tanh, y_before)
    rim = lax.ppermute(x_branch[rows - reach :], "seq", [(i, i + 1) for i in range(seq - 1)])
    extended = jnp.concatenate([rim, x_branch], axis=0).astype(F32)
    conv_low = (
        tap_bias
        + sum(taps[k] * extended[reach - k : reach - k + rows] for k in range(taps_count))
    ).astype(BF16)
    shared_conv = in_order(conv_low[:, full:], c_swap(conv_low[:, full:]), 1)
    heads = full // block

    def of_head(value, i):
        return value[:, i * block : (i + 1) * block]

    pre_parts = [
        multiply(of_head(conv_low, i), gate_all[i * block : (i + 1) * block]) for i in range(heads)
    ]
    shared_columns = jnp.where(
        c == 0,
        jnp.concatenate([shared_rows[:, :half], shared_rows[:, block : block + half]], axis=1),
        jnp.concatenate([shared_rows[:, half:block], shared_rows[:, block + half :]], axis=1),
    )
    shared_pre = multiply(shared_conv, shared_columns)
    decay_pre = decay_shift + jnp.concatenate(
        [part[:, :block] for part in pre_parts] + [shared_pre[:, :half]], axis=1
    )
    input_pre = input_shift + jnp.concatenate(
        [part[:, block:] for part in pre_parts] + [shared_pre[:, half:]], axis=1
    )
    (retain, inflow), terms_back = jax.vjp(
        recurrence_terms, decay_pre, input_pre, decay_log, conv_low.astype(F32)
    )
    states, state_in = full_scan(retain, inflow, False)
    before = jnp.concatenate([state_in, states[:-1]])
    lru_low = states.astype(BF16).astype(F32)
    mixed_rows = (lru_low * y_gated).astype(BF16)
    mixed_parts = mixed_rows.reshape(outer, C, rows_dev, lru_cols)

    def branch_of(at):
        part = pick(mixed_parts, at, 1).reshape(outer * rows_dev, lru_cols)
        return contract_last(part, out_kernel).reshape(outer, rows_dev, width)

    group_two, middle, up_kernel, down_kernel = branch_and_group(
        branch_of(1 - c), branch_of(c), tokens, gain_two[None], up_kernel, down_kernel
    )
    up_kernel = up_kernel.reshape(width, -1)
    down_kernel = down_kernel.reshape(width, -1)
    group_two = group_two.reshape(C * Z * rows_dev, width)

    gate_pre = multiply(group_two, gate_kernel)
    up_pre = multiply(group_two, up_kernel)
    active, gelu_gate_back = jax.vjp(gelu_tanh, gate_pre)
    hidden = (active * up_pre).astype(BF16)

    d_hidden = multiply(grad_group, down_kernel)
    d_up = (d_hidden * active).astype(BF16)
    d_gate = gelu_gate_back(d_hidden * up_pre)[0].astype(BF16)
    half_rows = Z * rows_dev

    def d_normed_of(part):
        total = contract_last(d_gate[part], gate_kernel) + contract_last(d_up[part], up_kernel)
        return total.reshape(Z, rows_dev, width)

    def terms_of(left_side, right_side):
        share = right_side.shape[1] // outer
        return [
            contract_rows(left_side, right_side[:, i * share : (i + 1) * share])
            .astype(BF16)
            .reshape(Z, inner, weight_rows, share)
            for i in range(outer)
        ]

    gate_terms = terms_of(group_two, d_gate)
    up_terms = terms_of(group_two, d_up)
    down_terms = terms_of(grad_group, hidden)
    def feed_of(part):
        return contract_last(hidden[part], down_kernel).reshape(Z, rows_dev, width)

    branch_rows, d_middle, gain_two_grad, block_out, *came = middle_and_rows(
        d_normed_of(slice(half_rows, None)).astype(BF16),
        d_normed_of(slice(0, half_rows)),
        middle,
        out_grad,
        gain_two[None],
        feed_of(slice(half_rows, None)).astype(BF16),
        feed_of(slice(0, half_rows)),
        gate_terms + up_terms + down_terms,
    )
    branch_rows = branch_rows.reshape(-1, width)

    def added_over_x(terms, moved):
        return [
            sum((moved[j - 1, i].astype(F32) for j in range(1, inner)), pick(term, x, 1).astype(F32))
            for i, term in enumerate(terms)
        ]

    def added_over_y(term, moved):
        return sum((moved[i - 1].astype(F32) for i in range(1, outer)), term.astype(F32))

    half_z = Z // 2
    gate_x = added_over_x(gate_terms, came[0])
    up_y = added_over_y(up_terms[0], came[1])
    down_x = added_over_x([term[:half_z] for term in down_terms], came[2])
    down_y = added_over_y(down_terms[0][half_z:], came[3])
    all_y = jnp.concatenate([up_y, down_y])
    kept_x = pick(all_y, x, 1)
    units = jnp.concatenate([gate_x[0], kept_x[:Z], down_x[0], kept_x[Z:]]).astype(BF16)
    units = units.reshape(3, Z, weight_rows, -1)
    units_y = jnp.stack(
        [jnp.concatenate([gate_x[i], down_x[i]]).astype(BF16) for i in range(1, outer)]
    )
    units_x = jnp.stack(
        [pick(all_y, (x + j) % inner, 1).astype(BF16) for j in range(1, inner)]
    )

    d_mixed = multiply(branch_rows, out_kernel)
    d_lru = (d_mixed * y_gated).astype(BF16).astype(F32)
    d_y = gelu_y_back(d_mixed * lru_low)[0].astype(BF16)
    passed, passed_in = full_scan(retain, retain * d_lru, True)
    d_total = d_lru + jnp.concatenate([passed[1:], passed_in])
    d_decay_pre, d_input_pre, decay_log_grad, d_conv_direct = terms_back(
        (d_total * before, d_total)
    )
    d_decay_low, d_input_low = d_decay_pre.astype(BF16), d_input_pre.astype(BF16)
    own_low = jnp.concatenate([d_decay_low[:, full:], d_input_low[:, full:]], axis=1)
    partner_low = c_swap(own_low)
    shared_low = jnp.concatenate(
        [
            in_order(own_low[:, :half], partner_low[:, :half], 1),
            in_order(own_low[:, half:], partner_low[:, half:], 1),
        ],
        axis=1,
    )
    lows = [
        jnp.concatenate([of_head(d_decay_low, i), of_head(d_input_low, i)], axis=1)
        for i in range(heads)
    ]
    d_conv = d_conv_direct + jnp.concatenate(
        [contract_last(lows[i], gate_all[i * block : (i + 1) * block]) for i in range(heads)]
        + [contract_last(shared_low, gate_all[full:])],
        axis=1,
    )
    gates_grad = jnp.concatenate(
        [contract_rows(of_head(conv_low, i), lows[i]) for i in range(heads)]
        + [contract_rows(conv_low[:, full:], shared_low)]
    )
    ahead = lax.ppermute(d_conv[:reach], "seq", [(i + 1, i) for i in range(seq - 1)])
    d_extended = jnp.concatenate([d_conv, ahead], axis=0)
    d_x_branch = sum(taps[k] * d_extended[k : k + rows] for k in range(taps_count)).astype(BF16)
    dx_parts = d_x_branch.reshape(outer, C, rows_dev, lru_cols)
    dy_parts = d_y.reshape(outer, C, rows_dev, lru_cols)

    def d_normed_one_of(at):
        dx, dy = (
            pick(parts, at, 1).reshape(outer * rows_dev, lru_cols) for parts in (dx_parts, dy_parts)
        )
        total = contract_last(dx, xy_kernel[:, :lru_cols]) + contract_last(
            dy, xy_kernel[:, lru_cols:]
        )
        return total.reshape(outer, rows_dev, width)

    narrow = turned_back(gates_grad, 0).astype(BF16).reshape(Z, inner, chunk, 2 * block)
    narrow = jnp.pad(narrow, ((0, 0), (0, 0), (0, -chunk % 16), (0, 0)))
    own_sums = jnp.stack(
        [jnp.sum(d_conv, axis=0), jnp.sum(d_decay_pre, axis=0), jnp.sum(d_input_pre, axis=0)]
        + [decay_log_grad]
        + [jnp.sum(d_conv * extended[reach - k : reach - k + rows], axis=0) for k in range(taps_count)],
    )
    own_sums = turned_back(own_sums, 1)
    placed, wide, narrow, tokens_grad, gains, own_sums = last_sums(
        units, units_y, units_x, group_one, branch_rows, narrow,
        d_normed_one_of(1 - c).astype(BF16), d_normed_one_of(c),
        turned_back(d_x_branch, 1), turned_back(d_y, 1), turned_back(mixed_rows, 1),
        tokens, gain_one[None], d_middle, gain_two_grad, own_sums,
    )
    weight_grads = [wide[:, n * lru_cols : (n + 1) * lru_cols] for n in range(3)]
    gate_grad, up_grad, down_grad = (placed[n, :, :hidden_cols].astype(F32) for n in range(3))
    gains = gains[4].reshape(2, 8, width).sum(axis=1)
    gains = lax.dynamic_slice(gains, (0, (lax.axis_index("seq") * wt + w) * chunk), (2, chunk))
    sums = lax.dynamic_slice(own_sums[1], (0, lax.axis_index("seq") * chunk), (taps_count + 4, chunk))
    own_sums = jnp.concatenate([narrow[:chunk], sums.T], axis=1)
    own_sums = lax.ppermute(own_sums, ("seq", "wt"), [(to, at) for at, to in across])
    sums = own_sums[:, 2 * block :]
    return (
        block_out,
        tokens_grad,
        gains[0],
        weight_grads[0],
        weight_grads[1],
        sums[:, 4:],
        sums[:, 0],
        own_sums[:, :block],
        sums[:, 1],
        own_sums[:, block : 2 * block],
        sums[:, 2],
        sums[:, 3],
        weight_grads[2],
        gains[1],
        gate_grad,
        up_grad,
        down_grad,
    )


def solution(mesh):
    rows, both, lone = P(("seq", "wt"), None), P("seq", "wt"), P(("seq", "wt"))
    in_specs = (
        rows, lone, both, both, rows, lone, rows, lone, rows, lone, lone,
        both, lone, both, both, both, rows,
    )
    out_specs = (
        rows, rows, lone, both, both, rows, lone, rows, lone, rows, lone, lone,
        both, lone, both, both, both,
    )
    return jax.shard_map(
        per_device, mesh=mesh, in_specs=in_specs, out_specs=out_specs, check_vma=False
    )
```

```python
import functools

import jax
import jax.numpy as jnp
from jax import lax
from jax.experimental import pallas as pl
from jax.experimental.pallas import tpu as pltpu
from jax.sharding import PartitionSpec as P

EPSILON = 1e-06
DECAY_SCALE = 8.0
Z = 4
C = 2
LANES = 128
F32 = jnp.float32
BF16 = jnp.bfloat16
MESH = pl.DeviceIdType.MESH


def gelu_tanh(values):
    return jax.nn.gelu(values, approximate=True)


def sizes():
    return lax.axis_size("seq") // Z, lax.axis_size("wt") // C


def places():
    inner, outer = sizes()
    s, w = lax.axis_index("seq"), lax.axis_index("wt")
    return s // inner, s % inner, w // C, w % C


def z_move(value, by, senders):
    inner, _ = sizes()
    pairs = [(z * inner + x, (z + by) % Z * inner + x) for z in senders for x in range(inner)]
    return lax.ppermute(value, "seq", pairs)


def c_swap(value):
    _, outer = sizes()
    pairs = [(y * C + c, y * C + 1 - c) for y in range(outer) for c in range(C)]
    return lax.ppermute(value, "wt", pairs)


def line_scatter(parts):
    up = down = None
    for step in range(1, Z):
        rising = parts[step] if up is None else parts[step] + up
        falling = parts[Z - step] if down is None else parts[Z - step] + down
        up = z_move(rising.astype(BF16), 1, range(0, step)).astype(F32)
        down = z_move(falling.astype(BF16), -1, range(Z - step, Z)).astype(F32)
    return parts[0] + up + down


def pick(value, index, axis):
    return lax.dynamic_index_in_dim(value, index, axis, keepdims=False)


def contract_last(left_side, right_side):
    return lax.dot_general(
        left_side, right_side, (((1,), (1,)), ((), ())), preferred_element_type=F32
    )


def contract_rows(left_side, right_side):
    return lax.dot_general(
        left_side, right_side, (((0,), (0,)), ((), ())), preferred_element_type=F32
    )


def multiply(left_side, right_side):
    return jnp.dot(left_side, right_side, preferred_element_type=F32)


class Sends:
    def __init__(self, sems):
        self.sems, self.started = sems, []

    def start(self, when, source, target, arrival, device):
        copy = pltpu.make_async_remote_copy(
            src_ref=source,
            dst_ref=target,
            send_sem=self.sems.at[len(self.started)],
            recv_sem=arrival,
            device_id=device,
            device_id_type=MESH,
        )
        if when is True:
            copy.start()
        else:
            pl.when(when)(copy.start)
        self.started.append((when, copy))

    def finish(self):
        for when, copy in self.started:
            if when is True:
                copy.wait_send()
            else:
                pl.when(when)(copy.wait_send)


def arrived(target, arrival, device):
    pltpu.make_async_remote_copy(
        src_ref=target, dst_ref=target, send_sem=arrival, recv_sem=arrival,
        device_id=device, device_id_type=MESH,
    ).wait_recv()


def gather_kernel(shape, *refs):
    inner, outer = shape
    (tokens, grads, vectors, gates, xy, out, gate, up, down) = refs[:9]
    (tokens_to, grads_to, vectors_to, gates_to, xy_to, out_to, gate_to, up_to, down_to) = refs[9:18]
    gates_own, send_sems, local_sems, line_sems, plane_sems, rows_sems = refs[18:24]
    vector_sems, turn_sems, group_sems = refs[24:]
    seq, wt = Z * inner, outer * C
    s, w = lax.axis_index("seq"), lax.axis_index("wt")
    z, x, y, c = s // inner, s % inner, w // C, w % C
    sends = Sends(send_sems)
    group = GroupRows(Place(shape), sends, grads, grads_to, group_sems)
    here = []

    def at_z(to):
        return {"seq": to * inner + x, "wt": w}

    def at_x(by):
        return {"seq": z * inner + (x + by) % inner, "wt": w}

    def at_y(by):
        return {"seq": s, "wt": (y + by) % outer * C + c}

    at_c = {"seq": s, "wt": y * C + 1 - c}

    def keep(source, target, waited=False):
        copy = pltpu.make_async_copy(source, target, local_sems.at[len(here)])
        copy.start()
        here.append((waited, copy))
        return copy

    barrier = pltpu.get_barrier_semaphore()

    def greet(i, carried):
        @pl.when(i != s * wt + w)
        def _():
            pl.semaphore_signal(
                barrier, inc=1, device_id={"seq": i // wt, "wt": i % wt}, device_id_type=MESH
            )

        return carried

    lax.fori_loop(0, seq * wt, greet, 0)
    pl.semaphore_wait(barrier, seq * wt - 1)

    class Line:
        def __init__(self, index, source, target):
            self.source, self.target = source, target
            self.sems = line_sems.at[index]

        def forward(self, block, at, up_when, down_when):
            place = self.target.at[at, x]
            arrival = self.sems.at[at, x]
            sends.start(up_when, block, place, arrival, at_z(jnp.minimum(z + 1, Z - 1)))
            sends.start(down_when, block, place, arrival, at_z(jnp.maximum(z - 1, 0)))
            return place, arrival

        def across(self, when, block, at):
            for j in range(1, inner):
                sends.start(when, block, self.target.at[at, x], self.sems.at[at, x], at_x(j))

        def begin_z(self):
            keep(self.source, self.target.at[z, x])
            self.forward(self.source, z, z < Z - 1, z > 0)

        def begin_x(self):
            self.across(True, self.source, z)

        def begin(self):
            self.begin_z()
            self.begin_x()

        def step(self, k):
            for at, there, up_when, down_when in (
                (jnp.maximum(z - k, 0), z - k >= 0, (z - k >= 0) & (z < Z - 1), None),
                (jnp.minimum(z + k, Z - 1), z + k < Z, None, (z + k < Z) & (z > 0)),
            ):
                place, arrival = self.target.at[at, x], self.sems.at[at, x]

                @pl.when(there)
                def _(place=place, arrival=arrival):
                    arrived(place, arrival, at_c)

                if up_when is not None:
                    sends.start(up_when, place, place, arrival, at_z(jnp.minimum(z + 1, Z - 1)))
                else:
                    sends.start(down_when, place, place, arrival, at_z(jnp.maximum(z - 1, 0)))
                self.across(there, place, at)

        def finish(self):
            for at in range(Z):
                for j in range(1, inner):
                    from_x = (x + inner - j) % inner
                    arrived(self.target.at[at, from_x], self.sems.at[at, from_x], at_c)

    class Plane:
        def __init__(self, index, source, target, x_first, whole):
            self.source, self.target, self.x_first, self.whole = source, target, x_first, whole
            self.share = source.shape[1] // Z
            self.sems = plane_sems.at[index]

        def cut(self, at):
            return self.source.at[:, pl.ds(pl.multiple_of(at * self.share, LANES), self.share)]

        def place(self, at, x_at, i):
            return self.target.at[at, x_at, :, i * self.share : (i + 1) * self.share]

        def begin(self):
            self.own = keep(self.cut(z), self.place(z, x, 0), True)
            for k in range(1, Z):
                to = (z + k) % Z
                sends.start(True, self.cut(to), self.place(z, x, 0), self.sems.at[z, 0, 0], at_z(to))

        def over_x(self, at, i):
            place = self.place(at, x, i)
            for j in range(1, inner):
                sends.start(True, place, place, self.sems.at[at, j, i], at_x(j))

        def over_y(self, at, j):
            x_at = (x + inner - j) % inner
            for i in range(1, outer):
                sends.start(
                    True, self.place(at, x_at, 0), self.place(at, x_at, i),
                    self.sems.at[at, j, i], at_y(i),
                )

        def got(self, at, j, i):
            arrived(self.place(at, (x + inner - j) % inner, i), self.sems.at[at, j, i], at_c)

        def first(self, k):
            at = (z + Z - k) % Z
            if k == 0:
                self.own.wait()
            else:
                self.got(at, 0, 0)
            if self.x_first or self.whole:
                self.over_x(at, 0)
            if self.whole or not self.x_first:
                self.over_y(at, 0)

        def second(self, k):
            at = (z + Z - k) % Z
            if self.x_first:
                for j in range(1, inner):
                    self.got(at, j, 0)
                    if self.whole:
                        self.over_y(at, j)
            else:
                for i in range(1, outer):
                    self.got(at, 0, i)

        def finish(self, k):
            if self.whole:
                at = (z + Z - k) % Z
                for j in range(inner):
                    for i in range(1, outer):
                        self.got(at, j, i)

    lines = [Line(0, xy, xy_to), Line(1, gates_own, gates_to), Line(2, out, out_to)]
    planes = [
        Plane(0, gate, gate_to, True, True),
        Plane(1, up, up_to, False, False),
        Plane(2, down, down_to, True, False),
    ]

    me = s * wt + w
    keep(vectors, vectors_to.at[me])

    def vector_copy(i):
        return pltpu.make_async_remote_copy(
            src_ref=vectors, dst_ref=vectors_to.at[me],
            send_sem=vector_sems.at[0, i], recv_sem=vector_sems.at[1, me],
            device_id={"seq": i // wt, "wt": i % wt}, device_id_type=MESH,
        )

    def vector_send(i, carried):
        pl.when(i != me)(lambda: vector_copy(i).start())
        return carried

    def tokens_begin():
        keep(tokens, tokens_to.at[w])
        sends.start(True, tokens, tokens_to.at[w], rows_sems.at[w], at_c)
        for i in range(1, outer):
            sends.start(True, tokens, tokens_to.at[w], rows_sems.at[w], at_y(i))

    def tokens_step():
        for i in range(1, outer):
            at = (y + outer - i) % outer * C + c
            arrived(tokens_to.at[at], rows_sems.at[at], at_c)
            sends.start(True, tokens_to.at[at], tokens_to.at[at], rows_sems.at[at], at_c)

    def tokens_finish():
        for i in range(outer):
            at = (y + outer - i) % outer * C + 1 - c
            arrived(tokens_to.at[at], rows_sems.at[at], at_c)

    to_seq, to_wt = me % seq, me // seq
    from_me = w * seq + s
    turn = pltpu.make_async_remote_copy(
        src_ref=gates, dst_ref=gates_own, send_sem=turn_sems.at[0], recv_sem=turn_sems.at[1],
        device_id={"seq": to_seq, "wt": to_wt}, device_id_type=MESH,
    )
    stay = pltpu.make_async_copy(gates, gates_own, turn_sems.at[2])
    here_too = from_me == me

    pl.when(jnp.logical_not(here_too))(turn.start)
    pl.when(here_too)(stay.start)
    lines[0].begin()
    tokens_begin()

    @pl.when(jnp.logical_not(here_too))
    def _():
        arrived(gates_own, turn_sems.at[1], at_c)

    pl.when(here_too)(stay.wait)
    lines[1].begin()
    lines[2].begin_z()
    lax.fori_loop(0, seq * wt, vector_send, 0)
    for k in range(1, Z):
        lines[1].step(k)
        lines[0].step(k)
        if k == 1:
            tokens_step()
    lines[2].begin_x()
    for k in range(1, Z):
        lines[2].step(k)
        if k == Z - 2:
            planes[0].begin()
            planes[2].begin()
            planes[1].begin()
    for k in range(Z):
        planes[0].first(k)
    for k in range(Z):
        planes[2].first(k)
    keep(grads, group.place(0, z, z))
    group.begin()
    for k in range(Z):
        planes[1].first(k)
        planes[0].second(k)
    for k in range(1, Z):
        group.step(k)
    group.finish()

    for line in lines:
        line.finish()
    tokens_finish()
    for k in range(Z):
        planes[1].second(k)
        planes[2].second(k)
        planes[0].finish(k)

    def vector_wait(i, carried):
        @pl.when(i != me)
        def _():
            vector_copy(i).wait_send()
            arrived(vectors_to.at[i], vector_sems.at[1, i], at_c)

        return carried

    pl.when(jnp.logical_not(here_too))(turn.wait_send)
    lax.fori_loop(0, seq * wt, vector_wait, 0)
    sends.finish()
    for waited, copy in here:
        if not waited:
            copy.wait()


def gather_all(tokens, grads, vectors, gates, xy, out, gate, up, down):
    inner, outer = sizes()
    seq, wt = Z * inner, outer * C

    def buffer(*shape, like):
        return jax.ShapeDtypeStruct(shape, like.dtype)

    def plane(weight):
        rows, columns = weight.shape
        return buffer(Z, inner, rows, outer * columns // Z, like=weight)

    shapes = (
        buffer(wt, *tokens.shape, like=tokens),
        buffer(C, Z, *grads.shape, like=grads),
        buffer(seq * wt, *vectors.shape, like=vectors),
        buffer(Z, inner, *gates.shape, like=gates),
        buffer(Z, inner, *xy.shape, like=xy),
        buffer(Z, inner, *out.shape, like=out),
        plane(gate),
        plane(up),
        plane(down),
    )
    copies = 3 * (2 + inner + (Z - 1) * 2 * inner) + 3 * (Z - 1 + Z * (inner + 2 * outer + inner * outer))
    copies += 2 * outer + 3 + 4 * Z
    dma = pltpu.SemaphoreType.DMA
    return pl.pallas_call(
        functools.partial(gather_kernel, (inner, outer)),
        out_shape=shapes,
        in_specs=[pl.BlockSpec(memory_space=pl.ANY)] * 9,
        out_specs=[pl.BlockSpec(memory_space=pl.ANY)] * 9,
        scratch_shapes=[
            pltpu.VMEM(gates.shape, gates.dtype),
            dma((copies,)),
            dma((16,)),
            dma((3, Z, inner)),
            dma((3, Z, inner, outer)),
            dma((wt,)),
            dma((2, seq * wt)),
            dma((3,)),
            dma((C, Z)),
        ],
        compiler_params=pltpu.CompilerParams(collective_id=0, has_side_effects=True),
        name="gather_all",
    )(tokens, grads, vectors, gates, xy, out, gate, up, down)


class Place:
    def __init__(self, shape):
        self.inner, self.outer = shape
        self.s, self.w = lax.axis_index("seq"), lax.axis_index("wt")
        self.z, self.x = self.s // self.inner, self.s % self.inner
        self.y, self.c = self.w // C, self.w % C
        self.at_c = {"seq": self.s, "wt": self.y * C + 1 - self.c}
        self.z_up, self.z_down = jnp.minimum(self.z + 1, Z - 1), jnp.maximum(self.z - 1, 0)

    def at_z(self, to):
        return {"seq": to * self.inner + self.x, "wt": self.w}

    def at_x(self, by):
        return {"seq": self.z * self.inner + (self.x + by) % self.inner, "wt": self.w}

    def at_y(self, by):
        return {"seq": self.s, "wt": (self.y + self.outer + by) % self.outer * C + self.c}

    def greet(self):
        barrier = pltpu.get_barrier_semaphore()
        devices = [self.at_c]
        devices += [self.at_z((self.z + k) % Z) for k in range(1, Z)]
        devices += [self.at_x(j) for j in range(1, self.inner)]
        devices += [self.at_y(i) for i in range(1, self.outer)]
        for device in devices:
            pl.semaphore_signal(barrier, inc=1, device_id=device, device_id_type=MESH)
        pl.semaphore_wait(barrier, len(devices))


def each_rows(count, step, body):
    def run(i, carried):
        body(pl.ds(pl.multiple_of(i * step, step), step))
        return carried

    lax.fori_loop(0, count // step, run, 0)


class WtRows:
    def __init__(self, me, sends, source, target, sems):
        self.me, self.sends, self.source, self.target, self.sems = me, sends, source, target, sems

    def begin(self):
        me = self.me
        for device in [me.at_y(i) for i in range(1, me.outer)] + [me.at_c]:
            self.sends.start(True, self.source, self.target.at[me.w], self.sems.at[me.w], device)

    def step(self):
        me = self.me
        for i in range(1, me.outer):
            at = (me.y + me.outer - i) % me.outer * C + me.c
            arrived(self.target.at[at], self.sems.at[at], me.at_c)
            self.sends.start(True, self.target.at[at], self.target.at[at], self.sems.at[at], me.at_c)

    def finish(self):
        me = self.me
        for i in range(me.outer):
            at = (me.y + me.outer - i) % me.outer * C + 1 - me.c
            arrived(self.target.at[at], self.sems.at[at], me.at_c)


class GroupRows:
    def __init__(self, me, sends, source, target, sems):
        self.me, self.sends, self.source, self.target, self.sems = me, sends, source, target, sems

    def place(self, own, at, z_to):
        return self.target.at[own, (z_to - at + Z) % Z]

    def forward(self, at, source, there, way):
        me = self.me
        z_to = me.z_up if way > 0 else me.z_down
        room = me.z < Z - 1 if way > 0 else me.z > 0
        when = room if there is None else there & room
        self.sends.start(
            when, source, self.place(0, at, z_to), self.sems.at[0, at], me.at_z(z_to)
        )

    def begin(self):
        me = self.me
        self.forward(me.z, self.source, None, 1)
        self.forward(me.z, self.source, None, -1)
        self.sends.start(
            True, self.source, self.place(1, me.z, me.z), self.sems.at[1, me.z], me.at_c
        )

    def step(self, k):
        me = self.me
        for at, there, way in (
            (jnp.maximum(me.z - k, 0), me.z - k >= 0, 1),
            (jnp.minimum(me.z + k, Z - 1), me.z + k < Z, -1),
        ):
            place = self.place(0, at, me.z)

            @pl.when(there)
            def _(place=place, at=at):
                arrived(place, self.sems.at[0, at], me.at_c)

            self.forward(at, place, there, way)
            self.sends.start(there, place, self.place(1, at, me.z), self.sems.at[1, at], me.at_c)

    def finish(self):
        me = self.me
        for at in range(Z):
            arrived(self.place(1, at, me.z), self.sems.at[1, at], me.at_c)


def branch_kernel(
    shape, sent, own, tokens, gain, up_held, down_held, group_to, middle, up_to, down_to,
    own_v, c_in, y_out, y_in, low,
    send_sems, local_sems, c_sems, y_sems, group_sems, up_sems, down_sems,
):
    del up_held, down_held
    me = Place(shape)
    inner, outer = shape
    share = up_to.shape[3] // outer
    rows = tokens.shape[0]
    sends = Sends(send_sems)
    load = pltpu.make_async_copy(own, own_v, local_sems.at[0])
    load.start()
    me.greet()
    order = [(me.y + i) % outer for i in list(range(1, outer)) + [0]]
    for at in order:
        sends.start(True, sent.at[at], c_in.at[at], c_sems.at[at], me.at_c)

    def columns(held, x_at, i):
        return held.at[:, x_at, :, i * share : (i + 1) * share]

    for j in range(1, inner):
        for i in range(outer):
            place = columns(up_to, me.x, i)
            sends.start(True, place, place, up_sems.at[j - 1, i], me.at_x(j))
    load.wait()
    for i, at in enumerate(order):
        arrived(c_in.at[at], c_sems.at[at], me.at_c)
        if i < outer - 1:
            each_rows(rows, 16, lambda r, i=i, at=at: y_out.__setitem__(
                (i, r), (own_v[at, r] + c_in[at, r]).astype(BF16)))
            sends.start(True, y_out.at[i], y_in.at[i], y_sems.at[i], me.at_y(i + 1))
    for i in range(outer - 1):
        arrived(y_in.at[i], y_sems.at[i], me.at_c)
    for i in range(1, outer):
        for j in range(inner):
            x_at = (me.x + inner - j) % inner
            sends.start(
                True, columns(down_to, x_at, 0), columns(down_to, x_at, i),
                down_sems.at[i - 1, j], me.at_y(i),
            )

    def work(r):
        total = tokens[r].astype(F32) + own_v[me.y, r] + c_in[me.y, r]
        for i in range(outer - 1):
            total = total + y_in[i, r].astype(F32)
        inverse = lax.rsqrt(jnp.mean(total * total, axis=1, keepdims=True) + EPSILON)
        middle[r] = total
        low[r] = (total * inverse * gain[...]).astype(BF16)

    each_rows(rows, 16, work)
    keep = pltpu.make_async_copy(low, group_to.at[0, 0], local_sems.at[1])
    keep.start()
    group = GroupRows(me, sends, low, group_to, group_sems)
    group.begin()
    for k in range(1, Z):
        group.step(k)
    group.finish()
    for j in range(1, inner):
        for i in range(outer):
            x_at = (me.x + inner - j) % inner
            arrived(columns(up_to, x_at, i), up_sems.at[j - 1, i], me.at_c)
    for i in range(1, outer):
        for j in range(inner):
            x_at = (me.x + inner - j) % inner
            arrived(columns(down_to, x_at, i), down_sems.at[i - 1, j], me.at_c)
    sends.finish()
    keep.wait()


def branch_and_group(sent, own, tokens, gain, up, down):
    inner, outer = sizes()
    rows, width = tokens.shape
    dma = pltpu.SemaphoreType.DMA
    vmem, anywhere = pl.BlockSpec(memory_space=pltpu.VMEM), pl.BlockSpec(memory_space=pl.ANY)
    return pl.pallas_call(
        functools.partial(branch_kernel, (inner, outer)),
        out_shape=(
            jax.ShapeDtypeStruct((C, Z, rows, width), BF16),
            jax.ShapeDtypeStruct((rows, width), F32),
            jax.ShapeDtypeStruct(up.shape, up.dtype),
            jax.ShapeDtypeStruct(down.shape, down.dtype),
        ),
        in_specs=[anywhere, anywhere, vmem, vmem, anywhere, anywhere],
        out_specs=(anywhere, vmem, anywhere, anywhere),
        input_output_aliases={4: 2, 5: 3},
        scratch_shapes=[
            pltpu.VMEM((outer, rows, width), F32),
            pltpu.VMEM((outer, rows, width), F32),
            pltpu.VMEM((outer - 1, rows, width), BF16),
            pltpu.VMEM((outer - 1, rows, width), BF16),
            pltpu.VMEM((rows, width), BF16),
            dma((2 * outer + 3 + 4 * (Z - 1) + (inner - 1) * outer + inner * (outer - 1),)),
            dma((2,)),
            dma((outer,)),
            dma((outer - 1,)),
            dma((C, Z)),
            dma((inner - 1, outer)),
            dma((outer - 1, inner)),
        ],
        compiler_params=pltpu.CompilerParams(
            collective_id=1, has_side_effects=True, vmem_limit_bytes=40 * 1024 * 1024
        ),
        name="branch_and_group",
    )(sent, own, tokens, gain, up, down)


def line_order():
    order = []
    for k in [n for t in range(1, Z) for n in (t, Z - t)] + [0]:
        if k not in order:
            order.append(k)
    return order


def line_sum(me, sends, rows, term, ready, store, held, up, down, between=None):
    z = me.z

    def add(when, target, slot, k, received=None, came=0):
        def body(r):
            value = term(k, r)
            if received is not None:
                value = value + received[came, r].astype(F32)
            target[slot, r] = value.astype(BF16)

        pl.when(when)(lambda: each_rows(rows, 16, body))

    for t in range(1, Z):
        slot = t - 1
        for k, (out, into, sems), out_slot, has, when, to in (
            (t, up, slot, z > 0, (z <= t - 1) & (z < Z - 1), me.z_up),
            (Z - t, down, Z - 1 - t, z < Z - 1, (z >= Z - t) & (z > 0), me.z_down),
        ):
            pl.when(when)(lambda k=k: ready(k))
            if t == 1:
                add(when, out, out_slot, k)
            else:
                pl.when(when & has)(
                    lambda into=into, sems=sems, slot=slot: arrived(
                        into.at[slot - 1], sems.at[slot - 1], me.at_c
                    )
                )
                add(when & has, out, out_slot, k, into, slot - 1)
                add(when & jnp.logical_not(has), out, out_slot, k)
            sends.start(when, out.at[out_slot], into.at[slot], sems.at[slot], me.at_z(to))
        if between is not None:
            between(t)
    ready(0)
    each_rows(rows, 16, lambda r: store(r, term(0, r)))
    for (_, into, sems), has in ((up, z > 0), (down, z < Z - 1)):

        @pl.when(has)
        def _(into=into, sems=sems):
            arrived(into.at[Z - 2], sems.at[Z - 2], me.at_c)
            each_rows(rows, 16, lambda r: store(r, held(r) + into[Z - 2, r].astype(F32)))


class PlaneTerms:
    def __init__(self, me, sends, parts, over_x, blocks, scratch):
        self.me, self.sends, self.parts, self.over_x, self.blocks = me, sends, parts, over_x, blocks
        self.came, self.mine, self.sems, self.local_sems = scratch

    def begin(self):
        me = self.me
        if self.over_x:
            for j in range(1, me.inner):
                for i, part in enumerate(self.parts):
                    self.sends.start(
                        True, part.at[self.blocks, (me.x + j) % me.inner],
                        self.came.at[j - 1, i], self.sems.at[j - 1, i], me.at_x(j),
                    )
            pairs = [(part.at[self.blocks, me.x], self.mine.at[i]) for i, part in enumerate(self.parts)]
        else:
            for i in range(1, me.outer):
                self.sends.start(
                    True, self.parts[i].at[self.blocks], self.came.at[i - 1],
                    self.sems.at[0, i - 1], me.at_y(-i),
                )
            pairs = [(self.parts[0].at[self.blocks], self.mine)]
        self.loads = self.moved(pairs)

    def moved(self, pairs):
        copies = [
            pltpu.make_async_copy(source, target, self.local_sems.at[n])
            for n, (source, target) in enumerate(pairs)
        ]
        for copy in copies:
            copy.start()
        return copies

    def add(self):
        me = self.me
        if self.over_x:
            count, places = me.inner - 1, [(i,) for i in range(me.outer)]
        else:
            count, places = me.outer - 1, [()]
        for n in range(count):
            for place in places:
                sems = self.sems.at[n, place[0]] if place else self.sems.at[0, n]
                arrived(self.came.at[(n, *place)], sems, me.at_c)
        for copy in self.loads:
            copy.wait()
        shape = self.mine.shape[:2]

        def body(r):
            for first in range(shape[0]):
                for second in range(shape[1]):
                    total = self.mine[first, second, r].astype(F32)
                    for n in range(count):
                        total = total + self.came[n, first, second, r].astype(F32)
                    self.mine[first, second, r] = total.astype(BF16)

        each_rows(self.mine.shape[2], 16, body)

    def hand_on(self, kept, sent):
        me = self.me
        if self.over_x:
            pairs = [(self.mine.at[i], kept if i == 0 else sent(i - 1)) for i in range(me.outer)]
        else:
            pairs = [
                (self.mine.at[:, (me.x + j) % me.inner], kept if j == 0 else sent(j - 1))
                for j in range(me.inner)
            ]
        self.loads = self.moved(pairs)

    def finish(self):
        for copy in self.loads:
            copy.wait()


def middle_kernel(shape, *refs):
    outer = shape[1]
    sent, own, middle, grads, gain, feed_sent, feed_own = refs[:7]
    parts = refs[7 : 7 + 3 * outer]
    rows_to, d_middle, gain_grad, block_out = refs[7 + 3 * outer : 11 + 3 * outer]
    targets = refs[11 + 3 * outer : 14 + 3 * outer]
    scratch = refs[14 + 3 * outer :]
    middle_body(
        shape, sent, own, middle, grads, gain, feed_sent, feed_own, parts, targets,
        rows_to, d_middle, gain_grad, block_out, scratch[:9], scratch[9:18],
        [scratch[18 + 4 * n : 22 + 4 * n] for n in range(4)], *scratch[34:],
    )


class PairSum:
    def __init__(self, me, sends, sent, own, scratch):
        self.me, self.sends, self.sent = me, sends, sent
        (
            self.held, self.c_in, up_out, up_in, down_out, down_in,
            self.c_sems, up_sems, down_sems,
        ) = scratch
        self.up, self.down = (up_out, up_in, up_sems), (down_out, down_in, down_sems)

    def begin(self):
        for k in line_order():
            self.sends.start(
                True, self.sent.at[k], self.c_in.at[k], self.c_sems.at[k], self.me.at_c
            )

    def run(self, between=None):
        def ready(k):
            arrived(self.c_in.at[k], self.c_sems.at[k], self.me.at_c)

        def term(k, r):
            return self.held[k, r] + self.c_in[k, r].astype(F32)

        def store(r, value):
            self.held[0, r] = value

        line_sum(
            self.me, self.sends, self.held.shape[1], term, ready, store,
            lambda r: self.held[0, r], self.up, self.down, between,
        )


def plane_units(me, sends, parts, scratch):
    outer = me.outer
    gate, up, down = (parts[n * outer : (n + 1) * outer] for n in range(3))
    every, low, high = slice(0, Z), slice(0, Z // 2), slice(Z // 2, Z)
    return [
        PlaneTerms(me, sends, gate, True, every, scratch[0]),
        PlaneTerms(me, sends, up, False, every, scratch[1]),
        PlaneTerms(me, sends, down, True, low, scratch[2]),
        PlaneTerms(me, sends, down, False, high, scratch[3]),
    ]


def middle_body(
    shape, sent, own, middle, grads, gain, feed_sent, feed_own, parts, targets,
    rows_to, d_middle, gain_grad, block_out, sum_scratch, feed_scratch, unit_scratch, low,
    send_sems, local_sems, rows_sems,
):
    me = Place(shape)
    rows = middle.shape[0]
    sends = Sends(send_sems)
    total = PairSum(me, sends, sent, own, sum_scratch)
    feed = PairSum(me, sends, feed_sent, feed_own, feed_scratch)
    load = pltpu.make_async_copy(own, total.held, local_sems.at[0])
    feed_load = pltpu.make_async_copy(feed_own, feed.held, local_sems.at[2])
    load.start()
    me.greet()
    total.begin()
    units = plane_units(me, sends, parts, unit_scratch)
    units_to, units_y, units_x = targets
    for unit in units:
        unit.begin()
    feed_load.start()
    load.wait()
    total.run()
    own_v = total.held
    gain_grad[...] = jnp.zeros_like(gain_grad)

    def work(r):
        values = middle[r]
        inverse = lax.rsqrt(jnp.mean(values * values, axis=1, keepdims=True) + EPSILON)
        normed = values * inverse
        d_normed = own_v[0, r]
        gain_grad[...] += d_normed * normed
        scaled = d_normed * gain[...]
        passed = inverse * (scaled - normed * jnp.mean(scaled * normed, axis=1, keepdims=True))
        total = grads[r].astype(F32) + passed
        d_middle[r] = total
        low[r] = total.astype(BF16)

    each_rows(rows, 16, work)
    keep = pltpu.make_async_copy(low, rows_to.at[me.w], local_sems.at[1])
    keep.start()
    gather = WtRows(me, sends, low, rows_to, rows_sems)
    gather.begin()
    feed.begin()
    feed_load.wait()
    half, extra = Z // 2, slice(Z, Z + Z // 2)

    def between(t):
        if t == 1:
            units[0].add()
            units[0].hand_on(units_to.at[0], lambda i: units_y.at[i, 0:Z])
        if t == 2:
            units[1].add()
            units[1].hand_on(units_to.at[1], lambda j: units_x.at[j, 0:Z])
        if t == 3:
            units[2].add()
            units[2].hand_on(units_to.at[2, 0:half], lambda i: units_y.at[i, extra])
            units[3].add()
            units[3].hand_on(units_to.at[2, half:Z], lambda j: units_x.at[j, extra])

    feed.run(between)
    each_rows(rows, 16, lambda r: block_out.__setitem__(
        r, (middle[r] + feed.held[0, r]).astype(BF16)))
    gather.step()
    gather.finish()
    for unit in units:
        unit.finish()
    sends.finish()
    keep.wait()


def middle_and_rows(sent, own, middle, grads, gain, feed_sent, feed_own, parts):
    inner, outer = sizes()
    rows, width = middle.shape
    unit_rows, share = parts[0].shape[2:]
    block = (unit_rows, share)
    targets = [
        jax.ShapeDtypeStruct((*shape, *block), BF16)
        for shape in ((3, Z), (outer - 1, Z + Z // 2), (inner - 1, Z + Z // 2))
    ]
    unit_copies = 2 * (inner - 1) * outer + 2 * (outer - 1)
    pair_scratch = [pltpu.VMEM((Z, rows, width), F32), pltpu.VMEM((Z, rows, width), BF16)]
    pair_scratch += [pltpu.VMEM((Z - 1, rows, width), BF16)] * 4
    dma = pltpu.SemaphoreType.DMA
    pair_scratch += [dma((Z,)), dma((Z - 1,)), dma((Z - 1,))]
    unit_scratch = []
    for came, mine in (
        ((inner - 1, outer, Z), (outer, Z)),
        ((outer - 1, Z, inner), (Z, inner)),
        ((inner - 1, outer, Z // 2), (outer, Z // 2)),
        ((outer - 1, Z // 2, inner), (Z // 2, inner)),
    ):
        unit_scratch += [pltpu.VMEM((*came, *block), BF16), pltpu.VMEM((*mine, *block), BF16)]
        unit_scratch += [dma((inner - 1, outer)), dma((max(inner, outer),))]
    vmem, anywhere = pl.BlockSpec(memory_space=pltpu.VMEM), pl.BlockSpec(memory_space=pl.ANY)
    return pl.pallas_call(
        functools.partial(middle_kernel, (inner, outer)),
        out_shape=(
            jax.ShapeDtypeStruct((outer * C, rows, width), BF16),
            jax.ShapeDtypeStruct((rows, width), F32),
            jax.ShapeDtypeStruct((16, width), F32),
            jax.ShapeDtypeStruct((rows, width), BF16),
            *targets,
        ),
        in_specs=[anywhere, anywhere, vmem, vmem, vmem] + [anywhere] * (2 + 3 * outer),
        out_specs=(anywhere, vmem, vmem, vmem) + (anywhere,) * 3,
        scratch_shapes=pair_scratch * 2
        + unit_scratch
        + [
            pltpu.VMEM((rows, width), BF16),
            dma((2 * (Z + 2 * (Z - 1)) + 2 * outer + unit_copies,)),
            dma((3,)),
            dma((outer * C,)),
        ],
        compiler_params=pltpu.CompilerParams(
            collective_id=2, has_side_effects=True, vmem_limit_bytes=60 * 1024 * 1024
        ),
        name="middle_and_rows",
    )(sent, own, middle, grads, gain, feed_sent, feed_own, *parts)


class RowsSum:
    def __init__(self, me, sends, terms, total, scratch, sems):
        self.me, self.sends, self.terms, self.total = me, sends, terms, total
        self.own, self.x_in, *ways = scratch
        self.own_sems, self.x_sems, up_sems, down_sems = sems
        self.up, self.down = (*ways[:2], up_sems), (*ways[2:], down_sems)

    def load(self):
        me = self.me
        self.loads = []
        for k in range(Z):
            self.loads.append(
                pltpu.make_async_copy(
                    self.terms.at[(me.z + Z - k) % Z, me.x], self.own.at[k], self.own_sems.at[k]
                )
            )
            self.loads[k].start()

    def begin(self, turns):
        me = self.me
        for turn in turns:
            if turn == Z - 1:
                k = 0
            else:
                k = (jnp.minimum(me.z, Z - 1 - me.z) + turn) % (Z - 1) + 1
                k = jnp.where(me.z < Z // 2, k, Z - k)
            at = (me.z + Z - k) % Z
            for j in range(1, me.inner):
                self.sends.start(
                    True, self.terms.at[at, (me.x + j) % me.inner], self.x_in.at[j - 1, k],
                    self.x_sems.at[j - 1, k], me.at_x(j),
                )

    def run(self, between=None):
        me = self.me

        def ready(k):
            self.loads[k].wait()
            for j in range(1, me.inner):
                arrived(self.x_in.at[j - 1, k], self.x_sems.at[j - 1, k], me.at_c)

        def term(k, r):
            value = self.own[k, r].astype(F32)
            for j in range(1, me.inner):
                value = value + self.x_in[j - 1, k, r].astype(F32)
            return value

        def store(r, value):
            self.total[r] = value

        line_sum(
            me, self.sends, self.total.shape[0], term, ready, store, lambda r: self.total[r],
            self.up, self.down, between,
        )


class ProductsSum(RowsSum):
    def __init__(self, me, sends, factors, total, scratch, sems):
        self.me, self.sends, self.total = me, sends, total
        self.factors = factors
        self.held, self.x_in, out, up_in, down_in, *self.lefts = scratch
        self.own_sems, self.x_sems, up_sems, down_sems = sems
        self.up, self.down = (out, up_in, up_sems), (out, down_in, down_sems)

    def load(self):
        self.loads = []
        for n, (left, _) in enumerate(self.factors):
            copy = pltpu.make_async_copy(left, self.lefts[n], self.own_sems.at[n])
            copy.start()
            self.loads.append(copy)

    def begin(self, turns):
        me = self.me
        while self.loads:
            self.loads.pop().wait()
        rows, span = self.total.shape[0], self.held.shape[1]
        for turn in turns:
            if turn == Z - 1:
                k = 0
            else:
                k = (jnp.minimum(me.z, Z - 1 - me.z) + turn) % (Z - 1) + 1
                k = jnp.where(me.z < Z // 2, k, Z - k)
            at = (me.z + Z - k) % Z

            def tile(i, carried, k=k, at=at):
                first = 0
                down = pl.ds(pl.multiple_of(i * LANES, LANES), LANES)
                across = pl.ds(pl.multiple_of(at * span + i * LANES, LANES), LANES)
                for n, (_, rights) in enumerate(self.factors):
                    left = self.lefts[n][:, across]
                    for right in rights:
                        columns = slice(first, first + right.shape[1])
                        self.held[k, down, columns] = contract_rows(left, right[...]).astype(BF16)
                        first += right.shape[1]
                return carried

            lax.fori_loop(0, span // LANES, tile, 0)
            for j in range(1, me.inner):
                part = pl.ds(pl.multiple_of((me.x + j) % me.inner * rows, 16), rows)
                self.sends.start(
                    True, self.held.at[k, part], self.x_in.at[j - 1, k], self.x_sems.at[j - 1, k],
                    me.at_x(j),
                )

    def run(self, between=None):
        me = self.me
        rows = self.total.shape[0]

        def ready(k):
            for j in range(1, me.inner):
                arrived(self.x_in.at[j - 1, k], self.x_sems.at[j - 1, k], me.at_c)

        def term(k, r):
            mine = pl.ds(pl.multiple_of(me.x * rows + r.start, 16), r.size)
            value = self.held[k, mine].astype(F32)
            for j in range(1, me.inner):
                value = value + self.x_in[j - 1, k, r].astype(F32)
            return value

        def store(r, value):
            self.total[r] = value

        line_sum(
            me, self.sends, rows, term, ready, store, lambda r: self.total[r],
            self.up, self.down, between,
        )


def sums_kernel(shape, *refs):
    inner, outer = shape
    units, units_y, units_x, normed_rows_one, branch_rows, narrow, sent, own = refs[:8]
    d_x, d_y, mixed, tokens, gain, d_middle, gain_two_grad, vectors = refs[8:16]
    units_to, wide_to, narrow_to, tokens_grad, gains, vectors_to = refs[16:22]
    refs = refs[22:]
    wide_scratch, narrow_scratch = refs[:7], refs[7:13]
    (own_v, c_in, y_out, y_in, all_in, vec_in) = refs[13:19]
    (send_sems, local_sems, c_sems, y_sems, all_sems, vec_sems) = refs[19:25]
    wide_sems, narrow_sems = refs[25:29], refs[29:33]
    units_v, units_y_in, units_x_in, unit_sems, units_y_sems, units_x_sems = refs[33:]
    share = units.shape[3]
    me = Place(shape)
    rows = tokens.shape[0]
    sends = Sends(send_sems)
    load = pltpu.make_async_copy(own, own_v, local_sems.at[0])
    load.start()
    units_load = pltpu.make_async_copy(units, units_v, local_sems.at[1])
    units_load.start()
    me.greet()

    order = [(me.y + i) % outer for i in list(range(1, outer)) + [0]]
    for at in order:
        sends.start(True, sent.at[at], c_in.at[at], c_sems.at[at], me.at_c)
    narrow_sum = RowsSum(me, sends, narrow, narrow_to, narrow_scratch, narrow_sems)
    factors = [(normed_rows_one, [d_x, d_y]), (branch_rows, [mixed])]
    wide_sum = ProductsSum(me, sends, factors, wide_to, wide_scratch, wide_sems)
    narrow_sum.load()
    wide_sum.load()
    narrow_sum.begin(range(Z))

    def columns(n, at):
        return units_to.at[n, :, pl.ds(pl.multiple_of(at * share, LANES), share)]

    low, high, extra = slice(0, Z // 2), slice(Z // 2, Z), slice(Z, Z + Z // 2)
    every = slice(0, Z)

    def units_begin_y():
        for n, blocks in enumerate((every, extra)):
            for i in range(1, outer):
                sends.start(
                    True, units_y.at[i - 1, blocks], units_y_in.at[i - 1, blocks],
                    units_y_sems.at[i - 1, n], me.at_y(-i),
                )

    def units_begin_x():
        for n, blocks in enumerate((every, extra)):
            for j in range(1, inner):
                sends.start(
                    True, units_x.at[j - 1, blocks], units_x_in.at[j - 1, blocks],
                    units_x_sems.at[j - 1, n], me.at_x(j),
                )

    kept = []

    def unit_add(n, blocks, came, came_blocks, sems, count):
        for i in range(count):
            arrived(came.at[i, came_blocks], sems.at[i], me.at_c)

        def body(r):
            for at in range(blocks.stop - blocks.start):
                total = units_v[n, blocks.start + at, r].astype(F32)
                for i in range(count):
                    total = total + came[i, came_blocks.start + at, r].astype(F32)
                units_v[n, blocks.start + at, r] = total.astype(BF16)

        each_rows(units_v.shape[2], 16, body)

    def unit_pass_on(n):
        copy = pltpu.make_async_copy(units_v.at[n, me.z], columns(n, me.z), local_sems.at[2 + n])
        copy.start()
        kept.append(copy)
        for k in range(1, Z):
            to = (me.z + k) % Z
            sends.start(
                True, units_v.at[n, to], columns(n, me.z), unit_sems.at[n, me.z], me.at_z(to)
            )

    def unit_gate():
        unit_add(0, every, units_y_in, every, units_y_sems.at[:, 0], outer - 1)
        unit_pass_on(0)

    def unit_down():
        unit_add(2, low, units_y_in, extra, units_y_sems.at[:, 1], outer - 1)
        unit_add(2, high, units_x_in, extra, units_x_sems.at[:, 1], inner - 1)
        unit_pass_on(2)

    def unit_up():
        unit_add(1, every, units_x_in, every, units_x_sems.at[:, 0], inner - 1)
        unit_pass_on(1)

    def units_finish():
        for n in range(3):
            for k in range(1, Z):
                at = (me.z + Z - k) % Z
                arrived(columns(n, at), unit_sems.at[n, at], me.at_c)
        for copy in kept:
            copy.wait()

    def exchange(held, into, sems, first, devices):
        for n, device in enumerate(devices):
            sends.start(True, held, into.at[first + n], sems.at[first + n], device)

    def gathered(held, into, sems, first, devices):
        for n, _ in enumerate(devices):
            arrived(into.at[first + n], sems.at[first + n], me.at_c)
        total = into[first]
        for n in range(1, len(devices)):
            total = total + into[first + n]
        return held[...] + total

    stages = [
        [me.at_c],
        [me.at_y(i) for i in range(1, outer)],
        [me.at_z((me.z + k) % Z) for k in range(1, Z)],
        [me.at_x(j) for j in range(1, inner)],
    ]
    at_stage = [0]
    for stage in stages:
        at_stage.append(at_stage[-1] + len(stage))

    z_stage, x_stage = stages[2], stages[3]
    exchange(vectors, vec_in, vec_sems, 0, x_stage)
    units_begin_x()

    units_begin_y()

    load.wait()
    for i, at in enumerate(order):
        arrived(c_in.at[at], c_sems.at[at], me.at_c)
        if i < outer - 1:
            each_rows(rows, 16, lambda r, i=i, at=at: y_out.__setitem__(
                (i, r), (own_v[at, r] + c_in[at, r].astype(F32)).astype(BF16)))
            sends.start(True, y_out.at[i], y_in.at[i], y_sems.at[i], me.at_y(i + 1))
    vectors_to[0] = gathered(vectors, vec_in, vec_sems, 0, x_stage)
    exchange(vectors_to.at[0], vec_in, vec_sems, len(x_stage), z_stage)
    narrow_sum.run()
    vectors_to[1] = gathered(vectors_to.at[0], vec_in, vec_sems, len(x_stage), z_stage)
    units_load.wait()
    wide_sum.begin(range(1))
    unit_gate()
    wide_sum.begin(range(1, 2))
    unit_up()
    unit_down()
    wide_sum.begin(range(2, Z))

    def work(r):
        d_normed = own_v[me.y, r] + c_in[me.y, r].astype(F32)
        for i in range(outer - 1):
            d_normed = d_normed + y_in[i, r].astype(F32)
        stream = tokens[r].astype(F32)
        inverse = lax.rsqrt(jnp.mean(stream * stream, axis=1, keepdims=True) + EPSILON)
        normed = stream * inverse
        part = d_normed * normed
        gains[0, 0:8] += part[0:8] + part[8:16]
        scaled = d_normed * gain[...]
        passed = inverse * (scaled - normed * jnp.mean(scaled * normed, axis=1, keepdims=True))
        tokens_grad[r] = (d_middle[r] + passed).astype(BF16)

    def gains_step(n):
        if n > 0:
            gains[n] = gathered(
                gains.at[n - 1], all_in, all_sems, at_stage[n - 1], stages[n - 1]
            )
        if n < len(stages):
            exchange(gains.at[n], all_in, all_sems, at_stage[n], stages[n])

    def between(t):
        if t == 1:
            for i in range(outer - 1):
                arrived(y_in.at[i], y_sems.at[i], me.at_c)
            gains[0] = jnp.zeros_like(gains[0])
            each_rows(rows, 16, work)
            gains[0, 8:16] = gain_two_grad[0:8] + gain_two_grad[8:16]
        gains_step(t - 1)

    wide_sum.run(between)
    for n in range(Z - 1, len(stages) + 1):
        gains_step(n)
    units_finish()
    sends.finish()


def last_sums(
    units, units_y, units_x, normed_one, branch_rows, narrow, sent, own,
    d_x, d_y, mixed, tokens, gain, d_middle, gain_two_grad, vectors,
):
    inner, outer = sizes()
    rows, width = tokens.shape
    dma = pltpu.SemaphoreType.DMA
    vmem, anywhere = pl.BlockSpec(memory_space=pltpu.VMEM), pl.BlockSpec(memory_space=pl.ANY)

    def scratch(terms):
        one = terms.shape[2:]
        return [pltpu.VMEM((Z, *one), BF16), pltpu.VMEM((inner - 1, Z, *one), BF16)] + [
            pltpu.VMEM((Z - 1, *one), BF16)
        ] * 4

    peers = 1 + (outer - 1) + (inner - 1) + (Z - 1)
    copies = 2 * outer - 1 + 2 * (Z * (inner - 1) + 2 * (Z - 1))
    copies += peers + (inner - 1) + (Z - 1) + 2 * (outer - 1) + 2 * (inner - 1) + 3 * (Z - 1)
    _, _, unit_rows, share = units.shape
    block = (unit_rows, d_x.shape[1] + d_y.shape[1] + mixed.shape[1])
    line_sems = [dma((Z,)), dma((inner - 1, Z)), dma((Z - 1,)), dma((Z - 1,))]
    return pl.pallas_call(
        functools.partial(sums_kernel, (inner, outer)),
        out_shape=(
            jax.ShapeDtypeStruct((3, unit_rows, Z * share), BF16),
            jax.ShapeDtypeStruct(block, F32),
            jax.ShapeDtypeStruct(narrow.shape[2:], F32),
            jax.ShapeDtypeStruct((rows, width), BF16),
            jax.ShapeDtypeStruct((5, 16, width), F32),
            jax.ShapeDtypeStruct((2, *vectors.shape), F32),
        ),
        in_specs=[anywhere] * 8 + [vmem] * 8,
        out_specs=(anywhere,) + (vmem,) * 5,
        scratch_shapes=[
            pltpu.VMEM((Z, inner * block[0], block[1]), BF16),
            pltpu.VMEM((inner - 1, Z, *block), BF16),
        ]
        + [pltpu.VMEM((Z - 1, *block), BF16)] * 3
        + [pltpu.VMEM(normed_one.shape, BF16), pltpu.VMEM(branch_rows.shape, BF16)]
        + scratch(narrow)
        + [
            pltpu.VMEM((outer, rows, width), F32),
            pltpu.VMEM((outer, rows, width), BF16),
            pltpu.VMEM((outer - 1, rows, width), BF16),
            pltpu.VMEM((outer - 1, rows, width), BF16),
            pltpu.VMEM((peers, 16, width), F32),
            pltpu.VMEM((inner - 1 + Z - 1, *vectors.shape), F32),
            dma((copies,)),
            dma((5,)),
            dma((outer,)),
            dma((outer - 1,)),
            dma((peers,)),
            dma((inner - 1 + Z - 1,)),
        ]
        + line_sems * 2
        + [
            pltpu.VMEM(units.shape, BF16),
            pltpu.VMEM(units_y.shape, BF16),
            pltpu.VMEM(units_x.shape, BF16),
            dma((3, Z)),
            dma((outer - 1, 2)),
            dma((inner - 1, 2)),
        ],
        compiler_params=pltpu.CompilerParams(
            collective_id=5, has_side_effects=True, vmem_limit_bytes=60 * 1024 * 1024
        ),
        name="last_sums",
    )(
        units, units_y, units_x, normed_one, branch_rows, narrow, sent, own,
        d_x, d_y, mixed, tokens, gain, d_middle, gain_two_grad, vectors,
    )


def scan_kernel(backward, factors, inflows, states, entered, products, ends, ends_in, carry, send_sems, arrivals):
    seq = ends_in.shape[0]
    s = lax.axis_index("seq")
    rows, width = factors.shape
    barrier = pltpu.get_barrier_semaphore()

    def device(at):
        return {"seq": at, "wt": lax.axis_index("wt")}

    def greet(i, carried):
        @pl.when(i != s)
        def _():
            pl.semaphore_signal(barrier, inc=1, device_id=device(i), device_id_type=MESH)

        return carried

    lax.fori_loop(0, seq, greet, 0)
    group = 8
    at_row = lax.broadcasted_iota(jnp.int32, (group, width), 0)

    def step(i, carried):
        held, product = carried
        i = rows // group - 1 - i if backward else i
        where = pl.ds(pl.multiple_of(i * group, group), group)
        factor, inflow = factors[where, :], inflows[where, :]
        for by in (1, 2, 4):
            inside = at_row < group - by if backward else at_row >= by
            turn = group - by if backward else by
            inflow = factor * jnp.where(inside, pltpu.roll(inflow, turn, 0), 0.0) + inflow
            factor = factor * jnp.where(inside, pltpu.roll(factor, turn, 0), 1.0)
        inflow = inflow + factor * held
        factor = factor * product
        states[where, :] = inflow
        products[where, :] = factor
        last = slice(0, 1) if backward else slice(group - 1, group)
        return inflow[last], factor[last]

    held, product = lax.fori_loop(
        0, rows // group, step, (jnp.zeros((1, width), F32), jnp.ones((1, width), F32))
    )
    ends[0:1] = product
    ends[1:2] = held
    pl.semaphore_wait(barrier, seq - 1)

    def copy_to(i):
        return pltpu.make_async_remote_copy(
            src_ref=ends, dst_ref=ends_in.at[s], send_sem=send_sems.at[i], recv_sem=arrivals.at[s],
            device_id=device(i), device_id_type=MESH,
        )

    def later(i):
        return i < s if backward else i > s

    def send(i, carried):
        pl.when(later(i))(lambda: copy_to(i).start())
        return carried

    lax.fori_loop(0, seq, send, 0)
    carry[...] = jnp.zeros_like(carry)

    def receive(n, carried):
        i = seq - 1 - n if backward else n

        @pl.when(jnp.logical_not(later(i)) & (i != s))
        def _():
            arrived(ends_in.at[i], arrivals.at[i], device((s + 1) % seq))
            carry[0:1] = ends_in[i, 0:1] * carry[0:1] + ends_in[i, 1:2]

        return carried

    lax.fori_loop(0, seq, receive, 0)
    entering = carry[0:1]
    entered[...] = entering

    def spread(i, carried):
        where = pl.ds(pl.multiple_of(i * group, group), group)
        states[where, :] += products[where, :] * entering
        return carried

    lax.fori_loop(0, rows // group, spread, 0)

    def sent(i, carried):
        pl.when(later(i))(lambda: copy_to(i).wait_send())
        return carried

    lax.fori_loop(0, seq, sent, 0)


def full_scan(factor, inflow, backward):
    seq = lax.axis_size("seq")
    rows, width = factor.shape
    vmem = pl.BlockSpec(memory_space=pltpu.VMEM)
    return pl.pallas_call(
        functools.partial(scan_kernel, backward),
        out_shape=(
            jax.ShapeDtypeStruct((rows, width), F32),
            jax.ShapeDtypeStruct((1, width), F32),
        ),
        in_specs=[vmem, vmem],
        out_specs=(vmem, vmem),
        scratch_shapes=[
            pltpu.VMEM((rows, width), F32),
            pltpu.VMEM((8, width), F32),
            pltpu.VMEM((seq, 8, width), F32),
            pltpu.VMEM((8, width), F32),
            pltpu.SemaphoreType.DMA((seq,)),
            pltpu.SemaphoreType.DMA((seq,)),
        ],
        compiler_params=pltpu.CompilerParams(
            collective_id=4 if backward else 3,
            has_side_effects=True,
            vmem_limit_bytes=32 * 1024 * 1024,
        ),
        name="scan_back" if backward else "scan_ahead",
    )(factor, inflow)


def recurrence_terms(decay_pre, input_pre, decay_log, conv_float):
    log_decay = -DECAY_SCALE * jax.nn.softplus(-decay_log) * jax.nn.sigmoid(decay_pre)
    return (
        jnp.exp(log_decay),
        jnp.sqrt(-jnp.expm1(2.0 * log_decay)) * jax.nn.sigmoid(input_pre) * conv_float,
    )


def normed_rows(stream):
    inverse = lax.rsqrt(jnp.mean(stream * stream, axis=1, keepdims=True) + EPSILON)
    return stream * inverse, inverse


def per_device(
    tokens,
    norm1_gain,
    x_weight,
    y_weight,
    conv_weight,
    conv_bias,
    decay_gate_weight,
    decay_bias,
    input_gate_weight,
    input_bias,
    decay_param,
    out_weight,
    norm2_gain,
    gate_weight,
    up_weight,
    down_weight,
    out_grad,
):
    seq, wt = lax.axis_size("seq"), lax.axis_size("wt")
    inner, outer = sizes()
    z, x, y, c = places()
    w = lax.axis_index("wt")
    rows_dev, width = tokens.shape
    weight_rows, lru_cols = x_weight.shape
    chunk, block = decay_gate_weight.shape
    half = block // 2
    full = lru_cols - half
    taps_count = conv_weight.shape[1]
    reach = taps_count - 1
    hidden_cols = gate_weight.shape[1]

    def turned(value, axis):
        return jnp.where(c == 0, value, jnp.roll(value, -half, axis))

    def turned_back(value, axis):
        return jnp.where(c == 0, value, jnp.roll(value, half, axis))

    def in_order(own, partner, axis):
        return jnp.where(
            c == 0,
            jnp.concatenate([own, partner], axis),
            jnp.concatenate([partner, own], axis),
        )

    vectors = jnp.stack(
        [v.astype(F32) for v in (norm1_gain, norm2_gain, conv_bias, decay_bias, input_bias)]
        + [decay_param]
        + [conv_weight[:, k].astype(F32) for k in range(taps_count)]
    )
    vectors = jnp.pad(vectors, ((0, -vectors.shape[0] % 8), (0, -chunk % LANES)))

    across = [(i, i % seq * wt + i // seq) for i in range(seq * wt)]
    gates = jnp.concatenate([decay_gate_weight, input_gate_weight], axis=1)

    def padded(weight):
        share = -(-hidden_cols // (Z * LANES)) * LANES
        return jnp.pad(weight, ((0, 0), (0, Z * share - hidden_cols)))

    xy_unit = jnp.concatenate([turned(x_weight, 1), turned(y_weight, 1)], axis=1)
    (
        group_tokens, grad_group, vectors, gate_all, xy_kernel, out_kernel,
        gate_kernel, up_kernel, down_kernel,
    ) = gather_all(
        tokens, out_grad, vectors, gates, xy_unit, turned(out_weight, 1),
        padded(gate_weight), padded(up_weight), padded(down_weight),
    )
    group_tokens = group_tokens.reshape(-1, width)
    grad_group = grad_group.reshape(-1, width)
    vectors = jnp.moveaxis(vectors[:, : 6 + taps_count, :chunk], 0, 1).reshape(6 + taps_count, -1)
    gain_one, gain_two = vectors[0], vectors[1]
    own_vectors = turned(
        lax.dynamic_slice(vectors[2:], (0, w * lru_cols), (taps_count + 4, lru_cols)), 1
    )
    tap_bias, decay_shift, input_shift, decay_log = (own_vectors[i] for i in range(4))
    taps = own_vectors[4:]
    xy_kernel = xy_kernel.reshape(width, -1)
    out_kernel = out_kernel.reshape(width, -1)
    gate_kernel = gate_kernel.reshape(width, -1)
    gate_all = turned(gate_all.reshape(lru_cols, 2 * block), 0)
    partner_rows = c_swap(gate_all[full:])
    shared_rows = in_order(gate_all[full:], partner_rows, 0)

    stream = tokens.astype(F32)
    group_normed, _ = normed_rows(group_tokens.astype(F32))
    group_one = (group_normed * gain_one).astype(BF16)
    rows = group_one.shape[0]
    xy = multiply(group_one, xy_kernel)
    x_branch = xy[:, :lru_cols].astype(BF16)
    y_before = xy[:, lru_cols:]
    y_gated, gelu_y_back = jax.vjp(gelu_tanh, y_before)
    rim = lax.ppermute(x_branch[rows - reach :], "seq", [(i, i + 1) for i in range(seq - 1)])
    extended = jnp.concatenate([rim, x_branch], axis=0).astype(F32)
    conv_low = (
        tap_bias
        + sum(taps[k] * extended[reach - k : reach - k + rows] for k in range(taps_count))
    ).astype(BF16)
    shared_conv = in_order(conv_low[:, full:], c_swap(conv_low[:, full:]), 1)
    heads = full // block

    def of_head(value, i):
        return value[:, i * block : (i + 1) * block]

    pre_parts = [
        multiply(of_head(conv_low, i), gate_all[i * block : (i + 1) * block]) for i in range(heads)
    ]
    shared_columns = jnp.where(
        c == 0,
        jnp.concatenate([shared_rows[:, :half], shared_rows[:, block : block + half]], axis=1),
        jnp.concatenate([shared_rows[:, half:block], shared_rows[:, block + half :]], axis=1),
    )
    shared_pre = multiply(shared_conv, shared_columns)
    decay_pre = decay_shift + jnp.concatenate(
        [part[:, :block] for part in pre_parts] + [shared_pre[:, :half]], axis=1
    )
    input_pre = input_shift + jnp.concatenate(
        [part[:, block:] for part in pre_parts] + [shared_pre[:, half:]], axis=1
    )
    (retain, inflow), terms_back = jax.vjp(
        recurrence_terms, decay_pre, input_pre, decay_log, conv_low.astype(F32)
    )
    states, state_in = full_scan(retain, inflow, False)
    before = jnp.concatenate([state_in, states[:-1]])
    lru_low = states.astype(BF16).astype(F32)
    mixed_rows = (lru_low * y_gated).astype(BF16)
    mixed_parts = mixed_rows.reshape(outer, C, rows_dev, lru_cols)

    def branch_of(at):
        part = pick(mixed_parts, at, 1).reshape(outer * rows_dev, lru_cols)
        return contract_last(part, out_kernel).reshape(outer, rows_dev, width)

    group_two, middle, up_kernel, down_kernel = branch_and_group(
        branch_of(1 - c), branch_of(c), tokens, gain_two[None], up_kernel, down_kernel
    )
    up_kernel = up_kernel.reshape(width, -1)
    down_kernel = down_kernel.reshape(width, -1)
    group_two = group_two.reshape(C * Z * rows_dev, width)

    gate_pre = multiply(group_two, gate_kernel)
    up_pre = multiply(group_two, up_kernel)
    active, gelu_gate_back = jax.vjp(gelu_tanh, gate_pre)
    hidden = (active * up_pre).astype(BF16)

    d_hidden = multiply(grad_group, down_kernel)
    d_up = (d_hidden * active).astype(BF16)
    d_gate = gelu_gate_back(d_hidden * up_pre)[0].astype(BF16)
    half_rows = Z * rows_dev

    def d_normed_of(part):
        total = contract_last(d_gate[part], gate_kernel) + contract_last(d_up[part], up_kernel)
        return total.reshape(Z, rows_dev, width)

    def terms_of(left_side, right_side):
        share = right_side.shape[1] // outer
        return [
            contract_rows(left_side, right_side[:, i * share : (i + 1) * share])
            .astype(BF16)
            .reshape(Z, inner, weight_rows, share)
            for i in range(outer)
        ]

    gate_terms = terms_of(group_two, d_gate)
    up_terms = terms_of(group_two, d_up)
    down_terms = terms_of(grad_group, hidden)
    def feed_of(part):
        return contract_last(hidden[part], down_kernel).reshape(Z, rows_dev, width)

    branch_rows, d_middle, gain_two_grad, block_out, units, units_y, units_x = middle_and_rows(
        d_normed_of(slice(half_rows, None)).astype(BF16),
        d_normed_of(slice(0, half_rows)),
        middle,
        out_grad,
        gain_two[None],
        feed_of(slice(half_rows, None)).astype(BF16),
        feed_of(slice(0, half_rows)),
        gate_terms + up_terms + down_terms,
    )
    branch_rows = branch_rows.reshape(-1, width)

    d_mixed = multiply(branch_rows, out_kernel)
    d_lru = (d_mixed * y_gated).astype(BF16).astype(F32)
    d_y = gelu_y_back(d_mixed * lru_low)[0].astype(BF16)
    passed, passed_in = full_scan(retain, retain * d_lru, True)
    d_total = d_lru + jnp.concatenate([passed[1:], passed_in])
    d_decay_pre, d_input_pre, decay_log_grad, d_conv_direct = terms_back(
        (d_total * before, d_total)
    )
    d_decay_low, d_input_low = d_decay_pre.astype(BF16), d_input_pre.astype(BF16)
    own_low = jnp.concatenate([d_decay_low[:, full:], d_input_low[:, full:]], axis=1)
    partner_low = c_swap(own_low)
    shared_low = jnp.concatenate(
        [
            in_order(own_low[:, :half], partner_low[:, :half], 1),
            in_order(own_low[:, half:], partner_low[:, half:], 1),
        ],
        axis=1,
    )
    lows = [
        jnp.concatenate([of_head(d_decay_low, i), of_head(d_input_low, i)], axis=1)
        for i in range(heads)
    ]
    d_conv = d_conv_direct + jnp.concatenate(
        [contract_last(lows[i], gate_all[i * block : (i + 1) * block]) for i in range(heads)]
        + [contract_last(shared_low, gate_all[full:])],
        axis=1,
    )
    gates_grad = jnp.concatenate(
        [contract_rows(of_head(conv_low, i), lows[i]) for i in range(heads)]
        + [contract_rows(conv_low[:, full:], shared_low)]
    )
    ahead = lax.ppermute(d_conv[:reach], "seq", [(i + 1, i) for i in range(seq - 1)])
    d_extended = jnp.concatenate([d_conv, ahead], axis=0)
    d_x_branch = sum(taps[k] * d_extended[k : k + rows] for k in range(taps_count)).astype(BF16)
    dx_parts = d_x_branch.reshape(outer, C, rows_dev, lru_cols)
    dy_parts = d_y.reshape(outer, C, rows_dev, lru_cols)

    def d_normed_one_of(at):
        dx, dy = (
            pick(parts, at, 1).reshape(outer * rows_dev, lru_cols) for parts in (dx_parts, dy_parts)
        )
        total = contract_last(dx, xy_kernel[:, :lru_cols]) + contract_last(
            dy, xy_kernel[:, lru_cols:]
        )
        return total.reshape(outer, rows_dev, width)

    narrow = turned_back(gates_grad, 0).astype(BF16).reshape(Z, inner, chunk, 2 * block)
    narrow = jnp.pad(narrow, ((0, 0), (0, 0), (0, -chunk % 16), (0, 0)))
    own_sums = jnp.stack(
        [jnp.sum(d_conv, axis=0), jnp.sum(d_decay_pre, axis=0), jnp.sum(d_input_pre, axis=0)]
        + [decay_log_grad]
        + [jnp.sum(d_conv * extended[reach - k : reach - k + rows], axis=0) for k in range(taps_count)],
    )
    own_sums = turned_back(own_sums, 1)
    placed, wide, narrow, tokens_grad, gains, own_sums = last_sums(
        units, units_y, units_x, group_one, branch_rows, narrow,
        d_normed_one_of(1 - c).astype(BF16), d_normed_one_of(c),
        turned_back(d_x_branch, 1), turned_back(d_y, 1), turned_back(mixed_rows, 1),
        tokens, gain_one[None], d_middle, gain_two_grad, own_sums,
    )
    weight_grads = [wide[:, n * lru_cols : (n + 1) * lru_cols] for n in range(3)]
    gate_grad, up_grad, down_grad = (placed[n, :, :hidden_cols].astype(F32) for n in range(3))
    gains = gains[4].reshape(2, 8, width).sum(axis=1)
    gains = lax.dynamic_slice(gains, (0, (lax.axis_index("seq") * wt + w) * chunk), (2, chunk))
    sums = lax.dynamic_slice(own_sums[1], (0, lax.axis_index("seq") * chunk), (taps_count + 4, chunk))
    own_sums = jnp.concatenate([narrow[:chunk], sums.T], axis=1)
    own_sums = lax.ppermute(own_sums, ("seq", "wt"), [(to, at) for at, to in across])
    sums = own_sums[:, 2 * block :]
    return (
        block_out,
        tokens_grad,
        gains[0],
        weight_grads[0],
        weight_grads[1],
        sums[:, 4:],
        sums[:, 0],
        own_sums[:, :block],
        sums[:, 1],
        own_sums[:, block : 2 * block],
        sums[:, 2],
        sums[:, 3],
        weight_grads[2],
        gains[1],
        gate_grad,
        up_grad,
        down_grad,
    )


def solution(mesh):
    rows, both, lone = P(("seq", "wt"), None), P("seq", "wt"), P(("seq", "wt"))
    in_specs = (
        rows, lone, both, both, rows, lone, rows, lone, rows, lone, lone,
        both, lone, both, both, both, rows,
    )
    out_specs = (
        rows, rows, lone, both, both, rows, lone, rows, lone, rows, lone, lone,
        both, lone, both, both, both,
    )
    return jax.shard_map(
        per_device, mesh=mesh, in_specs=in_specs, out_specs=out_specs, check_vma=False
    )
```

```python
import functools

import jax
import jax.numpy as jnp
from jax import lax
from jax.experimental import pallas as pl
from jax.experimental.pallas import tpu as pltpu
from jax.sharding import PartitionSpec as P

EPSILON = 1e-06
DECAY_SCALE = 8.0
Z = 4
C = 2
LANES = 128
F32 = jnp.float32
BF16 = jnp.bfloat16
MESH = pl.DeviceIdType.MESH


def gelu_tanh(values):
    return jax.nn.gelu(values, approximate=True)


def sizes():
    return lax.axis_size("seq") // Z, lax.axis_size("wt") // C


def places():
    inner, outer = sizes()
    s, w = lax.axis_index("seq"), lax.axis_index("wt")
    return s // inner, s % inner, w // C, w % C


def z_move(value, by, senders):
    inner, _ = sizes()
    pairs = [(z * inner + x, (z + by) % Z * inner + x) for z in senders for x in range(inner)]
    return lax.ppermute(value, "seq", pairs)


def c_swap(value):
    _, outer = sizes()
    pairs = [(y * C + c, y * C + 1 - c) for y in range(outer) for c in range(C)]
    return lax.ppermute(value, "wt", pairs)


def line_scatter(parts):
    up = down = None
    for step in range(1, Z):
        rising = parts[step] if up is None else parts[step] + up
        falling = parts[Z - step] if down is None else parts[Z - step] + down
        up = z_move(rising.astype(BF16), 1, range(0, step)).astype(F32)
        down = z_move(falling.astype(BF16), -1, range(Z - step, Z)).astype(F32)
    return parts[0] + up + down


def pick(value, index, axis):
    return lax.dynamic_index_in_dim(value, index, axis, keepdims=False)


def contract_last(left_side, right_side):
    return lax.dot_general(
        left_side, right_side, (((1,), (1,)), ((), ())), preferred_element_type=F32
    )


def contract_rows(left_side, right_side):
    return lax.dot_general(
        left_side, right_side, (((0,), (0,)), ((), ())), preferred_element_type=F32
    )


def multiply(left_side, right_side):
    return jnp.dot(left_side, right_side, preferred_element_type=F32)


class Sends:
    def __init__(self, sems):
        self.sems, self.started = sems, []

    def start(self, when, source, target, arrival, device):
        copy = pltpu.make_async_remote_copy(
            src_ref=source,
            dst_ref=target,
            send_sem=self.sems.at[len(self.started)],
            recv_sem=arrival,
            device_id=device,
            device_id_type=MESH,
        )
        if when is True:
            copy.start()
        else:
            pl.when(when)(copy.start)
        self.started.append((when, copy))

    def finish(self):
        for when, copy in self.started:
            if when is True:
                copy.wait_send()
            else:
                pl.when(when)(copy.wait_send)


def arrived(target, arrival, device):
    pltpu.make_async_remote_copy(
        src_ref=target, dst_ref=target, send_sem=arrival, recv_sem=arrival,
        device_id=device, device_id_type=MESH,
    ).wait_recv()


def gather_kernel(shape, *refs):
    inner, outer = shape
    (tokens, grads, vectors, gates, xy, out, gate, up, down) = refs[:9]
    (tokens_to, grads_to, vectors_to, gates_to, xy_to, out_to, gate_to, up_to, down_to) = refs[9:18]
    gates_own, send_sems, local_sems, line_sems, plane_sems, rows_sems = refs[18:24]
    vector_sems, turn_sems, group_sems = refs[24:]
    seq, wt = Z * inner, outer * C
    s, w = lax.axis_index("seq"), lax.axis_index("wt")
    z, x, y, c = s // inner, s % inner, w // C, w % C
    sends = Sends(send_sems)
    group = GroupRows(Place(shape), sends, grads, grads_to, group_sems)
    here = []

    def at_z(to):
        return {"seq": to * inner + x, "wt": w}

    def at_x(by):
        return {"seq": z * inner + (x + by) % inner, "wt": w}

    def at_y(by):
        return {"seq": s, "wt": (y + by) % outer * C + c}

    at_c = {"seq": s, "wt": y * C + 1 - c}

    def keep(source, target, waited=False):
        copy = pltpu.make_async_copy(source, target, local_sems.at[len(here)])
        copy.start()
        here.append((waited, copy))
        return copy

    barrier = pltpu.get_barrier_semaphore()

    def greet(i, carried):
        @pl.when(i != s * wt + w)
        def _():
            pl.semaphore_signal(
                barrier, inc=1, device_id={"seq": i // wt, "wt": i % wt}, device_id_type=MESH
            )

        return carried

    lax.fori_loop(0, seq * wt, greet, 0)
    pl.semaphore_wait(barrier, seq * wt - 1)

    class Line:
        def __init__(self, index, source, target):
            self.source, self.target = source, target
            self.sems = line_sems.at[index]

        def forward(self, block, at, up_when, down_when):
            place = self.target.at[at, x]
            arrival = self.sems.at[at, x]
            sends.start(up_when, block, place, arrival, at_z(jnp.minimum(z + 1, Z - 1)))
            sends.start(down_when, block, place, arrival, at_z(jnp.maximum(z - 1, 0)))
            return place, arrival

        def across(self, when, block, at):
            for j in range(1, inner):
                sends.start(when, block, self.target.at[at, x], self.sems.at[at, x], at_x(j))

        def begin_z(self):
            keep(self.source, self.target.at[z, x])
            self.forward(self.source, z, z < Z - 1, z > 0)

        def begin_x(self):
            self.across(True, self.source, z)

        def begin(self):
            self.begin_z()
            self.begin_x()

        def step(self, k):
            for at, there, up_when, down_when in (
                (jnp.maximum(z - k, 0), z - k >= 0, (z - k >= 0) & (z < Z - 1), None),
                (jnp.minimum(z + k, Z - 1), z + k < Z, None, (z + k < Z) & (z > 0)),
            ):
                place, arrival = self.target.at[at, x], self.sems.at[at, x]

                @pl.when(there)
                def _(place=place, arrival=arrival):
                    arrived(place, arrival, at_c)

                if up_when is not None:
                    sends.start(up_when, place, place, arrival, at_z(jnp.minimum(z + 1, Z - 1)))
                else:
                    sends.start(down_when, place, place, arrival, at_z(jnp.maximum(z - 1, 0)))
                self.across(there, place, at)

        def finish(self):
            for at in range(Z):
                for j in range(1, inner):
                    from_x = (x + inner - j) % inner
                    arrived(self.target.at[at, from_x], self.sems.at[at, from_x], at_c)

    class Plane:
        def __init__(self, index, source, target, x_first, whole):
            self.source, self.target, self.x_first, self.whole = source, target, x_first, whole
            self.share = source.shape[1] // Z
            self.sems = plane_sems.at[index]

        def cut(self, at):
            return self.source.at[:, pl.ds(pl.multiple_of(at * self.share, LANES), self.share)]

        def place(self, at, x_at, i):
            return self.target.at[at, x_at, :, i * self.share : (i + 1) * self.share]

        def begin(self):
            self.own = keep(self.cut(z), self.place(z, x, 0), True)
            for k in range(1, Z):
                to = (z + k) % Z
                sends.start(True, self.cut(to), self.place(z, x, 0), self.sems.at[z, 0, 0], at_z(to))

        def over_x(self, at, i):
            place = self.place(at, x, i)
            for j in range(1, inner):
                sends.start(True, place, place, self.sems.at[at, j, i], at_x(j))

        def over_y(self, at, j):
            x_at = (x + inner - j) % inner
            for i in range(1, outer):
                sends.start(
                    True, self.place(at, x_at, 0), self.place(at, x_at, i),
                    self.sems.at[at, j, i], at_y(i),
                )

        def got(self, at, j, i):
            arrived(self.place(at, (x + inner - j) % inner, i), self.sems.at[at, j, i], at_c)

        def first(self, k):
            at = (z + Z - k) % Z
            if k == 0:
                self.own.wait()
            else:
                self.got(at, 0, 0)
            if self.x_first or self.whole:
                self.over_x(at, 0)
            if self.whole or not self.x_first:
                self.over_y(at, 0)

        def second(self, k):
            at = (z + Z - k) % Z
            if self.x_first:
                for j in range(1, inner):
                    self.got(at, j, 0)
                    if self.whole:
                        self.over_y(at, j)
            else:
                for i in range(1, outer):
                    self.got(at, 0, i)

        def finish(self, k):
            if self.whole:
                at = (z + Z - k) % Z
                for j in range(inner):
                    for i in range(1, outer):
                        self.got(at, j, i)

    lines = [Line(0, xy, xy_to), Line(1, gates_own, gates_to), Line(2, out, out_to)]
    planes = [
        Plane(0, gate, gate_to, True, True),
        Plane(1, up, up_to, False, False),
        Plane(2, down, down_to, True, False),
    ]

    me = s * wt + w
    keep(vectors, vectors_to.at[me])

    def vector_copy(i):
        return pltpu.make_async_remote_copy(
            src_ref=vectors, dst_ref=vectors_to.at[me],
            send_sem=vector_sems.at[0, i], recv_sem=vector_sems.at[1, me],
            device_id={"seq": i // wt, "wt": i % wt}, device_id_type=MESH,
        )

    def vector_send(i, carried):
        pl.when(i != me)(lambda: vector_copy(i).start())
        return carried

    def tokens_begin():
        keep(tokens, tokens_to.at[w])
        sends.start(True, tokens, tokens_to.at[w], rows_sems.at[w], at_c)
        for i in range(1, outer):
            sends.start(True, tokens, tokens_to.at[w], rows_sems.at[w], at_y(i))

    def tokens_step():
        for i in range(1, outer):
            at = (y + outer - i) % outer * C + c
            arrived(tokens_to.at[at], rows_sems.at[at], at_c)
            sends.start(True, tokens_to.at[at], tokens_to.at[at], rows_sems.at[at], at_c)

    def tokens_finish():
        for i in range(outer):
            at = (y + outer - i) % outer * C + 1 - c
            arrived(tokens_to.at[at], rows_sems.at[at], at_c)

    to_seq, to_wt = me % seq, me // seq
    from_me = w * seq + s
    turn = pltpu.make_async_remote_copy(
        src_ref=gates, dst_ref=gates_own, send_sem=turn_sems.at[0], recv_sem=turn_sems.at[1],
        device_id={"seq": to_seq, "wt": to_wt}, device_id_type=MESH,
    )
    stay = pltpu.make_async_copy(gates, gates_own, turn_sems.at[2])
    here_too = from_me == me

    pl.when(jnp.logical_not(here_too))(turn.start)
    pl.when(here_too)(stay.start)
    lines[0].begin()
    tokens_begin()

    @pl.when(jnp.logical_not(here_too))
    def _():
        arrived(gates_own, turn_sems.at[1], at_c)

    pl.when(here_too)(stay.wait)
    lines[1].begin()
    lines[2].begin_z()
    lax.fori_loop(0, seq * wt, vector_send, 0)
    for k in range(1, Z):
        lines[1].step(k)
        lines[0].step(k)
        if k == 1:
            tokens_step()
    lines[2].begin_x()
    for k in range(1, Z):
        lines[2].step(k)
        if k == Z - 2:
            planes[0].begin()
            planes[2].begin()
            planes[1].begin()
    for k in range(Z):
        planes[0].first(k)
    for k in range(Z):
        planes[2].first(k)
    keep(grads, group.place(0, z, z))
    group.begin()
    for k in range(Z):
        planes[1].first(k)
        planes[0].second(k)
    for k in range(1, Z):
        group.step(k)
    group.finish()

    for line in lines:
        line.finish()
    tokens_finish()
    for k in range(Z):
        planes[1].second(k)
        planes[2].second(k)
        planes[0].finish(k)

    def vector_wait(i, carried):
        @pl.when(i != me)
        def _():
            vector_copy(i).wait_send()
            arrived(vectors_to.at[i], vector_sems.at[1, i], at_c)

        return carried

    pl.when(jnp.logical_not(here_too))(turn.wait_send)
    lax.fori_loop(0, seq * wt, vector_wait, 0)
    sends.finish()
    for waited, copy in here:
        if not waited:
            copy.wait()


def gather_all(tokens, grads, vectors, gates, xy, out, gate, up, down):
    inner, outer = sizes()
    seq, wt = Z * inner, outer * C

    def buffer(*shape, like):
        return jax.ShapeDtypeStruct(shape, like.dtype)

    def plane(weight):
        rows, columns = weight.shape
        return buffer(Z, inner, rows, outer * columns // Z, like=weight)

    shapes = (
        buffer(wt, *tokens.shape, like=tokens),
        buffer(C, Z, *grads.shape, like=grads),
        buffer(seq * wt, *vectors.shape, like=vectors),
        buffer(Z, inner, *gates.shape, like=gates),
        buffer(Z, inner, *xy.shape, like=xy),
        buffer(Z, inner, *out.shape, like=out),
        plane(gate),
        plane(up),
        plane(down),
    )
    copies = 3 * (2 + inner + (Z - 1) * 2 * inner) + 3 * (Z - 1 + Z * (inner + 2 * outer + inner * outer))
    copies += 2 * outer + 3 + 4 * Z
    dma = pltpu.SemaphoreType.DMA
    return pl.pallas_call(
        functools.partial(gather_kernel, (inner, outer)),
        out_shape=shapes,
        in_specs=[pl.BlockSpec(memory_space=pl.ANY)] * 9,
        out_specs=[pl.BlockSpec(memory_space=pl.ANY)] * 9,
        scratch_shapes=[
            pltpu.VMEM(gates.shape, gates.dtype),
            dma((copies,)),
            dma((16,)),
            dma((3, Z, inner)),
            dma((3, Z, inner, outer)),
            dma((wt,)),
            dma((2, seq * wt)),
            dma((3,)),
            dma((C, Z)),
        ],
        compiler_params=pltpu.CompilerParams(collective_id=0, has_side_effects=True),
        name="gather_all",
    )(tokens, grads, vectors, gates, xy, out, gate, up, down)


class Place:
    def __init__(self, shape):
        self.inner, self.outer = shape
        self.s, self.w = lax.axis_index("seq"), lax.axis_index("wt")
        self.z, self.x = self.s // self.inner, self.s % self.inner
        self.y, self.c = self.w // C, self.w % C
        self.at_c = {"seq": self.s, "wt": self.y * C + 1 - self.c}
        self.z_up, self.z_down = jnp.minimum(self.z + 1, Z - 1), jnp.maximum(self.z - 1, 0)

    def at_z(self, to):
        return {"seq": to * self.inner + self.x, "wt": self.w}

    def at_x(self, by):
        return {"seq": self.z * self.inner + (self.x + by) % self.inner, "wt": self.w}

    def at_y(self, by):
        return {"seq": self.s, "wt": (self.y + self.outer + by) % self.outer * C + self.c}

    def greet_all(self):
        barrier = pltpu.get_barrier_semaphore()
        wt = self.outer * C
        count = Z * self.inner * wt

        def signal(i, carried):
            @pl.when(i != self.s * wt + self.w)
            def _():
                pl.semaphore_signal(
                    barrier, inc=1, device_id={"seq": i // wt, "wt": i % wt}, device_id_type=MESH
                )

            return carried

        lax.fori_loop(0, count, signal, 0)
        pl.semaphore_wait(barrier, count - 1)

    def greet(self):
        barrier = pltpu.get_barrier_semaphore()
        devices = [self.at_c]
        devices += [self.at_z((self.z + k) % Z) for k in range(1, Z)]
        devices += [self.at_x(j) for j in range(1, self.inner)]
        devices += [self.at_y(i) for i in range(1, self.outer)]
        for device in devices:
            pl.semaphore_signal(barrier, inc=1, device_id=device, device_id_type=MESH)
        pl.semaphore_wait(barrier, len(devices))


def each_rows(count, step, body):
    def run(i, carried):
        body(pl.ds(pl.multiple_of(i * step, step), step))
        return carried

    lax.fori_loop(0, count // step, run, 0)


class WtRows:
    def __init__(self, me, sends, source, target, sems):
        self.me, self.sends, self.source, self.target, self.sems = me, sends, source, target, sems

    def begin(self):
        me = self.me
        for device in [me.at_y(i) for i in range(1, me.outer)] + [me.at_c]:
            self.sends.start(True, self.source, self.target.at[me.w], self.sems.at[me.w], device)

    def step(self):
        me = self.me
        for i in range(1, me.outer):
            at = (me.y + me.outer - i) % me.outer * C + me.c
            arrived(self.target.at[at], self.sems.at[at], me.at_c)
            self.sends.start(True, self.target.at[at], self.target.at[at], self.sems.at[at], me.at_c)

    def finish(self):
        me = self.me
        for i in range(me.outer):
            at = (me.y + me.outer - i) % me.outer * C + 1 - me.c
            arrived(self.target.at[at], self.sems.at[at], me.at_c)


class GroupRows:
    def __init__(self, me, sends, source, target, sems):
        self.me, self.sends, self.source, self.target, self.sems = me, sends, source, target, sems

    def place(self, own, at, z_to):
        return self.target.at[own, (z_to - at + Z) % Z]

    def forward(self, at, source, there, way):
        me = self.me
        z_to = me.z_up if way > 0 else me.z_down
        room = me.z < Z - 1 if way > 0 else me.z > 0
        when = room if there is None else there & room
        self.sends.start(
            when, source, self.place(0, at, z_to), self.sems.at[0, at], me.at_z(z_to)
        )

    def begin(self):
        me = self.me
        self.forward(me.z, self.source, None, 1)
        self.forward(me.z, self.source, None, -1)
        self.sends.start(
            True, self.source, self.place(1, me.z, me.z), self.sems.at[1, me.z], me.at_c
        )

    def step(self, k):
        me = self.me
        for at, there, way in (
            (jnp.maximum(me.z - k, 0), me.z - k >= 0, 1),
            (jnp.minimum(me.z + k, Z - 1), me.z + k < Z, -1),
        ):
            place = self.place(0, at, me.z)

            @pl.when(there)
            def _(place=place, at=at):
                arrived(place, self.sems.at[0, at], me.at_c)

            self.forward(at, place, there, way)
            self.sends.start(there, place, self.place(1, at, me.z), self.sems.at[1, at], me.at_c)

    def finish(self):
        me = self.me
        for at in range(Z):
            arrived(self.place(1, at, me.z), self.sems.at[1, at], me.at_c)


def branch_kernel(
    shape, sent, own, tokens, gain, up_held, down_held, group_to, middle, up_to, down_to,
    own_v, c_in, y_out, y_in, low,
    send_sems, local_sems, c_sems, y_sems, group_sems, up_sems, down_sems,
):
    del up_held, down_held
    me = Place(shape)
    inner, outer = shape
    share = up_to.shape[3] // outer
    rows = tokens.shape[0]
    sends = Sends(send_sems)
    load = pltpu.make_async_copy(own, own_v, local_sems.at[0])
    load.start()
    me.greet()
    order = [(me.y + i) % outer for i in list(range(1, outer)) + [0]]
    for at in order:
        sends.start(True, sent.at[at], c_in.at[at], c_sems.at[at], me.at_c)

    def columns(held, x_at, i):
        return held.at[:, x_at, :, i * share : (i + 1) * share]

    for j in range(1, inner):
        for i in range(outer):
            place = columns(up_to, me.x, i)
            sends.start(True, place, place, up_sems.at[j - 1, i], me.at_x(j))
    load.wait()
    for i, at in enumerate(order):
        arrived(c_in.at[at], c_sems.at[at], me.at_c)
        if i < outer - 1:
            each_rows(rows, 16, lambda r, i=i, at=at: y_out.__setitem__(
                (i, r), (own_v[at, r] + c_in[at, r]).astype(BF16)))
            sends.start(True, y_out.at[i], y_in.at[i], y_sems.at[i], me.at_y(i + 1))
    for i in range(outer - 1):
        arrived(y_in.at[i], y_sems.at[i], me.at_c)
    for i in range(1, outer):
        for j in range(inner):
            x_at = (me.x + inner - j) % inner
            sends.start(
                True, columns(down_to, x_at, 0), columns(down_to, x_at, i),
                down_sems.at[i - 1, j], me.at_y(i),
            )

    def work(r):
        total = tokens[r].astype(F32) + own_v[me.y, r] + c_in[me.y, r]
        for i in range(outer - 1):
            total = total + y_in[i, r].astype(F32)
        inverse = lax.rsqrt(jnp.mean(total * total, axis=1, keepdims=True) + EPSILON)
        middle[r] = total
        low[r] = (total * inverse * gain[...]).astype(BF16)

    each_rows(rows, 16, work)
    keep = pltpu.make_async_copy(low, group_to.at[0, 0], local_sems.at[1])
    keep.start()
    group = GroupRows(me, sends, low, group_to, group_sems)
    group.begin()
    for k in range(1, Z):
        group.step(k)
    group.finish()
    for j in range(1, inner):
        for i in range(outer):
            x_at = (me.x + inner - j) % inner
            arrived(columns(up_to, x_at, i), up_sems.at[j - 1, i], me.at_c)
    for i in range(1, outer):
        for j in range(inner):
            x_at = (me.x + inner - j) % inner
            arrived(columns(down_to, x_at, i), down_sems.at[i - 1, j], me.at_c)
    sends.finish()
    keep.wait()


def branch_and_group(sent, own, tokens, gain, up, down):
    inner, outer = sizes()
    rows, width = tokens.shape
    dma = pltpu.SemaphoreType.DMA
    vmem, anywhere = pl.BlockSpec(memory_space=pltpu.VMEM), pl.BlockSpec(memory_space=pl.ANY)
    return pl.pallas_call(
        functools.partial(branch_kernel, (inner, outer)),
        out_shape=(
            jax.ShapeDtypeStruct((C, Z, rows, width), BF16),
            jax.ShapeDtypeStruct((rows, width), F32),
            jax.ShapeDtypeStruct(up.shape, up.dtype),
            jax.ShapeDtypeStruct(down.shape, down.dtype),
        ),
        in_specs=[anywhere, anywhere, vmem, vmem, anywhere, anywhere],
        out_specs=(anywhere, vmem, anywhere, anywhere),
        input_output_aliases={4: 2, 5: 3},
        scratch_shapes=[
            pltpu.VMEM((outer, rows, width), F32),
            pltpu.VMEM((outer, rows, width), F32),
            pltpu.VMEM((outer - 1, rows, width), BF16),
            pltpu.VMEM((outer - 1, rows, width), BF16),
            pltpu.VMEM((rows, width), BF16),
            dma((2 * outer + 3 + 4 * (Z - 1) + (inner - 1) * outer + inner * (outer - 1),)),
            dma((2,)),
            dma((outer,)),
            dma((outer - 1,)),
            dma((C, Z)),
            dma((inner - 1, outer)),
            dma((outer - 1, inner)),
        ],
        compiler_params=pltpu.CompilerParams(
            collective_id=1, has_side_effects=True, vmem_limit_bytes=40 * 1024 * 1024
        ),
        name="branch_and_group",
    )(sent, own, tokens, gain, up, down)


def line_order():
    order = []
    for k in [n for t in range(1, Z) for n in (t, Z - t)] + [0]:
        if k not in order:
            order.append(k)
    return order


def line_sum(me, sends, rows, term, ready, store, held, up, down, between=None):
    z = me.z

    def add(when, target, slot, k, received=None, came=0):
        def body(r):
            value = term(k, r)
            if received is not None:
                value = value + received[came, r].astype(F32)
            target[slot, r] = value.astype(BF16)

        pl.when(when)(lambda: each_rows(rows, 16, body))

    for t in range(1, Z):
        slot = t - 1
        for k, (out, into, sems), out_slot, has, when, to in (
            (t, up, slot, z > 0, (z <= t - 1) & (z < Z - 1), me.z_up),
            (Z - t, down, Z - 1 - t, z < Z - 1, (z >= Z - t) & (z > 0), me.z_down),
        ):
            pl.when(when)(lambda k=k: ready(k))
            if t == 1:
                add(when, out, out_slot, k)
            else:
                pl.when(when & has)(
                    lambda into=into, sems=sems, slot=slot: arrived(
                        into.at[slot - 1], sems.at[slot - 1], me.at_c
                    )
                )
                add(when & has, out, out_slot, k, into, slot - 1)
                add(when & jnp.logical_not(has), out, out_slot, k)
            sends.start(when, out.at[out_slot], into.at[slot], sems.at[slot], me.at_z(to))
        if between is not None:
            between(t)
    ready(0)
    each_rows(rows, 16, lambda r: store(r, term(0, r)))
    for (_, into, sems), has in ((up, z > 0), (down, z < Z - 1)):

        @pl.when(has)
        def _(into=into, sems=sems):
            arrived(into.at[Z - 2], sems.at[Z - 2], me.at_c)
            each_rows(rows, 16, lambda r: store(r, held(r) + into[Z - 2, r].astype(F32)))


class PlaneTerms:
    def __init__(self, me, sends, parts, over_x, blocks, scratch):
        self.me, self.sends, self.parts, self.over_x, self.blocks = me, sends, parts, over_x, blocks
        self.came, self.mine, self.sems, self.local_sems = scratch

    def begin(self):
        me = self.me
        if self.over_x:
            for j in range(1, me.inner):
                for i, part in enumerate(self.parts):
                    self.sends.start(
                        True, part.at[self.blocks, (me.x + j) % me.inner],
                        self.came.at[j - 1, i], self.sems.at[j - 1, i], me.at_x(j),
                    )
            pairs = [(part.at[self.blocks, me.x], self.mine.at[i]) for i, part in enumerate(self.parts)]
        else:
            for i in range(1, me.outer):
                self.sends.start(
                    True, self.parts[i].at[self.blocks], self.came.at[i - 1],
                    self.sems.at[0, i - 1], me.at_y(-i),
                )
            pairs = [(self.parts[0].at[self.blocks], self.mine)]
        self.loads = self.moved(pairs)

    def moved(self, pairs):
        copies = [
            pltpu.make_async_copy(source, target, self.local_sems.at[n])
            for n, (source, target) in enumerate(pairs)
        ]
        for copy in copies:
            copy.start()
        return copies

    def add(self):
        me = self.me
        if self.over_x:
            count, places = me.inner - 1, [(i,) for i in range(me.outer)]
        else:
            count, places = me.outer - 1, [()]
        for n in range(count):
            for place in places:
                sems = self.sems.at[n, place[0]] if place else self.sems.at[0, n]
                arrived(self.came.at[(n, *place)], sems, me.at_c)
        for copy in self.loads:
            copy.wait()
        shape = self.mine.shape[:2]

        def body(r):
            for first in range(shape[0]):
                for second in range(shape[1]):
                    total = self.mine[first, second, r].astype(F32)
                    for n in range(count):
                        total = total + self.came[n, first, second, r].astype(F32)
                    self.mine[first, second, r] = total.astype(BF16)

        each_rows(self.mine.shape[2], 16, body)

    def hand_on(self, kept, sent):
        me = self.me
        if self.over_x:
            pairs = [(self.mine.at[i], kept if i == 0 else sent(i - 1)) for i in range(me.outer)]
        else:
            pairs = [
                (self.mine.at[:, (me.x + j) % me.inner], kept if j == 0 else sent(j - 1))
                for j in range(me.inner)
            ]
        self.loads = self.moved(pairs)

    def second(self, into, sems):
        me = self.me
        for j in range(1, me.inner):
            self.sends.start(
                True, self.mine.at[:, (me.x + j) % me.inner], into.at[j - 1], sems.at[j - 1],
                me.at_x(j),
            )

    def add_second(self, into, sems, kept):
        me = self.me
        for j in range(1, me.inner):
            arrived(into.at[j - 1], sems.at[j - 1], me.at_c)

        def body(r):
            for first in range(self.mine.shape[0]):
                total = self.mine[first, me.x, r].astype(F32)
                for j in range(1, me.inner):
                    total = total + into[j - 1, first, r].astype(F32)
                self.mine[first, me.x, r] = total.astype(BF16)

        each_rows(self.mine.shape[2], 16, body)
        self.loads = self.moved([(self.mine.at[:, me.x], kept)])

    def finish(self):
        for copy in self.loads:
            copy.wait()


def middle_kernel(shape, *refs):
    outer = shape[1]
    sent, own, middle, grads, gain, feed_sent, feed_own = refs[:7]
    parts = refs[7 : 7 + 3 * outer]
    rows_to, d_middle, gain_grad, block_out = refs[7 + 3 * outer : 11 + 3 * outer]
    targets = refs[11 + 3 * outer : 14 + 3 * outer]
    scratch = refs[14 + 3 * outer :]
    middle_body(
        shape, sent, own, middle, grads, gain, feed_sent, feed_own, parts, targets,
        rows_to, d_middle, gain_grad, block_out, scratch[:9], scratch[9:18],
        [scratch[18 + 4 * n : 22 + 4 * n] for n in range(4)], *scratch[34:],
    )


class PairSum:
    def __init__(self, me, sends, sent, own, scratch):
        self.me, self.sends, self.sent = me, sends, sent
        (
            self.held, self.c_in, up_out, up_in, down_out, down_in,
            self.c_sems, up_sems, down_sems,
        ) = scratch
        self.up, self.down = (up_out, up_in, up_sems), (down_out, down_in, down_sems)

    def begin(self):
        for k in line_order():
            self.sends.start(
                True, self.sent.at[k], self.c_in.at[k], self.c_sems.at[k], self.me.at_c
            )

    def run(self, between=None):
        def ready(k):
            arrived(self.c_in.at[k], self.c_sems.at[k], self.me.at_c)

        def term(k, r):
            return self.held[k, r] + self.c_in[k, r].astype(F32)

        def store(r, value):
            self.held[0, r] = value

        line_sum(
            self.me, self.sends, self.held.shape[1], term, ready, store,
            lambda r: self.held[0, r], self.up, self.down, between,
        )


def plane_units(me, sends, parts, scratch):
    outer = me.outer
    gate, up, down = (parts[n * outer : (n + 1) * outer] for n in range(3))
    every, low, high = slice(0, Z), slice(0, Z // 2), slice(Z // 2, Z)
    return [
        PlaneTerms(me, sends, gate, True, every, scratch[0]),
        PlaneTerms(me, sends, up, False, every, scratch[1]),
        PlaneTerms(me, sends, down, True, low, scratch[2]),
        PlaneTerms(me, sends, down, False, high, scratch[3]),
    ]


def middle_body(
    shape, sent, own, middle, grads, gain, feed_sent, feed_own, parts, targets,
    rows_to, d_middle, gain_grad, block_out, sum_scratch, feed_scratch, unit_scratch, low,
    up_in, send_sems, local_sems, rows_sems, up_sems,
):
    me = Place(shape)
    rows = middle.shape[0]
    sends = Sends(send_sems)
    total = PairSum(me, sends, sent, own, sum_scratch)
    feed = PairSum(me, sends, feed_sent, feed_own, feed_scratch)
    load = pltpu.make_async_copy(own, total.held, local_sems.at[0])
    feed_load = pltpu.make_async_copy(feed_own, feed.held, local_sems.at[2])
    load.start()
    me.greet()
    total.begin()
    units = plane_units(me, sends, parts, unit_scratch)
    units_to, units_y, units_x = targets
    for unit in units:
        unit.begin()
    feed_load.start()
    load.wait()
    total.run()
    own_v = total.held
    gain_grad[...] = jnp.zeros_like(gain_grad)

    def work(r):
        values = middle[r]
        inverse = lax.rsqrt(jnp.mean(values * values, axis=1, keepdims=True) + EPSILON)
        normed = values * inverse
        d_normed = own_v[0, r]
        gain_grad[...] += d_normed * normed
        scaled = d_normed * gain[...]
        passed = inverse * (scaled - normed * jnp.mean(scaled * normed, axis=1, keepdims=True))
        total = grads[r].astype(F32) + passed
        d_middle[r] = total
        low[r] = total.astype(BF16)

    each_rows(rows, 16, work)
    keep = pltpu.make_async_copy(low, rows_to.at[me.w], local_sems.at[1])
    keep.start()
    gather = WtRows(me, sends, low, rows_to, rows_sems)
    gather.begin()
    feed.begin()
    feed_load.wait()
    half, extra = Z // 2, slice(Z, Z + Z // 2)

    def between(t):
        if t == 1:
            units[0].add()
            units[0].hand_on(units_to.at[0], lambda i: units_y.at[i, 0:Z])
        if t == 2:
            units[1].add()
            units[1].second(up_in, up_sems)
        if t == 3:
            units[2].add()
            units[2].hand_on(units_to.at[2, 0:half], lambda i: units_y.at[i, extra])
            units[3].add()
            units[3].hand_on(units_to.at[2, half:Z], lambda j: units_x.at[j])

    feed.run(between)
    each_rows(rows, 16, lambda r: block_out.__setitem__(
        r, (middle[r] + feed.held[0, r]).astype(BF16)))
    gather.step()
    gather.finish()
    units[1].add_second(up_in, up_sems, units_to.at[1])
    for unit in units:
        unit.finish()
    sends.finish()
    keep.wait()


def middle_and_rows(sent, own, middle, grads, gain, feed_sent, feed_own, parts):
    inner, outer = sizes()
    rows, width = middle.shape
    unit_rows, share = parts[0].shape[2:]
    block = (unit_rows, share)
    targets = [
        jax.ShapeDtypeStruct((*shape, *block), BF16)
        for shape in ((3, Z), (outer - 1, Z + Z // 2), (inner - 1, Z // 2))
    ]
    unit_copies = 2 * (inner - 1) * outer + 2 * (outer - 1) + (inner - 1)
    pair_scratch = [pltpu.VMEM((Z, rows, width), F32), pltpu.VMEM((Z, rows, width), BF16)]
    pair_scratch += [pltpu.VMEM((Z - 1, rows, width), BF16)] * 4
    dma = pltpu.SemaphoreType.DMA
    pair_scratch += [dma((Z,)), dma((Z - 1,)), dma((Z - 1,))]
    unit_scratch = []
    for came, mine in (
        ((inner - 1, outer, Z), (outer, Z)),
        ((outer - 1, Z, inner), (Z, inner)),
        ((inner - 1, outer, Z // 2), (outer, Z // 2)),
        ((outer - 1, Z // 2, inner), (Z // 2, inner)),
    ):
        unit_scratch += [pltpu.VMEM((*came, *block), BF16), pltpu.VMEM((*mine, *block), BF16)]
        unit_scratch += [dma((inner - 1, outer)), dma((max(inner, outer),))]
    vmem, anywhere = pl.BlockSpec(memory_space=pltpu.VMEM), pl.BlockSpec(memory_space=pl.ANY)
    return pl.pallas_call(
        functools.partial(middle_kernel, (inner, outer)),
        out_shape=(
            jax.ShapeDtypeStruct((outer * C, rows, width), BF16),
            jax.ShapeDtypeStruct((rows, width), F32),
            jax.ShapeDtypeStruct((16, width), F32),
            jax.ShapeDtypeStruct((rows, width), BF16),
            *targets,
        ),
        in_specs=[anywhere, anywhere, vmem, vmem, vmem] + [anywhere] * (2 + 3 * outer),
        out_specs=(anywhere, vmem, vmem, vmem) + (anywhere,) * 3,
        scratch_shapes=pair_scratch * 2
        + unit_scratch
        + [
            pltpu.VMEM((rows, width), BF16),
            pltpu.VMEM((inner - 1, Z, *block), BF16),
            dma((2 * (Z + 2 * (Z - 1)) + 2 * outer + unit_copies,)),
            dma((3,)),
            dma((outer * C,)),
            dma((inner - 1,)),
        ],
        compiler_params=pltpu.CompilerParams(
            collective_id=2, has_side_effects=True, vmem_limit_bytes=60 * 1024 * 1024
        ),
        name="middle_and_rows",
    )(sent, own, middle, grads, gain, feed_sent, feed_own, *parts)


class RowsSum:
    def __init__(self, me, sends, terms, total, scratch, sems):
        self.me, self.sends, self.terms, self.total = me, sends, terms, total
        self.own, self.x_in, *ways = scratch
        self.own_sems, self.x_sems, up_sems, down_sems = sems
        self.up, self.down = (*ways[:2], up_sems), (*ways[2:], down_sems)

    def load(self):
        me = self.me
        self.loads = []
        for k in range(Z):
            self.loads.append(
                pltpu.make_async_copy(
                    self.terms.at[(me.z + Z - k) % Z, me.x], self.own.at[k], self.own_sems.at[k]
                )
            )
            self.loads[k].start()

    def begin(self, turns):
        me = self.me
        for turn in turns:
            if turn == Z - 1:
                k = 0
            else:
                k = (jnp.minimum(me.z, Z - 1 - me.z) + turn) % (Z - 1) + 1
                k = jnp.where(me.z < Z // 2, k, Z - k)
            at = (me.z + Z - k) % Z
            for j in range(1, me.inner):
                self.sends.start(
                    True, self.terms.at[at, (me.x + j) % me.inner], self.x_in.at[j - 1, k],
                    self.x_sems.at[j - 1, k], me.at_x(j),
                )

    def run(self, between=None):
        me = self.me

        def ready(k):
            self.loads[k].wait()
            for j in range(1, me.inner):
                arrived(self.x_in.at[j - 1, k], self.x_sems.at[j - 1, k], me.at_c)

        def term(k, r):
            value = self.own[k, r].astype(F32)
            for j in range(1, me.inner):
                value = value + self.x_in[j - 1, k, r].astype(F32)
            return value

        def store(r, value):
            self.total[r] = value

        line_sum(
            me, self.sends, self.total.shape[0], term, ready, store, lambda r: self.total[r],
            self.up, self.down, between,
        )


class ProductsSum(RowsSum):
    def __init__(self, me, sends, factors, total, scratch, sems):
        self.me, self.sends, self.total = me, sends, total
        self.factors = factors
        self.held, self.x_in, out, up_in, down_in, *self.lefts = scratch
        self.own_sems, self.x_sems, up_sems, down_sems = sems
        self.up, self.down = (out, up_in, up_sems), (out, down_in, down_sems)

    def load(self):
        self.loads = []
        for n, (left, _) in enumerate(self.factors):
            copy = pltpu.make_async_copy(left, self.lefts[n], self.own_sems.at[n])
            copy.start()
            self.loads.append(copy)

    def begin(self, turns):
        me = self.me
        while self.loads:
            self.loads.pop().wait()
        rows, span = self.total.shape[0], self.held.shape[1]
        for turn in turns:
            if turn == Z - 1:
                k = 0
            else:
                k = (jnp.minimum(me.z, Z - 1 - me.z) + turn) % (Z - 1) + 1
                k = jnp.where(me.z < Z // 2, k, Z - k)
            at = (me.z + Z - k) % Z

            def tile(i, carried, k=k, at=at):
                first = 0
                down = pl.ds(pl.multiple_of(i * LANES, LANES), LANES)
                across = pl.ds(pl.multiple_of(at * span + i * LANES, LANES), LANES)
                for n, (_, rights) in enumerate(self.factors):
                    left = self.lefts[n][:, across]
                    for right in rights:
                        columns = slice(first, first + right.shape[1])
                        self.held[k, down, columns] = contract_rows(left, right[...]).astype(BF16)
                        first += right.shape[1]
                return carried

            lax.fori_loop(0, span // LANES, tile, 0)
            for j in range(1, me.inner):
                part = pl.ds(pl.multiple_of((me.x + j) % me.inner * rows, 16), rows)
                self.sends.start(
                    True, self.held.at[k, part], self.x_in.at[j - 1, k], self.x_sems.at[j - 1, k],
                    me.at_x(j),
                )

    def run(self, between=None):
        me = self.me
        rows = self.total.shape[0]

        def ready(k):
            for j in range(1, me.inner):
                arrived(self.x_in.at[j - 1, k], self.x_sems.at[j - 1, k], me.at_c)

        def term(k, r):
            mine = pl.ds(pl.multiple_of(me.x * rows + r.start, 16), r.size)
            value = self.held[k, mine].astype(F32)
            for j in range(1, me.inner):
                value = value + self.x_in[j - 1, k, r].astype(F32)
            return value

        def store(r, value):
            self.total[r] = value

        line_sum(
            me, self.sends, rows, term, ready, store, lambda r: self.total[r],
            self.up, self.down, between,
        )


def sums_kernel(shape, *refs):
    inner, outer = shape
    units, units_y, units_x, normed_rows_one, branch_rows, narrow, sent, own = refs[:8]
    d_x, d_y, mixed, tokens, gain, d_middle, gain_two_grad, vectors = refs[8:16]
    units_to, wide_to, narrow_to, tokens_grad, gains, vectors_to = refs[16:22]
    refs = refs[22:]
    wide_scratch, narrow_scratch = refs[:7], refs[7:13]
    (own_v, c_in, y_out, y_in, parts_out, parts_in, gains_v, vec_in) = refs[13:21]
    refs = refs[2:]
    (send_sems, local_sems, c_sems, y_sems, all_sems, vec_sems) = refs[19:25]
    wide_sems, narrow_sems = refs[25:29], refs[29:33]
    units_v, units_y_in, units_x_in, unit_sems, units_y_sems, units_x_sems = refs[33:]
    share = units.shape[3]
    me = Place(shape)
    rows = tokens.shape[0]
    sends = Sends(send_sems)
    load = pltpu.make_async_copy(own, own_v, local_sems.at[0])
    load.start()
    units_load = pltpu.make_async_copy(units, units_v, local_sems.at[1])
    units_load.start()
    me.greet_all()

    order = [(me.y + i) % outer for i in list(range(1, outer)) + [0]]
    for at in order:
        sends.start(True, sent.at[at], c_in.at[at], c_sems.at[at], me.at_c)
    narrow_sum = RowsSum(me, sends, narrow, narrow_to, narrow_scratch, narrow_sems)
    factors = [(normed_rows_one, [d_x, d_y]), (branch_rows, [mixed])]
    wide_sum = ProductsSum(me, sends, factors, wide_to, wide_scratch, wide_sems)
    narrow_sum.load()
    wide_sum.load()
    narrow_sum.begin(range(Z))

    def columns(n, at):
        return units_to.at[n, :, pl.ds(pl.multiple_of(at * share, LANES), share)]

    low, high, extra = slice(0, Z // 2), slice(Z // 2, Z), slice(Z, Z + Z // 2)
    every = slice(0, Z)

    def units_begin_y():
        for n, blocks in enumerate((every, extra)):
            for i in range(1, outer):
                sends.start(
                    True, units_y.at[i - 1, blocks], units_y_in.at[i - 1, blocks],
                    units_y_sems.at[i - 1, n], me.at_y(-i),
                )

    def units_begin_x():
        for j in range(1, inner):
            sends.start(
                True, units_x.at[j - 1], units_x_in.at[j - 1], units_x_sems.at[j - 1], me.at_x(j)
            )

    kept = []

    def unit_add(n, blocks, came, came_blocks, sems, count):
        for i in range(count):
            arrived(came.at[i, came_blocks], sems.at[i], me.at_c)

        def body(r):
            for at in range(blocks.stop - blocks.start):
                total = units_v[n, blocks.start + at, r].astype(F32)
                for i in range(count):
                    total = total + came[i, came_blocks.start + at, r].astype(F32)
                units_v[n, blocks.start + at, r] = total.astype(BF16)

        each_rows(units_v.shape[2], 16, body)

    def unit_pass_on(n):
        copy = pltpu.make_async_copy(units_v.at[n, me.z], columns(n, me.z), local_sems.at[2 + n])
        copy.start()
        kept.append(copy)
        for k in range(1, Z):
            to = (me.z + k) % Z
            sends.start(
                True, units_v.at[n, to], columns(n, me.z), unit_sems.at[n, me.z], me.at_z(to)
            )

    def unit_gate():
        unit_add(0, every, units_y_in, every, units_y_sems.at[:, 0], outer - 1)
        unit_pass_on(0)

    def unit_down():
        unit_add(2, low, units_y_in, extra, units_y_sems.at[:, 1], outer - 1)
        unit_add(2, high, units_x_in, low, units_x_sems, inner - 1)
        unit_pass_on(2)


    def units_finish():
        for n in range(3):
            for k in range(1, Z):
                at = (me.z + Z - k) % Z
                arrived(columns(n, at), unit_sems.at[n, at], me.at_c)
        for copy in kept:
            copy.wait()

    def exchange(held, into, sems, first, devices):
        for n, device in enumerate(devices):
            sends.start(True, held, into.at[first + n], sems.at[first + n], device)

    def gathered(held, into, sems, first, devices):
        for n, _ in enumerate(devices):
            arrived(into.at[first + n], sems.at[first + n], me.at_c)
        total = into[first]
        for n in range(1, len(devices)):
            total = total + into[first + n]
        return held[...] + total

    z_stage = [me.at_z((me.z + k) % Z) for k in range(1, Z)]
    x_stage = [me.at_x(j) for j in range(1, inner)]

    devices = Z * inner * outer * C
    wt = outer * C
    here = me.s * wt + me.w
    width = tokens.shape[1]
    channels = width // devices

    def gains_cut():
        for i in range(devices):
            first = i * channels // LANES * LANES
            first = min(first, width - 2 * LANES)
            window = gains_v[:, first : first + 2 * LANES]
            turn = i * channels - first
            if turn:
                window = pltpu.roll(window, 2 * LANES - turn, 1)
            parts_out[i] = window[:, :LANES]

    def gains_copy(i):
        return pltpu.make_async_remote_copy(
            src_ref=parts_out.at[i], dst_ref=parts_in.at[here],
            send_sem=all_sems.at[0, i], recv_sem=all_sems.at[1, here],
            device_id={"seq": i // wt, "wt": i % wt}, device_id_type=MESH,
        )

    def gains_send(i, carried):
        pl.when(i != here)(lambda: gains_copy(i).start())
        return carried

    def gains_add(i, carried):
        @pl.when(i != here)
        def _():
            gains_copy(i).wait_send()
            arrived(parts_in.at[i], all_sems.at[1, i], me.at_c)
            gains[...] += parts_in[i]

        return carried

    exchange(vectors, vec_in, vec_sems, 0, x_stage)
    units_begin_x()

    units_begin_y()
    units_load.wait()
    unit_pass_on(1)

    load.wait()
    for i, at in enumerate(order):
        arrived(c_in.at[at], c_sems.at[at], me.at_c)
        if i < outer - 1:
            each_rows(rows, 16, lambda r, i=i, at=at: y_out.__setitem__(
                (i, r), (own_v[at, r] + c_in[at, r].astype(F32)).astype(BF16)))
            sends.start(True, y_out.at[i], y_in.at[i], y_sems.at[i], me.at_y(i + 1))
    vectors_to[0] = gathered(vectors, vec_in, vec_sems, 0, x_stage)
    exchange(vectors_to.at[0], vec_in, vec_sems, len(x_stage), z_stage)
    narrow_sum.run()
    vectors_to[1] = gathered(vectors_to.at[0], vec_in, vec_sems, len(x_stage), z_stage)
    wide_sum.begin(range(1))
    unit_gate()
    wide_sum.begin(range(1, 2))
    unit_down()
    wide_sum.begin(range(2, Z))

    def work(r):
        d_normed = own_v[me.y, r] + c_in[me.y, r].astype(F32)
        for i in range(outer - 1):
            d_normed = d_normed + y_in[i, r].astype(F32)
        stream = tokens[r].astype(F32)
        inverse = lax.rsqrt(jnp.mean(stream * stream, axis=1, keepdims=True) + EPSILON)
        normed = stream * inverse
        part = d_normed * normed
        gains_v[0:8] += part[0:8] + part[8:16]
        scaled = d_normed * gain[...]
        passed = inverse * (scaled - normed * jnp.mean(scaled * normed, axis=1, keepdims=True))
        tokens_grad[r] = (d_middle[r] + passed).astype(BF16)

    def between(t):
        if t == 1:
            for i in range(outer - 1):
                arrived(y_in.at[i], y_sems.at[i], me.at_c)
            gains_v[...] = jnp.zeros_like(gains_v)
            each_rows(rows, 16, work)
            gains_v[8:16] = gain_two_grad[0:8] + gain_two_grad[8:16]
            gains_cut()
            lax.fori_loop(0, devices, gains_send, 0)

    wide_sum.run(between)
    gains[...] = parts_out[here]
    lax.fori_loop(0, devices, gains_add, 0)
    units_finish()
    sends.finish()


def last_sums(
    units, units_y, units_x, normed_one, branch_rows, narrow, sent, own,
    d_x, d_y, mixed, tokens, gain, d_middle, gain_two_grad, vectors,
):
    inner, outer = sizes()
    rows, width = tokens.shape
    dma = pltpu.SemaphoreType.DMA
    vmem, anywhere = pl.BlockSpec(memory_space=pltpu.VMEM), pl.BlockSpec(memory_space=pl.ANY)

    def scratch(terms):
        one = terms.shape[2:]
        return [pltpu.VMEM((Z, *one), BF16), pltpu.VMEM((inner - 1, Z, *one), BF16)] + [
            pltpu.VMEM((Z - 1, *one), BF16)
        ] * 4

    devices = Z * inner * outer * C
    copies = 2 * outer - 1 + 2 * (Z * (inner - 1) + 2 * (Z - 1))
    copies += (inner - 1) + (Z - 1) + 2 * (outer - 1) + 2 * (inner - 1) + 3 * (Z - 1)
    _, _, unit_rows, share = units.shape
    block = (unit_rows, d_x.shape[1] + d_y.shape[1] + mixed.shape[1])
    line_sems = [dma((Z,)), dma((inner - 1, Z)), dma((Z - 1,)), dma((Z - 1,))]
    return pl.pallas_call(
        functools.partial(sums_kernel, (inner, outer)),
        out_shape=(
            jax.ShapeDtypeStruct((3, unit_rows, Z * share), BF16),
            jax.ShapeDtypeStruct(block, F32),
            jax.ShapeDtypeStruct(narrow.shape[2:], F32),
            jax.ShapeDtypeStruct((rows, width), BF16),
            jax.ShapeDtypeStruct((16, LANES), F32),
            jax.ShapeDtypeStruct((2, *vectors.shape), F32),
        ),
        in_specs=[anywhere] * 8 + [vmem] * 8,
        out_specs=(anywhere,) + (vmem,) * 5,
        scratch_shapes=[
            pltpu.VMEM((Z, inner * block[0], block[1]), BF16),
            pltpu.VMEM((inner - 1, Z, *block), BF16),
        ]
        + [pltpu.VMEM((Z - 1, *block), BF16)] * 3
        + [pltpu.VMEM(normed_one.shape, BF16), pltpu.VMEM(branch_rows.shape, BF16)]
        + scratch(narrow)
        + [
            pltpu.VMEM((outer, rows, width), F32),
            pltpu.VMEM((outer, rows, width), BF16),
            pltpu.VMEM((outer - 1, rows, width), BF16),
            pltpu.VMEM((outer - 1, rows, width), BF16),
            pltpu.VMEM((devices, 16, LANES), F32),
            pltpu.VMEM((devices, 16, LANES), F32),
            pltpu.VMEM((16, width), F32),
            pltpu.VMEM((inner - 1 + Z - 1, *vectors.shape), F32),
            dma((copies,)),
            dma((5,)),
            dma((outer,)),
            dma((outer - 1,)),
            dma((2, devices)),
            dma((inner - 1 + Z - 1,)),
        ]
        + line_sems * 2
        + [
            pltpu.VMEM(units.shape, BF16),
            pltpu.VMEM(units_y.shape, BF16),
            pltpu.VMEM(units_x.shape, BF16),
            dma((3, Z)),
            dma((outer - 1, 2)),
            dma((inner - 1,)),
        ],
        compiler_params=pltpu.CompilerParams(
            collective_id=5, has_side_effects=True, vmem_limit_bytes=60 * 1024 * 1024
        ),
        name="last_sums",
    )(
        units, units_y, units_x, normed_one, branch_rows, narrow, sent, own,
        d_x, d_y, mixed, tokens, gain, d_middle, gain_two_grad, vectors,
    )


def scan_kernel(backward, factors, inflows, states, entered, products, ends, ends_in, carry, send_sems, arrivals):
    seq = ends_in.shape[0]
    s = lax.axis_index("seq")
    rows, width = factors.shape
    barrier = pltpu.get_barrier_semaphore()

    def device(at):
        return {"seq": at, "wt": lax.axis_index("wt")}

    def greet(i, carried):
        @pl.when(i != s)
        def _():
            pl.semaphore_signal(barrier, inc=1, device_id=device(i), device_id_type=MESH)

        return carried

    lax.fori_loop(0, seq, greet, 0)
    group = 8
    at_row = lax.broadcasted_iota(jnp.int32, (group, width), 0)

    def step(i, carried):
        held, product = carried
        i = rows // group - 1 - i if backward else i
        where = pl.ds(pl.multiple_of(i * group, group), group)
        factor, inflow = factors[where, :], inflows[where, :]
        for by in (1, 2, 4):
            inside = at_row < group - by if backward else at_row >= by
            turn = group - by if backward else by
            inflow = factor * jnp.where(inside, pltpu.roll(inflow, turn, 0), 0.0) + inflow
            factor = factor * jnp.where(inside, pltpu.roll(factor, turn, 0), 1.0)
        inflow = inflow + factor * held
        factor = factor * product
        states[where, :] = inflow
        products[where, :] = factor
        last = slice(0, 1) if backward else slice(group - 1, group)
        return inflow[last], factor[last]

    held, product = lax.fori_loop(
        0, rows // group, step, (jnp.zeros((1, width), F32), jnp.ones((1, width), F32))
    )
    ends[0:1] = product
    ends[1:2] = held
    pl.semaphore_wait(barrier, seq - 1)

    def copy_to(i):
        return pltpu.make_async_remote_copy(
            src_ref=ends, dst_ref=ends_in.at[s], send_sem=send_sems.at[i], recv_sem=arrivals.at[s],
            device_id=device(i), device_id_type=MESH,
        )

    def later(i):
        return i < s if backward else i > s

    def send(i, carried):
        pl.when(later(i))(lambda: copy_to(i).start())
        return carried

    lax.fori_loop(0, seq, send, 0)
    carry[...] = jnp.zeros_like(carry)

    def receive(n, carried):
        i = seq - 1 - n if backward else n

        @pl.when(jnp.logical_not(later(i)) & (i != s))
        def _():
            arrived(ends_in.at[i], arrivals.at[i], device((s + 1) % seq))
            carry[0:1] = ends_in[i, 0:1] * carry[0:1] + ends_in[i, 1:2]

        return carried

    lax.fori_loop(0, seq, receive, 0)
    entering = carry[0:1]
    entered[...] = entering

    def spread(i, carried):
        where = pl.ds(pl.multiple_of(i * group, group), group)
        states[where, :] += products[where, :] * entering
        return carried

    lax.fori_loop(0, rows // group, spread, 0)

    def sent(i, carried):
        pl.when(later(i))(lambda: copy_to(i).wait_send())
        return carried

    lax.fori_loop(0, seq, sent, 0)


def full_scan(factor, inflow, backward):
    seq = lax.axis_size("seq")
    rows, width = factor.shape
    vmem = pl.BlockSpec(memory_space=pltpu.VMEM)
    return pl.pallas_call(
        functools.partial(scan_kernel, backward),
        out_shape=(
            jax.ShapeDtypeStruct((rows, width), F32),
            jax.ShapeDtypeStruct((1, width), F32),
        ),
        in_specs=[vmem, vmem],
        out_specs=(vmem, vmem),
        scratch_shapes=[
            pltpu.VMEM((rows, width), F32),
            pltpu.VMEM((8, width), F32),
            pltpu.VMEM((seq, 8, width), F32),
            pltpu.VMEM((8, width), F32),
            pltpu.SemaphoreType.DMA((seq,)),
            pltpu.SemaphoreType.DMA((seq,)),
        ],
        compiler_params=pltpu.CompilerParams(
            collective_id=4 if backward else 3,
            has_side_effects=True,
            vmem_limit_bytes=32 * 1024 * 1024,
        ),
        name="scan_back" if backward else "scan_ahead",
    )(factor, inflow)


def recurrence_terms(decay_pre, input_pre, decay_log, conv_float):
    log_decay = -DECAY_SCALE * jax.nn.softplus(-decay_log) * jax.nn.sigmoid(decay_pre)
    return (
        jnp.exp(log_decay),
        jnp.sqrt(-jnp.expm1(2.0 * log_decay)) * jax.nn.sigmoid(input_pre) * conv_float,
    )


def normed_rows(stream):
    inverse = lax.rsqrt(jnp.mean(stream * stream, axis=1, keepdims=True) + EPSILON)
    return stream * inverse, inverse


def per_device(
    tokens,
    norm1_gain,
    x_weight,
    y_weight,
    conv_weight,
    conv_bias,
    decay_gate_weight,
    decay_bias,
    input_gate_weight,
    input_bias,
    decay_param,
    out_weight,
    norm2_gain,
    gate_weight,
    up_weight,
    down_weight,
    out_grad,
):
    seq, wt = lax.axis_size("seq"), lax.axis_size("wt")
    inner, outer = sizes()
    z, x, y, c = places()
    w = lax.axis_index("wt")
    rows_dev, width = tokens.shape
    weight_rows, lru_cols = x_weight.shape
    chunk, block = decay_gate_weight.shape
    half = block // 2
    full = lru_cols - half
    taps_count = conv_weight.shape[1]
    reach = taps_count - 1
    hidden_cols = gate_weight.shape[1]

    def turned(value, axis):
        return jnp.where(c == 0, value, jnp.roll(value, -half, axis))

    def turned_back(value, axis):
        return jnp.where(c == 0, value, jnp.roll(value, half, axis))

    def in_order(own, partner, axis):
        return jnp.where(
            c == 0,
            jnp.concatenate([own, partner], axis),
            jnp.concatenate([partner, own], axis),
        )

    vectors = jnp.stack(
        [v.astype(F32) for v in (norm1_gain, norm2_gain, conv_bias, decay_bias, input_bias)]
        + [decay_param]
        + [conv_weight[:, k].astype(F32) for k in range(taps_count)]
    )
    vectors = jnp.pad(vectors, ((0, -vectors.shape[0] % 8), (0, -chunk % LANES)))

    across = [(i, i % seq * wt + i // seq) for i in range(seq * wt)]
    gates = jnp.concatenate([decay_gate_weight, input_gate_weight], axis=1)

    def padded(weight):
        share = -(-hidden_cols // (Z * LANES)) * LANES
        return jnp.pad(weight, ((0, 0), (0, Z * share - hidden_cols)))

    xy_unit = jnp.concatenate([turned(x_weight, 1), turned(y_weight, 1)], axis=1)
    (
        group_tokens, grad_group, vectors, gate_all, xy_kernel, out_kernel,
        gate_kernel, up_kernel, down_kernel,
    ) = gather_all(
        tokens, out_grad, vectors, gates, xy_unit, turned(out_weight, 1),
        padded(gate_weight), padded(up_weight), padded(down_weight),
    )
    group_tokens = group_tokens.reshape(-1, width)
    grad_group = grad_group.reshape(-1, width)
    vectors = jnp.moveaxis(vectors[:, : 6 + taps_count, :chunk], 0, 1).reshape(6 + taps_count, -1)
    gain_one, gain_two = vectors[0], vectors[1]
    own_vectors = turned(
        lax.dynamic_slice(vectors[2:], (0, w * lru_cols), (taps_count + 4, lru_cols)), 1
    )
    tap_bias, decay_shift, input_shift, decay_log = (own_vectors[i] for i in range(4))
    taps = own_vectors[4:]
    xy_kernel = xy_kernel.reshape(width, -1)
    out_kernel = out_kernel.reshape(width, -1)
    gate_kernel = gate_kernel.reshape(width, -1)
    gate_all = turned(gate_all.reshape(lru_cols, 2 * block), 0)
    partner_rows = c_swap(gate_all[full:])
    shared_rows = in_order(gate_all[full:], partner_rows, 0)

    stream = tokens.astype(F32)
    group_normed, _ = normed_rows(group_tokens.astype(F32))
    group_one = (group_normed * gain_one).astype(BF16)
    rows = group_one.shape[0]
    xy = multiply(group_one, xy_kernel)
    x_branch = xy[:, :lru_cols].astype(BF16)
    y_before = xy[:, lru_cols:]
    y_gated, gelu_y_back = jax.vjp(gelu_tanh, y_before)
    rim = lax.ppermute(x_branch[rows - reach :], "seq", [(i, i + 1) for i in range(seq - 1)])
    extended = jnp.concatenate([rim, x_branch], axis=0).astype(F32)
    conv_low = (
        tap_bias
        + sum(taps[k] * extended[reach - k : reach - k + rows] for k in range(taps_count))
    ).astype(BF16)
    shared_conv = in_order(conv_low[:, full:], c_swap(conv_low[:, full:]), 1)
    heads = full // block

    def of_head(value, i):
        return value[:, i * block : (i + 1) * block]

    pre_parts = [
        multiply(of_head(conv_low, i), gate_all[i * block : (i + 1) * block]) for i in range(heads)
    ]
    shared_columns = jnp.where(
        c == 0,
        jnp.concatenate([shared_rows[:, :half], shared_rows[:, block : block + half]], axis=1),
        jnp.concatenate([shared_rows[:, half:block], shared_rows[:, block + half :]], axis=1),
    )
    shared_pre = multiply(shared_conv, shared_columns)
    decay_pre = decay_shift + jnp.concatenate(
        [part[:, :block] for part in pre_parts] + [shared_pre[:, :half]], axis=1
    )
    input_pre = input_shift + jnp.concatenate(
        [part[:, block:] for part in pre_parts] + [shared_pre[:, half:]], axis=1
    )
    (retain, inflow), terms_back = jax.vjp(
        recurrence_terms, decay_pre, input_pre, decay_log, conv_low.astype(F32)
    )
    states, state_in = full_scan(retain, inflow, False)
    before = jnp.concatenate([state_in, states[:-1]])
    lru_low = states.astype(BF16).astype(F32)
    mixed_rows = (lru_low * y_gated).astype(BF16)
    mixed_parts = mixed_rows.reshape(outer, C, rows_dev, lru_cols)

    def branch_of(at):
        part = pick(mixed_parts, at, 1).reshape(outer * rows_dev, lru_cols)
        return contract_last(part, out_kernel).reshape(outer, rows_dev, width)

    group_two, middle, up_kernel, down_kernel = branch_and_group(
        branch_of(1 - c), branch_of(c), tokens, gain_two[None], up_kernel, down_kernel
    )
    up_kernel = up_kernel.reshape(width, -1)
    down_kernel = down_kernel.reshape(width, -1)
    group_two = group_two.reshape(C * Z * rows_dev, width)

    gate_pre = multiply(group_two, gate_kernel)
    up_pre = multiply(group_two, up_kernel)
    active, gelu_gate_back = jax.vjp(gelu_tanh, gate_pre)
    hidden = (active * up_pre).astype(BF16)

    d_hidden = multiply(grad_group, down_kernel)
    d_up = (d_hidden * active).astype(BF16)
    d_gate = gelu_gate_back(d_hidden * up_pre)[0].astype(BF16)
    half_rows = Z * rows_dev

    def d_normed_of(part):
        total = contract_last(d_gate[part], gate_kernel) + contract_last(d_up[part], up_kernel)
        return total.reshape(Z, rows_dev, width)

    def terms_of(left_side, right_side):
        share = right_side.shape[1] // outer
        return [
            contract_rows(left_side, right_side[:, i * share : (i + 1) * share])
            .astype(BF16)
            .reshape(Z, inner, weight_rows, share)
            for i in range(outer)
        ]

    gate_terms = terms_of(group_two, d_gate)
    up_terms = terms_of(group_two, d_up)
    down_terms = terms_of(grad_group, hidden)
    def feed_of(part):
        return contract_last(hidden[part], down_kernel).reshape(Z, rows_dev, width)

    branch_rows, d_middle, gain_two_grad, block_out, units, units_y, units_x = middle_and_rows(
        d_normed_of(slice(half_rows, None)).astype(BF16),
        d_normed_of(slice(0, half_rows)),
        middle,
        out_grad,
        gain_two[None],
        feed_of(slice(half_rows, None)).astype(BF16),
        feed_of(slice(0, half_rows)),
        gate_terms + up_terms + down_terms,
    )
    branch_rows = branch_rows.reshape(-1, width)

    d_mixed = multiply(branch_rows, out_kernel)
    d_lru = (d_mixed * y_gated).astype(BF16).astype(F32)
    d_y = gelu_y_back(d_mixed * lru_low)[0].astype(BF16)
    passed, passed_in = full_scan(retain, retain * d_lru, True)
    d_total = d_lru + jnp.concatenate([passed[1:], passed_in])
    d_decay_pre, d_input_pre, decay_log_grad, d_conv_direct = terms_back(
        (d_total * before, d_total)
    )
    d_decay_low, d_input_low = d_decay_pre.astype(BF16), d_input_pre.astype(BF16)
    own_low = jnp.concatenate([d_decay_low[:, full:], d_input_low[:, full:]], axis=1)
    partner_low = c_swap(own_low)
    shared_low = jnp.concatenate(
        [
            in_order(own_low[:, :half], partner_low[:, :half], 1),
            in_order(own_low[:, half:], partner_low[:, half:], 1),
        ],
        axis=1,
    )
    lows = [
        jnp.concatenate([of_head(d_decay_low, i), of_head(d_input_low, i)], axis=1)
        for i in range(heads)
    ]
    d_conv = d_conv_direct + jnp.concatenate(
        [contract_last(lows[i], gate_all[i * block : (i + 1) * block]) for i in range(heads)]
        + [contract_last(shared_low, gate_all[full:])],
        axis=1,
    )
    gates_grad = jnp.concatenate(
        [contract_rows(of_head(conv_low, i), lows[i]) for i in range(heads)]
        + [contract_rows(conv_low[:, full:], shared_low)]
    )
    ahead = lax.ppermute(d_conv[:reach], "seq", [(i + 1, i) for i in range(seq - 1)])
    d_extended = jnp.concatenate([d_conv, ahead], axis=0)
    d_x_branch = sum(taps[k] * d_extended[k : k + rows] for k in range(taps_count)).astype(BF16)
    dx_parts = d_x_branch.reshape(outer, C, rows_dev, lru_cols)
    dy_parts = d_y.reshape(outer, C, rows_dev, lru_cols)

    def d_normed_one_of(at):
        dx, dy = (
            pick(parts, at, 1).reshape(outer * rows_dev, lru_cols) for parts in (dx_parts, dy_parts)
        )
        total = contract_last(dx, xy_kernel[:, :lru_cols]) + contract_last(
            dy, xy_kernel[:, lru_cols:]
        )
        return total.reshape(outer, rows_dev, width)

    narrow = turned_back(gates_grad, 0).astype(BF16).reshape(Z, inner, chunk, 2 * block)
    narrow = jnp.pad(narrow, ((0, 0), (0, 0), (0, -chunk % 16), (0, 0)))
    own_sums = jnp.stack(
        [jnp.sum(d_conv, axis=0), jnp.sum(d_decay_pre, axis=0), jnp.sum(d_input_pre, axis=0)]
        + [decay_log_grad]
        + [jnp.sum(d_conv * extended[reach - k : reach - k + rows], axis=0) for k in range(taps_count)],
    )
    own_sums = turned_back(own_sums, 1)
    placed, wide, narrow, tokens_grad, gains, own_sums = last_sums(
        units, units_y, units_x, group_one, branch_rows, narrow,
        d_normed_one_of(1 - c).astype(BF16), d_normed_one_of(c),
        turned_back(d_x_branch, 1), turned_back(d_y, 1), turned_back(mixed_rows, 1),
        tokens, gain_one[None], d_middle, gain_two_grad, own_sums,
    )
    weight_grads = [wide[:, n * lru_cols : (n + 1) * lru_cols] for n in range(3)]
    gate_grad, up_grad, down_grad = (placed[n, :, :hidden_cols].astype(F32) for n in range(3))
    gains = gains.reshape(2, 8, LANES).sum(axis=1)[:, :chunk]
    sums = lax.dynamic_slice(own_sums[1], (0, lax.axis_index("seq") * chunk), (taps_count + 4, chunk))
    own_sums = jnp.concatenate([narrow[:chunk], sums.T], axis=1)
    own_sums = lax.ppermute(own_sums, ("seq", "wt"), [(to, at) for at, to in across])
    sums = own_sums[:, 2 * block :]
    return (
        block_out,
        tokens_grad,
        gains[0],
        weight_grads[0],
        weight_grads[1],
        sums[:, 4:],
        sums[:, 0],
        own_sums[:, :block],
        sums[:, 1],
        own_sums[:, block : 2 * block],
        sums[:, 2],
        sums[:, 3],
        weight_grads[2],
        gains[1],
        gate_grad,
        up_grad,
        down_grad,
    )


def solution(mesh):
    rows, both, lone = P(("seq", "wt"), None), P("seq", "wt"), P(("seq", "wt"))
    in_specs = (
        rows, lone, both, both, rows, lone, rows, lone, rows, lone, lone,
        both, lone, both, both, both, rows,
    )
    out_specs = (
        rows, rows, lone, both, both, rows, lone, rows, lone, rows, lone, lone,
        both, lone, both, both, both,
    )
    return jax.shard_map(
        per_device, mesh=mesh, in_specs=in_specs, out_specs=out_specs, check_vma=False
    )
```

```python
import functools

import jax
import jax.numpy as jnp
from jax import lax
from jax.experimental import pallas as pl
from jax.experimental.pallas import tpu as pltpu
from jax.sharding import PartitionSpec as P

EPSILON = 1e-06
DECAY_SCALE = 8.0
Z = 4
C = 2
LANES = 128
F32 = jnp.float32
BF16 = jnp.bfloat16
MESH = pl.DeviceIdType.MESH


def gelu_tanh(values):
    return jax.nn.gelu(values, approximate=True)


def sizes():
    return lax.axis_size("seq") // Z, lax.axis_size("wt") // C


def places():
    inner, outer = sizes()
    s, w = lax.axis_index("seq"), lax.axis_index("wt")
    return s // inner, s % inner, w // C, w % C


def z_move(value, by, senders):
    inner, _ = sizes()
    pairs = [(z * inner + x, (z + by) % Z * inner + x) for z in senders for x in range(inner)]
    return lax.ppermute(value, "seq", pairs)


def c_swap(value):
    _, outer = sizes()
    pairs = [(y * C + c, y * C + 1 - c) for y in range(outer) for c in range(C)]
    return lax.ppermute(value, "wt", pairs)


def line_scatter(parts):
    up = down = None
    for step in range(1, Z):
        rising = parts[step] if up is None else parts[step] + up
        falling = parts[Z - step] if down is None else parts[Z - step] + down
        up = z_move(rising.astype(BF16), 1, range(0, step)).astype(F32)
        down = z_move(falling.astype(BF16), -1, range(Z - step, Z)).astype(F32)
    return parts[0] + up + down


def pick(value, index, axis):
    return lax.dynamic_index_in_dim(value, index, axis, keepdims=False)


def contract_last(left_side, right_side):
    return lax.dot_general(
        left_side, right_side, (((1,), (1,)), ((), ())), preferred_element_type=F32
    )


def contract_rows(left_side, right_side):
    return lax.dot_general(
        left_side, right_side, (((0,), (0,)), ((), ())), preferred_element_type=F32
    )


def multiply(left_side, right_side):
    return jnp.dot(left_side, right_side, preferred_element_type=F32)


class Sends:
    def __init__(self, sems):
        self.sems, self.started = sems, []

    def start(self, when, source, target, arrival, device):
        copy = pltpu.make_async_remote_copy(
            src_ref=source,
            dst_ref=target,
            send_sem=self.sems.at[len(self.started)],
            recv_sem=arrival,
            device_id=device,
            device_id_type=MESH,
        )
        if when is True:
            copy.start()
        else:
            pl.when(when)(copy.start)
        self.started.append((when, copy))

    def finish(self):
        for when, copy in self.started:
            if when is True:
                copy.wait_send()
            else:
                pl.when(when)(copy.wait_send)


def arrived(target, arrival, device):
    pltpu.make_async_remote_copy(
        src_ref=target, dst_ref=target, send_sem=arrival, recv_sem=arrival,
        device_id=device, device_id_type=MESH,
    ).wait_recv()


def gather_kernel(shape, *refs):
    inner, outer = shape
    (tokens, grads, vectors, gates, xy, out, gate, up, down) = refs[:9]
    (grads_to, vectors_to, gates_to, xy_to, out_to, gate_to, up_to, down_to) = refs[9:17]
    rows_one, xy_one = refs[17:19]
    gates_own, send_sems, local_sems, line_sems, plane_sems, rows_sems = refs[19:25]
    vector_sems, turn_sems, group_sems, tokens_to, xy_v, vectors_v, spread, read_sems = refs[25:]
    seq, wt = Z * inner, outer * C
    s, w = lax.axis_index("seq"), lax.axis_index("wt")
    z, x, y, c = s // inner, s % inner, w // C, w % C
    sends = Sends(send_sems)
    group = GroupRows(Place(shape), sends, grads, grads_to, group_sems)
    here, counter = [], iter(range(16))

    def at_z(to):
        return {"seq": to * inner + x, "wt": w}

    def at_x(by):
        return {"seq": z * inner + (x + by) % inner, "wt": w}

    def at_y(by):
        return {"seq": s, "wt": (y + by) % outer * C + c}

    at_c = {"seq": s, "wt": y * C + 1 - c}

    def keep(source, target, waited=False):
        copy = pltpu.make_async_copy(source, target, local_sems.at[next(counter)])
        copy.start()
        here.append((waited, copy))
        return copy

    barrier = pltpu.get_barrier_semaphore()

    def greet(i, carried):
        @pl.when(i != s * wt + w)
        def _():
            pl.semaphore_signal(
                barrier, inc=1, device_id={"seq": i // wt, "wt": i % wt}, device_id_type=MESH
            )

        return carried

    lax.fori_loop(0, seq * wt, greet, 0)
    pl.semaphore_wait(barrier, seq * wt - 1)

    class Line:
        def __init__(self, index, source, target):
            self.source, self.target = source, target
            self.sems = line_sems.at[index]

        def forward(self, block, at, up_when, down_when):
            place = self.target.at[at, x]
            arrival = self.sems.at[at, x]
            sends.start(up_when, block, place, arrival, at_z(jnp.minimum(z + 1, Z - 1)))
            sends.start(down_when, block, place, arrival, at_z(jnp.maximum(z - 1, 0)))
            return place, arrival

        def across(self, when, block, at):
            for j in range(1, inner):
                sends.start(when, block, self.target.at[at, x], self.sems.at[at, x], at_x(j))

        def begin_z(self):
            keep(self.source, self.target.at[z, x])
            self.forward(self.source, z, z < Z - 1, z > 0)

        def begin_x(self):
            self.across(True, self.source, z)

        def begin(self):
            self.begin_z()
            self.begin_x()

        def step(self, k):
            for at, there, up_when, down_when in (
                (jnp.maximum(z - k, 0), z - k >= 0, (z - k >= 0) & (z < Z - 1), None),
                (jnp.minimum(z + k, Z - 1), z + k < Z, None, (z + k < Z) & (z > 0)),
            ):
                place, arrival = self.target.at[at, x], self.sems.at[at, x]

                @pl.when(there)
                def _(place=place, arrival=arrival):
                    arrived(place, arrival, at_c)

                if up_when is not None:
                    sends.start(up_when, place, place, arrival, at_z(jnp.minimum(z + 1, Z - 1)))
                else:
                    sends.start(down_when, place, place, arrival, at_z(jnp.maximum(z - 1, 0)))
                self.across(there, place, at)

        def finish(self):
            for at in range(Z):
                for j in range(1, inner):
                    from_x = (x + inner - j) % inner
                    arrived(self.target.at[at, from_x], self.sems.at[at, from_x], at_c)

    class Plane:
        def __init__(self, index, source, target, x_first, whole):
            self.source, self.target, self.x_first, self.whole = source, target, x_first, whole
            self.share = source.shape[1] // Z
            self.sems = plane_sems.at[index]

        def cut(self, at):
            return self.source.at[:, pl.ds(pl.multiple_of(at * self.share, LANES), self.share)]

        def place(self, at, x_at, i):
            return self.target.at[at, x_at, :, i * self.share : (i + 1) * self.share]

        def begin(self):
            self.own = keep(self.cut(z), self.place(z, x, 0), True)
            for k in range(1, Z):
                to = (z + k) % Z
                sends.start(True, self.cut(to), self.place(z, x, 0), self.sems.at[z, 0, 0], at_z(to))

        def over_x(self, at, i):
            place = self.place(at, x, i)
            for j in range(1, inner):
                sends.start(True, place, place, self.sems.at[at, j, i], at_x(j))

        def over_y(self, at, j):
            x_at = (x + inner - j) % inner
            for i in range(1, outer):
                sends.start(
                    True, self.place(at, x_at, 0), self.place(at, x_at, i),
                    self.sems.at[at, j, i], at_y(i),
                )

        def got(self, at, j, i):
            arrived(self.place(at, (x + inner - j) % inner, i), self.sems.at[at, j, i], at_c)

        def first(self, k):
            at = (z + Z - k) % Z
            if k == 0:
                self.own.wait()
            else:
                self.got(at, 0, 0)
            if self.x_first or self.whole:
                self.over_x(at, 0)
            if self.whole or not self.x_first:
                self.over_y(at, 0)

        def second(self, k):
            at = (z + Z - k) % Z
            if self.x_first:
                for j in range(1, inner):
                    self.got(at, j, 0)
                    if self.whole:
                        self.over_y(at, j)
            else:
                for i in range(1, outer):
                    self.got(at, 0, i)

        def finish(self, k):
            if self.whole:
                at = (z + Z - k) % Z
                for j in range(inner):
                    for i in range(1, outer):
                        self.got(at, j, i)

    lines = [Line(0, xy, xy_to), Line(1, gates_own, gates_to), Line(2, out, out_to)]
    planes = [
        Plane(0, gate, gate_to, True, True),
        Plane(1, up, up_to, False, False),
        Plane(2, down, down_to, True, False),
    ]

    me = s * wt + w
    keep(vectors, vectors_to.at[me])

    def vector_copy(i):
        return pltpu.make_async_remote_copy(
            src_ref=vectors, dst_ref=vectors_to.at[me],
            send_sem=vector_sems.at[0, i], recv_sem=vector_sems.at[1, me],
            device_id={"seq": i // wt, "wt": i % wt}, device_id_type=MESH,
        )

    def vector_send(i, carried):
        pl.when(i != me)(lambda: vector_copy(i).start())
        return carried

    def tokens_begin():
        keep(tokens, tokens_to.at[w])
        sends.start(True, tokens, tokens_to.at[w], rows_sems.at[w], at_c)
        for i in range(1, outer):
            sends.start(True, tokens, tokens_to.at[w], rows_sems.at[w], at_y(i))

    def tokens_step():
        for i in range(1, outer):
            at = (y + outer - i) % outer * C + c
            arrived(tokens_to.at[at], rows_sems.at[at], at_c)
            sends.start(True, tokens_to.at[at], tokens_to.at[at], rows_sems.at[at], at_c)

    def tokens_finish():
        for i in range(outer):
            at = (y + outer - i) % outer * C + 1 - c
            arrived(tokens_to.at[at], rows_sems.at[at], at_c)

    to_seq, to_wt = me % seq, me // seq
    from_me = w * seq + s
    turn = pltpu.make_async_remote_copy(
        src_ref=gates, dst_ref=gates_own, send_sem=turn_sems.at[0], recv_sem=turn_sems.at[1],
        device_id={"seq": to_seq, "wt": to_wt}, device_id_type=MESH,
    )
    stay = pltpu.make_async_copy(gates, gates_own, turn_sems.at[2])
    here_too = from_me == me

    pl.when(jnp.logical_not(here_too))(turn.start)
    pl.when(here_too)(stay.start)
    def vector_wait(i, carried):
        @pl.when(i != me)
        def _():
            vector_copy(i).wait_send()
            arrived(vectors_to.at[i], vector_sems.at[1, i], at_c)

        return carried

    def first_projection():
        lines[0].finish()
        tokens_finish()
        lax.fori_loop(0, seq * wt, vector_wait, 0)
        for copy in here_first:
            copy.wait()
        rows_each = xy.shape[0]
        copies = [pltpu.make_async_copy(vectors_to, vectors_v, read_sems.at[0])]
        for z_at in range(Z):
            for x_at in range(inner):
                n = z_at * inner + x_at
                copies.append(
                    pltpu.make_async_copy(
                        xy_to.at[z_at, x_at], xy_v.at[n * rows_each : (n + 1) * rows_each],
                        read_sems.at[1 + n],
                    )
                )
        for copy in copies:
            copy.start()
        copies[0].wait()
        width = tokens.shape[1]
        devices = seq * wt
        channels = width // devices
        spread[...] = jnp.zeros_like(spread)
        for i in range(devices):
            first = min(i * channels // LANES * LANES, width - 2 * LANES)
            turn = i * channels - first
            part = vectors_v[i, 0:8]
            part = jnp.concatenate([part, jnp.zeros_like(part)], axis=1)
            if turn:
                part = pltpu.roll(part, turn, 1)
            spread[:, first : first + 2 * LANES] += part
        gain = spread[0:1]
        count = tokens.shape[0]
        for at in range(wt):

            def norm(r, at=at):
                stream = tokens_to[at, r].astype(F32)
                inverse = lax.rsqrt(jnp.mean(stream * stream, axis=1, keepdims=True) + EPSILON)
                rows_one[pl.ds(pl.multiple_of(at * count + r.start, 16), 16)] = (
                    stream * inverse * gain
                ).astype(BF16)

            each_rows(count, 16, norm)
        for copy in copies[1:]:
            copy.wait()
        tile = 2 * LANES

        def project(n, carried):
            down = pl.ds(pl.multiple_of(n % wt * count, LANES), count)
            across = pl.ds(pl.multiple_of(n // wt * tile, tile), tile)
            xy_one[down, across] = multiply(rows_one[down], xy_v[:, across])
            return carried

        lax.fori_loop(0, wt * (xy_v.shape[1] // tile), project, 0)

    lines[0].begin()
    tokens_begin()
    here_first = [copy for _, copy in here]
    here.clear()

    @pl.when(jnp.logical_not(here_too))
    def _():
        arrived(gates_own, turn_sems.at[1], at_c)

    pl.when(here_too)(stay.wait)
    lines[1].begin()
    lines[2].begin_z()
    lax.fori_loop(0, seq * wt, vector_send, 0)
    for k in range(1, Z):
        lines[1].step(k)
        lines[0].step(k)
        if k == 1:
            tokens_step()
    lines[2].begin_x()
    for k in range(1, Z):
        lines[2].step(k)
        if k == Z - 2:
            planes[0].begin()
            planes[2].begin()
            planes[1].begin()
    for k in range(Z):
        planes[0].first(k)
    for k in range(Z):
        planes[2].first(k)
    keep(grads, group.place(0, z, z))
    group.begin()
    for k in range(Z):
        planes[1].first(k)
    for k in range(Z):
        planes[0].second(k)
    group.step(1)
    first_projection()
    for k in range(2, Z):
        group.step(k)
    group.finish()

    for line in lines[1:]:
        line.finish()
    for k in range(Z):
        planes[1].second(k)
        planes[2].second(k)
        planes[0].finish(k)

    pl.when(jnp.logical_not(here_too))(turn.wait_send)
    sends.finish()
    for waited, copy in here:
        if not waited:
            copy.wait()


def gather_all(tokens, grads, vectors, gates, xy, out, gate, up, down):
    inner, outer = sizes()
    seq, wt = Z * inner, outer * C

    def buffer(*shape, like):
        return jax.ShapeDtypeStruct(shape, like.dtype)

    def plane(weight):
        rows, columns = weight.shape
        return buffer(Z, inner, rows, outer * columns // Z, like=weight)

    shapes = (
        buffer(C, Z, *grads.shape, like=grads),
        buffer(seq * wt, *vectors.shape, like=vectors),
        buffer(Z, inner, *gates.shape, like=gates),
        buffer(Z, inner, *xy.shape, like=xy),
        buffer(Z, inner, *out.shape, like=out),
        plane(gate),
        plane(up),
        plane(down),
        buffer(wt * tokens.shape[0], tokens.shape[1], like=tokens),
        jax.ShapeDtypeStruct((wt * tokens.shape[0], xy.shape[1]), F32),
    )
    copies = 3 * (2 + inner + (Z - 1) * 2 * inner) + 3 * (Z - 1 + Z * (inner + 2 * outer + inner * outer))
    copies += 2 * outer + 3 + 4 * Z
    dma = pltpu.SemaphoreType.DMA
    return pl.pallas_call(
        functools.partial(gather_kernel, (inner, outer)),
        out_shape=shapes,
        in_specs=[pl.BlockSpec(memory_space=pl.ANY)] * 9,
        out_specs=[pl.BlockSpec(memory_space=pl.ANY)] * 8 + [pl.BlockSpec(memory_space=pltpu.VMEM)] * 2,
        scratch_shapes=[
            pltpu.VMEM(gates.shape, gates.dtype),
            dma((copies,)),
            dma((16,)),
            dma((3, Z, inner)),
            dma((3, Z, inner, outer)),
            dma((wt,)),
            dma((2, seq * wt)),
            dma((3,)),
            dma((C, Z)),
            pltpu.VMEM((wt, *tokens.shape), tokens.dtype),
            pltpu.VMEM((Z * inner * xy.shape[0], xy.shape[1]), xy.dtype),
            pltpu.VMEM((seq * wt, *vectors.shape), F32),
            pltpu.VMEM((8, tokens.shape[1]), F32),
            dma((1 + Z * inner,)),
        ],
        compiler_params=pltpu.CompilerParams(
            collective_id=0, has_side_effects=True, vmem_limit_bytes=40 * 1024 * 1024
        ),
        name="gather_all",
    )(tokens, grads, vectors, gates, xy, out, gate, up, down)


class Place:
    def __init__(self, shape):
        self.inner, self.outer = shape
        self.s, self.w = lax.axis_index("seq"), lax.axis_index("wt")
        self.z, self.x = self.s // self.inner, self.s % self.inner
        self.y, self.c = self.w // C, self.w % C
        self.at_c = {"seq": self.s, "wt": self.y * C + 1 - self.c}
        self.z_up, self.z_down = jnp.minimum(self.z + 1, Z - 1), jnp.maximum(self.z - 1, 0)

    def at_z(self, to):
        return {"seq": to * self.inner + self.x, "wt": self.w}

    def at_x(self, by):
        return {"seq": self.z * self.inner + (self.x + by) % self.inner, "wt": self.w}

    def at_y(self, by):
        return {"seq": self.s, "wt": (self.y + self.outer + by) % self.outer * C + self.c}

    def greet_all(self):
        barrier = pltpu.get_barrier_semaphore()
        wt = self.outer * C
        count = Z * self.inner * wt

        def signal(i, carried):
            @pl.when(i != self.s * wt + self.w)
            def _():
                pl.semaphore_signal(
                    barrier, inc=1, device_id={"seq": i // wt, "wt": i % wt}, device_id_type=MESH
                )

            return carried

        lax.fori_loop(0, count, signal, 0)
        pl.semaphore_wait(barrier, count - 1)

    def greet(self):
        barrier = pltpu.get_barrier_semaphore()
        devices = [self.at_c]
        devices += [self.at_z((self.z + k) % Z) for k in range(1, Z)]
        devices += [self.at_x(j) for j in range(1, self.inner)]
        devices += [self.at_y(i) for i in range(1, self.outer)]
        for device in devices:
            pl.semaphore_signal(barrier, inc=1, device_id=device, device_id_type=MESH)
        pl.semaphore_wait(barrier, len(devices))


def each_rows(count, step, body):
    def run(i, carried):
        body(pl.ds(pl.multiple_of(i * step, step), step))
        return carried

    lax.fori_loop(0, count // step, run, 0)


class WtRows:
    def __init__(self, me, sends, source, target, sems):
        self.me, self.sends, self.source, self.target, self.sems = me, sends, source, target, sems

    def begin(self):
        me = self.me
        for device in [me.at_y(i) for i in range(1, me.outer)] + [me.at_c]:
            self.sends.start(True, self.source, self.target.at[me.w], self.sems.at[me.w], device)

    def step(self):
        me = self.me
        for i in range(1, me.outer):
            at = (me.y + me.outer - i) % me.outer * C + me.c
            arrived(self.target.at[at], self.sems.at[at], me.at_c)
            self.sends.start(True, self.target.at[at], self.target.at[at], self.sems.at[at], me.at_c)

    def finish(self):
        me = self.me
        for i in range(me.outer):
            at = (me.y + me.outer - i) % me.outer * C + 1 - me.c
            arrived(self.target.at[at], self.sems.at[at], me.at_c)


class GroupRows:
    def __init__(self, me, sends, source, target, sems):
        self.me, self.sends, self.source, self.target, self.sems = me, sends, source, target, sems

    def place(self, own, at, z_to):
        return self.target.at[own, (z_to - at + Z) % Z]

    def forward(self, at, source, there, way):
        me = self.me
        z_to = me.z_up if way > 0 else me.z_down
        room = me.z < Z - 1 if way > 0 else me.z > 0
        when = room if there is None else there & room
        self.sends.start(
            when, source, self.place(0, at, z_to), self.sems.at[0, at], me.at_z(z_to)
        )

    def begin(self):
        me = self.me
        self.forward(me.z, self.source, None, 1)
        self.forward(me.z, self.source, None, -1)
        self.sends.start(
            True, self.source, self.place(1, me.z, me.z), self.sems.at[1, me.z], me.at_c
        )

    def step(self, k):
        me = self.me
        for at, there, way in (
            (jnp.maximum(me.z - k, 0), me.z - k >= 0, 1),
            (jnp.minimum(me.z + k, Z - 1), me.z + k < Z, -1),
        ):
            place = self.place(0, at, me.z)

            @pl.when(there)
            def _(place=place, at=at):
                arrived(place, self.sems.at[0, at], me.at_c)

            self.forward(at, place, there, way)
            self.sends.start(there, place, self.place(1, at, me.z), self.sems.at[1, at], me.at_c)

    def finish(self):
        me = self.me
        for at in range(Z):
            arrived(self.place(1, at, me.z), self.sems.at[1, at], me.at_c)


def branch_kernel(
    shape, sent, own, tokens, gain, up_held, down_held, group_to, middle, up_to, down_to,
    own_v, c_in, y_out, y_in, low,
    send_sems, local_sems, c_sems, y_sems, group_sems, up_sems, down_sems,
):
    del up_held, down_held
    me = Place(shape)
    inner, outer = shape
    share = up_to.shape[3] // outer
    rows = tokens.shape[0]
    sends = Sends(send_sems)
    load = pltpu.make_async_copy(own, own_v, local_sems.at[0])
    load.start()
    me.greet()
    order = [(me.y + i) % outer for i in list(range(1, outer)) + [0]]
    for at in order:
        sends.start(True, sent.at[at], c_in.at[at], c_sems.at[at], me.at_c)

    def columns(held, x_at, i):
        return held.at[:, x_at, :, i * share : (i + 1) * share]

    for j in range(1, inner):
        for i in range(outer):
            place = columns(up_to, me.x, i)
            sends.start(True, place, place, up_sems.at[j - 1, i], me.at_x(j))
    load.wait()
    for i, at in enumerate(order):
        arrived(c_in.at[at], c_sems.at[at], me.at_c)
        if i < outer - 1:
            each_rows(rows, 16, lambda r, i=i, at=at: y_out.__setitem__(
                (i, r), (own_v[at, r] + c_in[at, r]).astype(BF16)))
            sends.start(True, y_out.at[i], y_in.at[i], y_sems.at[i], me.at_y(i + 1))
    for i in range(outer - 1):
        arrived(y_in.at[i], y_sems.at[i], me.at_c)
    for i in range(1, outer):
        for j in range(inner):
            x_at = (me.x + inner - j) % inner
            sends.start(
                True, columns(down_to, x_at, 0), columns(down_to, x_at, i),
                down_sems.at[i - 1, j], me.at_y(i),
            )

    def work(r):
        total = tokens[r].astype(F32) + own_v[me.y, r] + c_in[me.y, r]
        for i in range(outer - 1):
            total = total + y_in[i, r].astype(F32)
        inverse = lax.rsqrt(jnp.mean(total * total, axis=1, keepdims=True) + EPSILON)
        middle[r] = total
        low[r] = (total * inverse * gain[...]).astype(BF16)

    each_rows(rows, 16, work)
    keep = pltpu.make_async_copy(low, group_to.at[0, 0], local_sems.at[1])
    keep.start()
    group = GroupRows(me, sends, low, group_to, group_sems)
    group.begin()
    for k in range(1, Z):
        group.step(k)
    group.finish()
    for j in range(1, inner):
        for i in range(outer):
            x_at = (me.x + inner - j) % inner
            arrived(columns(up_to, x_at, i), up_sems.at[j - 1, i], me.at_c)
    for i in range(1, outer):
        for j in range(inner):
            x_at = (me.x + inner - j) % inner
            arrived(columns(down_to, x_at, i), down_sems.at[i - 1, j], me.at_c)
    sends.finish()
    keep.wait()


def branch_and_group(sent, own, tokens, gain, up, down):
    inner, outer = sizes()
    rows, width = tokens.shape
    dma = pltpu.SemaphoreType.DMA
    vmem, anywhere = pl.BlockSpec(memory_space=pltpu.VMEM), pl.BlockSpec(memory_space=pl.ANY)
    return pl.pallas_call(
        functools.partial(branch_kernel, (inner, outer)),
        out_shape=(
            jax.ShapeDtypeStruct((C, Z, rows, width), BF16),
            jax.ShapeDtypeStruct((rows, width), F32),
            jax.ShapeDtypeStruct(up.shape, up.dtype),
            jax.ShapeDtypeStruct(down.shape, down.dtype),
        ),
        in_specs=[anywhere, anywhere, vmem, vmem, anywhere, anywhere],
        out_specs=(anywhere, vmem, anywhere, anywhere),
        input_output_aliases={4: 2, 5: 3},
        scratch_shapes=[
            pltpu.VMEM((outer, rows, width), F32),
            pltpu.VMEM((outer, rows, width), F32),
            pltpu.VMEM((outer - 1, rows, width), BF16),
            pltpu.VMEM((outer - 1, rows, width), BF16),
            pltpu.VMEM((rows, width), BF16),
            dma((2 * outer + 3 + 4 * (Z - 1) + (inner - 1) * outer + inner * (outer - 1),)),
            dma((2,)),
            dma((outer,)),
            dma((outer - 1,)),
            dma((C, Z)),
            dma((inner - 1, outer)),
            dma((outer - 1, inner)),
        ],
        compiler_params=pltpu.CompilerParams(
            collective_id=1, has_side_effects=True, vmem_limit_bytes=40 * 1024 * 1024
        ),
        name="branch_and_group",
    )(sent, own, tokens, gain, up, down)


def line_order():
    order = []
    for k in [n for t in range(1, Z) for n in (t, Z - t)] + [0]:
        if k not in order:
            order.append(k)
    return order


def line_sum(me, sends, rows, term, ready, store, held, up, down, between=None):
    z = me.z

    def add(when, target, slot, k, received=None, came=0):
        def body(r):
            value = term(k, r)
            if received is not None:
                value = value + received[came, r].astype(F32)
            target[slot, r] = value.astype(BF16)

        pl.when(when)(lambda: each_rows(rows, 16, body))

    for t in range(1, Z):
        slot = t - 1
        for k, (out, into, sems), out_slot, has, when, to in (
            (t, up, slot, z > 0, (z <= t - 1) & (z < Z - 1), me.z_up),
            (Z - t, down, Z - 1 - t, z < Z - 1, (z >= Z - t) & (z > 0), me.z_down),
        ):
            pl.when(when)(lambda k=k: ready(k))
            if t == 1:
                add(when, out, out_slot, k)
            else:
                pl.when(when & has)(
                    lambda into=into, sems=sems, slot=slot: arrived(
                        into.at[slot - 1], sems.at[slot - 1], me.at_c
                    )
                )
                add(when & has, out, out_slot, k, into, slot - 1)
                add(when & jnp.logical_not(has), out, out_slot, k)
            sends.start(when, out.at[out_slot], into.at[slot], sems.at[slot], me.at_z(to))
        if between is not None:
            between(t)
    ready(0)
    each_rows(rows, 16, lambda r: store(r, term(0, r)))
    for (_, into, sems), has in ((up, z > 0), (down, z < Z - 1)):

        @pl.when(has)
        def _(into=into, sems=sems):
            arrived(into.at[Z - 2], sems.at[Z - 2], me.at_c)
            each_rows(rows, 16, lambda r: store(r, held(r) + into[Z - 2, r].astype(F32)))


class PlaneTerms:
    def __init__(self, me, sends, parts, over_x, blocks, scratch):
        self.me, self.sends, self.parts, self.over_x, self.blocks = me, sends, parts, over_x, blocks
        self.came, self.mine, self.sems, self.local_sems = scratch

    def begin(self):
        me = self.me
        if self.over_x:
            for j in range(1, me.inner):
                for i, part in enumerate(self.parts):
                    self.sends.start(
                        True, part.at[self.blocks, (me.x + j) % me.inner],
                        self.came.at[j - 1, i], self.sems.at[j - 1, i], me.at_x(j),
                    )
            pairs = [(part.at[self.blocks, me.x], self.mine.at[i]) for i, part in enumerate(self.parts)]
        else:
            for i in range(1, me.outer):
                self.sends.start(
                    True, self.parts[i].at[self.blocks], self.came.at[i - 1],
                    self.sems.at[0, i - 1], me.at_y(-i),
                )
            pairs = [(self.parts[0].at[self.blocks], self.mine)]
        self.loads = self.moved(pairs)

    def moved(self, pairs):
        copies = [
            pltpu.make_async_copy(source, target, self.local_sems.at[n])
            for n, (source, target) in enumerate(pairs)
        ]
        for copy in copies:
            copy.start()
        return copies

    def add(self):
        me = self.me
        if self.over_x:
            count, places = me.inner - 1, [(i,) for i in range(me.outer)]
        else:
            count, places = me.outer - 1, [()]
        for n in range(count):
            for place in places:
                sems = self.sems.at[n, place[0]] if place else self.sems.at[0, n]
                arrived(self.came.at[(n, *place)], sems, me.at_c)
        for copy in self.loads:
            copy.wait()
        shape = self.mine.shape[:2]

        def body(r):
            for first in range(shape[0]):
                for second in range(shape[1]):
                    total = self.mine[first, second, r].astype(F32)
                    for n in range(count):
                        total = total + self.came[n, first, second, r].astype(F32)
                    self.mine[first, second, r] = total.astype(BF16)

        each_rows(self.mine.shape[2], 16, body)

    def hand_on(self, kept, sent):
        me = self.me
        if self.over_x:
            pairs = [(self.mine.at[i], kept if i == 0 else sent(i - 1)) for i in range(me.outer)]
        else:
            pairs = [
                (self.mine.at[:, (me.x + j) % me.inner], kept if j == 0 else sent(j - 1))
                for j in range(me.inner)
            ]
        self.loads = self.moved(pairs)

    def second(self, into, sems):
        me = self.me
        for j in range(1, me.inner):
            self.sends.start(
                True, self.mine.at[:, (me.x + j) % me.inner], into.at[j - 1], sems.at[j - 1],
                me.at_x(j),
            )

    def add_second(self, into, sems, kept):
        me = self.me
        for j in range(1, me.inner):
            arrived(into.at[j - 1], sems.at[j - 1], me.at_c)

        def body(r):
            for first in range(self.mine.shape[0]):
                total = self.mine[first, me.x, r].astype(F32)
                for j in range(1, me.inner):
                    total = total + into[j - 1, first, r].astype(F32)
                self.mine[first, me.x, r] = total.astype(BF16)

        each_rows(self.mine.shape[2], 16, body)
        self.loads = self.moved([(self.mine.at[:, me.x], kept)])

    def finish(self):
        for copy in self.loads:
            copy.wait()


def middle_kernel(shape, *refs):
    outer = shape[1]
    sent, own, middle, grads, gain, feed_sent, feed_own = refs[:7]
    parts = refs[7 : 7 + 3 * outer]
    rows_to, d_middle, gain_grad, block_out = refs[7 + 3 * outer : 11 + 3 * outer]
    targets = refs[11 + 3 * outer : 14 + 3 * outer]
    scratch = refs[14 + 3 * outer :]
    middle_body(
        shape, sent, own, middle, grads, gain, feed_sent, feed_own, parts, targets,
        rows_to, d_middle, gain_grad, block_out, scratch[:9], scratch[9:18],
        [scratch[18 + 4 * n : 22 + 4 * n] for n in range(4)], *scratch[34:],
    )


class PairSum:
    def __init__(self, me, sends, sent, own, scratch):
        self.me, self.sends, self.sent = me, sends, sent
        (
            self.held, self.c_in, up_out, up_in, down_out, down_in,
            self.c_sems, up_sems, down_sems,
        ) = scratch
        self.up, self.down = (up_out, up_in, up_sems), (down_out, down_in, down_sems)

    def begin(self):
        for k in line_order():
            self.sends.start(
                True, self.sent.at[k], self.c_in.at[k], self.c_sems.at[k], self.me.at_c
            )

    def run(self, between=None):
        def ready(k):
            arrived(self.c_in.at[k], self.c_sems.at[k], self.me.at_c)

        def term(k, r):
            return self.held[k, r] + self.c_in[k, r].astype(F32)

        def store(r, value):
            self.held[0, r] = value

        line_sum(
            self.me, self.sends, self.held.shape[1], term, ready, store,
            lambda r: self.held[0, r], self.up, self.down, between,
        )


def plane_units(me, sends, parts, scratch):
    outer = me.outer
    gate, up, down = (parts[n * outer : (n + 1) * outer] for n in range(3))
    every, low, high = slice(0, Z), slice(0, Z // 2), slice(Z // 2, Z)
    return [
        PlaneTerms(me, sends, gate, True, every, scratch[0]),
        PlaneTerms(me, sends, up, False, every, scratch[1]),
        PlaneTerms(me, sends, down, True, low, scratch[2]),
        PlaneTerms(me, sends, down, False, high, scratch[3]),
    ]


def middle_body(
    shape, sent, own, middle, grads, gain, feed_sent, feed_own, parts, targets,
    rows_to, d_middle, gain_grad, block_out, sum_scratch, feed_scratch, unit_scratch, low,
    up_in, send_sems, local_sems, rows_sems, up_sems,
):
    me = Place(shape)
    rows = middle.shape[0]
    sends = Sends(send_sems)
    total = PairSum(me, sends, sent, own, sum_scratch)
    feed = PairSum(me, sends, feed_sent, feed_own, feed_scratch)
    load = pltpu.make_async_copy(own, total.held, local_sems.at[0])
    feed_load = pltpu.make_async_copy(feed_own, feed.held, local_sems.at[2])
    load.start()
    me.greet()
    total.begin()
    units = plane_units(me, sends, parts, unit_scratch)
    units_to, units_y, units_x = targets
    for unit in units:
        unit.begin()
    feed_load.start()
    load.wait()
    total.run()
    own_v = total.held
    gain_grad[...] = jnp.zeros_like(gain_grad)

    def work(r):
        values = middle[r]
        inverse = lax.rsqrt(jnp.mean(values * values, axis=1, keepdims=True) + EPSILON)
        normed = values * inverse
        d_normed = own_v[0, r]
        gain_grad[...] += d_normed * normed
        scaled = d_normed * gain[...]
        passed = inverse * (scaled - normed * jnp.mean(scaled * normed, axis=1, keepdims=True))
        total = grads[r].astype(F32) + passed
        d_middle[r] = total
        low[r] = total.astype(BF16)

    each_rows(rows, 16, work)
    keep = pltpu.make_async_copy(low, rows_to.at[me.w], local_sems.at[1])
    keep.start()
    gather = WtRows(me, sends, low, rows_to, rows_sems)
    gather.begin()
    feed.begin()
    feed_load.wait()
    half, extra = Z // 2, slice(Z, Z + Z // 2)

    def between(t):
        if t == 1:
            units[0].add()
            units[0].hand_on(units_to.at[0], lambda i: units_y.at[i, 0:Z])
        if t == 2:
            units[1].add()
            units[1].second(up_in, up_sems)
        if t == 3:
            units[2].add()
            units[2].hand_on(units_to.at[2, 0:half], lambda i: units_y.at[i, extra])
            units[3].add()
            units[3].hand_on(units_to.at[2, half:Z], lambda j: units_x.at[j])

    feed.run(between)
    each_rows(rows, 16, lambda r: block_out.__setitem__(
        r, (middle[r] + feed.held[0, r]).astype(BF16)))
    gather.step()
    gather.finish()
    units[1].add_second(up_in, up_sems, units_to.at[1])
    for unit in units:
        unit.finish()
    sends.finish()
    keep.wait()


def middle_and_rows(sent, own, middle, grads, gain, feed_sent, feed_own, parts):
    inner, outer = sizes()
    rows, width = middle.shape
    unit_rows, share = parts[0].shape[2:]
    block = (unit_rows, share)
    targets = [
        jax.ShapeDtypeStruct((*shape, *block), BF16)
        for shape in ((3, Z), (outer - 1, Z + Z // 2), (inner - 1, Z // 2))
    ]
    unit_copies = 2 * (inner - 1) * outer + 2 * (outer - 1) + (inner - 1)
    pair_scratch = [pltpu.VMEM((Z, rows, width), F32), pltpu.VMEM((Z, rows, width), BF16)]
    pair_scratch += [pltpu.VMEM((Z - 1, rows, width), BF16)] * 4
    dma = pltpu.SemaphoreType.DMA
    pair_scratch += [dma((Z,)), dma((Z - 1,)), dma((Z - 1,))]
    unit_scratch = []
    for came, mine in (
        ((inner - 1, outer, Z), (outer, Z)),
        ((outer - 1, Z, inner), (Z, inner)),
        ((inner - 1, outer, Z // 2), (outer, Z // 2)),
        ((outer - 1, Z // 2, inner), (Z // 2, inner)),
    ):
        unit_scratch += [pltpu.VMEM((*came, *block), BF16), pltpu.VMEM((*mine, *block), BF16)]
        unit_scratch += [dma((inner - 1, outer)), dma((max(inner, outer),))]
    vmem, anywhere = pl.BlockSpec(memory_space=pltpu.VMEM), pl.BlockSpec(memory_space=pl.ANY)
    return pl.pallas_call(
        functools.partial(middle_kernel, (inner, outer)),
        out_shape=(
            jax.ShapeDtypeStruct((outer * C, rows, width), BF16),
            jax.ShapeDtypeStruct((rows, width), F32),
            jax.ShapeDtypeStruct((16, width), F32),
            jax.ShapeDtypeStruct((rows, width), BF16),
            *targets,
        ),
        in_specs=[anywhere, anywhere, vmem, vmem, vmem] + [anywhere] * (2 + 3 * outer),
        out_specs=(anywhere, vmem, vmem, vmem) + (anywhere,) * 3,
        scratch_shapes=pair_scratch * 2
        + unit_scratch
        + [
            pltpu.VMEM((rows, width), BF16),
            pltpu.VMEM((inner - 1, Z, *block), BF16),
            dma((2 * (Z + 2 * (Z - 1)) + 2 * outer + unit_copies,)),
            dma((3,)),
            dma((outer * C,)),
            dma((inner - 1,)),
        ],
        compiler_params=pltpu.CompilerParams(
            collective_id=2, has_side_effects=True, vmem_limit_bytes=60 * 1024 * 1024
        ),
        name="middle_and_rows",
    )(sent, own, middle, grads, gain, feed_sent, feed_own, *parts)


class RowsSum:
    def __init__(self, me, sends, terms, total, scratch, sems):
        self.me, self.sends, self.terms, self.total = me, sends, terms, total
        self.own, self.x_in, *ways = scratch
        self.own_sems, self.x_sems, up_sems, down_sems = sems
        self.up, self.down = (*ways[:2], up_sems), (*ways[2:], down_sems)

    def load(self):
        me = self.me
        self.loads = []
        for k in range(Z):
            self.loads.append(
                pltpu.make_async_copy(
                    self.terms.at[(me.z + Z - k) % Z, me.x], self.own.at[k], self.own_sems.at[k]
                )
            )
            self.loads[k].start()

    def begin(self, turns):
        me = self.me
        for turn in turns:
            if turn == Z - 1:
                k = 0
            else:
                k = (jnp.minimum(me.z, Z - 1 - me.z) + turn) % (Z - 1) + 1
                k = jnp.where(me.z < Z // 2, k, Z - k)
            at = (me.z + Z - k) % Z
            for j in range(1, me.inner):
                self.sends.start(
                    True, self.terms.at[at, (me.x + j) % me.inner], self.x_in.at[j - 1, k],
                    self.x_sems.at[j - 1, k], me.at_x(j),
                )

    def run(self, between=None):
        me = self.me

        def ready(k):
            self.loads[k].wait()
            for j in range(1, me.inner):
                arrived(self.x_in.at[j - 1, k], self.x_sems.at[j - 1, k], me.at_c)

        def term(k, r):
            value = self.own[k, r].astype(F32)
            for j in range(1, me.inner):
                value = value + self.x_in[j - 1, k, r].astype(F32)
            return value

        def store(r, value):
            self.total[r] = value

        line_sum(
            me, self.sends, self.total.shape[0], term, ready, store, lambda r: self.total[r],
            self.up, self.down, between,
        )


class ProductsSum(RowsSum):
    def __init__(self, me, sends, factors, total, scratch, sems):
        self.me, self.sends, self.total = me, sends, total
        self.factors = factors
        self.held, self.x_in, out, up_in, down_in, *self.lefts = scratch
        self.own_sems, self.x_sems, up_sems, down_sems = sems
        self.up, self.down = (out, up_in, up_sems), (out, down_in, down_sems)

    def load(self):
        self.loads = []
        for n, (left, _) in enumerate(self.factors):
            copy = pltpu.make_async_copy(left, self.lefts[n], self.own_sems.at[n])
            copy.start()
            self.loads.append(copy)

    def begin(self, turns):
        me = self.me
        while self.loads:
            self.loads.pop().wait()
        rows, span = self.total.shape[0], self.held.shape[1]
        for turn in turns:
            if turn == Z - 1:
                k = 0
            else:
                k = (jnp.minimum(me.z, Z - 1 - me.z) + turn) % (Z - 1) + 1
                k = jnp.where(me.z < Z // 2, k, Z - k)
            at = (me.z + Z - k) % Z

            def tile(i, carried, k=k, at=at):
                first = 0
                down = pl.ds(pl.multiple_of(i * LANES, LANES), LANES)
                across = pl.ds(pl.multiple_of(at * span + i * LANES, LANES), LANES)
                for n, (_, rights) in enumerate(self.factors):
                    left = self.lefts[n][:, across]
                    for right in rights:
                        columns = slice(first, first + right.shape[1])
                        self.held[k, down, columns] = contract_rows(left, right[...]).astype(BF16)
                        first += right.shape[1]
                return carried

            lax.fori_loop(0, span // LANES, tile, 0)
            for j in range(1, me.inner):
                part = pl.ds(pl.multiple_of((me.x + j) % me.inner * rows, 16), rows)
                self.sends.start(
                    True, self.held.at[k, part], self.x_in.at[j - 1, k], self.x_sems.at[j - 1, k],
                    me.at_x(j),
                )

    def run(self, between=None):
        me = self.me
        rows = self.total.shape[0]

        def ready(k):
            for j in range(1, me.inner):
                arrived(self.x_in.at[j - 1, k], self.x_sems.at[j - 1, k], me.at_c)

        def term(k, r):
            mine = pl.ds(pl.multiple_of(me.x * rows + r.start, 16), r.size)
            value = self.held[k, mine].astype(F32)
            for j in range(1, me.inner):
                value = value + self.x_in[j - 1, k, r].astype(F32)
            return value

        def store(r, value):
            self.total[r] = value

        line_sum(
            me, self.sends, rows, term, ready, store, lambda r: self.total[r],
            self.up, self.down, between,
        )


def sums_kernel(shape, *refs):
    inner, outer = shape
    units, units_y, units_x, normed_rows_one, branch_rows, narrow, sent, own = refs[:8]
    d_x, d_y, mixed, tokens, gain, d_middle, gain_two_grad, vectors = refs[8:16]
    units_to, wide_to, narrow_to, tokens_grad, gains, vectors_to = refs[16:22]
    refs = refs[22:]
    wide_scratch, narrow_scratch = refs[:7], refs[7:13]
    (own_v, c_in, y_out, y_in, parts_out, parts_in, gains_v, vec_in) = refs[13:21]
    refs = refs[2:]
    (send_sems, local_sems, c_sems, y_sems, all_sems, vec_sems) = refs[19:25]
    wide_sems, narrow_sems = refs[25:29], refs[29:33]
    units_v, units_y_in, units_x_in, unit_sems, units_y_sems, units_x_sems = refs[33:]
    share = units.shape[3]
    me = Place(shape)
    rows = tokens.shape[0]
    sends = Sends(send_sems)
    load = pltpu.make_async_copy(own, own_v, local_sems.at[0])
    load.start()
    units_load = pltpu.make_async_copy(units, units_v, local_sems.at[1])
    units_load.start()
    me.greet_all()

    order = [(me.y + i) % outer for i in list(range(1, outer)) + [0]]
    for at in order:
        sends.start(True, sent.at[at], c_in.at[at], c_sems.at[at], me.at_c)
    narrow_sum = RowsSum(me, sends, narrow, narrow_to, narrow_scratch, narrow_sems)
    factors = [(normed_rows_one, [d_x, d_y]), (branch_rows, [mixed])]
    wide_sum = ProductsSum(me, sends, factors, wide_to, wide_scratch, wide_sems)
    narrow_sum.load()
    wide_sum.load()
    narrow_sum.begin(range(Z))

    def columns(n, at):
        return units_to.at[n, :, pl.ds(pl.multiple_of(at * share, LANES), share)]

    low, high, extra = slice(0, Z // 2), slice(Z // 2, Z), slice(Z, Z + Z // 2)
    every = slice(0, Z)

    def units_begin_y():
        for n, blocks in enumerate((every, extra)):
            for i in range(1, outer):
                sends.start(
                    True, units_y.at[i - 1, blocks], units_y_in.at[i - 1, blocks],
                    units_y_sems.at[i - 1, n], me.at_y(-i),
                )

    def units_begin_x():
        for j in range(1, inner):
            sends.start(
                True, units_x.at[j - 1], units_x_in.at[j - 1], units_x_sems.at[j - 1], me.at_x(j)
            )

    kept = []

    def unit_add(n, blocks, came, came_blocks, sems, count):
        for i in range(count):
            arrived(came.at[i, came_blocks], sems.at[i], me.at_c)

        def body(r):
            for at in range(blocks.stop - blocks.start):
                total = units_v[n, blocks.start + at, r].astype(F32)
                for i in range(count):
                    total = total + came[i, came_blocks.start + at, r].astype(F32)
                units_v[n, blocks.start + at, r] = total.astype(BF16)

        each_rows(units_v.shape[2], 16, body)

    def unit_pass_on(n):
        copy = pltpu.make_async_copy(units_v.at[n, me.z], columns(n, me.z), local_sems.at[2 + n])
        copy.start()
        kept.append(copy)
        for k in range(1, Z):
            to = (me.z + k) % Z
            sends.start(
                True, units_v.at[n, to], columns(n, me.z), unit_sems.at[n, me.z], me.at_z(to)
            )

    def unit_gate():
        unit_add(0, every, units_y_in, every, units_y_sems.at[:, 0], outer - 1)
        unit_pass_on(0)

    def unit_down():
        unit_add(2, low, units_y_in, extra, units_y_sems.at[:, 1], outer - 1)
        unit_add(2, high, units_x_in, low, units_x_sems, inner - 1)
        unit_pass_on(2)


    def units_finish():
        for n in range(3):
            for k in range(1, Z):
                at = (me.z + Z - k) % Z
                arrived(columns(n, at), unit_sems.at[n, at], me.at_c)
        for copy in kept:
            copy.wait()

    def exchange(held, into, sems, first, devices):
        for n, device in enumerate(devices):
            sends.start(True, held, into.at[first + n], sems.at[first + n], device)

    def gathered(held, into, sems, first, devices):
        for n, _ in enumerate(devices):
            arrived(into.at[first + n], sems.at[first + n], me.at_c)
        total = into[first]
        for n in range(1, len(devices)):
            total = total + into[first + n]
        return held[...] + total

    z_stage = [me.at_z((me.z + k) % Z) for k in range(1, Z)]
    x_stage = [me.at_x(j) for j in range(1, inner)]

    devices = Z * inner * outer * C
    wt = outer * C
    here = me.s * wt + me.w
    width = tokens.shape[1]
    channels = width // devices

    def gains_cut():
        for i in range(devices):
            first = i * channels // LANES * LANES
            first = min(first, width - 2 * LANES)
            window = gains_v[:, first : first + 2 * LANES]
            turn = i * channels - first
            if turn:
                window = pltpu.roll(window, 2 * LANES - turn, 1)
            parts_out[i] = window[:, :LANES]

    def gains_copy(i):
        return pltpu.make_async_remote_copy(
            src_ref=parts_out.at[i], dst_ref=parts_in.at[here],
            send_sem=all_sems.at[0, i], recv_sem=all_sems.at[1, here],
            device_id={"seq": i // wt, "wt": i % wt}, device_id_type=MESH,
        )

    def gains_send(i, carried):
        pl.when(i != here)(lambda: gains_copy(i).start())
        return carried

    def gains_add(i, carried):
        @pl.when(i != here)
        def _():
            gains_copy(i).wait_send()
            arrived(parts_in.at[i], all_sems.at[1, i], me.at_c)
            gains[...] += parts_in[i]

        return carried

    exchange(vectors, vec_in, vec_sems, 0, x_stage)
    units_begin_x()

    units_begin_y()
    units_load.wait()
    unit_pass_on(1)

    load.wait()
    for i, at in enumerate(order):
        arrived(c_in.at[at], c_sems.at[at], me.at_c)
        if i < outer - 1:
            each_rows(rows, 16, lambda r, i=i, at=at: y_out.__setitem__(
                (i, r), (own_v[at, r] + c_in[at, r].astype(F32)).astype(BF16)))
            sends.start(True, y_out.at[i], y_in.at[i], y_sems.at[i], me.at_y(i + 1))
    vectors_to[0] = gathered(vectors, vec_in, vec_sems, 0, x_stage)
    exchange(vectors_to.at[0], vec_in, vec_sems, len(x_stage), z_stage)
    narrow_sum.run()
    vectors_to[1] = gathered(vectors_to.at[0], vec_in, vec_sems, len(x_stage), z_stage)
    wide_sum.begin(range(1))
    unit_gate()
    wide_sum.begin(range(1, 2))
    unit_down()
    wide_sum.begin(range(2, Z))

    def work(r):
        d_normed = own_v[me.y, r] + c_in[me.y, r].astype(F32)
        for i in range(outer - 1):
            d_normed = d_normed + y_in[i, r].astype(F32)
        stream = tokens[r].astype(F32)
        inverse = lax.rsqrt(jnp.mean(stream * stream, axis=1, keepdims=True) + EPSILON)
        normed = stream * inverse
        part = d_normed * normed
        gains_v[0:8] += part[0:8] + part[8:16]
        scaled = d_normed * gain[...]
        passed = inverse * (scaled - normed * jnp.mean(scaled * normed, axis=1, keepdims=True))
        tokens_grad[r] = (d_middle[r] + passed).astype(BF16)

    def between(t):
        if t == 1:
            for i in range(outer - 1):
                arrived(y_in.at[i], y_sems.at[i], me.at_c)
            gains_v[...] = jnp.zeros_like(gains_v)
            each_rows(rows, 16, work)
            gains_v[8:16] = gain_two_grad[0:8] + gain_two_grad[8:16]
            gains_cut()
            lax.fori_loop(0, devices, gains_send, 0)

    wide_sum.run(between)
    gains[...] = parts_out[here]
    lax.fori_loop(0, devices, gains_add, 0)
    units_finish()
    sends.finish()


def last_sums(
    units, units_y, units_x, normed_one, branch_rows, narrow, sent, own,
    d_x, d_y, mixed, tokens, gain, d_middle, gain_two_grad, vectors,
):
    inner, outer = sizes()
    rows, width = tokens.shape
    dma = pltpu.SemaphoreType.DMA
    vmem, anywhere = pl.BlockSpec(memory_space=pltpu.VMEM), pl.BlockSpec(memory_space=pl.ANY)

    def scratch(terms):
        one = terms.shape[2:]
        return [pltpu.VMEM((Z, *one), BF16), pltpu.VMEM((inner - 1, Z, *one), BF16)] + [
            pltpu.VMEM((Z - 1, *one), BF16)
        ] * 4

    devices = Z * inner * outer * C
    copies = 2 * outer - 1 + 2 * (Z * (inner - 1) + 2 * (Z - 1))
    copies += (inner - 1) + (Z - 1) + 2 * (outer - 1) + 2 * (inner - 1) + 3 * (Z - 1)
    _, _, unit_rows, share = units.shape
    block = (unit_rows, d_x.shape[1] + d_y.shape[1] + mixed.shape[1])
    line_sems = [dma((Z,)), dma((inner - 1, Z)), dma((Z - 1,)), dma((Z - 1,))]
    return pl.pallas_call(
        functools.partial(sums_kernel, (inner, outer)),
        out_shape=(
            jax.ShapeDtypeStruct((3, unit_rows, Z * share), BF16),
            jax.ShapeDtypeStruct(block, F32),
            jax.ShapeDtypeStruct(narrow.shape[2:], F32),
            jax.ShapeDtypeStruct((rows, width), BF16),
            jax.ShapeDtypeStruct((16, LANES), F32),
            jax.ShapeDtypeStruct((2, *vectors.shape), F32),
        ),
        in_specs=[anywhere] * 8 + [vmem] * 8,
        out_specs=(anywhere,) + (vmem,) * 5,
        scratch_shapes=[
            pltpu.VMEM((Z, inner * block[0], block[1]), BF16),
            pltpu.VMEM((inner - 1, Z, *block), BF16),
        ]
        + [pltpu.VMEM((Z - 1, *block), BF16)] * 3
        + [pltpu.VMEM(normed_one.shape, BF16), pltpu.VMEM(branch_rows.shape, BF16)]
        + scratch(narrow)
        + [
            pltpu.VMEM((outer, rows, width), F32),
            pltpu.VMEM((outer, rows, width), BF16),
            pltpu.VMEM((outer - 1, rows, width), BF16),
            pltpu.VMEM((outer - 1, rows, width), BF16),
            pltpu.VMEM((devices, 16, LANES), F32),
            pltpu.VMEM((devices, 16, LANES), F32),
            pltpu.VMEM((16, width), F32),
            pltpu.VMEM((inner - 1 + Z - 1, *vectors.shape), F32),
            dma((copies,)),
            dma((5,)),
            dma((outer,)),
            dma((outer - 1,)),
            dma((2, devices)),
            dma((inner - 1 + Z - 1,)),
        ]
        + line_sems * 2
        + [
            pltpu.VMEM(units.shape, BF16),
            pltpu.VMEM(units_y.shape, BF16),
            pltpu.VMEM(units_x.shape, BF16),
            dma((3, Z)),
            dma((outer - 1, 2)),
            dma((inner - 1,)),
        ],
        compiler_params=pltpu.CompilerParams(
            collective_id=5, has_side_effects=True, vmem_limit_bytes=60 * 1024 * 1024
        ),
        name="last_sums",
    )(
        units, units_y, units_x, normed_one, branch_rows, narrow, sent, own,
        d_x, d_y, mixed, tokens, gain, d_middle, gain_two_grad, vectors,
    )


def scan_kernel(backward, factors, inflows, states, entered, products, ends, ends_in, carry, send_sems, arrivals):
    seq = ends_in.shape[0]
    s = lax.axis_index("seq")
    rows, width = factors.shape
    barrier = pltpu.get_barrier_semaphore()

    def device(at):
        return {"seq": at, "wt": lax.axis_index("wt")}

    def greet(i, carried):
        @pl.when(i != s)
        def _():
            pl.semaphore_signal(barrier, inc=1, device_id=device(i), device_id_type=MESH)

        return carried

    lax.fori_loop(0, seq, greet, 0)
    group = 8
    at_row = lax.broadcasted_iota(jnp.int32, (group, width), 0)

    def step(i, carried):
        held, product = carried
        i = rows // group - 1 - i if backward else i
        where = pl.ds(pl.multiple_of(i * group, group), group)
        factor, inflow = factors[where, :], inflows[where, :]
        for by in (1, 2, 4):
            inside = at_row < group - by if backward else at_row >= by
            turn = group - by if backward else by
            inflow = factor * jnp.where(inside, pltpu.roll(inflow, turn, 0), 0.0) + inflow
            factor = factor * jnp.where(inside, pltpu.roll(factor, turn, 0), 1.0)
        inflow = inflow + factor * held
        factor = factor * product
        states[where, :] = inflow
        products[where, :] = factor
        last = slice(0, 1) if backward else slice(group - 1, group)
        return inflow[last], factor[last]

    held, product = lax.fori_loop(
        0, rows // group, step, (jnp.zeros((1, width), F32), jnp.ones((1, width), F32))
    )
    ends[0:1] = product
    ends[1:2] = held
    pl.semaphore_wait(barrier, seq - 1)

    def copy_to(i):
        return pltpu.make_async_remote_copy(
            src_ref=ends, dst_ref=ends_in.at[s], send_sem=send_sems.at[i], recv_sem=arrivals.at[s],
            device_id=device(i), device_id_type=MESH,
        )

    def later(i):
        return i < s if backward else i > s

    def send(i, carried):
        pl.when(later(i))(lambda: copy_to(i).start())
        return carried

    lax.fori_loop(0, seq, send, 0)
    carry[...] = jnp.zeros_like(carry)

    def receive(n, carried):
        i = seq - 1 - n if backward else n

        @pl.when(jnp.logical_not(later(i)) & (i != s))
        def _():
            arrived(ends_in.at[i], arrivals.at[i], device((s + 1) % seq))
            carry[0:1] = ends_in[i, 0:1] * carry[0:1] + ends_in[i, 1:2]

        return carried

    lax.fori_loop(0, seq, receive, 0)
    entering = carry[0:1]
    entered[...] = entering

    def spread(i, carried):
        where = pl.ds(pl.multiple_of(i * group, group), group)
        states[where, :] += products[where, :] * entering
        return carried

    lax.fori_loop(0, rows // group, spread, 0)

    def sent(i, carried):
        pl.when(later(i))(lambda: copy_to(i).wait_send())
        return carried

    lax.fori_loop(0, seq, sent, 0)


def full_scan(factor, inflow, backward):
    seq = lax.axis_size("seq")
    rows, width = factor.shape
    vmem = pl.BlockSpec(memory_space=pltpu.VMEM)
    return pl.pallas_call(
        functools.partial(scan_kernel, backward),
        out_shape=(
            jax.ShapeDtypeStruct((rows, width), F32),
            jax.ShapeDtypeStruct((1, width), F32),
        ),
        in_specs=[vmem, vmem],
        out_specs=(vmem, vmem),
        scratch_shapes=[
            pltpu.VMEM((rows, width), F32),
            pltpu.VMEM((8, width), F32),
            pltpu.VMEM((seq, 8, width), F32),
            pltpu.VMEM((8, width), F32),
            pltpu.SemaphoreType.DMA((seq,)),
            pltpu.SemaphoreType.DMA((seq,)),
        ],
        compiler_params=pltpu.CompilerParams(
            collective_id=4 if backward else 3,
            has_side_effects=True,
            vmem_limit_bytes=32 * 1024 * 1024,
        ),
        name="scan_back" if backward else "scan_ahead",
    )(factor, inflow)


def recurrence_terms(decay_pre, input_pre, decay_log, conv_float):
    log_decay = -DECAY_SCALE * jax.nn.softplus(-decay_log) * jax.nn.sigmoid(decay_pre)
    return (
        jnp.exp(log_decay),
        jnp.sqrt(-jnp.expm1(2.0 * log_decay)) * jax.nn.sigmoid(input_pre) * conv_float,
    )


def per_device(
    tokens,
    norm1_gain,
    x_weight,
    y_weight,
    conv_weight,
    conv_bias,
    decay_gate_weight,
    decay_bias,
    input_gate_weight,
    input_bias,
    decay_param,
    out_weight,
    norm2_gain,
    gate_weight,
    up_weight,
    down_weight,
    out_grad,
):
    seq, wt = lax.axis_size("seq"), lax.axis_size("wt")
    inner, outer = sizes()
    z, x, y, c = places()
    w = lax.axis_index("wt")
    rows_dev, width = tokens.shape
    weight_rows, lru_cols = x_weight.shape
    chunk, block = decay_gate_weight.shape
    half = block // 2
    full = lru_cols - half
    taps_count = conv_weight.shape[1]
    reach = taps_count - 1
    hidden_cols = gate_weight.shape[1]

    def turned(value, axis):
        return jnp.where(c == 0, value, jnp.roll(value, -half, axis))

    def turned_back(value, axis):
        return jnp.where(c == 0, value, jnp.roll(value, half, axis))

    def in_order(own, partner, axis):
        return jnp.where(
            c == 0,
            jnp.concatenate([own, partner], axis),
            jnp.concatenate([partner, own], axis),
        )

    vectors = jnp.stack(
        [v.astype(F32) for v in (norm1_gain, norm2_gain, conv_bias, decay_bias, input_bias)]
        + [decay_param]
        + [conv_weight[:, k].astype(F32) for k in range(taps_count)]
    )
    vectors = jnp.pad(vectors, ((0, -vectors.shape[0] % 8), (0, -chunk % LANES)))

    across = [(i, i % seq * wt + i // seq) for i in range(seq * wt)]
    gates = jnp.concatenate([decay_gate_weight, input_gate_weight], axis=1)

    def padded(weight):
        share = -(-hidden_cols // (Z * LANES)) * LANES
        return jnp.pad(weight, ((0, 0), (0, Z * share - hidden_cols)))

    xy_unit = jnp.concatenate([turned(x_weight, 1), turned(y_weight, 1)], axis=1)
    (
        grad_group, vectors, gate_all, xy_kernel, out_kernel, gate_kernel, up_kernel, down_kernel,
        group_one, xy,
    ) = gather_all(
        tokens, out_grad, vectors, gates, xy_unit, turned(out_weight, 1),
        padded(gate_weight), padded(up_weight), padded(down_weight),
    )
    grad_group = grad_group.reshape(-1, width)
    vectors = jnp.moveaxis(vectors[:, : 6 + taps_count, :chunk], 0, 1).reshape(6 + taps_count, -1)
    gain_one, gain_two = vectors[0], vectors[1]
    own_vectors = turned(
        lax.dynamic_slice(vectors[2:], (0, w * lru_cols), (taps_count + 4, lru_cols)), 1
    )
    tap_bias, decay_shift, input_shift, decay_log = (own_vectors[i] for i in range(4))
    taps = own_vectors[4:]
    xy_kernel = xy_kernel.reshape(width, -1)
    out_kernel = out_kernel.reshape(width, -1)
    gate_kernel = gate_kernel.reshape(width, -1)
    gate_all = turned(gate_all.reshape(lru_cols, 2 * block), 0)
    partner_rows = c_swap(gate_all[full:])
    shared_rows = in_order(gate_all[full:], partner_rows, 0)

    stream = tokens.astype(F32)
    rows = group_one.shape[0]
    x_branch = xy[:, :lru_cols].astype(BF16)
    y_before = xy[:, lru_cols:]
    y_gated, gelu_y_back = jax.vjp(gelu_tanh, y_before)
    rim = lax.ppermute(x_branch[rows - reach :], "seq", [(i, i + 1) for i in range(seq - 1)])
    extended = jnp.concatenate([rim, x_branch], axis=0).astype(F32)
    conv_low = (
        tap_bias
        + sum(taps[k] * extended[reach - k : reach - k + rows] for k in range(taps_count))
    ).astype(BF16)
    shared_conv = in_order(conv_low[:, full:], c_swap(conv_low[:, full:]), 1)
    heads = full // block

    def of_head(value, i):
        return value[:, i * block : (i + 1) * block]

    pre_parts = [
        multiply(of_head(conv_low, i), gate_all[i * block : (i + 1) * block]) for i in range(heads)
    ]
    shared_columns = jnp.where(
        c == 0,
        jnp.concatenate([shared_rows[:, :half], shared_rows[:, block : block + half]], axis=1),
        jnp.concatenate([shared_rows[:, half:block], shared_rows[:, block + half :]], axis=1),
    )
    shared_pre = multiply(shared_conv, shared_columns)
    decay_pre = decay_shift + jnp.concatenate(
        [part[:, :block] for part in pre_parts] + [shared_pre[:, :half]], axis=1
    )
    input_pre = input_shift + jnp.concatenate(
        [part[:, block:] for part in pre_parts] + [shared_pre[:, half:]], axis=1
    )
    (retain, inflow), terms_back = jax.vjp(
        recurrence_terms, decay_pre, input_pre, decay_log, conv_low.astype(F32)
    )
    states, state_in = full_scan(retain, inflow, False)
    before = jnp.concatenate([state_in, states[:-1]])
    lru_low = states.astype(BF16).astype(F32)
    mixed_rows = (lru_low * y_gated).astype(BF16)
    mixed_parts = mixed_rows.reshape(outer, C, rows_dev, lru_cols)

    def branch_of(at):
        part = pick(mixed_parts, at, 1).reshape(outer * rows_dev, lru_cols)
        return contract_last(part, out_kernel).reshape(outer, rows_dev, width)

    group_two, middle, up_kernel, down_kernel = branch_and_group(
        branch_of(1 - c), branch_of(c), tokens, gain_two[None], up_kernel, down_kernel
    )
    up_kernel = up_kernel.reshape(width, -1)
    down_kernel = down_kernel.reshape(width, -1)
    group_two = group_two.reshape(C * Z * rows_dev, width)

    gate_pre = multiply(group_two, gate_kernel)
    up_pre = multiply(group_two, up_kernel)
    active, gelu_gate_back = jax.vjp(gelu_tanh, gate_pre)
    hidden = (active * up_pre).astype(BF16)

    d_hidden = multiply(grad_group, down_kernel)
    d_up = (d_hidden * active).astype(BF16)
    d_gate = gelu_gate_back(d_hidden * up_pre)[0].astype(BF16)
    half_rows = Z * rows_dev

    def d_normed_of(part):
        total = contract_last(d_gate[part], gate_kernel) + contract_last(d_up[part], up_kernel)
        return total.reshape(Z, rows_dev, width)

    def terms_of(left_side, right_side):
        share = right_side.shape[1] // outer
        return [
            contract_rows(left_side, right_side[:, i * share : (i + 1) * share])
            .astype(BF16)
            .reshape(Z, inner, weight_rows, share)
            for i in range(outer)
        ]

    gate_terms = terms_of(group_two, d_gate)
    up_terms = terms_of(group_two, d_up)
    down_terms = terms_of(grad_group, hidden)
    def feed_of(part):
        return contract_last(hidden[part], down_kernel).reshape(Z, rows_dev, width)

    branch_rows, d_middle, gain_two_grad, block_out, units, units_y, units_x = middle_and_rows(
        d_normed_of(slice(half_rows, None)).astype(BF16),
        d_normed_of(slice(0, half_rows)),
        middle,
        out_grad,
        gain_two[None],
        feed_of(slice(half_rows, None)).astype(BF16),
        feed_of(slice(0, half_rows)),
        gate_terms + up_terms + down_terms,
    )
    branch_rows = branch_rows.reshape(-1, width)

    d_mixed = multiply(branch_rows, out_kernel)
    d_lru = (d_mixed * y_gated).astype(BF16).astype(F32)
    d_y = gelu_y_back(d_mixed * lru_low)[0].astype(BF16)
    passed, passed_in = full_scan(retain, retain * d_lru, True)
    d_total = d_lru + jnp.concatenate([passed[1:], passed_in])
    d_decay_pre, d_input_pre, decay_log_grad, d_conv_direct = terms_back(
        (d_total * before, d_total)
    )
    d_decay_low, d_input_low = d_decay_pre.astype(BF16), d_input_pre.astype(BF16)
    own_low = jnp.concatenate([d_decay_low[:, full:], d_input_low[:, full:]], axis=1)
    partner_low = c_swap(own_low)
    shared_low = jnp.concatenate(
        [
            in_order(own_low[:, :half], partner_low[:, :half], 1),
            in_order(own_low[:, half:], partner_low[:, half:], 1),
        ],
        axis=1,
    )
    lows = [
        jnp.concatenate([of_head(d_decay_low, i), of_head(d_input_low, i)], axis=1)
        for i in range(heads)
    ]
    d_conv = d_conv_direct + jnp.concatenate(
        [contract_last(lows[i], gate_all[i * block : (i + 1) * block]) for i in range(heads)]
        + [contract_last(shared_low, gate_all[full:])],
        axis=1,
    )
    gates_grad = jnp.concatenate(
        [contract_rows(of_head(conv_low, i), lows[i]) for i in range(heads)]
        + [contract_rows(conv_low[:, full:], shared_low)]
    )
    ahead = lax.ppermute(d_conv[:reach], "seq", [(i + 1, i) for i in range(seq - 1)])
    d_extended = jnp.concatenate([d_conv, ahead], axis=0)
    d_x_branch = sum(taps[k] * d_extended[k : k + rows] for k in range(taps_count)).astype(BF16)
    dx_parts = d_x_branch.reshape(outer, C, rows_dev, lru_cols)
    dy_parts = d_y.reshape(outer, C, rows_dev, lru_cols)

    def d_normed_one_of(at):
        dx, dy = (
            pick(parts, at, 1).reshape(outer * rows_dev, lru_cols) for parts in (dx_parts, dy_parts)
        )
        total = contract_last(dx, xy_kernel[:, :lru_cols]) + contract_last(
            dy, xy_kernel[:, lru_cols:]
        )
        return total.reshape(outer, rows_dev, width)

    narrow = turned_back(gates_grad, 0).astype(BF16).reshape(Z, inner, chunk, 2 * block)
    narrow = jnp.pad(narrow, ((0, 0), (0, 0), (0, -chunk % 16), (0, 0)))
    own_sums = jnp.stack(
        [jnp.sum(d_conv, axis=0), jnp.sum(d_decay_pre, axis=0), jnp.sum(d_input_pre, axis=0)]
        + [decay_log_grad]
        + [jnp.sum(d_conv * extended[reach - k : reach - k + rows], axis=0) for k in range(taps_count)],
    )
    own_sums = turned_back(own_sums, 1)
    placed, wide, narrow, tokens_grad, gains, own_sums = last_sums(
        units, units_y, units_x, group_one, branch_rows, narrow,
        d_normed_one_of(1 - c).astype(BF16), d_normed_one_of(c),
        turned_back(d_x_branch, 1), turned_back(d_y, 1), turned_back(mixed_rows, 1),
        tokens, gain_one[None], d_middle, gain_two_grad, own_sums,
    )
    weight_grads = [wide[:, n * lru_cols : (n + 1) * lru_cols] for n in range(3)]
    gate_grad, up_grad, down_grad = (placed[n, :, :hidden_cols].astype(F32) for n in range(3))
    gains = gains.reshape(2, 8, LANES).sum(axis=1)[:, :chunk]
    sums = lax.dynamic_slice(own_sums[1], (0, lax.axis_index("seq") * chunk), (taps_count + 4, chunk))
    own_sums = jnp.concatenate([narrow[:chunk], sums.T], axis=1)
    own_sums = lax.ppermute(own_sums, ("seq", "wt"), [(to, at) for at, to in across])
    sums = own_sums[:, 2 * block :]
    return (
        block_out,
        tokens_grad,
        gains[0],
        weight_grads[0],
        weight_grads[1],
        sums[:, 4:],
        sums[:, 0],
        own_sums[:, :block],
        sums[:, 1],
        own_sums[:, block : 2 * block],
        sums[:, 2],
        sums[:, 3],
        weight_grads[2],
        gains[1],
        gate_grad,
        up_grad,
        down_grad,
    )


def solution(mesh):
    rows, both, lone = P(("seq", "wt"), None), P("seq", "wt"), P(("seq", "wt"))
    in_specs = (
        rows, lone, both, both, rows, lone, rows, lone, rows, lone, lone,
        both, lone, both, both, both, rows,
    )
    out_specs = (
        rows, rows, lone, both, both, rows, lone, rows, lone, rows, lone, lone,
        both, lone, both, both, both,
    )
    return jax.shard_map(
        per_device, mesh=mesh, in_specs=in_specs, out_specs=out_specs, check_vma=False
    )
```

```python
import functools

import jax
import jax.numpy as jnp
from jax import lax
from jax.experimental import pallas as pl
from jax.experimental.pallas import tpu as pltpu
from jax.sharding import PartitionSpec as P

EPSILON = 1e-06
DECAY_SCALE = 8.0
Z = 4
C = 2
LANES = 128
F32 = jnp.float32
BF16 = jnp.bfloat16
MESH = pl.DeviceIdType.MESH


def gelu_tanh(values):
    return jax.nn.gelu(values, approximate=True)


def sizes():
    return lax.axis_size("seq") // Z, lax.axis_size("wt") // C


def places():
    inner, outer = sizes()
    s, w = lax.axis_index("seq"), lax.axis_index("wt")
    return s // inner, s % inner, w // C, w % C


def z_move(value, by, senders):
    inner, _ = sizes()
    pairs = [(z * inner + x, (z + by) % Z * inner + x) for z in senders for x in range(inner)]
    return lax.ppermute(value, "seq", pairs)


def c_swap(value):
    _, outer = sizes()
    pairs = [(y * C + c, y * C + 1 - c) for y in range(outer) for c in range(C)]
    return lax.ppermute(value, "wt", pairs)


def line_scatter(parts):
    up = down = None
    for step in range(1, Z):
        rising = parts[step] if up is None else parts[step] + up
        falling = parts[Z - step] if down is None else parts[Z - step] + down
        up = z_move(rising.astype(BF16), 1, range(0, step)).astype(F32)
        down = z_move(falling.astype(BF16), -1, range(Z - step, Z)).astype(F32)
    return parts[0] + up + down


def pick(value, index, axis):
    return lax.dynamic_index_in_dim(value, index, axis, keepdims=False)


def contract_last(left_side, right_side):
    return lax.dot_general(
        left_side, right_side, (((1,), (1,)), ((), ())), preferred_element_type=F32
    )


def contract_rows(left_side, right_side):
    return lax.dot_general(
        left_side, right_side, (((0,), (0,)), ((), ())), preferred_element_type=F32
    )


def multiply(left_side, right_side):
    return jnp.dot(left_side, right_side, preferred_element_type=F32)


class Sends:
    def __init__(self, sems):
        self.sems, self.started = sems, []

    def start(self, when, source, target, arrival, device):
        copy = pltpu.make_async_remote_copy(
            src_ref=source,
            dst_ref=target,
            send_sem=self.sems.at[len(self.started)],
            recv_sem=arrival,
            device_id=device,
            device_id_type=MESH,
        )
        if when is True:
            copy.start()
        else:
            pl.when(when)(copy.start)
        self.started.append((when, copy))

    def finish(self):
        for when, copy in self.started:
            if when is True:
                copy.wait_send()
            else:
                pl.when(when)(copy.wait_send)


def arrived(target, arrival, device):
    pltpu.make_async_remote_copy(
        src_ref=target, dst_ref=target, send_sem=arrival, recv_sem=arrival,
        device_id=device, device_id_type=MESH,
    ).wait_recv()


def gather_kernel(shape, *refs):
    inner, outer = shape
    (tokens, grads, vectors, gates, xy, out, gate, up, down) = refs[:9]
    (grads_to, vectors_to, gates_to, xy_to, out_to, gate_to, up_to, down_to) = refs[9:17]
    rows_one, xy_one = refs[17:19]
    gates_own, send_sems, local_sems, line_sems, plane_sems, rows_sems = refs[19:25]
    vector_sems, turn_sems, group_sems, tokens_to, xy_v, vectors_v, spread, read_sems = refs[25:]
    seq, wt = Z * inner, outer * C
    s, w = lax.axis_index("seq"), lax.axis_index("wt")
    z, x, y, c = s // inner, s % inner, w // C, w % C
    sends = Sends(send_sems)
    group = GroupRows(Place(shape), sends, grads, grads_to, group_sems)
    here, counter = [], iter(range(16))

    def at_z(to):
        return {"seq": to * inner + x, "wt": w}

    def at_x(by):
        return {"seq": z * inner + (x + by) % inner, "wt": w}

    def at_y(by):
        return {"seq": s, "wt": (y + by) % outer * C + c}

    at_c = {"seq": s, "wt": y * C + 1 - c}

    def keep(source, target, waited=False):
        copy = pltpu.make_async_copy(source, target, local_sems.at[next(counter)])
        copy.start()
        here.append((waited, copy))
        return copy

    barrier = pltpu.get_barrier_semaphore()

    def greet(i, carried):
        @pl.when(i != s * wt + w)
        def _():
            pl.semaphore_signal(
                barrier, inc=1, device_id={"seq": i // wt, "wt": i % wt}, device_id_type=MESH
            )

        return carried

    lax.fori_loop(0, seq * wt, greet, 0)
    pl.semaphore_wait(barrier, seq * wt - 1)

    class Line:
        def __init__(self, index, source, target):
            self.source, self.target = source, target
            self.sems = line_sems.at[index]

        def forward(self, block, at, up_when, down_when):
            place = self.target.at[at, x]
            arrival = self.sems.at[at, x]
            sends.start(up_when, block, place, arrival, at_z(jnp.minimum(z + 1, Z - 1)))
            sends.start(down_when, block, place, arrival, at_z(jnp.maximum(z - 1, 0)))
            return place, arrival

        def across(self, when, block, at):
            for j in range(1, inner):
                sends.start(when, block, self.target.at[at, x], self.sems.at[at, x], at_x(j))

        def begin_z(self):
            keep(self.source, self.target.at[z, x])
            self.forward(self.source, z, z < Z - 1, z > 0)

        def begin_x(self):
            self.across(True, self.source, z)

        def begin(self):
            self.begin_z()
            self.begin_x()

        def step(self, k):
            for at, there, up_when, down_when in (
                (jnp.maximum(z - k, 0), z - k >= 0, (z - k >= 0) & (z < Z - 1), None),
                (jnp.minimum(z + k, Z - 1), z + k < Z, None, (z + k < Z) & (z > 0)),
            ):
                place, arrival = self.target.at[at, x], self.sems.at[at, x]

                @pl.when(there)
                def _(place=place, arrival=arrival):
                    arrived(place, arrival, at_c)

                if up_when is not None:
                    sends.start(up_when, place, place, arrival, at_z(jnp.minimum(z + 1, Z - 1)))
                else:
                    sends.start(down_when, place, place, arrival, at_z(jnp.maximum(z - 1, 0)))
                self.across(there, place, at)

        def finish(self):
            for at in range(Z):
                for j in range(1, inner):
                    from_x = (x + inner - j) % inner
                    arrived(self.target.at[at, from_x], self.sems.at[at, from_x], at_c)

    class Plane:
        def __init__(self, index, source, target, x_first, whole):
            self.source, self.target, self.x_first, self.whole = source, target, x_first, whole
            self.share = source.shape[1] // Z
            self.sems = plane_sems.at[index]

        def cut(self, at):
            return self.source.at[:, pl.ds(pl.multiple_of(at * self.share, LANES), self.share)]

        def place(self, at, x_at, i):
            return self.target.at[at, x_at, :, i * self.share : (i + 1) * self.share]

        def begin(self):
            self.own = keep(self.cut(z), self.place(z, x, 0), True)
            for k in range(1, Z):
                to = (z + k) % Z
                sends.start(True, self.cut(to), self.place(z, x, 0), self.sems.at[z, 0, 0], at_z(to))

        def over_x(self, at, i):
            place = self.place(at, x, i)
            for j in range(1, inner):
                sends.start(True, place, place, self.sems.at[at, j, i], at_x(j))

        def over_y(self, at, j):
            x_at = (x + inner - j) % inner
            for i in range(1, outer):
                sends.start(
                    True, self.place(at, x_at, 0), self.place(at, x_at, i),
                    self.sems.at[at, j, i], at_y(i),
                )

        def got(self, at, j, i):
            arrived(self.place(at, (x + inner - j) % inner, i), self.sems.at[at, j, i], at_c)

        def first(self, k):
            at = (z + Z - k) % Z
            if k == 0:
                self.own.wait()
            else:
                self.got(at, 0, 0)
            if self.x_first or self.whole:
                self.over_x(at, 0)
            if self.whole or not self.x_first:
                self.over_y(at, 0)

        def second(self, k):
            at = (z + Z - k) % Z
            if self.x_first:
                for j in range(1, inner):
                    self.got(at, j, 0)
                    if self.whole:
                        self.over_y(at, j)
            else:
                for i in range(1, outer):
                    self.got(at, 0, i)

        def finish(self, k):
            if self.whole:
                at = (z + Z - k) % Z
                for j in range(inner):
                    for i in range(1, outer):
                        self.got(at, j, i)

    lines = [Line(0, xy, xy_to), Line(1, gates_own, gates_to), Line(2, out, out_to)]
    planes = [
        Plane(0, gate, gate_to, True, True),
        Plane(1, up, up_to, False, False),
        Plane(2, down, down_to, True, False),
    ]

    me = s * wt + w
    keep(vectors, vectors_to.at[me])

    def vector_copy(i):
        return pltpu.make_async_remote_copy(
            src_ref=vectors, dst_ref=vectors_to.at[me],
            send_sem=vector_sems.at[0, i], recv_sem=vector_sems.at[1, me],
            device_id={"seq": i // wt, "wt": i % wt}, device_id_type=MESH,
        )

    def vector_send(i, carried):
        pl.when(i != me)(lambda: vector_copy(i).start())
        return carried

    def tokens_begin():
        keep(tokens, tokens_to.at[w])
        sends.start(True, tokens, tokens_to.at[w], rows_sems.at[w], at_c)
        for i in range(1, outer):
            sends.start(True, tokens, tokens_to.at[w], rows_sems.at[w], at_y(i))

    def tokens_step():
        for i in range(1, outer):
            at = (y + outer - i) % outer * C + c
            arrived(tokens_to.at[at], rows_sems.at[at], at_c)
            sends.start(True, tokens_to.at[at], tokens_to.at[at], rows_sems.at[at], at_c)

    def tokens_finish():
        for i in range(outer):
            at = (y + outer - i) % outer * C + 1 - c
            arrived(tokens_to.at[at], rows_sems.at[at], at_c)

    to_seq, to_wt = me % seq, me // seq
    from_me = w * seq + s
    turn = pltpu.make_async_remote_copy(
        src_ref=gates, dst_ref=gates_own, send_sem=turn_sems.at[0], recv_sem=turn_sems.at[1],
        device_id={"seq": to_seq, "wt": to_wt}, device_id_type=MESH,
    )
    stay = pltpu.make_async_copy(gates, gates_own, turn_sems.at[2])
    here_too = from_me == me

    pl.when(jnp.logical_not(here_too))(turn.start)
    pl.when(here_too)(stay.start)
    def vector_wait(i, carried):
        @pl.when(i != me)
        def _():
            vector_copy(i).wait_send()
            arrived(vectors_to.at[i], vector_sems.at[1, i], at_c)

        return carried

    def first_projection():
        lines[0].finish()
        tokens_finish()
        lax.fori_loop(0, seq * wt, vector_wait, 0)
        for copy in here_first:
            copy.wait()
        rows_each = xy.shape[0]
        copies = [pltpu.make_async_copy(vectors_to, vectors_v, read_sems.at[0])]
        for z_at in range(Z):
            for x_at in range(inner):
                n = z_at * inner + x_at
                copies.append(
                    pltpu.make_async_copy(
                        xy_to.at[z_at, x_at], xy_v.at[n * rows_each : (n + 1) * rows_each],
                        read_sems.at[1 + n],
                    )
                )
        for copy in copies:
            copy.start()
        copies[0].wait()
        width = tokens.shape[1]
        devices = seq * wt
        channels = width // devices
        spread[...] = jnp.zeros_like(spread)
        for i in range(devices):
            first = min(i * channels // LANES * LANES, width - 2 * LANES)
            turn = i * channels - first
            part = vectors_v[i, 0:8]
            part = jnp.concatenate([part, jnp.zeros_like(part)], axis=1)
            if turn:
                part = pltpu.roll(part, turn, 1)
            spread[:, first : first + 2 * LANES] += part
        gain = spread[0:1]
        count = tokens.shape[0]
        for at in range(wt):

            def norm(r, at=at):
                stream = tokens_to[at, r].astype(F32)
                inverse = lax.rsqrt(jnp.mean(stream * stream, axis=1, keepdims=True) + EPSILON)
                rows_one[pl.ds(pl.multiple_of(at * count + r.start, 16), 16)] = (
                    stream * inverse * gain
                ).astype(BF16)

            each_rows(count, 16, norm)
        for copy in copies[1:]:
            copy.wait()
        tile = 2 * LANES

        def project(n, carried):
            down = pl.ds(pl.multiple_of(n % wt * count, LANES), count)
            across = pl.ds(pl.multiple_of(n // wt * tile, tile), tile)
            xy_one[down, across] = multiply(rows_one[down], xy_v[:, across])
            return carried

        lax.fori_loop(0, wt * (xy_v.shape[1] // tile), project, 0)

    lines[0].begin()
    tokens_begin()
    here_first = [copy for _, copy in here]
    here.clear()

    @pl.when(jnp.logical_not(here_too))
    def _():
        arrived(gates_own, turn_sems.at[1], at_c)

    pl.when(here_too)(stay.wait)
    lines[1].begin()
    lines[2].begin_z()
    lax.fori_loop(0, seq * wt, vector_send, 0)
    for k in range(1, Z):
        lines[1].step(k)
        lines[0].step(k)
        if k == 1:
            tokens_step()
    lines[2].begin_x()
    for k in range(1, Z):
        lines[2].step(k)
        if k == Z - 2:
            planes[0].begin()
            planes[2].begin()
            planes[1].begin()
    for k in range(Z):
        planes[0].first(k)
    for k in range(Z):
        planes[2].first(k)
    keep(grads, group.place(0, z, z))
    group.begin()
    for k in range(Z):
        planes[1].first(k)
    for k in range(Z):
        planes[0].second(k)
    group.step(1)
    first_projection()
    for k in range(2, Z):
        group.step(k)
    group.finish()

    for line in lines[1:]:
        line.finish()
    for k in range(Z):
        planes[1].second(k)
        planes[2].second(k)
        planes[0].finish(k)

    pl.when(jnp.logical_not(here_too))(turn.wait_send)
    sends.finish()
    for waited, copy in here:
        if not waited:
            copy.wait()


def gather_all(tokens, grads, vectors, gates, xy, out, gate, up, down):
    inner, outer = sizes()
    seq, wt = Z * inner, outer * C

    def buffer(*shape, like):
        return jax.ShapeDtypeStruct(shape, like.dtype)

    def plane(weight):
        rows, columns = weight.shape
        return buffer(Z, inner, rows, outer * columns // Z, like=weight)

    shapes = (
        buffer(C, Z, *grads.shape, like=grads),
        buffer(seq * wt, *vectors.shape, like=vectors),
        buffer(Z, inner, *gates.shape, like=gates),
        buffer(Z, inner, *xy.shape, like=xy),
        buffer(Z, inner, *out.shape, like=out),
        plane(gate),
        plane(up),
        plane(down),
        buffer(wt * tokens.shape[0], tokens.shape[1], like=tokens),
        jax.ShapeDtypeStruct((wt * tokens.shape[0], xy.shape[1]), F32),
    )
    copies = 3 * (2 + inner + (Z - 1) * 2 * inner) + 3 * (Z - 1 + Z * (inner + 2 * outer + inner * outer))
    copies += 2 * outer + 3 + 4 * Z
    dma = pltpu.SemaphoreType.DMA
    return pl.pallas_call(
        functools.partial(gather_kernel, (inner, outer)),
        out_shape=shapes,
        in_specs=[pl.BlockSpec(memory_space=pl.ANY)] * 9,
        out_specs=[pl.BlockSpec(memory_space=pl.ANY)] * 8 + [pl.BlockSpec(memory_space=pltpu.VMEM)] * 2,
        scratch_shapes=[
            pltpu.VMEM(gates.shape, gates.dtype),
            dma((copies,)),
            dma((16,)),
            dma((3, Z, inner)),
            dma((3, Z, inner, outer)),
            dma((wt,)),
            dma((2, seq * wt)),
            dma((3,)),
            dma((C, Z)),
            pltpu.VMEM((wt, *tokens.shape), tokens.dtype),
            pltpu.VMEM((Z * inner * xy.shape[0], xy.shape[1]), xy.dtype),
            pltpu.VMEM((seq * wt, *vectors.shape), F32),
            pltpu.VMEM((8, tokens.shape[1]), F32),
            dma((1 + Z * inner,)),
        ],
        compiler_params=pltpu.CompilerParams(
            collective_id=0, has_side_effects=True, vmem_limit_bytes=40 * 1024 * 1024
        ),
        name="gather_all",
    )(tokens, grads, vectors, gates, xy, out, gate, up, down)


class Place:
    def __init__(self, shape):
        self.inner, self.outer = shape
        self.s, self.w = lax.axis_index("seq"), lax.axis_index("wt")
        self.z, self.x = self.s // self.inner, self.s % self.inner
        self.y, self.c = self.w // C, self.w % C
        self.at_c = {"seq": self.s, "wt": self.y * C + 1 - self.c}
        self.z_up, self.z_down = jnp.minimum(self.z + 1, Z - 1), jnp.maximum(self.z - 1, 0)

    def at_z(self, to):
        return {"seq": to * self.inner + self.x, "wt": self.w}

    def at_x(self, by):
        return {"seq": self.z * self.inner + (self.x + by) % self.inner, "wt": self.w}

    def at_y(self, by):
        return {"seq": self.s, "wt": (self.y + self.outer + by) % self.outer * C + self.c}

    def greet_all(self):
        barrier = pltpu.get_barrier_semaphore()
        wt = self.outer * C
        count = Z * self.inner * wt

        def signal(i, carried):
            @pl.when(i != self.s * wt + self.w)
            def _():
                pl.semaphore_signal(
                    barrier, inc=1, device_id={"seq": i // wt, "wt": i % wt}, device_id_type=MESH
                )

            return carried

        lax.fori_loop(0, count, signal, 0)
        pl.semaphore_wait(barrier, count - 1)

    def greet(self):
        barrier = pltpu.get_barrier_semaphore()
        devices = [self.at_c]
        devices += [self.at_z((self.z + k) % Z) for k in range(1, Z)]
        devices += [self.at_x(j) for j in range(1, self.inner)]
        devices += [self.at_y(i) for i in range(1, self.outer)]
        for device in devices:
            pl.semaphore_signal(barrier, inc=1, device_id=device, device_id_type=MESH)
        pl.semaphore_wait(barrier, len(devices))


def each_rows(count, step, body):
    def run(i, carried):
        body(pl.ds(pl.multiple_of(i * step, step), step))
        return carried

    lax.fori_loop(0, count // step, run, 0)


class WtRows:
    def __init__(self, me, sends, source, target, sems):
        self.me, self.sends, self.source, self.target, self.sems = me, sends, source, target, sems

    def begin(self):
        me = self.me
        for device in [me.at_y(i) for i in range(1, me.outer)] + [me.at_c]:
            self.sends.start(True, self.source, self.target.at[me.w], self.sems.at[me.w], device)

    def step(self):
        me = self.me
        for i in range(1, me.outer):
            at = (me.y + me.outer - i) % me.outer * C + me.c
            arrived(self.target.at[at], self.sems.at[at], me.at_c)
            self.sends.start(True, self.target.at[at], self.target.at[at], self.sems.at[at], me.at_c)

    def finish(self):
        me = self.me
        for i in range(me.outer):
            at = (me.y + me.outer - i) % me.outer * C + 1 - me.c
            arrived(self.target.at[at], self.sems.at[at], me.at_c)


class GroupRows:
    def __init__(self, me, sends, source, target, sems):
        self.me, self.sends, self.source, self.target, self.sems = me, sends, source, target, sems

    def place(self, own, at, z_to):
        return self.target.at[own, (z_to - at + Z) % Z]

    def forward(self, at, source, there, way):
        me = self.me
        z_to = me.z_up if way > 0 else me.z_down
        room = me.z < Z - 1 if way > 0 else me.z > 0
        when = room if there is None else there & room
        self.sends.start(
            when, source, self.place(0, at, z_to), self.sems.at[0, at], me.at_z(z_to)
        )

    def begin(self):
        me = self.me
        self.forward(me.z, self.source, None, 1)
        self.forward(me.z, self.source, None, -1)
        self.sends.start(
            True, self.source, self.place(1, me.z, me.z), self.sems.at[1, me.z], me.at_c
        )

    def step(self, k):
        me = self.me
        for at, there, way in (
            (jnp.maximum(me.z - k, 0), me.z - k >= 0, 1),
            (jnp.minimum(me.z + k, Z - 1), me.z + k < Z, -1),
        ):
            place = self.place(0, at, me.z)

            @pl.when(there)
            def _(place=place, at=at):
                arrived(place, self.sems.at[0, at], me.at_c)

            self.forward(at, place, there, way)
            self.sends.start(there, place, self.place(1, at, me.z), self.sems.at[1, at], me.at_c)

    def finish(self):
        me = self.me
        for at in range(Z):
            arrived(self.place(1, at, me.z), self.sems.at[1, at], me.at_c)


def branch_kernel(
    shape, sent, own, tokens, gain, up_held, down_held, group_to, middle, up_to, down_to,
    own_v, c_in, y_out, y_in, low,
    send_sems, local_sems, c_sems, y_sems, group_sems, up_sems, down_sems,
):
    del up_held, down_held
    me = Place(shape)
    inner, outer = shape
    share = up_to.shape[3] // outer
    rows = tokens.shape[0]
    sends = Sends(send_sems)
    load = pltpu.make_async_copy(own, own_v, local_sems.at[0])
    load.start()
    me.greet()
    order = [(me.y + i) % outer for i in list(range(1, outer)) + [0]]
    for at in order:
        sends.start(True, sent.at[at], c_in.at[at], c_sems.at[at], me.at_c)

    def columns(held, x_at, i):
        return held.at[:, x_at, :, i * share : (i + 1) * share]

    for j in range(1, inner):
        for i in range(outer):
            place = columns(up_to, me.x, i)
            sends.start(True, place, place, up_sems.at[j - 1, i], me.at_x(j))
    load.wait()
    for i, at in enumerate(order):
        arrived(c_in.at[at], c_sems.at[at], me.at_c)
        if i < outer - 1:
            each_rows(rows, 16, lambda r, i=i, at=at: y_out.__setitem__(
                (i, r), (own_v[at, r] + c_in[at, r]).astype(BF16)))
            sends.start(True, y_out.at[i], y_in.at[i], y_sems.at[i], me.at_y(i + 1))
    for i in range(outer - 1):
        arrived(y_in.at[i], y_sems.at[i], me.at_c)
    for i in range(1, outer):
        for j in range(inner):
            x_at = (me.x + inner - j) % inner
            sends.start(
                True, columns(down_to, x_at, 0), columns(down_to, x_at, i),
                down_sems.at[i - 1, j], me.at_y(i),
            )

    def work(r):
        total = tokens[r].astype(F32) + own_v[me.y, r] + c_in[me.y, r]
        for i in range(outer - 1):
            total = total + y_in[i, r].astype(F32)
        inverse = lax.rsqrt(jnp.mean(total * total, axis=1, keepdims=True) + EPSILON)
        middle[r] = total
        low[r] = (total * inverse * gain[...]).astype(BF16)

    each_rows(rows, 16, work)
    keep = pltpu.make_async_copy(low, group_to.at[0, 0], local_sems.at[1])
    keep.start()
    group = GroupRows(me, sends, low, group_to, group_sems)
    group.begin()
    for k in range(1, Z):
        group.step(k)
    group.finish()
    for j in range(1, inner):
        for i in range(outer):
            x_at = (me.x + inner - j) % inner
            arrived(columns(up_to, x_at, i), up_sems.at[j - 1, i], me.at_c)
    for i in range(1, outer):
        for j in range(inner):
            x_at = (me.x + inner - j) % inner
            arrived(columns(down_to, x_at, i), down_sems.at[i - 1, j], me.at_c)
    sends.finish()
    keep.wait()


def branch_and_group(sent, own, tokens, gain, up, down):
    inner, outer = sizes()
    rows, width = tokens.shape
    dma = pltpu.SemaphoreType.DMA
    vmem, anywhere = pl.BlockSpec(memory_space=pltpu.VMEM), pl.BlockSpec(memory_space=pl.ANY)
    return pl.pallas_call(
        functools.partial(branch_kernel, (inner, outer)),
        out_shape=(
            jax.ShapeDtypeStruct((C, Z, rows, width), BF16),
            jax.ShapeDtypeStruct((rows, width), F32),
            jax.ShapeDtypeStruct(up.shape, up.dtype),
            jax.ShapeDtypeStruct(down.shape, down.dtype),
        ),
        in_specs=[anywhere, anywhere, vmem, vmem, anywhere, anywhere],
        out_specs=(anywhere, vmem, anywhere, anywhere),
        input_output_aliases={4: 2, 5: 3},
        scratch_shapes=[
            pltpu.VMEM((outer, rows, width), F32),
            pltpu.VMEM((outer, rows, width), F32),
            pltpu.VMEM((outer - 1, rows, width), BF16),
            pltpu.VMEM((outer - 1, rows, width), BF16),
            pltpu.VMEM((rows, width), BF16),
            dma((2 * outer + 3 + 4 * (Z - 1) + (inner - 1) * outer + inner * (outer - 1),)),
            dma((2,)),
            dma((outer,)),
            dma((outer - 1,)),
            dma((C, Z)),
            dma((inner - 1, outer)),
            dma((outer - 1, inner)),
        ],
        compiler_params=pltpu.CompilerParams(
            collective_id=1, has_side_effects=True, vmem_limit_bytes=40 * 1024 * 1024
        ),
        name="branch_and_group",
    )(sent, own, tokens, gain, up, down)


def line_order():
    order = []
    for k in [n for t in range(1, Z) for n in (t, Z - t)] + [0]:
        if k not in order:
            order.append(k)
    return order


def line_sum(me, sends, rows, term, ready, store, held, up, down, between=None):
    z = me.z

    def add(when, target, slot, k, received=None, came=0):
        def body(r):
            value = term(k, r)
            if received is not None:
                value = value + received[came, r].astype(F32)
            target[slot, r] = value.astype(BF16)

        pl.when(when)(lambda: each_rows(rows, 16, body))

    for t in range(1, Z):
        slot = t - 1
        for k, (out, into, sems), out_slot, has, when, to in (
            (t, up, slot, z > 0, (z <= t - 1) & (z < Z - 1), me.z_up),
            (Z - t, down, Z - 1 - t, z < Z - 1, (z >= Z - t) & (z > 0), me.z_down),
        ):
            pl.when(when)(lambda k=k: ready(k))
            if t == 1:
                add(when, out, out_slot, k)
            else:
                pl.when(when & has)(
                    lambda into=into, sems=sems, slot=slot: arrived(
                        into.at[slot - 1], sems.at[slot - 1], me.at_c
                    )
                )
                add(when & has, out, out_slot, k, into, slot - 1)
                add(when & jnp.logical_not(has), out, out_slot, k)
            sends.start(when, out.at[out_slot], into.at[slot], sems.at[slot], me.at_z(to))
        if between is not None:
            between(t)
    ready(0)
    each_rows(rows, 16, lambda r: store(r, term(0, r)))
    for (_, into, sems), has in ((up, z > 0), (down, z < Z - 1)):

        @pl.when(has)
        def _(into=into, sems=sems):
            arrived(into.at[Z - 2], sems.at[Z - 2], me.at_c)
            each_rows(rows, 16, lambda r: store(r, held(r) + into[Z - 2, r].astype(F32)))


class PlaneTerms:
    def __init__(self, me, sends, parts, over_x, blocks, scratch):
        self.me, self.sends, self.parts, self.over_x, self.blocks = me, sends, parts, over_x, blocks
        self.came, self.mine, self.sems, self.local_sems = scratch

    def begin(self):
        me = self.me
        if self.over_x:
            for j in range(1, me.inner):
                for i, part in enumerate(self.parts):
                    self.sends.start(
                        True, part.at[self.blocks, (me.x + j) % me.inner],
                        self.came.at[j - 1, i], self.sems.at[j - 1, i], me.at_x(j),
                    )
            pairs = [(part.at[self.blocks, me.x], self.mine.at[i]) for i, part in enumerate(self.parts)]
        else:
            for i in range(1, me.outer):
                self.sends.start(
                    True, self.parts[i].at[self.blocks], self.came.at[i - 1],
                    self.sems.at[0, i - 1], me.at_y(-i),
                )
            pairs = [(self.parts[0].at[self.blocks], self.mine)]
        self.loads = self.moved(pairs)

    def moved(self, pairs):
        copies = [
            pltpu.make_async_copy(source, target, self.local_sems.at[n])
            for n, (source, target) in enumerate(pairs)
        ]
        for copy in copies:
            copy.start()
        return copies

    def add(self):
        me = self.me
        if self.over_x:
            count, places = me.inner - 1, [(i,) for i in range(me.outer)]
        else:
            count, places = me.outer - 1, [()]
        for n in range(count):
            for place in places:
                sems = self.sems.at[n, place[0]] if place else self.sems.at[0, n]
                arrived(self.came.at[(n, *place)], sems, me.at_c)
        for copy in self.loads:
            copy.wait()
        shape = self.mine.shape[:2]

        def body(r):
            for first in range(shape[0]):
                for second in range(shape[1]):
                    total = self.mine[first, second, r].astype(F32)
                    for n in range(count):
                        total = total + self.came[n, first, second, r].astype(F32)
                    self.mine[first, second, r] = total.astype(BF16)

        each_rows(self.mine.shape[2], 16, body)

    def hand_on(self, kept, sent):
        me = self.me
        if self.over_x:
            pairs = [(self.mine.at[i], kept if i == 0 else sent(i - 1)) for i in range(me.outer)]
        else:
            pairs = [
                (self.mine.at[:, (me.x + j) % me.inner], kept if j == 0 else sent(j - 1))
                for j in range(me.inner)
            ]
        self.loads = self.moved(pairs)

    def second(self, into, sems):
        me = self.me
        for j in range(1, me.inner):
            self.sends.start(
                True, self.mine.at[:, (me.x + j) % me.inner], into.at[j - 1], sems.at[j - 1],
                me.at_x(j),
            )

    def add_second(self, into, sems, kept):
        me = self.me
        for j in range(1, me.inner):
            arrived(into.at[j - 1], sems.at[j - 1], me.at_c)

        def body(r):
            for first in range(self.mine.shape[0]):
                total = self.mine[first, me.x, r].astype(F32)
                for j in range(1, me.inner):
                    total = total + into[j - 1, first, r].astype(F32)
                self.mine[first, me.x, r] = total.astype(BF16)

        each_rows(self.mine.shape[2], 16, body)
        self.loads = self.moved([(self.mine.at[:, me.x], kept)])

    def finish(self):
        for copy in self.loads:
            copy.wait()


def middle_kernel(shape, *refs):
    outer = shape[1]
    sent, own, middle, grads, gain, hidden, down_kernel = refs[:7]
    parts = refs[7 : 7 + 3 * outer]
    rows_to, d_middle, gain_grad, block_out = refs[7 + 3 * outer : 11 + 3 * outer]
    targets = refs[11 + 3 * outer : 14 + 3 * outer]
    scratch = refs[14 + 3 * outer :]
    middle_body(
        shape, sent, own, middle, grads, gain, hidden, down_kernel, parts, targets,
        rows_to, d_middle, gain_grad, block_out, scratch[:8], scratch[8:16],
        [scratch[16 + 4 * n : 20 + 4 * n] for n in range(4)], *scratch[32:],
    )


class PairSum:
    def __init__(self, me, sends, sent, own, scratch):
        self.me, self.sends, self.sent = me, sends, sent
        self.held, self.c_in, out, up_in, down_in, self.c_sems, up_sems, down_sems = scratch
        self.up, self.down = (out, up_in, up_sems), (out, down_in, down_sems)

    def begin(self):
        for k in line_order():
            self.sends.start(
                True, self.sent.at[k], self.c_in.at[k], self.c_sems.at[k], self.me.at_c
            )

    def run(self, between=None):
        def ready(k):
            arrived(self.c_in.at[k], self.c_sems.at[k], self.me.at_c)

        def term(k, r):
            return self.held[k, r] + self.c_in[k, r].astype(F32)

        def store(r, value):
            self.held[0, r] = value

        line_sum(
            self.me, self.sends, self.held.shape[1], term, ready, store,
            lambda r: self.held[0, r], self.up, self.down, between,
        )


def plane_units(me, sends, parts, scratch):
    outer = me.outer
    gate, up, down = (parts[n * outer : (n + 1) * outer] for n in range(3))
    every, low, high = slice(0, Z), slice(0, Z // 2), slice(Z // 2, Z)
    return [
        PlaneTerms(me, sends, gate, True, every, scratch[0]),
        PlaneTerms(me, sends, up, False, every, scratch[1]),
        PlaneTerms(me, sends, down, True, low, scratch[2]),
        PlaneTerms(me, sends, down, False, high, scratch[3]),
    ]


def middle_body(
    shape, sent, own, middle, grads, gain, hidden, down_kernel, parts, targets,
    rows_to, d_middle, gain_grad, block_out, sum_scratch, feed_scratch, unit_scratch, low,
    up_in, hidden_v, feed_sent, down_v, send_sems, local_sems, rows_sems, up_sems, down_sems,
):
    me = Place(shape)
    rows = middle.shape[0]
    sends = Sends(send_sems)
    total = PairSum(me, sends, sent, own, sum_scratch)
    feed = PairSum(me, sends, feed_sent, None, feed_scratch)
    load = pltpu.make_async_copy(own, total.held, local_sems.at[0])
    hidden_load = pltpu.make_async_copy(hidden, hidden_v, local_sems.at[2])
    load.start()
    hidden_load.start()
    me.greet()
    total.begin()
    units = plane_units(me, sends, parts, unit_scratch)
    units_to, units_y, units_x = targets
    for unit in units:
        unit.begin()

    step = down_v.shape[1]
    half_rows = Z * rows

    def down_load(n, slot):
        part = down_kernel.at[pl.ds(pl.multiple_of(n * step, LANES), step)]
        return pltpu.make_async_copy(part, down_v.at[slot], down_sems.at[slot])

    def feed_product(n, carried):
        slot = n % 2
        down_load(n, slot).wait()
        pl.when(n + 1 < down_kernel.shape[0] // step)(lambda: down_load(n + 1, 1 - slot).start())
        across = pl.ds(pl.multiple_of(n * step, LANES), step)
        weight = down_v[slot]
        for k in range(Z):
            kept = hidden_v[k * rows : (k + 1) * rows]
            other = hidden_v[half_rows + k * rows : half_rows + (k + 1) * rows]
            feed.held[k, :, across] = contract_last(kept, weight)
            feed_sent[k, :, across] = contract_last(other, weight).astype(BF16)
        return carried

    down_load(0, 0).start()
    load.wait()
    hidden_load.wait()
    pieces = down_kernel.shape[0] // step
    ends = [pieces * t // (Z - 1) for t in range(Z)]
    total.run(lambda t: lax.fori_loop(ends[t - 1], ends[t], feed_product, 0))
    own_v = total.held
    gain_grad[...] = jnp.zeros_like(gain_grad)

    def work(r):
        values = middle[r]
        inverse = lax.rsqrt(jnp.mean(values * values, axis=1, keepdims=True) + EPSILON)
        normed = values * inverse
        d_normed = own_v[0, r]
        gain_grad[...] += d_normed * normed
        scaled = d_normed * gain[...]
        passed = inverse * (scaled - normed * jnp.mean(scaled * normed, axis=1, keepdims=True))
        total = grads[r].astype(F32) + passed
        d_middle[r] = total
        low[r] = total.astype(BF16)

    each_rows(rows, 16, work)
    keep = pltpu.make_async_copy(low, rows_to.at[me.w], local_sems.at[1])
    keep.start()
    gather = WtRows(me, sends, low, rows_to, rows_sems)
    gather.begin()
    feed.begin()
    half, extra = Z // 2, slice(Z, Z + Z // 2)

    def between(t):
        if t == 1:
            units[0].add()
            units[0].hand_on(units_to.at[0], lambda i: units_y.at[i, 0:Z])
        if t == 2:
            units[1].add()
            units[1].second(up_in, up_sems)
        if t == 3:
            units[2].add()
            units[2].hand_on(units_to.at[2, 0:half], lambda i: units_y.at[i, extra])
            units[3].add()
            units[3].hand_on(units_to.at[2, half:Z], lambda j: units_x.at[j])

    feed.run(between)
    each_rows(rows, 16, lambda r: block_out.__setitem__(
        r, (middle[r] + feed.held[0, r]).astype(BF16)))
    gather.step()
    gather.finish()
    units[1].add_second(up_in, up_sems, units_to.at[1])
    for unit in units:
        unit.finish()
    sends.finish()
    keep.wait()


def middle_and_rows(sent, own, middle, grads, gain, hidden, down_kernel, parts):
    inner, outer = sizes()
    rows, width = middle.shape
    unit_rows, share = parts[0].shape[2:]
    block = (unit_rows, share)
    targets = [
        jax.ShapeDtypeStruct((*shape, *block), BF16)
        for shape in ((3, Z), (outer - 1, Z + Z // 2), (inner - 1, Z // 2))
    ]
    unit_copies = 2 * (inner - 1) * outer + 2 * (outer - 1) + (inner - 1)
    pair_scratch = [pltpu.VMEM((Z, rows, width), F32), pltpu.VMEM((Z, rows, width), BF16)]
    pair_scratch += [pltpu.VMEM((Z - 1, rows, width), BF16)] * 3
    dma = pltpu.SemaphoreType.DMA
    pair_scratch += [dma((Z,)), dma((Z - 1,)), dma((Z - 1,))]
    unit_scratch = []
    for came, mine in (
        ((inner - 1, outer, Z), (outer, Z)),
        ((outer - 1, Z, inner), (Z, inner)),
        ((inner - 1, outer, Z // 2), (outer, Z // 2)),
        ((outer - 1, Z // 2, inner), (Z // 2, inner)),
    ):
        unit_scratch += [pltpu.VMEM((*came, *block), BF16), pltpu.VMEM((*mine, *block), BF16)]
        unit_scratch += [dma((inner - 1, outer)), dma((max(inner, outer),))]
    vmem, anywhere = pl.BlockSpec(memory_space=pltpu.VMEM), pl.BlockSpec(memory_space=pl.ANY)
    return pl.pallas_call(
        functools.partial(middle_kernel, (inner, outer)),
        out_shape=(
            jax.ShapeDtypeStruct((outer * C, rows, width), BF16),
            jax.ShapeDtypeStruct((rows, width), F32),
            jax.ShapeDtypeStruct((16, width), F32),
            jax.ShapeDtypeStruct((rows, width), BF16),
            *targets,
        ),
        in_specs=[anywhere, anywhere, vmem, vmem, vmem] + [anywhere] * (2 + 3 * outer),
        out_specs=(anywhere, vmem, vmem, vmem) + (anywhere,) * 3,
        scratch_shapes=pair_scratch * 2
        + unit_scratch
        + [
            pltpu.VMEM((rows, width), BF16),
            pltpu.VMEM((inner - 1, Z, *block), BF16),
            pltpu.VMEM(hidden.shape, BF16),
            pltpu.VMEM((Z, rows, width), BF16),
            pltpu.VMEM((2, 2 * LANES, hidden.shape[1]), BF16),
            dma((2 * (Z + 2 * (Z - 1)) + 2 * outer + unit_copies,)),
            dma((3,)),
            dma((outer * C,)),
            dma((inner - 1,)),
            dma((2,)),
        ],
        compiler_params=pltpu.CompilerParams(
            collective_id=2, has_side_effects=True, vmem_limit_bytes=60 * 1024 * 1024
        ),
        name="middle_and_rows",
    )(sent, own, middle, grads, gain, hidden, down_kernel, *parts)


class RowsSum:
    def __init__(self, me, sends, terms, total, scratch, sems):
        self.me, self.sends, self.terms, self.total = me, sends, terms, total
        self.own, self.x_in, *ways = scratch
        self.own_sems, self.x_sems, up_sems, down_sems = sems
        self.up, self.down = (*ways[:2], up_sems), (*ways[2:], down_sems)

    def load(self):
        me = self.me
        self.loads = []
        for k in range(Z):
            self.loads.append(
                pltpu.make_async_copy(
                    self.terms.at[(me.z + Z - k) % Z, me.x], self.own.at[k], self.own_sems.at[k]
                )
            )
            self.loads[k].start()

    def begin(self, turns):
        me = self.me
        for turn in turns:
            if turn == Z - 1:
                k = 0
            else:
                k = (jnp.minimum(me.z, Z - 1 - me.z) + turn) % (Z - 1) + 1
                k = jnp.where(me.z < Z // 2, k, Z - k)
            at = (me.z + Z - k) % Z
            for j in range(1, me.inner):
                self.sends.start(
                    True, self.terms.at[at, (me.x + j) % me.inner], self.x_in.at[j - 1, k],
                    self.x_sems.at[j - 1, k], me.at_x(j),
                )

    def run(self, between=None):
        me = self.me

        def ready(k):
            self.loads[k].wait()
            for j in range(1, me.inner):
                arrived(self.x_in.at[j - 1, k], self.x_sems.at[j - 1, k], me.at_c)

        def term(k, r):
            value = self.own[k, r].astype(F32)
            for j in range(1, me.inner):
                value = value + self.x_in[j - 1, k, r].astype(F32)
            return value

        def store(r, value):
            self.total[r] = value

        line_sum(
            me, self.sends, self.total.shape[0], term, ready, store, lambda r: self.total[r],
            self.up, self.down, between,
        )


class ProductsSum(RowsSum):
    def __init__(self, me, sends, factors, total, scratch, sems):
        self.me, self.sends, self.total = me, sends, total
        self.factors = factors
        self.held, self.x_in, out, up_in, down_in, *self.lefts = scratch
        self.own_sems, self.x_sems, up_sems, down_sems = sems
        self.up, self.down = (out, up_in, up_sems), (out, down_in, down_sems)

    def load(self):
        self.loads = []
        for n, (left, _) in enumerate(self.factors):
            copy = pltpu.make_async_copy(left, self.lefts[n], self.own_sems.at[n])
            copy.start()
            self.loads.append(copy)

    def begin(self, turns):
        me = self.me
        while self.loads:
            self.loads.pop().wait()
        rows, span = self.total.shape[0], self.held.shape[1]
        for turn in turns:
            if turn == Z - 1:
                k = 0
            else:
                k = (jnp.minimum(me.z, Z - 1 - me.z) + turn) % (Z - 1) + 1
                k = jnp.where(me.z < Z // 2, k, Z - k)
            at = (me.z + Z - k) % Z

            def tile(i, carried, k=k, at=at):
                first = 0
                down = pl.ds(pl.multiple_of(i * LANES, LANES), LANES)
                across = pl.ds(pl.multiple_of(at * span + i * LANES, LANES), LANES)
                for n, (_, rights) in enumerate(self.factors):
                    left = self.lefts[n][:, across]
                    for right in rights:
                        columns = slice(first, first + right.shape[1])
                        self.held[k, down, columns] = contract_rows(left, right[...]).astype(BF16)
                        first += right.shape[1]
                return carried

            lax.fori_loop(0, span // LANES, tile, 0)
            for j in range(1, me.inner):
                part = pl.ds(pl.multiple_of((me.x + j) % me.inner * rows, 16), rows)
                self.sends.start(
                    True, self.held.at[k, part], self.x_in.at[j - 1, k], self.x_sems.at[j - 1, k],
                    me.at_x(j),
                )

    def run(self, between=None):
        me = self.me
        rows = self.total.shape[0]

        def ready(k):
            for j in range(1, me.inner):
                arrived(self.x_in.at[j - 1, k], self.x_sems.at[j - 1, k], me.at_c)

        def term(k, r):
            mine = pl.ds(pl.multiple_of(me.x * rows + r.start, 16), r.size)
            value = self.held[k, mine].astype(F32)
            for j in range(1, me.inner):
                value = value + self.x_in[j - 1, k, r].astype(F32)
            return value

        def store(r, value):
            self.total[r] = value

        line_sum(
            me, self.sends, rows, term, ready, store, lambda r: self.total[r],
            self.up, self.down, between,
        )


def sums_kernel(shape, *refs):
    inner, outer = shape
    units, units_y, units_x, normed_rows_one, branch_rows, narrow, sent, own = refs[:8]
    d_x, d_y, mixed, tokens, gain, d_middle, gain_two_grad, vectors = refs[8:16]
    units_to, wide_to, narrow_to, tokens_grad, gains, vectors_to = refs[16:22]
    refs = refs[22:]
    wide_scratch, narrow_scratch = refs[:7], refs[7:13]
    (own_v, c_in, y_out, y_in, parts_out, parts_in, gains_v, vec_in) = refs[13:21]
    refs = refs[2:]
    (send_sems, local_sems, c_sems, y_sems, all_sems, vec_sems) = refs[19:25]
    wide_sems, narrow_sems = refs[25:29], refs[29:33]
    units_v, units_y_in, units_x_in, unit_sems, units_y_sems, units_x_sems = refs[33:]
    share = units.shape[3]
    me = Place(shape)
    rows = tokens.shape[0]
    sends = Sends(send_sems)
    load = pltpu.make_async_copy(own, own_v, local_sems.at[0])
    load.start()
    units_load = pltpu.make_async_copy(units, units_v, local_sems.at[1])
    units_load.start()
    me.greet_all()

    order = [(me.y + i) % outer for i in list(range(1, outer)) + [0]]
    for at in order:
        sends.start(True, sent.at[at], c_in.at[at], c_sems.at[at], me.at_c)
    narrow_sum = RowsSum(me, sends, narrow, narrow_to, narrow_scratch, narrow_sems)
    factors = [(normed_rows_one, [d_x, d_y]), (branch_rows, [mixed])]
    wide_sum = ProductsSum(me, sends, factors, wide_to, wide_scratch, wide_sems)
    narrow_sum.load()
    wide_sum.load()
    narrow_sum.begin(range(Z))

    def columns(n, at):
        return units_to.at[n, :, pl.ds(pl.multiple_of(at * share, LANES), share)]

    low, high, extra = slice(0, Z // 2), slice(Z // 2, Z), slice(Z, Z + Z // 2)
    every = slice(0, Z)

    def units_begin_y():
        for n, blocks in enumerate((every, extra)):
            for i in range(1, outer):
                sends.start(
                    True, units_y.at[i - 1, blocks], units_y_in.at[i - 1, blocks],
                    units_y_sems.at[i - 1, n], me.at_y(-i),
                )

    def units_begin_x():
        for j in range(1, inner):
            sends.start(
                True, units_x.at[j - 1], units_x_in.at[j - 1], units_x_sems.at[j - 1], me.at_x(j)
            )

    kept = []

    def unit_add(n, blocks, came, came_blocks, sems, count):
        for i in range(count):
            arrived(came.at[i, came_blocks], sems.at[i], me.at_c)

        def body(r):
            for at in range(blocks.stop - blocks.start):
                total = units_v[n, blocks.start + at, r].astype(F32)
                for i in range(count):
                    total = total + came[i, came_blocks.start + at, r].astype(F32)
                units_v[n, blocks.start + at, r] = total.astype(BF16)

        each_rows(units_v.shape[2], 16, body)

    def unit_pass_on(n):
        copy = pltpu.make_async_copy(units_v.at[n, me.z], columns(n, me.z), local_sems.at[2 + n])
        copy.start()
        kept.append(copy)
        for k in range(1, Z):
            to = (me.z + k) % Z
            sends.start(
                True, units_v.at[n, to], columns(n, me.z), unit_sems.at[n, me.z], me.at_z(to)
            )

    def unit_gate():
        unit_add(0, every, units_y_in, every, units_y_sems.at[:, 0], outer - 1)
        unit_pass_on(0)

    def unit_down():
        unit_add(2, low, units_y_in, extra, units_y_sems.at[:, 1], outer - 1)
        unit_add(2, high, units_x_in, low, units_x_sems, inner - 1)
        unit_pass_on(2)


    def units_finish():
        for n in range(3):
            for k in range(1, Z):
                at = (me.z + Z - k) % Z
                arrived(columns(n, at), unit_sems.at[n, at], me.at_c)
        for copy in kept:
            copy.wait()

    def exchange(held, into, sems, first, devices):
        for n, device in enumerate(devices):
            sends.start(True, held, into.at[first + n], sems.at[first + n], device)

    def gathered(held, into, sems, first, devices):
        for n, _ in enumerate(devices):
            arrived(into.at[first + n], sems.at[first + n], me.at_c)
        total = into[first]
        for n in range(1, len(devices)):
            total = total + into[first + n]
        return held[...] + total

    z_stage = [me.at_z((me.z + k) % Z) for k in range(1, Z)]
    x_stage = [me.at_x(j) for j in range(1, inner)]

    devices = Z * inner * outer * C
    wt = outer * C
    here = me.s * wt + me.w
    width = tokens.shape[1]
    channels = width // devices

    def gains_cut():
        for i in range(devices):
            first = i * channels // LANES * LANES
            first = min(first, width - 2 * LANES)
            window = gains_v[:, first : first + 2 * LANES]
            turn = i * channels - first
            if turn:
                window = pltpu.roll(window, 2 * LANES - turn, 1)
            parts_out[i] = window[:, :LANES]

    def gains_copy(i):
        return pltpu.make_async_remote_copy(
            src_ref=parts_out.at[i], dst_ref=parts_in.at[here],
            send_sem=all_sems.at[0, i], recv_sem=all_sems.at[1, here],
            device_id={"seq": i // wt, "wt": i % wt}, device_id_type=MESH,
        )

    def gains_send(i, carried):
        pl.when(i != here)(lambda: gains_copy(i).start())
        return carried

    def gains_add(i, carried):
        @pl.when(i != here)
        def _():
            gains_copy(i).wait_send()
            arrived(parts_in.at[i], all_sems.at[1, i], me.at_c)
            gains[...] += parts_in[i]

        return carried

    exchange(vectors, vec_in, vec_sems, 0, x_stage)
    units_begin_x()

    units_begin_y()
    units_load.wait()
    unit_pass_on(1)

    load.wait()
    for i, at in enumerate(order):
        arrived(c_in.at[at], c_sems.at[at], me.at_c)
        if i < outer - 1:
            each_rows(rows, 16, lambda r, i=i, at=at: y_out.__setitem__(
                (i, r), (own_v[at, r] + c_in[at, r].astype(F32)).astype(BF16)))
            sends.start(True, y_out.at[i], y_in.at[i], y_sems.at[i], me.at_y(i + 1))
    vectors_to[0] = gathered(vectors, vec_in, vec_sems, 0, x_stage)
    exchange(vectors_to.at[0], vec_in, vec_sems, len(x_stage), z_stage)
    narrow_sum.run()
    vectors_to[1] = gathered(vectors_to.at[0], vec_in, vec_sems, len(x_stage), z_stage)
    wide_sum.begin(range(1))
    unit_gate()
    wide_sum.begin(range(1, 2))
    unit_down()
    wide_sum.begin(range(2, Z))

    def work(r):
        d_normed = own_v[me.y, r] + c_in[me.y, r].astype(F32)
        for i in range(outer - 1):
            d_normed = d_normed + y_in[i, r].astype(F32)
        stream = tokens[r].astype(F32)
        inverse = lax.rsqrt(jnp.mean(stream * stream, axis=1, keepdims=True) + EPSILON)
        normed = stream * inverse
        part = d_normed * normed
        gains_v[0:8] += part[0:8] + part[8:16]
        scaled = d_normed * gain[...]
        passed = inverse * (scaled - normed * jnp.mean(scaled * normed, axis=1, keepdims=True))
        tokens_grad[r] = (d_middle[r] + passed).astype(BF16)

    def between(t):
        if t == 1:
            for i in range(outer - 1):
                arrived(y_in.at[i], y_sems.at[i], me.at_c)
            gains_v[...] = jnp.zeros_like(gains_v)
            each_rows(rows, 16, work)
            gains_v[8:16] = gain_two_grad[0:8] + gain_two_grad[8:16]
            gains_cut()
            lax.fori_loop(0, devices, gains_send, 0)

    wide_sum.run(between)
    gains[...] = parts_out[here]
    lax.fori_loop(0, devices, gains_add, 0)
    units_finish()
    sends.finish()


def last_sums(
    units, units_y, units_x, normed_one, branch_rows, narrow, sent, own,
    d_x, d_y, mixed, tokens, gain, d_middle, gain_two_grad, vectors,
):
    inner, outer = sizes()
    rows, width = tokens.shape
    dma = pltpu.SemaphoreType.DMA
    vmem, anywhere = pl.BlockSpec(memory_space=pltpu.VMEM), pl.BlockSpec(memory_space=pl.ANY)

    def scratch(terms):
        one = terms.shape[2:]
        return [pltpu.VMEM((Z, *one), BF16), pltpu.VMEM((inner - 1, Z, *one), BF16)] + [
            pltpu.VMEM((Z - 1, *one), BF16)
        ] * 4

    devices = Z * inner * outer * C
    copies = 2 * outer - 1 + 2 * (Z * (inner - 1) + 2 * (Z - 1))
    copies += (inner - 1) + (Z - 1) + 2 * (outer - 1) + 2 * (inner - 1) + 3 * (Z - 1)
    _, _, unit_rows, share = units.shape
    block = (unit_rows, d_x.shape[1] + d_y.shape[1] + mixed.shape[1])
    line_sems = [dma((Z,)), dma((inner - 1, Z)), dma((Z - 1,)), dma((Z - 1,))]
    return pl.pallas_call(
        functools.partial(sums_kernel, (inner, outer)),
        out_shape=(
            jax.ShapeDtypeStruct((3, unit_rows, Z * share), BF16),
            jax.ShapeDtypeStruct(block, F32),
            jax.ShapeDtypeStruct(narrow.shape[2:], F32),
            jax.ShapeDtypeStruct((rows, width), BF16),
            jax.ShapeDtypeStruct((16, LANES), F32),
            jax.ShapeDtypeStruct((2, *vectors.shape), F32),
        ),
        in_specs=[anywhere] * 8 + [vmem] * 8,
        out_specs=(anywhere,) + (vmem,) * 5,
        scratch_shapes=[
            pltpu.VMEM((Z, inner * block[0], block[1]), BF16),
            pltpu.VMEM((inner - 1, Z, *block), BF16),
        ]
        + [pltpu.VMEM((Z - 1, *block), BF16)] * 3
        + [pltpu.VMEM(normed_one.shape, BF16), pltpu.VMEM(branch_rows.shape, BF16)]
        + scratch(narrow)
        + [
            pltpu.VMEM((outer, rows, width), F32),
            pltpu.VMEM((outer, rows, width), BF16),
            pltpu.VMEM((outer - 1, rows, width), BF16),
            pltpu.VMEM((outer - 1, rows, width), BF16),
            pltpu.VMEM((devices, 16, LANES), F32),
            pltpu.VMEM((devices, 16, LANES), F32),
            pltpu.VMEM((16, width), F32),
            pltpu.VMEM((inner - 1 + Z - 1, *vectors.shape), F32),
            dma((copies,)),
            dma((5,)),
            dma((outer,)),
            dma((outer - 1,)),
            dma((2, devices)),
            dma((inner - 1 + Z - 1,)),
        ]
        + line_sems * 2
        + [
            pltpu.VMEM(units.shape, BF16),
            pltpu.VMEM(units_y.shape, BF16),
            pltpu.VMEM(units_x.shape, BF16),
            dma((3, Z)),
            dma((outer - 1, 2)),
            dma((inner - 1,)),
        ],
        compiler_params=pltpu.CompilerParams(
            collective_id=5, has_side_effects=True, vmem_limit_bytes=60 * 1024 * 1024
        ),
        name="last_sums",
    )(
        units, units_y, units_x, normed_one, branch_rows, narrow, sent, own,
        d_x, d_y, mixed, tokens, gain, d_middle, gain_two_grad, vectors,
    )


def scan_kernel(backward, factors, inflows, states, entered, products, ends, ends_in, carry, send_sems, arrivals):
    seq = ends_in.shape[0]
    s = lax.axis_index("seq")
    rows, width = factors.shape
    barrier = pltpu.get_barrier_semaphore()

    def device(at):
        return {"seq": at, "wt": lax.axis_index("wt")}

    def greet(i, carried):
        @pl.when(i != s)
        def _():
            pl.semaphore_signal(barrier, inc=1, device_id=device(i), device_id_type=MESH)

        return carried

    lax.fori_loop(0, seq, greet, 0)
    group = 8
    at_row = lax.broadcasted_iota(jnp.int32, (group, width), 0)

    def step(i, carried):
        held, product = carried
        i = rows // group - 1 - i if backward else i
        where = pl.ds(pl.multiple_of(i * group, group), group)
        factor, inflow = factors[where, :], inflows[where, :]
        for by in (1, 2, 4):
            inside = at_row < group - by if backward else at_row >= by
            turn = group - by if backward else by
            inflow = factor * jnp.where(inside, pltpu.roll(inflow, turn, 0), 0.0) + inflow
            factor = factor * jnp.where(inside, pltpu.roll(factor, turn, 0), 1.0)
        inflow = inflow + factor * held
        factor = factor * product
        states[where, :] = inflow
        products[where, :] = factor
        last = slice(0, 1) if backward else slice(group - 1, group)
        return inflow[last], factor[last]

    held, product = lax.fori_loop(
        0, rows // group, step, (jnp.zeros((1, width), F32), jnp.ones((1, width), F32))
    )
    ends[0:1] = product
    ends[1:2] = held
    pl.semaphore_wait(barrier, seq - 1)

    def copy_to(i):
        return pltpu.make_async_remote_copy(
            src_ref=ends, dst_ref=ends_in.at[s], send_sem=send_sems.at[i], recv_sem=arrivals.at[s],
            device_id=device(i), device_id_type=MESH,
        )

    def later(i):
        return i < s if backward else i > s

    def send(i, carried):
        pl.when(later(i))(lambda: copy_to(i).start())
        return carried

    lax.fori_loop(0, seq, send, 0)
    carry[...] = jnp.zeros_like(carry)

    def receive(n, carried):
        i = seq - 1 - n if backward else n

        @pl.when(jnp.logical_not(later(i)) & (i != s))
        def _():
            arrived(ends_in.at[i], arrivals.at[i], device((s + 1) % seq))
            carry[0:1] = ends_in[i, 0:1] * carry[0:1] + ends_in[i, 1:2]

        return carried

    lax.fori_loop(0, seq, receive, 0)
    entering = carry[0:1]
    entered[...] = entering

    def spread(i, carried):
        where = pl.ds(pl.multiple_of(i * group, group), group)
        states[where, :] += products[where, :] * entering
        return carried

    lax.fori_loop(0, rows // group, spread, 0)

    def sent(i, carried):
        pl.when(later(i))(lambda: copy_to(i).wait_send())
        return carried

    lax.fori_loop(0, seq, sent, 0)


def full_scan(factor, inflow, backward):
    seq = lax.axis_size("seq")
    rows, width = factor.shape
    vmem = pl.BlockSpec(memory_space=pltpu.VMEM)
    return pl.pallas_call(
        functools.partial(scan_kernel, backward),
        out_shape=(
            jax.ShapeDtypeStruct((rows, width), F32),
            jax.ShapeDtypeStruct((1, width), F32),
        ),
        in_specs=[vmem, vmem],
        out_specs=(vmem, vmem),
        scratch_shapes=[
            pltpu.VMEM((rows, width), F32),
            pltpu.VMEM((8, width), F32),
            pltpu.VMEM((seq, 8, width), F32),
            pltpu.VMEM((8, width), F32),
            pltpu.SemaphoreType.DMA((seq,)),
            pltpu.SemaphoreType.DMA((seq,)),
        ],
        compiler_params=pltpu.CompilerParams(
            collective_id=4 if backward else 3,
            has_side_effects=True,
            vmem_limit_bytes=32 * 1024 * 1024,
        ),
        name="scan_back" if backward else "scan_ahead",
    )(factor, inflow)


def recurrence_terms(decay_pre, input_pre, decay_log, conv_float):
    log_decay = -DECAY_SCALE * jax.nn.softplus(-decay_log) * jax.nn.sigmoid(decay_pre)
    return (
        jnp.exp(log_decay),
        jnp.sqrt(-jnp.expm1(2.0 * log_decay)) * jax.nn.sigmoid(input_pre) * conv_float,
    )


def per_device(
    tokens,
    norm1_gain,
    x_weight,
    y_weight,
    conv_weight,
    conv_bias,
    decay_gate_weight,
    decay_bias,
    input_gate_weight,
    input_bias,
    decay_param,
    out_weight,
    norm2_gain,
    gate_weight,
    up_weight,
    down_weight,
    out_grad,
):
    seq, wt = lax.axis_size("seq"), lax.axis_size("wt")
    inner, outer = sizes()
    z, x, y, c = places()
    w = lax.axis_index("wt")
    rows_dev, width = tokens.shape
    weight_rows, lru_cols = x_weight.shape
    chunk, block = decay_gate_weight.shape
    half = block // 2
    full = lru_cols - half
    taps_count = conv_weight.shape[1]
    reach = taps_count - 1
    hidden_cols = gate_weight.shape[1]

    def turned(value, axis):
        return jnp.where(c == 0, value, jnp.roll(value, -half, axis))

    def turned_back(value, axis):
        return jnp.where(c == 0, value, jnp.roll(value, half, axis))

    def in_order(own, partner, axis):
        return jnp.where(
            c == 0,
            jnp.concatenate([own, partner], axis),
            jnp.concatenate([partner, own], axis),
        )

    vectors = jnp.stack(
        [v.astype(F32) for v in (norm1_gain, norm2_gain, conv_bias, decay_bias, input_bias)]
        + [decay_param]
        + [conv_weight[:, k].astype(F32) for k in range(taps_count)]
    )
    vectors = jnp.pad(vectors, ((0, -vectors.shape[0] % 8), (0, -chunk % LANES)))

    across = [(i, i % seq * wt + i // seq) for i in range(seq * wt)]
    gates = jnp.concatenate([decay_gate_weight, input_gate_weight], axis=1)

    def padded(weight):
        share = -(-hidden_cols // (Z * LANES)) * LANES
        return jnp.pad(weight, ((0, 0), (0, Z * share - hidden_cols)))

    xy_unit = jnp.concatenate([turned(x_weight, 1), turned(y_weight, 1)], axis=1)
    (
        grad_group, vectors, gate_all, xy_kernel, out_kernel, gate_kernel, up_kernel, down_kernel,
        group_one, xy,
    ) = gather_all(
        tokens, out_grad, vectors, gates, xy_unit, turned(out_weight, 1),
        padded(gate_weight), padded(up_weight), padded(down_weight),
    )
    grad_group = grad_group.reshape(-1, width)
    vectors = jnp.moveaxis(vectors[:, : 6 + taps_count, :chunk], 0, 1).reshape(6 + taps_count, -1)
    gain_one, gain_two = vectors[0], vectors[1]
    own_vectors = turned(
        lax.dynamic_slice(vectors[2:], (0, w * lru_cols), (taps_count + 4, lru_cols)), 1
    )
    tap_bias, decay_shift, input_shift, decay_log = (own_vectors[i] for i in range(4))
    taps = own_vectors[4:]
    xy_kernel = xy_kernel.reshape(width, -1)
    out_kernel = out_kernel.reshape(width, -1)
    gate_kernel = gate_kernel.reshape(width, -1)
    gate_all = turned(gate_all.reshape(lru_cols, 2 * block), 0)
    partner_rows = c_swap(gate_all[full:])
    shared_rows = in_order(gate_all[full:], partner_rows, 0)

    stream = tokens.astype(F32)
    rows = group_one.shape[0]
    x_branch = xy[:, :lru_cols].astype(BF16)
    y_before = xy[:, lru_cols:]
    y_gated, gelu_y_back = jax.vjp(gelu_tanh, y_before)
    rim = lax.ppermute(x_branch[rows - reach :], "seq", [(i, i + 1) for i in range(seq - 1)])
    extended = jnp.concatenate([rim, x_branch], axis=0).astype(F32)
    conv_low = (
        tap_bias
        + sum(taps[k] * extended[reach - k : reach - k + rows] for k in range(taps_count))
    ).astype(BF16)
    shared_conv = in_order(conv_low[:, full:], c_swap(conv_low[:, full:]), 1)
    heads = full // block

    def of_head(value, i):
        return value[:, i * block : (i + 1) * block]

    pre_parts = [
        multiply(of_head(conv_low, i), gate_all[i * block : (i + 1) * block]) for i in range(heads)
    ]
    shared_columns = jnp.where(
        c == 0,
        jnp.concatenate([shared_rows[:, :half], shared_rows[:, block : block + half]], axis=1),
        jnp.concatenate([shared_rows[:, half:block], shared_rows[:, block + half :]], axis=1),
    )
    shared_pre = multiply(shared_conv, shared_columns)
    decay_pre = decay_shift + jnp.concatenate(
        [part[:, :block] for part in pre_parts] + [shared_pre[:, :half]], axis=1
    )
    input_pre = input_shift + jnp.concatenate(
        [part[:, block:] for part in pre_parts] + [shared_pre[:, half:]], axis=1
    )
    (retain, inflow), terms_back = jax.vjp(
        recurrence_terms, decay_pre, input_pre, decay_log, conv_low.astype(F32)
    )
    states, state_in = full_scan(retain, inflow, False)
    before = jnp.concatenate([state_in, states[:-1]])
    lru_low = states.astype(BF16).astype(F32)
    mixed_rows = (lru_low * y_gated).astype(BF16)
    mixed_parts = mixed_rows.reshape(outer, C, rows_dev, lru_cols)

    def branch_of(at):
        part = pick(mixed_parts, at, 1).reshape(outer * rows_dev, lru_cols)
        return contract_last(part, out_kernel).reshape(outer, rows_dev, width)

    group_two, middle, up_kernel, down_kernel = branch_and_group(
        branch_of(1 - c), branch_of(c), tokens, gain_two[None], up_kernel, down_kernel
    )
    up_kernel = up_kernel.reshape(width, -1)
    down_kernel = down_kernel.reshape(width, -1)
    group_two = group_two.reshape(C * Z * rows_dev, width)

    gate_pre = multiply(group_two, gate_kernel)
    up_pre = multiply(group_two, up_kernel)
    active, gelu_gate_back = jax.vjp(gelu_tanh, gate_pre)
    hidden = (active * up_pre).astype(BF16)

    d_hidden = multiply(grad_group, down_kernel)
    d_up = (d_hidden * active).astype(BF16)
    d_gate = gelu_gate_back(d_hidden * up_pre)[0].astype(BF16)
    half_rows = Z * rows_dev

    def d_normed_of(part):
        total = contract_last(d_gate[part], gate_kernel) + contract_last(d_up[part], up_kernel)
        return total.reshape(Z, rows_dev, width)

    def terms_of(left_side, right_side):
        share = right_side.shape[1] // outer
        return [
            contract_rows(left_side, right_side[:, i * share : (i + 1) * share])
            .astype(BF16)
            .reshape(Z, inner, weight_rows, share)
            for i in range(outer)
        ]

    gate_terms = terms_of(group_two, d_gate)
    up_terms = terms_of(group_two, d_up)
    down_terms = terms_of(grad_group, hidden)
    branch_rows, d_middle, gain_two_grad, block_out, units, units_y, units_x = middle_and_rows(
        d_normed_of(slice(half_rows, None)).astype(BF16),
        d_normed_of(slice(0, half_rows)),
        middle,
        out_grad,
        gain_two[None],
        hidden,
        down_kernel,
        gate_terms + up_terms + down_terms,
    )
    branch_rows = branch_rows.reshape(-1, width)

    d_mixed = multiply(branch_rows, out_kernel)
    d_lru = (d_mixed * y_gated).astype(BF16).astype(F32)
    d_y = gelu_y_back(d_mixed * lru_low)[0].astype(BF16)
    passed, passed_in = full_scan(retain, retain * d_lru, True)
    d_total = d_lru + jnp.concatenate([passed[1:], passed_in])
    d_decay_pre, d_input_pre, decay_log_grad, d_conv_direct = terms_back(
        (d_total * before, d_total)
    )
    d_decay_low, d_input_low = d_decay_pre.astype(BF16), d_input_pre.astype(BF16)
    own_low = jnp.concatenate([d_decay_low[:, full:], d_input_low[:, full:]], axis=1)
    partner_low = c_swap(own_low)
    shared_low = jnp.concatenate(
        [
            in_order(own_low[:, :half], partner_low[:, :half], 1),
            in_order(own_low[:, half:], partner_low[:, half:], 1),
        ],
        axis=1,
    )
    lows = [
        jnp.concatenate([of_head(d_decay_low, i), of_head(d_input_low, i)], axis=1)
        for i in range(heads)
    ]
    d_conv = d_conv_direct + jnp.concatenate(
        [contract_last(lows[i], gate_all[i * block : (i + 1) * block]) for i in range(heads)]
        + [contract_last(shared_low, gate_all[full:])],
        axis=1,
    )
    gates_grad = jnp.concatenate(
        [contract_rows(of_head(conv_low, i), lows[i]) for i in range(heads)]
        + [contract_rows(conv_low[:, full:], shared_low)]
    )
    ahead = lax.ppermute(d_conv[:reach], "seq", [(i + 1, i) for i in range(seq - 1)])
    d_extended = jnp.concatenate([d_conv, ahead], axis=0)
    d_x_branch = sum(taps[k] * d_extended[k : k + rows] for k in range(taps_count)).astype(BF16)
    dx_parts = d_x_branch.reshape(outer, C, rows_dev, lru_cols)
    dy_parts = d_y.reshape(outer, C, rows_dev, lru_cols)

    def d_normed_one_of(at):
        dx, dy = (
            pick(parts, at, 1).reshape(outer * rows_dev, lru_cols) for parts in (dx_parts, dy_parts)
        )
        total = contract_last(dx, xy_kernel[:, :lru_cols]) + contract_last(
            dy, xy_kernel[:, lru_cols:]
        )
        return total.reshape(outer, rows_dev, width)

    narrow = turned_back(gates_grad, 0).astype(BF16).reshape(Z, inner, chunk, 2 * block)
    narrow = jnp.pad(narrow, ((0, 0), (0, 0), (0, -chunk % 16), (0, 0)))
    own_sums = jnp.stack(
        [jnp.sum(d_conv, axis=0), jnp.sum(d_decay_pre, axis=0), jnp.sum(d_input_pre, axis=0)]
        + [decay_log_grad]
        + [jnp.sum(d_conv * extended[reach - k : reach - k + rows], axis=0) for k in range(taps_count)],
    )
    own_sums = turned_back(own_sums, 1)
    placed, wide, narrow, tokens_grad, gains, own_sums = last_sums(
        units, units_y, units_x, group_one, branch_rows, narrow,
        d_normed_one_of(1 - c).astype(BF16), d_normed_one_of(c),
        turned_back(d_x_branch, 1), turned_back(d_y, 1), turned_back(mixed_rows, 1),
        tokens, gain_one[None], d_middle, gain_two_grad, own_sums,
    )
    weight_grads = [wide[:, n * lru_cols : (n + 1) * lru_cols] for n in range(3)]
    gate_grad, up_grad, down_grad = (placed[n, :, :hidden_cols].astype(F32) for n in range(3))
    gains = gains.reshape(2, 8, LANES).sum(axis=1)[:, :chunk]
    sums = lax.dynamic_slice(own_sums[1], (0, lax.axis_index("seq") * chunk), (taps_count + 4, chunk))
    own_sums = jnp.concatenate([narrow[:chunk], sums.T], axis=1)
    own_sums = lax.ppermute(own_sums, ("seq", "wt"), [(to, at) for at, to in across])
    sums = own_sums[:, 2 * block :]
    return (
        block_out,
        tokens_grad,
        gains[0],
        weight_grads[0],
        weight_grads[1],
        sums[:, 4:],
        sums[:, 0],
        own_sums[:, :block],
        sums[:, 1],
        own_sums[:, block : 2 * block],
        sums[:, 2],
        sums[:, 3],
        weight_grads[2],
        gains[1],
        gate_grad,
        up_grad,
        down_grad,
    )


def solution(mesh):
    rows, both, lone = P(("seq", "wt"), None), P("seq", "wt"), P(("seq", "wt"))
    in_specs = (
        rows, lone, both, both, rows, lone, rows, lone, rows, lone, lone,
        both, lone, both, both, both, rows,
    )
    out_specs = (
        rows, rows, lone, both, both, rows, lone, rows, lone, rows, lone, lone,
        both, lone, both, both, both,
    )
    return jax.shard_map(
        per_device, mesh=mesh, in_specs=in_specs, out_specs=out_specs, check_vma=False
    )
```

```python
import functools

import jax
import jax.numpy as jnp
from jax import lax
from jax.experimental import pallas as pl
from jax.experimental.pallas import tpu as pltpu
from jax.sharding import PartitionSpec as P

EPSILON = 1e-06
DECAY_SCALE = 8.0
Z = 4
C = 2
LANES = 128
F32 = jnp.float32
BF16 = jnp.bfloat16
MESH = pl.DeviceIdType.MESH


def gelu_tanh(values):
    return jax.nn.gelu(values, approximate=True)


def sizes():
    return lax.axis_size("seq") // Z, lax.axis_size("wt") // C


def places():
    inner, outer = sizes()
    s, w = lax.axis_index("seq"), lax.axis_index("wt")
    return s // inner, s % inner, w // C, w % C


def z_move(value, by, senders):
    inner, _ = sizes()
    pairs = [(z * inner + x, (z + by) % Z * inner + x) for z in senders for x in range(inner)]
    return lax.ppermute(value, "seq", pairs)


def c_swap(value):
    _, outer = sizes()
    pairs = [(y * C + c, y * C + 1 - c) for y in range(outer) for c in range(C)]
    return lax.ppermute(value, "wt", pairs)


def line_scatter(parts):
    up = down = None
    for step in range(1, Z):
        rising = parts[step] if up is None else parts[step] + up
        falling = parts[Z - step] if down is None else parts[Z - step] + down
        up = z_move(rising.astype(BF16), 1, range(0, step)).astype(F32)
        down = z_move(falling.astype(BF16), -1, range(Z - step, Z)).astype(F32)
    return parts[0] + up + down


def pick(value, index, axis):
    return lax.dynamic_index_in_dim(value, index, axis, keepdims=False)


def contract_last(left_side, right_side):
    return lax.dot_general(
        left_side, right_side, (((1,), (1,)), ((), ())), preferred_element_type=F32
    )


def contract_rows(left_side, right_side):
    return lax.dot_general(
        left_side, right_side, (((0,), (0,)), ((), ())), preferred_element_type=F32
    )


def multiply(left_side, right_side):
    return jnp.dot(left_side, right_side, preferred_element_type=F32)


class Sends:
    def __init__(self, sems):
        self.sems, self.started = sems, []

    def start(self, when, source, target, arrival, device):
        copy = pltpu.make_async_remote_copy(
            src_ref=source,
            dst_ref=target,
            send_sem=self.sems.at[len(self.started)],
            recv_sem=arrival,
            device_id=device,
            device_id_type=MESH,
        )
        if when is True:
            copy.start()
        else:
            pl.when(when)(copy.start)
        self.started.append((when, copy))

    def finish(self):
        for when, copy in self.started:
            if when is True:
                copy.wait_send()
            else:
                pl.when(when)(copy.wait_send)


def arrived(target, arrival, device):
    pltpu.make_async_remote_copy(
        src_ref=target, dst_ref=target, send_sem=arrival, recv_sem=arrival,
        device_id=device, device_id_type=MESH,
    ).wait_recv()


def gather_kernel(shape, *refs):
    inner, outer = shape
    (tokens, grads, vectors, gates, xy, out, gate, up, down) = refs[:9]
    (grads_to, vectors_to, gates_to, xy_to, out_to, gate_to, up_to, down_to) = refs[9:17]
    rows_one, xy_one = refs[17:19]
    gates_own, send_sems, local_sems, line_sems, plane_sems, rows_sems = refs[19:25]
    vector_sems, turn_sems, group_sems, tokens_to, xy_v, vectors_v, spread, read_sems = refs[25:]
    seq, wt = Z * inner, outer * C
    s, w = lax.axis_index("seq"), lax.axis_index("wt")
    z, x, y, c = s // inner, s % inner, w // C, w % C
    sends = Sends(send_sems)
    group = GroupRows(Place(shape), sends, grads, grads_to, group_sems)
    here, counter = [], iter(range(16))

    def at_z(to):
        return {"seq": to * inner + x, "wt": w}

    def at_x(by):
        return {"seq": z * inner + (x + by) % inner, "wt": w}

    def at_y(by):
        return {"seq": s, "wt": (y + by) % outer * C + c}

    at_c = {"seq": s, "wt": y * C + 1 - c}

    def keep(source, target, waited=False):
        copy = pltpu.make_async_copy(source, target, local_sems.at[next(counter)])
        copy.start()
        here.append((waited, copy))
        return copy

    barrier = pltpu.get_barrier_semaphore()

    def greet(i, carried):
        @pl.when(i != s * wt + w)
        def _():
            pl.semaphore_signal(
                barrier, inc=1, device_id={"seq": i // wt, "wt": i % wt}, device_id_type=MESH
            )

        return carried

    lax.fori_loop(0, seq * wt, greet, 0)
    pl.semaphore_wait(barrier, seq * wt - 1)

    class Line:
        def __init__(self, index, source, target):
            self.source, self.target = source, target
            self.sems = line_sems.at[index]

        def forward(self, block, at, up_when, down_when):
            place = self.target.at[at, x]
            arrival = self.sems.at[at, x]
            sends.start(up_when, block, place, arrival, at_z(jnp.minimum(z + 1, Z - 1)))
            sends.start(down_when, block, place, arrival, at_z(jnp.maximum(z - 1, 0)))
            return place, arrival

        def across(self, when, block, at):
            for j in range(1, inner):
                sends.start(when, block, self.target.at[at, x], self.sems.at[at, x], at_x(j))

        def begin_z(self):
            keep(self.source, self.target.at[z, x])
            self.forward(self.source, z, z < Z - 1, z > 0)

        def begin_x(self):
            self.across(True, self.source, z)

        def begin(self):
            self.begin_z()
            self.begin_x()

        def step(self, k):
            for at, there, up_when, down_when in (
                (jnp.maximum(z - k, 0), z - k >= 0, (z - k >= 0) & (z < Z - 1), None),
                (jnp.minimum(z + k, Z - 1), z + k < Z, None, (z + k < Z) & (z > 0)),
            ):
                place, arrival = self.target.at[at, x], self.sems.at[at, x]

                @pl.when(there)
                def _(place=place, arrival=arrival):
                    arrived(place, arrival, at_c)

                if up_when is not None:
                    sends.start(up_when, place, place, arrival, at_z(jnp.minimum(z + 1, Z - 1)))
                else:
                    sends.start(down_when, place, place, arrival, at_z(jnp.maximum(z - 1, 0)))
                self.across(there, place, at)

        def finish(self):
            for at in range(Z):
                for j in range(1, inner):
                    from_x = (x + inner - j) % inner
                    arrived(self.target.at[at, from_x], self.sems.at[at, from_x], at_c)

    class Plane:
        def __init__(self, index, source, target, x_first, whole):
            self.source, self.target, self.x_first, self.whole = source, target, x_first, whole
            self.share = source.shape[1] // Z
            self.sems = plane_sems.at[index]

        def cut(self, at):
            return self.source.at[:, pl.ds(pl.multiple_of(at * self.share, LANES), self.share)]

        def place(self, at, x_at, i):
            return self.target.at[at, x_at, :, i * self.share : (i + 1) * self.share]

        def begin(self):
            self.own = keep(self.cut(z), self.place(z, x, 0), True)
            for k in range(1, Z):
                to = (z + k) % Z
                sends.start(True, self.cut(to), self.place(z, x, 0), self.sems.at[z, 0, 0], at_z(to))

        def over_x(self, at, i):
            place = self.place(at, x, i)
            for j in range(1, inner):
                sends.start(True, place, place, self.sems.at[at, j, i], at_x(j))

        def over_y(self, at, j):
            x_at = (x + inner - j) % inner
            for i in range(1, outer):
                sends.start(
                    True, self.place(at, x_at, 0), self.place(at, x_at, i),
                    self.sems.at[at, j, i], at_y(i),
                )

        def got(self, at, j, i):
            arrived(self.place(at, (x + inner - j) % inner, i), self.sems.at[at, j, i], at_c)

        def first(self, k):
            at = (z + Z - k) % Z
            if k == 0:
                self.own.wait()
            else:
                self.got(at, 0, 0)
            if self.x_first or self.whole:
                self.over_x(at, 0)
            if self.whole or not self.x_first:
                self.over_y(at, 0)

        def second(self, k):
            at = (z + Z - k) % Z
            if self.x_first:
                for j in range(1, inner):
                    self.got(at, j, 0)
                    if self.whole:
                        self.over_y(at, j)
            else:
                for i in range(1, outer):
                    self.got(at, 0, i)

        def finish(self, k):
            if self.whole:
                at = (z + Z - k) % Z
                for j in range(inner):
                    for i in range(1, outer):
                        self.got(at, j, i)

    lines = [Line(0, xy, xy_to), Line(1, gates_own, gates_to), Line(2, out, out_to)]
    planes = [
        Plane(0, gate, gate_to, True, True),
        Plane(1, up, up_to, False, False),
        Plane(2, down, down_to, True, False),
    ]

    me = s * wt + w
    keep(vectors, vectors_to.at[me])

    def vector_copy(i):
        return pltpu.make_async_remote_copy(
            src_ref=vectors, dst_ref=vectors_to.at[me],
            send_sem=vector_sems.at[0, i], recv_sem=vector_sems.at[1, me],
            device_id={"seq": i // wt, "wt": i % wt}, device_id_type=MESH,
        )

    def vector_send(i, carried):
        pl.when(i != me)(lambda: vector_copy(i).start())
        return carried

    def tokens_begin():
        keep(tokens, tokens_to.at[w])
        sends.start(True, tokens, tokens_to.at[w], rows_sems.at[w], at_c)
        for i in range(1, outer):
            sends.start(True, tokens, tokens_to.at[w], rows_sems.at[w], at_y(i))

    def tokens_step():
        for i in range(1, outer):
            at = (y + outer - i) % outer * C + c
            arrived(tokens_to.at[at], rows_sems.at[at], at_c)
            sends.start(True, tokens_to.at[at], tokens_to.at[at], rows_sems.at[at], at_c)

    def tokens_finish():
        for i in range(outer):
            at = (y + outer - i) % outer * C + 1 - c
            arrived(tokens_to.at[at], rows_sems.at[at], at_c)

    to_seq, to_wt = me % seq, me // seq
    from_me = w * seq + s
    turn = pltpu.make_async_remote_copy(
        src_ref=gates, dst_ref=gates_own, send_sem=turn_sems.at[0], recv_sem=turn_sems.at[1],
        device_id={"seq": to_seq, "wt": to_wt}, device_id_type=MESH,
    )
    stay = pltpu.make_async_copy(gates, gates_own, turn_sems.at[2])
    here_too = from_me == me

    pl.when(jnp.logical_not(here_too))(turn.start)
    pl.when(here_too)(stay.start)
    def vector_wait(i, carried):
        @pl.when(i != me)
        def _():
            vector_copy(i).wait_send()
            arrived(vectors_to.at[i], vector_sems.at[1, i], at_c)

        return carried

    def first_projection():
        lines[0].finish()
        tokens_finish()
        lax.fori_loop(0, seq * wt, vector_wait, 0)
        for copy in here_first:
            copy.wait()
        rows_each = xy.shape[0]
        copies = [pltpu.make_async_copy(vectors_to, vectors_v, read_sems.at[0])]
        for z_at in range(Z):
            for x_at in range(inner):
                n = z_at * inner + x_at
                copies.append(
                    pltpu.make_async_copy(
                        xy_to.at[z_at, x_at], xy_v.at[n * rows_each : (n + 1) * rows_each],
                        read_sems.at[1 + n],
                    )
                )
        for copy in copies:
            copy.start()
        copies[0].wait()
        width = tokens.shape[1]
        devices = seq * wt
        channels = width // devices
        spread[...] = jnp.zeros_like(spread)
        for i in range(devices):
            first = min(i * channels // LANES * LANES, width - 2 * LANES)
            turn = i * channels - first
            part = vectors_v[i, 0:8]
            part = jnp.concatenate([part, jnp.zeros_like(part)], axis=1)
            if turn:
                part = pltpu.roll(part, turn, 1)
            spread[:, first : first + 2 * LANES] += part
        gain = spread[0:1]
        count = tokens.shape[0]
        for at in range(wt):

            def norm(r, at=at):
                stream = tokens_to[at, r].astype(F32)
                inverse = lax.rsqrt(jnp.mean(stream * stream, axis=1, keepdims=True) + EPSILON)
                rows_one[pl.ds(pl.multiple_of(at * count + r.start, 16), 16)] = (
                    stream * inverse * gain
                ).astype(BF16)

            each_rows(count, 16, norm)
        for copy in copies[1:]:
            copy.wait()
        tile = 2 * LANES

        def project(n, carried):
            down = pl.ds(pl.multiple_of(n % wt * count, LANES), count)
            across = pl.ds(pl.multiple_of(n // wt * tile, tile), tile)
            xy_one[down, across] = multiply(rows_one[down], xy_v[:, across])
            return carried

        lax.fori_loop(0, wt * (xy_v.shape[1] // tile), project, 0)

    lines[0].begin()
    tokens_begin()
    here_first = [copy for _, copy in here]
    here.clear()

    @pl.when(jnp.logical_not(here_too))
    def _():
        arrived(gates_own, turn_sems.at[1], at_c)

    pl.when(here_too)(stay.wait)
    lines[1].begin()
    lines[2].begin_z()
    lax.fori_loop(0, seq * wt, vector_send, 0)
    for k in range(1, Z):
        lines[1].step(k)
        lines[0].step(k)
        if k == 1:
            tokens_step()
    lines[2].begin_x()
    for k in range(1, Z):
        lines[2].step(k)
        if k == Z - 2:
            planes[0].begin()
            planes[2].begin()
            planes[1].begin()
    for k in range(Z):
        planes[0].first(k)
    for k in range(Z):
        planes[2].first(k)
    keep(grads, group.place(0, z, z))
    group.begin()
    for k in range(Z):
        planes[1].first(k)
    for k in range(Z):
        planes[0].second(k)
    group.step(1)
    first_projection()
    for k in range(2, Z):
        group.step(k)
    group.finish()

    for line in lines[1:]:
        line.finish()
    for k in range(Z):
        planes[1].second(k)
        planes[2].second(k)
        planes[0].finish(k)

    pl.when(jnp.logical_not(here_too))(turn.wait_send)
    sends.finish()
    for waited, copy in here:
        if not waited:
            copy.wait()


def gather_all(tokens, grads, vectors, gates, xy, out, gate, up, down):
    inner, outer = sizes()
    seq, wt = Z * inner, outer * C

    def buffer(*shape, like):
        return jax.ShapeDtypeStruct(shape, like.dtype)

    def plane(weight):
        rows, columns = weight.shape
        return buffer(Z, inner, rows, outer * columns // Z, like=weight)

    shapes = (
        buffer(C, Z, *grads.shape, like=grads),
        buffer(seq * wt, *vectors.shape, like=vectors),
        buffer(Z, inner, *gates.shape, like=gates),
        buffer(Z, inner, *xy.shape, like=xy),
        buffer(Z, inner, *out.shape, like=out),
        plane(gate),
        plane(up),
        plane(down),
        buffer(wt * tokens.shape[0], tokens.shape[1], like=tokens),
        jax.ShapeDtypeStruct((wt * tokens.shape[0], xy.shape[1]), F32),
    )
    copies = 3 * (2 + inner + (Z - 1) * 2 * inner) + 3 * (Z - 1 + Z * (inner + 2 * outer + inner * outer))
    copies += 2 * outer + 3 + 4 * Z
    dma = pltpu.SemaphoreType.DMA
    return pl.pallas_call(
        functools.partial(gather_kernel, (inner, outer)),
        out_shape=shapes,
        in_specs=[pl.BlockSpec(memory_space=pl.ANY)] * 9,
        out_specs=[pl.BlockSpec(memory_space=pl.ANY)] * 8 + [pl.BlockSpec(memory_space=pltpu.VMEM)] * 2,
        scratch_shapes=[
            pltpu.VMEM(gates.shape, gates.dtype),
            dma((copies,)),
            dma((16,)),
            dma((3, Z, inner)),
            dma((3, Z, inner, outer)),
            dma((wt,)),
            dma((2, seq * wt)),
            dma((3,)),
            dma((C, Z)),
            pltpu.VMEM((wt, *tokens.shape), tokens.dtype),
            pltpu.VMEM((Z * inner * xy.shape[0], xy.shape[1]), xy.dtype),
            pltpu.VMEM((seq * wt, *vectors.shape), F32),
            pltpu.VMEM((8, tokens.shape[1]), F32),
            dma((1 + Z * inner,)),
        ],
        compiler_params=pltpu.CompilerParams(
            collective_id=0, has_side_effects=True, vmem_limit_bytes=40 * 1024 * 1024
        ),
        name="gather_all",
    )(tokens, grads, vectors, gates, xy, out, gate, up, down)


class Place:
    def __init__(self, shape):
        self.inner, self.outer = shape
        self.s, self.w = lax.axis_index("seq"), lax.axis_index("wt")
        self.z, self.x = self.s // self.inner, self.s % self.inner
        self.y, self.c = self.w // C, self.w % C
        self.at_c = {"seq": self.s, "wt": self.y * C + 1 - self.c}
        self.z_up, self.z_down = jnp.minimum(self.z + 1, Z - 1), jnp.maximum(self.z - 1, 0)

    def at_z(self, to):
        return {"seq": to * self.inner + self.x, "wt": self.w}

    def at_x(self, by):
        return {"seq": self.z * self.inner + (self.x + by) % self.inner, "wt": self.w}

    def at_y(self, by):
        return {"seq": self.s, "wt": (self.y + self.outer + by) % self.outer * C + self.c}

    def greet_all(self):
        barrier = pltpu.get_barrier_semaphore()
        wt = self.outer * C
        count = Z * self.inner * wt

        def signal(i, carried):
            @pl.when(i != self.s * wt + self.w)
            def _():
                pl.semaphore_signal(
                    barrier, inc=1, device_id={"seq": i // wt, "wt": i % wt}, device_id_type=MESH
                )

            return carried

        lax.fori_loop(0, count, signal, 0)
        pl.semaphore_wait(barrier, count - 1)

    def greet(self):
        barrier = pltpu.get_barrier_semaphore()
        devices = [self.at_c]
        devices += [self.at_z((self.z + k) % Z) for k in range(1, Z)]
        devices += [self.at_x(j) for j in range(1, self.inner)]
        devices += [self.at_y(i) for i in range(1, self.outer)]
        for device in devices:
            pl.semaphore_signal(barrier, inc=1, device_id=device, device_id_type=MESH)
        pl.semaphore_wait(barrier, len(devices))


def each_rows(count, step, body):
    def run(i, carried):
        body(pl.ds(pl.multiple_of(i * step, step), step))
        return carried

    lax.fori_loop(0, count // step, run, 0)


class WtRows:
    def __init__(self, me, sends, source, target, sems):
        self.me, self.sends, self.source, self.target, self.sems = me, sends, source, target, sems

    def begin(self):
        me = self.me
        for device in [me.at_y(i) for i in range(1, me.outer)] + [me.at_c]:
            self.sends.start(True, self.source, self.target.at[me.w], self.sems.at[me.w], device)

    def step(self):
        me = self.me
        for i in range(1, me.outer):
            at = (me.y + me.outer - i) % me.outer * C + me.c
            arrived(self.target.at[at], self.sems.at[at], me.at_c)
            self.sends.start(True, self.target.at[at], self.target.at[at], self.sems.at[at], me.at_c)

    def finish(self):
        me = self.me
        for i in range(me.outer):
            at = (me.y + me.outer - i) % me.outer * C + 1 - me.c
            arrived(self.target.at[at], self.sems.at[at], me.at_c)


class GroupRows:
    def __init__(self, me, sends, source, target, sems):
        self.me, self.sends, self.source, self.target, self.sems = me, sends, source, target, sems

    def place(self, own, at, z_to):
        return self.target.at[own, (z_to - at + Z) % Z]

    def forward(self, at, source, there, way):
        me = self.me
        z_to = me.z_up if way > 0 else me.z_down
        room = me.z < Z - 1 if way > 0 else me.z > 0
        when = room if there is None else there & room
        self.sends.start(
            when, source, self.place(0, at, z_to), self.sems.at[0, at], me.at_z(z_to)
        )

    def begin(self):
        me = self.me
        self.forward(me.z, self.source, None, 1)
        self.forward(me.z, self.source, None, -1)
        self.sends.start(
            True, self.source, self.place(1, me.z, me.z), self.sems.at[1, me.z], me.at_c
        )

    def step(self, k):
        me = self.me
        for at, there, way in (
            (jnp.maximum(me.z - k, 0), me.z - k >= 0, 1),
            (jnp.minimum(me.z + k, Z - 1), me.z + k < Z, -1),
        ):
            place = self.place(0, at, me.z)

            @pl.when(there)
            def _(place=place, at=at):
                arrived(place, self.sems.at[0, at], me.at_c)

            self.forward(at, place, there, way)
            self.sends.start(there, place, self.place(1, at, me.z), self.sems.at[1, at], me.at_c)

    def finish(self):
        me = self.me
        for at in range(Z):
            arrived(self.place(1, at, me.z), self.sems.at[1, at], me.at_c)


def branch_kernel(
    shape, sent, own, tokens, gain, up_held, down_held, group_to, middle, up_to, down_to,
    own_v, c_in, y_out, y_in, low,
    send_sems, local_sems, c_sems, y_sems, group_sems, up_sems, down_sems,
):
    del up_held, down_held
    me = Place(shape)
    inner, outer = shape
    share = up_to.shape[3] // outer
    rows = tokens.shape[0]
    sends = Sends(send_sems)
    load = pltpu.make_async_copy(own, own_v, local_sems.at[0])
    load.start()
    me.greet()
    order = [(me.y + i) % outer for i in list(range(1, outer)) + [0]]
    for at in order:
        sends.start(True, sent.at[at], c_in.at[at], c_sems.at[at], me.at_c)

    def columns(held, x_at, i):
        return held.at[:, x_at, :, i * share : (i + 1) * share]

    for j in range(1, inner):
        for i in range(outer):
            place = columns(up_to, me.x, i)
            sends.start(True, place, place, up_sems.at[j - 1, i], me.at_x(j))
    load.wait()
    for i, at in enumerate(order):
        arrived(c_in.at[at], c_sems.at[at], me.at_c)
        if i < outer - 1:
            each_rows(rows, 16, lambda r, i=i, at=at: y_out.__setitem__(
                (i, r), (own_v[at, r] + c_in[at, r].astype(F32)).astype(BF16)))
            sends.start(True, y_out.at[i], y_in.at[i], y_sems.at[i], me.at_y(i + 1))
    for i in range(outer - 1):
        arrived(y_in.at[i], y_sems.at[i], me.at_c)
    for i in range(1, outer):
        for j in range(inner):
            x_at = (me.x + inner - j) % inner
            sends.start(
                True, columns(down_to, x_at, 0), columns(down_to, x_at, i),
                down_sems.at[i - 1, j], me.at_y(i),
            )

    def work(r):
        total = tokens[r].astype(F32) + own_v[me.y, r] + c_in[me.y, r].astype(F32)
        for i in range(outer - 1):
            total = total + y_in[i, r].astype(F32)
        inverse = lax.rsqrt(jnp.mean(total * total, axis=1, keepdims=True) + EPSILON)
        middle[r] = total
        low[r] = (total * inverse * gain[...]).astype(BF16)

    each_rows(rows, 16, work)
    keep = pltpu.make_async_copy(low, group_to.at[0, 0], local_sems.at[1])
    keep.start()
    group = GroupRows(me, sends, low, group_to, group_sems)
    group.begin()
    for k in range(1, Z):
        group.step(k)
    group.finish()
    for j in range(1, inner):
        for i in range(outer):
            x_at = (me.x + inner - j) % inner
            arrived(columns(up_to, x_at, i), up_sems.at[j - 1, i], me.at_c)
    for i in range(1, outer):
        for j in range(inner):
            x_at = (me.x + inner - j) % inner
            arrived(columns(down_to, x_at, i), down_sems.at[i - 1, j], me.at_c)
    sends.finish()
    keep.wait()


def branch_and_group(sent, own, tokens, gain, up, down):
    inner, outer = sizes()
    rows, width = tokens.shape
    dma = pltpu.SemaphoreType.DMA
    vmem, anywhere = pl.BlockSpec(memory_space=pltpu.VMEM), pl.BlockSpec(memory_space=pl.ANY)
    return pl.pallas_call(
        functools.partial(branch_kernel, (inner, outer)),
        out_shape=(
            jax.ShapeDtypeStruct((C, Z, rows, width), BF16),
            jax.ShapeDtypeStruct((rows, width), F32),
            jax.ShapeDtypeStruct(up.shape, up.dtype),
            jax.ShapeDtypeStruct(down.shape, down.dtype),
        ),
        in_specs=[anywhere, anywhere, vmem, vmem, anywhere, anywhere],
        out_specs=(anywhere, vmem, anywhere, anywhere),
        input_output_aliases={4: 2, 5: 3},
        scratch_shapes=[
            pltpu.VMEM((outer, rows, width), F32),
            pltpu.VMEM((outer, rows, width), BF16),
            pltpu.VMEM((outer - 1, rows, width), BF16),
            pltpu.VMEM((outer - 1, rows, width), BF16),
            pltpu.VMEM((rows, width), BF16),
            dma((2 * outer + 3 + 4 * (Z - 1) + (inner - 1) * outer + inner * (outer - 1),)),
            dma((2,)),
            dma((outer,)),
            dma((outer - 1,)),
            dma((C, Z)),
            dma((inner - 1, outer)),
            dma((outer - 1, inner)),
        ],
        compiler_params=pltpu.CompilerParams(
            collective_id=1, has_side_effects=True, vmem_limit_bytes=40 * 1024 * 1024
        ),
        name="branch_and_group",
    )(sent, own, tokens, gain, up, down)


def line_order():
    order = []
    for k in [n for t in range(1, Z) for n in (t, Z - t)] + [0]:
        if k not in order:
            order.append(k)
    return order


def line_sum(me, sends, rows, term, ready, store, held, up, down, between=None):
    z = me.z

    def add(when, target, slot, k, received=None, came=0):
        def body(r):
            value = term(k, r)
            if received is not None:
                value = value + received[came, r].astype(F32)
            target[slot, r] = value.astype(BF16)

        pl.when(when)(lambda: each_rows(rows, 16, body))

    for t in range(1, Z):
        slot = t - 1
        for k, (out, into, sems), out_slot, has, when, to in (
            (t, up, slot, z > 0, (z <= t - 1) & (z < Z - 1), me.z_up),
            (Z - t, down, Z - 1 - t, z < Z - 1, (z >= Z - t) & (z > 0), me.z_down),
        ):
            pl.when(when)(lambda k=k: ready(k))
            if t == 1:
                add(when, out, out_slot, k)
            else:
                pl.when(when & has)(
                    lambda into=into, sems=sems, slot=slot: arrived(
                        into.at[slot - 1], sems.at[slot - 1], me.at_c
                    )
                )
                add(when & has, out, out_slot, k, into, slot - 1)
                add(when & jnp.logical_not(has), out, out_slot, k)
            sends.start(when, out.at[out_slot], into.at[slot], sems.at[slot], me.at_z(to))
        if between is not None:
            between(t)
    ready(0)
    each_rows(rows, 16, lambda r: store(r, term(0, r)))
    for (_, into, sems), has in ((up, z > 0), (down, z < Z - 1)):

        @pl.when(has)
        def _(into=into, sems=sems):
            arrived(into.at[Z - 2], sems.at[Z - 2], me.at_c)
            each_rows(rows, 16, lambda r: store(r, held(r) + into[Z - 2, r].astype(F32)))


class PlaneTerms:
    def __init__(self, me, sends, parts, over_x, blocks, scratch):
        self.me, self.sends, self.parts, self.over_x, self.blocks = me, sends, parts, over_x, blocks
        self.came, self.mine, self.sems, self.local_sems = scratch

    def begin(self):
        me = self.me
        if self.over_x:
            for j in range(1, me.inner):
                for i, part in enumerate(self.parts):
                    self.sends.start(
                        True, part.at[self.blocks, (me.x + j) % me.inner],
                        self.came.at[j - 1, i], self.sems.at[j - 1, i], me.at_x(j),
                    )
            pairs = [(part.at[self.blocks, me.x], self.mine.at[i]) for i, part in enumerate(self.parts)]
        else:
            for i in range(1, me.outer):
                self.sends.start(
                    True, self.parts[i].at[self.blocks], self.came.at[i - 1],
                    self.sems.at[0, i - 1], me.at_y(-i),
                )
            pairs = [(self.parts[0].at[self.blocks], self.mine)]
        self.loads = self.moved(pairs)

    def moved(self, pairs):
        copies = [
            pltpu.make_async_copy(source, target, self.local_sems.at[n])
            for n, (source, target) in enumerate(pairs)
        ]
        for copy in copies:
            copy.start()
        return copies

    def add(self):
        me = self.me
        if self.over_x:
            count, places = me.inner - 1, [(i,) for i in range(me.outer)]
        else:
            count, places = me.outer - 1, [()]
        for n in range(count):
            for place in places:
                sems = self.sems.at[n, place[0]] if place else self.sems.at[0, n]
                arrived(self.came.at[(n, *place)], sems, me.at_c)
        for copy in self.loads:
            copy.wait()
        shape = self.mine.shape[:2]

        def body(r):
            for first in range(shape[0]):
                for second in range(shape[1]):
                    total = self.mine[first, second, r].astype(F32)
                    for n in range(count):
                        total = total + self.came[n, first, second, r].astype(F32)
                    self.mine[first, second, r] = total.astype(BF16)

        each_rows(self.mine.shape[2], 16, body)

    def hand_on(self, kept, sent):
        me = self.me
        if self.over_x:
            pairs = [(self.mine.at[i], kept if i == 0 else sent(i - 1)) for i in range(me.outer)]
        else:
            pairs = [
                (self.mine.at[:, (me.x + j) % me.inner], kept if j == 0 else sent(j - 1))
                for j in range(me.inner)
            ]
        self.loads = self.moved(pairs)

    def second(self, into, sems):
        me = self.me
        for j in range(1, me.inner):
            self.sends.start(
                True, self.mine.at[:, (me.x + j) % me.inner], into.at[j - 1], sems.at[j - 1],
                me.at_x(j),
            )

    def add_second(self, into, sems, kept):
        me = self.me
        for j in range(1, me.inner):
            arrived(into.at[j - 1], sems.at[j - 1], me.at_c)

        def body(r):
            for first in range(self.mine.shape[0]):
                total = self.mine[first, me.x, r].astype(F32)
                for j in range(1, me.inner):
                    total = total + into[j - 1, first, r].astype(F32)
                self.mine[first, me.x, r] = total.astype(BF16)

        each_rows(self.mine.shape[2], 16, body)
        self.loads = self.moved([(self.mine.at[:, me.x], kept)])

    def finish(self):
        for copy in self.loads:
            copy.wait()


def middle_kernel(shape, *refs):
    outer = shape[1]
    sent, own, middle, grads, gain, hidden, down_kernel = refs[:7]
    parts = refs[7 : 7 + 3 * outer]
    rows_to, d_middle, gain_grad, block_out = refs[7 + 3 * outer : 11 + 3 * outer]
    targets = refs[11 + 3 * outer : 14 + 3 * outer]
    scratch = refs[14 + 3 * outer :]
    middle_body(
        shape, sent, own, middle, grads, gain, hidden, down_kernel, parts, targets,
        rows_to, d_middle, gain_grad, block_out, scratch[:8], scratch[8:16],
        [scratch[16 + 4 * n : 20 + 4 * n] for n in range(4)], *scratch[32:],
    )


class PairSum:
    def __init__(self, me, sends, sent, own, scratch):
        self.me, self.sends, self.sent = me, sends, sent
        self.held, self.c_in, out, up_in, down_in, self.c_sems, up_sems, down_sems = scratch
        self.up, self.down = (out, up_in, up_sems), (out, down_in, down_sems)

    def begin(self):
        for k in line_order():
            self.sends.start(
                True, self.sent.at[k], self.c_in.at[k], self.c_sems.at[k], self.me.at_c
            )

    def run(self, between=None):
        def ready(k):
            arrived(self.c_in.at[k], self.c_sems.at[k], self.me.at_c)

        def term(k, r):
            return self.held[k, r] + self.c_in[k, r].astype(F32)

        def store(r, value):
            self.held[0, r] = value

        line_sum(
            self.me, self.sends, self.held.shape[1], term, ready, store,
            lambda r: self.held[0, r], self.up, self.down, between,
        )


def plane_units(me, sends, parts, scratch):
    outer = me.outer
    gate, up, down = (parts[n * outer : (n + 1) * outer] for n in range(3))
    every, low, high = slice(0, Z), slice(0, Z // 2), slice(Z // 2, Z)
    return [
        PlaneTerms(me, sends, gate, True, every, scratch[0]),
        PlaneTerms(me, sends, up, False, every, scratch[1]),
        PlaneTerms(me, sends, down, True, low, scratch[2]),
        PlaneTerms(me, sends, down, False, high, scratch[3]),
    ]


def middle_body(
    shape, sent, own, middle, grads, gain, hidden, down_kernel, parts, targets,
    rows_to, d_middle, gain_grad, block_out, sum_scratch, feed_scratch, unit_scratch, low,
    up_in, hidden_v, feed_sent, down_v, send_sems, local_sems, rows_sems, up_sems, down_sems,
):
    me = Place(shape)
    rows = middle.shape[0]
    sends = Sends(send_sems)
    total = PairSum(me, sends, sent, own, sum_scratch)
    feed = PairSum(me, sends, feed_sent, None, feed_scratch)
    load = pltpu.make_async_copy(own, total.held, local_sems.at[0])
    hidden_load = pltpu.make_async_copy(hidden, hidden_v, local_sems.at[2])
    load.start()
    hidden_load.start()
    me.greet()
    total.begin()
    units = plane_units(me, sends, parts, unit_scratch)
    units_to, units_y, units_x = targets
    for unit in units:
        unit.begin()

    step = down_v.shape[1]
    half_rows = Z * rows

    def down_load(n, slot):
        part = down_kernel.at[pl.ds(pl.multiple_of(n * step, LANES), step)]
        return pltpu.make_async_copy(part, down_v.at[slot], down_sems.at[slot])

    def feed_product(n, carried):
        slot = n % 2
        down_load(n, slot).wait()
        pl.when(n + 1 < down_kernel.shape[0] // step)(lambda: down_load(n + 1, 1 - slot).start())
        across = pl.ds(pl.multiple_of(n * step, LANES), step)
        weight = down_v[slot]
        for k in range(Z):
            kept = hidden_v[k * rows : (k + 1) * rows]
            other = hidden_v[half_rows + k * rows : half_rows + (k + 1) * rows]
            feed.held[k, :, across] = contract_last(kept, weight)
            feed_sent[k, :, across] = contract_last(other, weight).astype(BF16)
        return carried

    down_load(0, 0).start()
    load.wait()
    hidden_load.wait()
    pieces = down_kernel.shape[0] // step
    ends = [pieces * t // (Z - 1) for t in range(Z)]
    total.run(lambda t: lax.fori_loop(ends[t - 1], ends[t], feed_product, 0))
    own_v = total.held
    gain_grad[...] = jnp.zeros_like(gain_grad)

    def work(r):
        values = middle[r]
        inverse = lax.rsqrt(jnp.mean(values * values, axis=1, keepdims=True) + EPSILON)
        normed = values * inverse
        d_normed = own_v[0, r]
        gain_grad[...] += d_normed * normed
        scaled = d_normed * gain[...]
        passed = inverse * (scaled - normed * jnp.mean(scaled * normed, axis=1, keepdims=True))
        total = grads[r].astype(F32) + passed
        d_middle[r] = total
        low[r] = total.astype(BF16)

    each_rows(rows, 16, work)
    keep = pltpu.make_async_copy(low, rows_to.at[me.w], local_sems.at[1])
    keep.start()
    gather = WtRows(me, sends, low, rows_to, rows_sems)
    gather.begin()
    feed.begin()
    half, extra = Z // 2, slice(Z, Z + Z // 2)

    def between(t):
        if t == 1:
            units[0].add()
            units[0].hand_on(units_to.at[0], lambda i: units_y.at[i, 0:Z])
        if t == 2:
            units[1].add()
            units[1].second(up_in, up_sems)
        if t == 3:
            units[2].add()
            units[2].hand_on(units_to.at[2, 0:half], lambda i: units_y.at[i, extra])
            units[3].add()
            units[3].hand_on(units_to.at[2, half:Z], lambda j: units_x.at[j])

    feed.run(between)
    each_rows(rows, 16, lambda r: block_out.__setitem__(
        r, (middle[r] + feed.held[0, r]).astype(BF16)))
    gather.step()
    gather.finish()
    units[1].add_second(up_in, up_sems, units_to.at[1])
    for unit in units:
        unit.finish()
    sends.finish()
    keep.wait()


def middle_and_rows(sent, own, middle, grads, gain, hidden, down_kernel, parts):
    inner, outer = sizes()
    rows, width = middle.shape
    unit_rows, share = parts[0].shape[2:]
    block = (unit_rows, share)
    targets = [
        jax.ShapeDtypeStruct((*shape, *block), BF16)
        for shape in ((3, Z), (outer - 1, Z + Z // 2), (inner - 1, Z // 2))
    ]
    unit_copies = 2 * (inner - 1) * outer + 2 * (outer - 1) + (inner - 1)
    pair_scratch = [pltpu.VMEM((Z, rows, width), F32), pltpu.VMEM((Z, rows, width), BF16)]
    pair_scratch += [pltpu.VMEM((Z - 1, rows, width), BF16)] * 3
    dma = pltpu.SemaphoreType.DMA
    pair_scratch += [dma((Z,)), dma((Z - 1,)), dma((Z - 1,))]
    unit_scratch = []
    for came, mine in (
        ((inner - 1, outer, Z), (outer, Z)),
        ((outer - 1, Z, inner), (Z, inner)),
        ((inner - 1, outer, Z // 2), (outer, Z // 2)),
        ((outer - 1, Z // 2, inner), (Z // 2, inner)),
    ):
        unit_scratch += [pltpu.VMEM((*came, *block), BF16), pltpu.VMEM((*mine, *block), BF16)]
        unit_scratch += [dma((inner - 1, outer)), dma((max(inner, outer),))]
    vmem, anywhere = pl.BlockSpec(memory_space=pltpu.VMEM), pl.BlockSpec(memory_space=pl.ANY)
    return pl.pallas_call(
        functools.partial(middle_kernel, (inner, outer)),
        out_shape=(
            jax.ShapeDtypeStruct((outer * C, rows, width), BF16),
            jax.ShapeDtypeStruct((rows, width), F32),
            jax.ShapeDtypeStruct((16, width), F32),
            jax.ShapeDtypeStruct((rows, width), BF16),
            *targets,
        ),
        in_specs=[anywhere, anywhere, vmem, vmem, vmem] + [anywhere] * (2 + 3 * outer),
        out_specs=(anywhere, vmem, vmem, vmem) + (anywhere,) * 3,
        scratch_shapes=pair_scratch * 2
        + unit_scratch
        + [
            pltpu.VMEM((rows, width), BF16),
            pltpu.VMEM((inner - 1, Z, *block), BF16),
            pltpu.VMEM(hidden.shape, BF16),
            pltpu.VMEM((Z, rows, width), BF16),
            pltpu.VMEM((2, 2 * LANES, hidden.shape[1]), BF16),
            dma((2 * (Z + 2 * (Z - 1)) + 2 * outer + unit_copies,)),
            dma((3,)),
            dma((outer * C,)),
            dma((inner - 1,)),
            dma((2,)),
        ],
        compiler_params=pltpu.CompilerParams(
            collective_id=2, has_side_effects=True, vmem_limit_bytes=60 * 1024 * 1024
        ),
        name="middle_and_rows",
    )(sent, own, middle, grads, gain, hidden, down_kernel, *parts)


class RowsSum:
    def __init__(self, me, sends, terms, total, scratch, sems):
        self.me, self.sends, self.terms, self.total = me, sends, terms, total
        self.own, self.x_in, *ways = scratch
        self.own_sems, self.x_sems, up_sems, down_sems = sems
        self.up, self.down = (*ways[:2], up_sems), (*ways[2:], down_sems)

    def load(self):
        me = self.me
        self.loads = []
        for k in range(Z):
            self.loads.append(
                pltpu.make_async_copy(
                    self.terms.at[(me.z + Z - k) % Z, me.x], self.own.at[k], self.own_sems.at[k]
                )
            )
            self.loads[k].start()

    def begin(self, turns):
        me = self.me
        for turn in turns:
            if turn == Z - 1:
                k = 0
            else:
                k = (jnp.minimum(me.z, Z - 1 - me.z) + turn) % (Z - 1) + 1
                k = jnp.where(me.z < Z // 2, k, Z - k)
            at = (me.z + Z - k) % Z
            for j in range(1, me.inner):
                self.sends.start(
                    True, self.terms.at[at, (me.x + j) % me.inner], self.x_in.at[j - 1, k],
                    self.x_sems.at[j - 1, k], me.at_x(j),
                )

    def run(self, between=None):
        me = self.me

        def ready(k):
            self.loads[k].wait()
            for j in range(1, me.inner):
                arrived(self.x_in.at[j - 1, k], self.x_sems.at[j - 1, k], me.at_c)

        def term(k, r):
            value = self.own[k, r].astype(F32)
            for j in range(1, me.inner):
                value = value + self.x_in[j - 1, k, r].astype(F32)
            return value

        def store(r, value):
            self.total[r] = value

        line_sum(
            me, self.sends, self.total.shape[0], term, ready, store, lambda r: self.total[r],
            self.up, self.down, between,
        )


class ProductsSum(RowsSum):
    def __init__(self, me, sends, factors, total, scratch, sems):
        self.me, self.sends, self.total = me, sends, total
        self.factors = factors
        self.held, self.x_in, out, up_in, down_in, *self.lefts = scratch
        self.own_sems, self.x_sems, up_sems, down_sems = sems
        self.up, self.down = (out, up_in, up_sems), (out, down_in, down_sems)

    def load(self):
        self.loads = []
        for n, (left, _) in enumerate(self.factors):
            copy = pltpu.make_async_copy(left, self.lefts[n], self.own_sems.at[n])
            copy.start()
            self.loads.append(copy)

    def begin(self, turns):
        me = self.me
        while self.loads:
            self.loads.pop().wait()
        rows, span = self.total.shape[0], self.held.shape[1]
        for turn in turns:
            if turn == Z - 1:
                k = 0
            else:
                k = (jnp.minimum(me.z, Z - 1 - me.z) + turn) % (Z - 1) + 1
                k = jnp.where(me.z < Z // 2, k, Z - k)
            at = (me.z + Z - k) % Z

            def tile(i, carried, k=k, at=at):
                first = 0
                down = pl.ds(pl.multiple_of(i * LANES, LANES), LANES)
                across = pl.ds(pl.multiple_of(at * span + i * LANES, LANES), LANES)
                for n, (_, rights) in enumerate(self.factors):
                    left = self.lefts[n][:, across]
                    for right in rights:
                        columns = slice(first, first + right.shape[1])
                        self.held[k, down, columns] = contract_rows(left, right[...]).astype(BF16)
                        first += right.shape[1]
                return carried

            lax.fori_loop(0, span // LANES, tile, 0)
            for j in range(1, me.inner):
                part = pl.ds(pl.multiple_of((me.x + j) % me.inner * rows, 16), rows)
                self.sends.start(
                    True, self.held.at[k, part], self.x_in.at[j - 1, k], self.x_sems.at[j - 1, k],
                    me.at_x(j),
                )

    def run(self, between=None):
        me = self.me
        rows = self.total.shape[0]

        def ready(k):
            for j in range(1, me.inner):
                arrived(self.x_in.at[j - 1, k], self.x_sems.at[j - 1, k], me.at_c)

        def term(k, r):
            mine = pl.ds(pl.multiple_of(me.x * rows + r.start, 16), r.size)
            value = self.held[k, mine].astype(F32)
            for j in range(1, me.inner):
                value = value + self.x_in[j - 1, k, r].astype(F32)
            return value

        def store(r, value):
            self.total[r] = value

        line_sum(
            me, self.sends, rows, term, ready, store, lambda r: self.total[r],
            self.up, self.down, between,
        )


def sums_kernel(shape, *refs):
    inner, outer = shape
    units, units_y, units_x, normed_rows_one, branch_rows, narrow, sent, own = refs[:8]
    d_x, d_y, mixed, tokens, gain, d_middle, gain_two_grad, vectors = refs[8:16]
    units_to, wide_to, narrow_to, tokens_grad, gains, vectors_to = refs[16:22]
    refs = refs[22:]
    wide_scratch, narrow_scratch = refs[:7], refs[7:13]
    (own_v, c_in, y_out, y_in, parts_out, parts_in, gains_v, vec_in) = refs[13:21]
    refs = refs[2:]
    (send_sems, local_sems, c_sems, y_sems, all_sems, vec_sems) = refs[19:25]
    wide_sems, narrow_sems = refs[25:29], refs[29:33]
    units_v, units_y_in, units_x_in, unit_sems, units_y_sems, units_x_sems = refs[33:]
    share = units.shape[3]
    me = Place(shape)
    rows = tokens.shape[0]
    sends = Sends(send_sems)
    load = pltpu.make_async_copy(own, own_v, local_sems.at[0])
    load.start()
    units_load = pltpu.make_async_copy(units, units_v, local_sems.at[1])
    units_load.start()
    me.greet_all()

    order = [(me.y + i) % outer for i in list(range(1, outer)) + [0]]
    for at in order:
        sends.start(True, sent.at[at], c_in.at[at], c_sems.at[at], me.at_c)
    narrow_sum = RowsSum(me, sends, narrow, narrow_to, narrow_scratch, narrow_sems)
    factors = [(normed_rows_one, [d_x, d_y]), (branch_rows, [mixed])]
    wide_sum = ProductsSum(me, sends, factors, wide_to, wide_scratch, wide_sems)
    narrow_sum.load()
    wide_sum.load()
    narrow_sum.begin(range(Z))

    def columns(n, at):
        return units_to.at[n, :, pl.ds(pl.multiple_of(at * share, LANES), share)]

    low, high, extra = slice(0, Z // 2), slice(Z // 2, Z), slice(Z, Z + Z // 2)
    every = slice(0, Z)

    def units_begin_y():
        for n, blocks in enumerate((every, extra)):
            for i in range(1, outer):
                sends.start(
                    True, units_y.at[i - 1, blocks], units_y_in.at[i - 1, blocks],
                    units_y_sems.at[i - 1, n], me.at_y(-i),
                )

    def units_begin_x():
        for j in range(1, inner):
            sends.start(
                True, units_x.at[j - 1], units_x_in.at[j - 1], units_x_sems.at[j - 1], me.at_x(j)
            )

    kept = []

    def unit_add(n, blocks, came, came_blocks, sems, count):
        for i in range(count):
            arrived(came.at[i, came_blocks], sems.at[i], me.at_c)

        def body(r):
            for at in range(blocks.stop - blocks.start):
                total = units_v[n, blocks.start + at, r].astype(F32)
                for i in range(count):
                    total = total + came[i, came_blocks.start + at, r].astype(F32)
                units_v[n, blocks.start + at, r] = total.astype(BF16)

        each_rows(units_v.shape[2], 16, body)

    def unit_pass_on(n):
        copy = pltpu.make_async_copy(units_v.at[n, me.z], columns(n, me.z), local_sems.at[2 + n])
        copy.start()
        kept.append(copy)
        for k in range(1, Z):
            to = (me.z + k) % Z
            sends.start(
                True, units_v.at[n, to], columns(n, me.z), unit_sems.at[n, me.z], me.at_z(to)
            )

    def unit_gate():
        unit_add(0, every, units_y_in, every, units_y_sems.at[:, 0], outer - 1)
        unit_pass_on(0)

    def unit_down():
        unit_add(2, low, units_y_in, extra, units_y_sems.at[:, 1], outer - 1)
        unit_add(2, high, units_x_in, low, units_x_sems, inner - 1)
        unit_pass_on(2)


    def units_finish():
        for n in range(3):
            for k in range(1, Z):
                at = (me.z + Z - k) % Z
                arrived(columns(n, at), unit_sems.at[n, at], me.at_c)
        for copy in kept:
            copy.wait()

    def exchange(held, into, sems, first, devices):
        for n, device in enumerate(devices):
            sends.start(True, held, into.at[first + n], sems.at[first + n], device)

    def gathered(held, into, sems, first, devices):
        for n, _ in enumerate(devices):
            arrived(into.at[first + n], sems.at[first + n], me.at_c)
        total = into[first]
        for n in range(1, len(devices)):
            total = total + into[first + n]
        return held[...] + total

    z_stage = [me.at_z((me.z + k) % Z) for k in range(1, Z)]
    x_stage = [me.at_x(j) for j in range(1, inner)]

    devices = Z * inner * outer * C
    wt = outer * C
    here = me.s * wt + me.w
    width = tokens.shape[1]
    channels = width // devices

    def gains_cut():
        for i in range(devices):
            first = i * channels // LANES * LANES
            first = min(first, width - 2 * LANES)
            window = gains_v[:, first : first + 2 * LANES]
            turn = i * channels - first
            if turn:
                window = pltpu.roll(window, 2 * LANES - turn, 1)
            parts_out[i] = window[:, :LANES]

    def gains_copy(i):
        return pltpu.make_async_remote_copy(
            src_ref=parts_out.at[i], dst_ref=parts_in.at[here],
            send_sem=all_sems.at[0, i], recv_sem=all_sems.at[1, here],
            device_id={"seq": i // wt, "wt": i % wt}, device_id_type=MESH,
        )

    def gains_send(i, carried):
        pl.when(i != here)(lambda: gains_copy(i).start())
        return carried

    def gains_add(i, carried):
        @pl.when(i != here)
        def _():
            gains_copy(i).wait_send()
            arrived(parts_in.at[i], all_sems.at[1, i], me.at_c)
            gains[...] += parts_in[i]

        return carried

    exchange(vectors, vec_in, vec_sems, 0, x_stage)
    units_begin_x()

    units_begin_y()
    units_load.wait()
    unit_pass_on(1)

    load.wait()
    for i, at in enumerate(order):
        arrived(c_in.at[at], c_sems.at[at], me.at_c)
        if i < outer - 1:
            each_rows(rows, 16, lambda r, i=i, at=at: y_out.__setitem__(
                (i, r), (own_v[at, r] + c_in[at, r].astype(F32)).astype(BF16)))
            sends.start(True, y_out.at[i], y_in.at[i], y_sems.at[i], me.at_y(i + 1))
    vectors_to[0] = gathered(vectors, vec_in, vec_sems, 0, x_stage)
    exchange(vectors_to.at[0], vec_in, vec_sems, len(x_stage), z_stage)
    narrow_sum.run()
    vectors_to[1] = gathered(vectors_to.at[0], vec_in, vec_sems, len(x_stage), z_stage)
    wide_sum.begin(range(1))
    unit_gate()
    wide_sum.begin(range(1, 2))
    unit_down()
    wide_sum.begin(range(2, Z))

    def work(r):
        d_normed = own_v[me.y, r] + c_in[me.y, r].astype(F32)
        for i in range(outer - 1):
            d_normed = d_normed + y_in[i, r].astype(F32)
        stream = tokens[r].astype(F32)
        inverse = lax.rsqrt(jnp.mean(stream * stream, axis=1, keepdims=True) + EPSILON)
        normed = stream * inverse
        part = d_normed * normed
        gains_v[0:8] += part[0:8] + part[8:16]
        scaled = d_normed * gain[...]
        passed = inverse * (scaled - normed * jnp.mean(scaled * normed, axis=1, keepdims=True))
        tokens_grad[r] = (d_middle[r] + passed).astype(BF16)

    def between(t):
        if t == 1:
            for i in range(outer - 1):
                arrived(y_in.at[i], y_sems.at[i], me.at_c)
            gains_v[...] = jnp.zeros_like(gains_v)
            each_rows(rows, 16, work)
            gains_v[8:16] = gain_two_grad[0:8] + gain_two_grad[8:16]
            gains_cut()
            lax.fori_loop(0, devices, gains_send, 0)

    wide_sum.run(between)
    gains[...] = parts_out[here]
    lax.fori_loop(0, devices, gains_add, 0)
    units_finish()
    sends.finish()


def last_sums(
    units, units_y, units_x, normed_one, branch_rows, narrow, sent, own,
    d_x, d_y, mixed, tokens, gain, d_middle, gain_two_grad, vectors,
):
    inner, outer = sizes()
    rows, width = tokens.shape
    dma = pltpu.SemaphoreType.DMA
    vmem, anywhere = pl.BlockSpec(memory_space=pltpu.VMEM), pl.BlockSpec(memory_space=pl.ANY)

    def scratch(terms):
        one = terms.shape[2:]
        return [pltpu.VMEM((Z, *one), BF16), pltpu.VMEM((inner - 1, Z, *one), BF16)] + [
            pltpu.VMEM((Z - 1, *one), BF16)
        ] * 4

    devices = Z * inner * outer * C
    copies = 2 * outer - 1 + 2 * (Z * (inner - 1) + 2 * (Z - 1))
    copies += (inner - 1) + (Z - 1) + 2 * (outer - 1) + 2 * (inner - 1) + 3 * (Z - 1)
    _, _, unit_rows, share = units.shape
    block = (unit_rows, d_x.shape[1] + d_y.shape[1] + mixed.shape[1])
    line_sems = [dma((Z,)), dma((inner - 1, Z)), dma((Z - 1,)), dma((Z - 1,))]
    return pl.pallas_call(
        functools.partial(sums_kernel, (inner, outer)),
        out_shape=(
            jax.ShapeDtypeStruct((3, unit_rows, Z * share), BF16),
            jax.ShapeDtypeStruct(block, F32),
            jax.ShapeDtypeStruct(narrow.shape[2:], F32),
            jax.ShapeDtypeStruct((rows, width), BF16),
            jax.ShapeDtypeStruct((16, LANES), F32),
            jax.ShapeDtypeStruct((2, *vectors.shape), F32),
        ),
        in_specs=[anywhere] * 8 + [vmem] * 8,
        out_specs=(anywhere,) + (vmem,) * 5,
        scratch_shapes=[
            pltpu.VMEM((Z, inner * block[0], block[1]), BF16),
            pltpu.VMEM((inner - 1, Z, *block), BF16),
        ]
        + [pltpu.VMEM((Z - 1, *block), BF16)] * 3
        + [pltpu.VMEM(normed_one.shape, BF16), pltpu.VMEM(branch_rows.shape, BF16)]
        + scratch(narrow)
        + [
            pltpu.VMEM((outer, rows, width), F32),
            pltpu.VMEM((outer, rows, width), BF16),
            pltpu.VMEM((outer - 1, rows, width), BF16),
            pltpu.VMEM((outer - 1, rows, width), BF16),
            pltpu.VMEM((devices, 16, LANES), F32),
            pltpu.VMEM((devices, 16, LANES), F32),
            pltpu.VMEM((16, width), F32),
            pltpu.VMEM((inner - 1 + Z - 1, *vectors.shape), F32),
            dma((copies,)),
            dma((5,)),
            dma((outer,)),
            dma((outer - 1,)),
            dma((2, devices)),
            dma((inner - 1 + Z - 1,)),
        ]
        + line_sems * 2
        + [
            pltpu.VMEM(units.shape, BF16),
            pltpu.VMEM(units_y.shape, BF16),
            pltpu.VMEM(units_x.shape, BF16),
            dma((3, Z)),
            dma((outer - 1, 2)),
            dma((inner - 1,)),
        ],
        compiler_params=pltpu.CompilerParams(
            collective_id=5, has_side_effects=True, vmem_limit_bytes=60 * 1024 * 1024
        ),
        name="last_sums",
    )(
        units, units_y, units_x, normed_one, branch_rows, narrow, sent, own,
        d_x, d_y, mixed, tokens, gain, d_middle, gain_two_grad, vectors,
    )


def scan_kernel(backward, factors, inflows, states, entered, products, ends, ends_in, carry, send_sems, arrivals):
    seq = ends_in.shape[0]
    s = lax.axis_index("seq")
    rows, width = factors.shape
    barrier = pltpu.get_barrier_semaphore()

    def device(at):
        return {"seq": at, "wt": lax.axis_index("wt")}

    def greet(i, carried):
        @pl.when(i != s)
        def _():
            pl.semaphore_signal(barrier, inc=1, device_id=device(i), device_id_type=MESH)

        return carried

    lax.fori_loop(0, seq, greet, 0)
    group = 8
    at_row = lax.broadcasted_iota(jnp.int32, (group, width), 0)

    def step(i, carried):
        held, product = carried
        i = rows // group - 1 - i if backward else i
        where = pl.ds(pl.multiple_of(i * group, group), group)
        factor, inflow = factors[where, :], inflows[where, :]
        for by in (1, 2, 4):
            inside = at_row < group - by if backward else at_row >= by
            turn = group - by if backward else by
            inflow = factor * jnp.where(inside, pltpu.roll(inflow, turn, 0), 0.0) + inflow
            factor = factor * jnp.where(inside, pltpu.roll(factor, turn, 0), 1.0)
        inflow = inflow + factor * held
        factor = factor * product
        states[where, :] = inflow
        products[where, :] = factor
        last = slice(0, 1) if backward else slice(group - 1, group)
        return inflow[last], factor[last]

    held, product = lax.fori_loop(
        0, rows // group, step, (jnp.zeros((1, width), F32), jnp.ones((1, width), F32))
    )
    ends[0:1] = product
    ends[1:2] = held
    pl.semaphore_wait(barrier, seq - 1)

    def copy_to(i):
        return pltpu.make_async_remote_copy(
            src_ref=ends, dst_ref=ends_in.at[s], send_sem=send_sems.at[i], recv_sem=arrivals.at[s],
            device_id=device(i), device_id_type=MESH,
        )

    def later(i):
        return i < s if backward else i > s

    def send(i, carried):
        pl.when(later(i))(lambda: copy_to(i).start())
        return carried

    lax.fori_loop(0, seq, send, 0)
    carry[...] = jnp.zeros_like(carry)

    def receive(n, carried):
        i = seq - 1 - n if backward else n

        @pl.when(jnp.logical_not(later(i)) & (i != s))
        def _():
            arrived(ends_in.at[i], arrivals.at[i], device((s + 1) % seq))
            carry[0:1] = ends_in[i, 0:1] * carry[0:1] + ends_in[i, 1:2]

        return carried

    lax.fori_loop(0, seq, receive, 0)
    entering = carry[0:1]
    entered[...] = entering

    def spread(i, carried):
        where = pl.ds(pl.multiple_of(i * group, group), group)
        states[where, :] += products[where, :] * entering
        return carried

    lax.fori_loop(0, rows // group, spread, 0)

    def sent(i, carried):
        pl.when(later(i))(lambda: copy_to(i).wait_send())
        return carried

    lax.fori_loop(0, seq, sent, 0)


def full_scan(factor, inflow, backward):
    seq = lax.axis_size("seq")
    rows, width = factor.shape
    vmem = pl.BlockSpec(memory_space=pltpu.VMEM)
    return pl.pallas_call(
        functools.partial(scan_kernel, backward),
        out_shape=(
            jax.ShapeDtypeStruct((rows, width), F32),
            jax.ShapeDtypeStruct((1, width), F32),
        ),
        in_specs=[vmem, vmem],
        out_specs=(vmem, vmem),
        scratch_shapes=[
            pltpu.VMEM((rows, width), F32),
            pltpu.VMEM((8, width), F32),
            pltpu.VMEM((seq, 8, width), F32),
            pltpu.VMEM((8, width), F32),
            pltpu.SemaphoreType.DMA((seq,)),
            pltpu.SemaphoreType.DMA((seq,)),
        ],
        compiler_params=pltpu.CompilerParams(
            collective_id=4 if backward else 3,
            has_side_effects=True,
            vmem_limit_bytes=32 * 1024 * 1024,
        ),
        name="scan_back" if backward else "scan_ahead",
    )(factor, inflow)


def recurrence_terms(decay_pre, input_pre, decay_log, conv_float):
    log_decay = -DECAY_SCALE * jax.nn.softplus(-decay_log) * jax.nn.sigmoid(decay_pre)
    return (
        jnp.exp(log_decay),
        jnp.sqrt(-jnp.expm1(2.0 * log_decay)) * jax.nn.sigmoid(input_pre) * conv_float,
    )


def per_device(
    tokens,
    norm1_gain,
    x_weight,
    y_weight,
    conv_weight,
    conv_bias,
    decay_gate_weight,
    decay_bias,
    input_gate_weight,
    input_bias,
    decay_param,
    out_weight,
    norm2_gain,
    gate_weight,
    up_weight,
    down_weight,
    out_grad,
):
    seq, wt = lax.axis_size("seq"), lax.axis_size("wt")
    inner, outer = sizes()
    z, x, y, c = places()
    w = lax.axis_index("wt")
    rows_dev, width = tokens.shape
    weight_rows, lru_cols = x_weight.shape
    chunk, block = decay_gate_weight.shape
    half = block // 2
    full = lru_cols - half
    taps_count = conv_weight.shape[1]
    reach = taps_count - 1
    hidden_cols = gate_weight.shape[1]

    def turned(value, axis):
        return jnp.where(c == 0, value, jnp.roll(value, -half, axis))

    def turned_back(value, axis):
        return jnp.where(c == 0, value, jnp.roll(value, half, axis))

    def in_order(own, partner, axis):
        return jnp.where(
            c == 0,
            jnp.concatenate([own, partner], axis),
            jnp.concatenate([partner, own], axis),
        )

    vectors = jnp.stack(
        [v.astype(F32) for v in (norm1_gain, norm2_gain, conv_bias, decay_bias, input_bias)]
        + [decay_param]
        + [conv_weight[:, k].astype(F32) for k in range(taps_count)]
    )
    vectors = jnp.pad(vectors, ((0, -vectors.shape[0] % 8), (0, -chunk % LANES)))

    across = [(i, i % seq * wt + i // seq) for i in range(seq * wt)]
    gates = jnp.concatenate([decay_gate_weight, input_gate_weight], axis=1)

    def padded(weight):
        share = -(-hidden_cols // (Z * LANES)) * LANES
        return jnp.pad(weight, ((0, 0), (0, Z * share - hidden_cols)))

    xy_unit = jnp.concatenate([turned(x_weight, 1), turned(y_weight, 1)], axis=1)
    (
        grad_group, vectors, gate_all, xy_kernel, out_kernel, gate_kernel, up_kernel, down_kernel,
        group_one, xy,
    ) = gather_all(
        tokens, out_grad, vectors, gates, xy_unit, turned(out_weight, 1),
        padded(gate_weight), padded(up_weight), padded(down_weight),
    )
    grad_group = grad_group.reshape(-1, width)
    vectors = jnp.moveaxis(vectors[:, : 6 + taps_count, :chunk], 0, 1).reshape(6 + taps_count, -1)
    gain_one, gain_two = vectors[0], vectors[1]
    own_vectors = turned(
        lax.dynamic_slice(vectors[2:], (0, w * lru_cols), (taps_count + 4, lru_cols)), 1
    )
    tap_bias, decay_shift, input_shift, decay_log = (own_vectors[i] for i in range(4))
    taps = own_vectors[4:]
    xy_kernel = xy_kernel.reshape(width, -1)
    out_kernel = out_kernel.reshape(width, -1)
    gate_kernel = gate_kernel.reshape(width, -1)
    gate_all = turned(gate_all.reshape(lru_cols, 2 * block), 0)
    partner_rows = c_swap(gate_all[full:])
    shared_rows = in_order(gate_all[full:], partner_rows, 0)

    stream = tokens.astype(F32)
    rows = group_one.shape[0]
    x_branch = xy[:, :lru_cols].astype(BF16)
    y_before = xy[:, lru_cols:]
    y_gated, gelu_y_back = jax.vjp(gelu_tanh, y_before)
    rim = lax.ppermute(x_branch[rows - reach :], "seq", [(i, i + 1) for i in range(seq - 1)])
    extended = jnp.concatenate([rim, x_branch], axis=0).astype(F32)
    conv_low = (
        tap_bias
        + sum(taps[k] * extended[reach - k : reach - k + rows] for k in range(taps_count))
    ).astype(BF16)
    shared_conv = in_order(conv_low[:, full:], c_swap(conv_low[:, full:]), 1)
    heads = full // block

    def of_head(value, i):
        return value[:, i * block : (i + 1) * block]

    pre_parts = [
        multiply(of_head(conv_low, i), gate_all[i * block : (i + 1) * block]) for i in range(heads)
    ]
    shared_columns = jnp.where(
        c == 0,
        jnp.concatenate([shared_rows[:, :half], shared_rows[:, block : block + half]], axis=1),
        jnp.concatenate([shared_rows[:, half:block], shared_rows[:, block + half :]], axis=1),
    )
    shared_pre = multiply(shared_conv, shared_columns)
    decay_pre = decay_shift + jnp.concatenate(
        [part[:, :block] for part in pre_parts] + [shared_pre[:, :half]], axis=1
    )
    input_pre = input_shift + jnp.concatenate(
        [part[:, block:] for part in pre_parts] + [shared_pre[:, half:]], axis=1
    )
    (retain, inflow), terms_back = jax.vjp(
        recurrence_terms, decay_pre, input_pre, decay_log, conv_low.astype(F32)
    )
    states, state_in = full_scan(retain, inflow, False)
    before = jnp.concatenate([state_in, states[:-1]])
    lru_low = states.astype(BF16).astype(F32)
    mixed_rows = (lru_low * y_gated).astype(BF16)
    mixed_parts = mixed_rows.reshape(outer, C, rows_dev, lru_cols)

    def branch_of(at):
        part = pick(mixed_parts, at, 1).reshape(outer * rows_dev, lru_cols)
        return contract_last(part, out_kernel).reshape(outer, rows_dev, width)

    group_two, middle, up_kernel, down_kernel = branch_and_group(
        branch_of(1 - c).astype(BF16), branch_of(c), tokens, gain_two[None], up_kernel, down_kernel
    )
    up_kernel = up_kernel.reshape(width, -1)
    down_kernel = down_kernel.reshape(width, -1)
    group_two = group_two.reshape(C * Z * rows_dev, width)

    gate_pre = multiply(group_two, gate_kernel)
    up_pre = multiply(group_two, up_kernel)
    active, gelu_gate_back = jax.vjp(gelu_tanh, gate_pre)
    hidden = (active * up_pre).astype(BF16)

    d_hidden = multiply(grad_group, down_kernel)
    d_up = (d_hidden * active).astype(BF16)
    d_gate = gelu_gate_back(d_hidden * up_pre)[0].astype(BF16)
    half_rows = Z * rows_dev

    def d_normed_of(part):
        total = contract_last(d_gate[part], gate_kernel) + contract_last(d_up[part], up_kernel)
        return total.reshape(Z, rows_dev, width)

    def terms_of(left_side, right_side):
        share = right_side.shape[1] // outer
        return [
            contract_rows(left_side, right_side[:, i * share : (i + 1) * share])
            .astype(BF16)
            .reshape(Z, inner, weight_rows, share)
            for i in range(outer)
        ]

    gate_terms = terms_of(group_two, d_gate)
    up_terms = terms_of(group_two, d_up)
    down_terms = terms_of(grad_group, hidden)
    branch_rows, d_middle, gain_two_grad, block_out, units, units_y, units_x = middle_and_rows(
        d_normed_of(slice(half_rows, None)).astype(BF16),
        d_normed_of(slice(0, half_rows)),
        middle,
        out_grad,
        gain_two[None],
        hidden,
        down_kernel,
        gate_terms + up_terms + down_terms,
    )
    branch_rows = branch_rows.reshape(-1, width)

    d_mixed = multiply(branch_rows, out_kernel)
    d_lru = (d_mixed * y_gated).astype(BF16).astype(F32)
    d_y = gelu_y_back(d_mixed * lru_low)[0].astype(BF16)
    passed, passed_in = full_scan(retain, retain * d_lru, True)
    d_total = d_lru + jnp.concatenate([passed[1:], passed_in])
    d_decay_pre, d_input_pre, decay_log_grad, d_conv_direct = terms_back(
        (d_total * before, d_total)
    )
    d_decay_low, d_input_low = d_decay_pre.astype(BF16), d_input_pre.astype(BF16)
    own_low = jnp.concatenate([d_decay_low[:, full:], d_input_low[:, full:]], axis=1)
    partner_low = c_swap(own_low)
    shared_low = jnp.concatenate(
        [
            in_order(own_low[:, :half], partner_low[:, :half], 1),
            in_order(own_low[:, half:], partner_low[:, half:], 1),
        ],
        axis=1,
    )
    lows = [
        jnp.concatenate([of_head(d_decay_low, i), of_head(d_input_low, i)], axis=1)
        for i in range(heads)
    ]
    d_conv = d_conv_direct + jnp.concatenate(
        [contract_last(lows[i], gate_all[i * block : (i + 1) * block]) for i in range(heads)]
        + [contract_last(shared_low, gate_all[full:])],
        axis=1,
    )
    gates_grad = jnp.concatenate(
        [contract_rows(of_head(conv_low, i), lows[i]) for i in range(heads)]
        + [contract_rows(conv_low[:, full:], shared_low)]
    )
    ahead = lax.ppermute(d_conv[:reach], "seq", [(i + 1, i) for i in range(seq - 1)])
    d_extended = jnp.concatenate([d_conv, ahead], axis=0)
    d_x_branch = sum(taps[k] * d_extended[k : k + rows] for k in range(taps_count)).astype(BF16)
    dx_parts = d_x_branch.reshape(outer, C, rows_dev, lru_cols)
    dy_parts = d_y.reshape(outer, C, rows_dev, lru_cols)

    def d_normed_one_of(at):
        dx, dy = (
            pick(parts, at, 1).reshape(outer * rows_dev, lru_cols) for parts in (dx_parts, dy_parts)
        )
        total = contract_last(dx, xy_kernel[:, :lru_cols]) + contract_last(
            dy, xy_kernel[:, lru_cols:]
        )
        return total.reshape(outer, rows_dev, width)

    narrow = turned_back(gates_grad, 0).astype(BF16).reshape(Z, inner, chunk, 2 * block)
    narrow = jnp.pad(narrow, ((0, 0), (0, 0), (0, -chunk % 16), (0, 0)))
    own_sums = jnp.stack(
        [jnp.sum(d_conv, axis=0), jnp.sum(d_decay_pre, axis=0), jnp.sum(d_input_pre, axis=0)]
        + [decay_log_grad]
        + [jnp.sum(d_conv * extended[reach - k : reach - k + rows], axis=0) for k in range(taps_count)],
    )
    own_sums = turned_back(own_sums, 1)
    placed, wide, narrow, tokens_grad, gains, own_sums = last_sums(
        units, units_y, units_x, group_one, branch_rows, narrow,
        d_normed_one_of(1 - c).astype(BF16), d_normed_one_of(c),
        turned_back(d_x_branch, 1), turned_back(d_y, 1), turned_back(mixed_rows, 1),
        tokens, gain_one[None], d_middle, gain_two_grad, own_sums,
    )
    weight_grads = [wide[:, n * lru_cols : (n + 1) * lru_cols] for n in range(3)]
    gate_grad, up_grad, down_grad = (placed[n, :, :hidden_cols].astype(F32) for n in range(3))
    gains = gains.reshape(2, 8, LANES).sum(axis=1)[:, :chunk]
    sums = lax.dynamic_slice(own_sums[1], (0, lax.axis_index("seq") * chunk), (taps_count + 4, chunk))
    own_sums = jnp.concatenate([narrow[:chunk], sums.T], axis=1)
    own_sums = lax.ppermute(own_sums, ("seq", "wt"), [(to, at) for at, to in across])
    sums = own_sums[:, 2 * block :]
    return (
        block_out,
        tokens_grad,
        gains[0],
        weight_grads[0],
        weight_grads[1],
        sums[:, 4:],
        sums[:, 0],
        own_sums[:, :block],
        sums[:, 1],
        own_sums[:, block : 2 * block],
        sums[:, 2],
        sums[:, 3],
        weight_grads[2],
        gains[1],
        gate_grad,
        up_grad,
        down_grad,
    )


def solution(mesh):
    rows, both, lone = P(("seq", "wt"), None), P("seq", "wt"), P(("seq", "wt"))
    in_specs = (
        rows, lone, both, both, rows, lone, rows, lone, rows, lone, lone,
        both, lone, both, both, both, rows,
    )
    out_specs = (
        rows, rows, lone, both, both, rows, lone, rows, lone, rows, lone, lone,
        both, lone, both, both, both,
    )
    return jax.shard_map(
        per_device, mesh=mesh, in_specs=in_specs, out_specs=out_specs, check_vma=False
    )
```

```python
import functools

import jax
import jax.numpy as jnp
from jax import lax
from jax.experimental import pallas as pl
from jax.experimental.pallas import tpu as pltpu
from jax.sharding import PartitionSpec as P

EPSILON = 1e-06
DECAY_SCALE = 8.0
Z = 4
C = 2
LANES = 128
F32 = jnp.float32
BF16 = jnp.bfloat16
MESH = pl.DeviceIdType.MESH


def gelu_tanh(values):
    return jax.nn.gelu(values, approximate=True)


def sizes():
    return lax.axis_size("seq") // Z, lax.axis_size("wt") // C


def places():
    inner, outer = sizes()
    s, w = lax.axis_index("seq"), lax.axis_index("wt")
    return s // inner, s % inner, w // C, w % C


def z_move(value, by, senders):
    inner, _ = sizes()
    pairs = [(z * inner + x, (z + by) % Z * inner + x) for z in senders for x in range(inner)]
    return lax.ppermute(value, "seq", pairs)


def c_swap(value):
    _, outer = sizes()
    pairs = [(y * C + c, y * C + 1 - c) for y in range(outer) for c in range(C)]
    return lax.ppermute(value, "wt", pairs)


def line_scatter(parts):
    up = down = None
    for step in range(1, Z):
        rising = parts[step] if up is None else parts[step] + up
        falling = parts[Z - step] if down is None else parts[Z - step] + down
        up = z_move(rising.astype(BF16), 1, range(0, step)).astype(F32)
        down = z_move(falling.astype(BF16), -1, range(Z - step, Z)).astype(F32)
    return parts[0] + up + down


def pick(value, index, axis):
    return lax.dynamic_index_in_dim(value, index, axis, keepdims=False)


def contract_last(left_side, right_side):
    return lax.dot_general(
        left_side, right_side, (((1,), (1,)), ((), ())), preferred_element_type=F32
    )


def contract_rows(left_side, right_side):
    return lax.dot_general(
        left_side, right_side, (((0,), (0,)), ((), ())), preferred_element_type=F32
    )


def multiply(left_side, right_side):
    return jnp.dot(left_side, right_side, preferred_element_type=F32)


class Sends:
    def __init__(self, sems):
        self.sems, self.started = sems, []

    def start(self, when, source, target, arrival, device):
        copy = pltpu.make_async_remote_copy(
            src_ref=source,
            dst_ref=target,
            send_sem=self.sems.at[len(self.started)],
            recv_sem=arrival,
            device_id=device,
            device_id_type=MESH,
        )
        if when is True:
            copy.start()
        else:
            pl.when(when)(copy.start)
        self.started.append((when, copy))

    def finish(self):
        for when, copy in self.started:
            if when is True:
                copy.wait_send()
            else:
                pl.when(when)(copy.wait_send)


def arrived(target, arrival, device):
    pltpu.make_async_remote_copy(
        src_ref=target, dst_ref=target, send_sem=arrival, recv_sem=arrival,
        device_id=device, device_id_type=MESH,
    ).wait_recv()


def gather_kernel(shape, *refs):
    inner, outer = shape
    (tokens, grads, vectors, gates, xy, out, gate, up, down) = refs[:9]
    (grads_to, vectors_to, gates_to, xy_to, out_to, gate_to, up_to, down_to) = refs[9:17]
    rows_one, xy_one = refs[17:19]
    gates_own, send_sems, local_sems, line_sems, plane_sems, rows_sems = refs[19:25]
    vector_sems, turn_sems, group_sems, tokens_to, xy_v, vectors_v, spread, read_sems = refs[25:]
    seq, wt = Z * inner, outer * C
    s, w = lax.axis_index("seq"), lax.axis_index("wt")
    z, x, y, c = s // inner, s % inner, w // C, w % C
    sends = Sends(send_sems)
    group = GroupRows(Place(shape), sends, grads, grads_to, group_sems)
    here, counter = [], iter(range(16))

    def at_z(to):
        return {"seq": to * inner + x, "wt": w}

    def at_x(by):
        return {"seq": z * inner + (x + by) % inner, "wt": w}

    def at_y(by):
        return {"seq": s, "wt": (y + by) % outer * C + c}

    at_c = {"seq": s, "wt": y * C + 1 - c}

    def keep(source, target, waited=False):
        copy = pltpu.make_async_copy(source, target, local_sems.at[next(counter)])
        copy.start()
        here.append((waited, copy))
        return copy

    barrier = pltpu.get_barrier_semaphore()

    def greet(i, carried):
        @pl.when(i != s * wt + w)
        def _():
            pl.semaphore_signal(
                barrier, inc=1, device_id={"seq": i // wt, "wt": i % wt}, device_id_type=MESH
            )

        return carried

    lax.fori_loop(0, seq * wt, greet, 0)
    pl.semaphore_wait(barrier, seq * wt - 1)

    class Line:
        def __init__(self, index, source, target):
            self.source, self.target = source, target
            self.sems = line_sems.at[index]

        def forward(self, block, at, up_when, down_when):
            place = self.target.at[at, x]
            arrival = self.sems.at[at, x]
            sends.start(up_when, block, place, arrival, at_z(jnp.minimum(z + 1, Z - 1)))
            sends.start(down_when, block, place, arrival, at_z(jnp.maximum(z - 1, 0)))
            return place, arrival

        def across(self, when, block, at):
            for j in range(1, inner):
                sends.start(when, block, self.target.at[at, x], self.sems.at[at, x], at_x(j))

        def begin_z(self):
            keep(self.source, self.target.at[z, x])
            self.forward(self.source, z, z < Z - 1, z > 0)

        def begin_x(self):
            self.across(True, self.source, z)

        def begin(self):
            self.begin_z()
            self.begin_x()

        def step(self, k):
            for at, there, up_when, down_when in (
                (jnp.maximum(z - k, 0), z - k >= 0, (z - k >= 0) & (z < Z - 1), None),
                (jnp.minimum(z + k, Z - 1), z + k < Z, None, (z + k < Z) & (z > 0)),
            ):
                place, arrival = self.target.at[at, x], self.sems.at[at, x]

                @pl.when(there)
                def _(place=place, arrival=arrival):
                    arrived(place, arrival, at_c)

                if up_when is not None:
                    sends.start(up_when, place, place, arrival, at_z(jnp.minimum(z + 1, Z - 1)))
                else:
                    sends.start(down_when, place, place, arrival, at_z(jnp.maximum(z - 1, 0)))
                self.across(there, place, at)

        def finish(self):
            for at in range(Z):
                for j in range(1, inner):
                    from_x = (x + inner - j) % inner
                    arrived(self.target.at[at, from_x], self.sems.at[at, from_x], at_c)

    class Plane:
        def __init__(self, index, source, target, x_first, whole):
            self.source, self.target, self.x_first, self.whole = source, target, x_first, whole
            self.share = source.shape[1] // Z
            self.sems = plane_sems.at[index]

        def cut(self, at):
            return self.source.at[:, pl.ds(pl.multiple_of(at * self.share, LANES), self.share)]

        def place(self, at, x_at, i):
            return self.target.at[at, x_at, :, i * self.share : (i + 1) * self.share]

        def begin(self):
            self.own = keep(self.cut(z), self.place(z, x, 0), True)
            for k in range(1, Z):
                to = (z + k) % Z
                sends.start(True, self.cut(to), self.place(z, x, 0), self.sems.at[z, 0, 0], at_z(to))

        def over_x(self, at, i):
            place = self.place(at, x, i)
            for j in range(1, inner):
                sends.start(True, place, place, self.sems.at[at, j, i], at_x(j))

        def over_y(self, at, j):
            x_at = (x + inner - j) % inner
            for i in range(1, outer):
                sends.start(
                    True, self.place(at, x_at, 0), self.place(at, x_at, i),
                    self.sems.at[at, j, i], at_y(i),
                )

        def got(self, at, j, i):
            arrived(self.place(at, (x + inner - j) % inner, i), self.sems.at[at, j, i], at_c)

        def first(self, k):
            at = (z + Z - k) % Z
            if k == 0:
                self.own.wait()
            else:
                self.got(at, 0, 0)
            if self.x_first or self.whole:
                self.over_x(at, 0)
            if self.whole or not self.x_first:
                self.over_y(at, 0)

        def second(self, k):
            at = (z + Z - k) % Z
            if self.x_first:
                for j in range(1, inner):
                    self.got(at, j, 0)
                    if self.whole:
                        self.over_y(at, j)
            else:
                for i in range(1, outer):
                    self.got(at, 0, i)

        def finish(self, k):
            if self.whole:
                at = (z + Z - k) % Z
                for j in range(inner):
                    for i in range(1, outer):
                        self.got(at, j, i)

    lines = [Line(0, xy, xy_to), Line(1, gates_own, gates_to), Line(2, out, out_to)]
    planes = [
        Plane(0, gate, gate_to, True, True),
        Plane(1, up, up_to, False, False),
        Plane(2, down, down_to, True, False),
    ]

    me = s * wt + w
    keep(vectors, vectors_to.at[me])

    def vector_copy(i):
        return pltpu.make_async_remote_copy(
            src_ref=vectors, dst_ref=vectors_to.at[me],
            send_sem=vector_sems.at[0, i], recv_sem=vector_sems.at[1, me],
            device_id={"seq": i // wt, "wt": i % wt}, device_id_type=MESH,
        )

    def vector_send(i, carried):
        pl.when(i != me)(lambda: vector_copy(i).start())
        return carried

    def tokens_begin():
        keep(tokens, tokens_to.at[w])
        sends.start(True, tokens, tokens_to.at[w], rows_sems.at[w], at_c)
        for i in range(1, outer):
            sends.start(True, tokens, tokens_to.at[w], rows_sems.at[w], at_y(i))

    def tokens_step():
        for i in range(1, outer):
            at = (y + outer - i) % outer * C + c
            arrived(tokens_to.at[at], rows_sems.at[at], at_c)
            sends.start(True, tokens_to.at[at], tokens_to.at[at], rows_sems.at[at], at_c)

    def tokens_finish():
        for i in range(outer):
            at = (y + outer - i) % outer * C + 1 - c
            arrived(tokens_to.at[at], rows_sems.at[at], at_c)

    to_seq, to_wt = me % seq, me // seq
    from_me = w * seq + s
    turn = pltpu.make_async_remote_copy(
        src_ref=gates, dst_ref=gates_own, send_sem=turn_sems.at[0], recv_sem=turn_sems.at[1],
        device_id={"seq": to_seq, "wt": to_wt}, device_id_type=MESH,
    )
    stay = pltpu.make_async_copy(gates, gates_own, turn_sems.at[2])
    here_too = from_me == me

    pl.when(jnp.logical_not(here_too))(turn.start)
    pl.when(here_too)(stay.start)
    def vector_wait(i, carried):
        @pl.when(i != me)
        def _():
            vector_copy(i).wait_send()
            arrived(vectors_to.at[i], vector_sems.at[1, i], at_c)

        return carried

    def first_projection():
        lines[0].finish()
        tokens_finish()
        lax.fori_loop(0, seq * wt, vector_wait, 0)
        for copy in here_first:
            copy.wait()
        rows_each = xy.shape[0]
        copies = [pltpu.make_async_copy(vectors_to, vectors_v, read_sems.at[0])]
        for z_at in range(Z):
            for x_at in range(inner):
                n = z_at * inner + x_at
                copies.append(
                    pltpu.make_async_copy(
                        xy_to.at[z_at, x_at], xy_v.at[n * rows_each : (n + 1) * rows_each],
                        read_sems.at[1 + n],
                    )
                )
        for copy in copies:
            copy.start()
        copies[0].wait()
        width = tokens.shape[1]
        devices = seq * wt
        channels = width // devices
        spread[...] = jnp.zeros_like(spread)
        for i in range(devices):
            first = min(i * channels // LANES * LANES, width - 2 * LANES)
            turn = i * channels - first
            part = vectors_v[i, 0:8]
            part = jnp.concatenate([part, jnp.zeros_like(part)], axis=1)
            if turn:
                part = pltpu.roll(part, turn, 1)
            spread[:, first : first + 2 * LANES] += part
        gain = spread[0:1]
        count = tokens.shape[0]
        for at in range(wt):

            def norm(r, at=at):
                stream = tokens_to[at, r].astype(F32)
                inverse = lax.rsqrt(jnp.mean(stream * stream, axis=1, keepdims=True) + EPSILON)
                rows_one[pl.ds(pl.multiple_of(at * count + r.start, 16), 16)] = (
                    stream * inverse * gain
                ).astype(BF16)

            each_rows(count, 16, norm)
        for copy in copies[1:]:
            copy.wait()
        tile = 2 * LANES

        def project(n, carried):
            down = pl.ds(pl.multiple_of(n % wt * count, LANES), count)
            across = pl.ds(pl.multiple_of(n // wt * tile, tile), tile)
            xy_one[down, across] = multiply(rows_one[down], xy_v[:, across])
            return carried

        lax.fori_loop(0, wt * (xy_v.shape[1] // tile), project, 0)

    lines[0].begin()
    tokens_begin()
    here_first = [copy for _, copy in here]
    here.clear()

    @pl.when(jnp.logical_not(here_too))
    def _():
        arrived(gates_own, turn_sems.at[1], at_c)

    pl.when(here_too)(stay.wait)
    lines[1].begin()
    lines[2].begin_z()
    lax.fori_loop(0, seq * wt, vector_send, 0)
    for k in range(1, Z):
        lines[1].step(k)
        lines[0].step(k)
        if k == 1:
            tokens_step()
    lines[2].begin_x()
    for k in range(1, Z):
        lines[2].step(k)
        if k == Z - 2:
            planes[0].begin()
            planes[2].begin()
            planes[1].begin()
    for k in range(Z):
        planes[0].first(k)
    for k in range(Z):
        planes[2].first(k)
    keep(grads, group.place(0, z, z))
    group.begin()
    for k in range(Z):
        planes[1].first(k)
    for k in range(Z):
        planes[0].second(k)
    group.step(1)
    first_projection()
    for k in range(2, Z):
        group.step(k)
    group.finish()

    for line in lines[1:]:
        line.finish()
    for k in range(Z):
        planes[1].second(k)
        planes[2].second(k)
        planes[0].finish(k)

    pl.when(jnp.logical_not(here_too))(turn.wait_send)
    sends.finish()
    for waited, copy in here:
        if not waited:
            copy.wait()


def gather_all(tokens, grads, vectors, gates, xy, out, gate, up, down):
    inner, outer = sizes()
    seq, wt = Z * inner, outer * C

    def buffer(*shape, like):
        return jax.ShapeDtypeStruct(shape, like.dtype)

    def plane(weight):
        rows, columns = weight.shape
        return buffer(Z, inner, rows, outer * columns // Z, like=weight)

    shapes = (
        buffer(C, Z, *grads.shape, like=grads),
        buffer(seq * wt, *vectors.shape, like=vectors),
        buffer(Z, inner, *gates.shape, like=gates),
        buffer(Z, inner, *xy.shape, like=xy),
        buffer(Z, inner, *out.shape, like=out),
        plane(gate),
        plane(up),
        plane(down),
        buffer(wt * tokens.shape[0], tokens.shape[1], like=tokens),
        jax.ShapeDtypeStruct((wt * tokens.shape[0], xy.shape[1]), F32),
    )
    copies = 3 * (2 + inner + (Z - 1) * 2 * inner) + 3 * (Z - 1 + Z * (inner + 2 * outer + inner * outer))
    copies += 2 * outer + 3 + 4 * Z
    dma = pltpu.SemaphoreType.DMA
    return pl.pallas_call(
        functools.partial(gather_kernel, (inner, outer)),
        out_shape=shapes,
        in_specs=[pl.BlockSpec(memory_space=pl.ANY)] * 9,
        out_specs=[pl.BlockSpec(memory_space=pl.ANY)] * 8 + [pl.BlockSpec(memory_space=pltpu.VMEM)] * 2,
        scratch_shapes=[
            pltpu.VMEM(gates.shape, gates.dtype),
            dma((copies,)),
            dma((16,)),
            dma((3, Z, inner)),
            dma((3, Z, inner, outer)),
            dma((wt,)),
            dma((2, seq * wt)),
            dma((3,)),
            dma((C, Z)),
            pltpu.VMEM((wt, *tokens.shape), tokens.dtype),
            pltpu.VMEM((Z * inner * xy.shape[0], xy.shape[1]), xy.dtype),
            pltpu.VMEM((seq * wt, *vectors.shape), F32),
            pltpu.VMEM((8, tokens.shape[1]), F32),
            dma((1 + Z * inner,)),
        ],
        compiler_params=pltpu.CompilerParams(
            collective_id=0, has_side_effects=True, vmem_limit_bytes=40 * 1024 * 1024
        ),
        name="gather_all",
    )(tokens, grads, vectors, gates, xy, out, gate, up, down)


class Place:
    def __init__(self, shape):
        self.inner, self.outer = shape
        self.s, self.w = lax.axis_index("seq"), lax.axis_index("wt")
        self.z, self.x = self.s // self.inner, self.s % self.inner
        self.y, self.c = self.w // C, self.w % C
        self.at_c = {"seq": self.s, "wt": self.y * C + 1 - self.c}
        self.z_up, self.z_down = jnp.minimum(self.z + 1, Z - 1), jnp.maximum(self.z - 1, 0)

    def at_z(self, to):
        return {"seq": to * self.inner + self.x, "wt": self.w}

    def at_x(self, by):
        return {"seq": self.z * self.inner + (self.x + by) % self.inner, "wt": self.w}

    def at_y(self, by):
        return {"seq": self.s, "wt": (self.y + self.outer + by) % self.outer * C + self.c}

    def greet_all(self):
        barrier = pltpu.get_barrier_semaphore()
        wt = self.outer * C
        count = Z * self.inner * wt

        def signal(i, carried):
            @pl.when(i != self.s * wt + self.w)
            def _():
                pl.semaphore_signal(
                    barrier, inc=1, device_id={"seq": i // wt, "wt": i % wt}, device_id_type=MESH
                )

            return carried

        lax.fori_loop(0, count, signal, 0)
        pl.semaphore_wait(barrier, count - 1)

    def greet(self):
        barrier = pltpu.get_barrier_semaphore()
        devices = [self.at_c]
        devices += [self.at_z((self.z + k) % Z) for k in range(1, Z)]
        devices += [self.at_x(j) for j in range(1, self.inner)]
        devices += [self.at_y(i) for i in range(1, self.outer)]
        for device in devices:
            pl.semaphore_signal(barrier, inc=1, device_id=device, device_id_type=MESH)
        pl.semaphore_wait(barrier, len(devices))


def each_rows(count, step, body):
    def run(i, carried):
        body(pl.ds(pl.multiple_of(i * step, step), step))
        return carried

    lax.fori_loop(0, count // step, run, 0)


class WtRows:
    def __init__(self, me, sends, source, target, sems):
        self.me, self.sends, self.source, self.target, self.sems = me, sends, source, target, sems

    def begin(self):
        me = self.me
        for device in [me.at_y(i) for i in range(1, me.outer)] + [me.at_c]:
            self.sends.start(True, self.source, self.target.at[me.w], self.sems.at[me.w], device)

    def step(self):
        me = self.me
        for i in range(1, me.outer):
            at = (me.y + me.outer - i) % me.outer * C + me.c
            arrived(self.target.at[at], self.sems.at[at], me.at_c)
            self.sends.start(True, self.target.at[at], self.target.at[at], self.sems.at[at], me.at_c)

    def finish(self):
        me = self.me
        for i in range(me.outer):
            at = (me.y + me.outer - i) % me.outer * C + 1 - me.c
            arrived(self.target.at[at], self.sems.at[at], me.at_c)


class GroupRows:
    def __init__(self, me, sends, source, target, sems):
        self.me, self.sends, self.source, self.target, self.sems = me, sends, source, target, sems

    def place(self, own, at, z_to):
        return self.target.at[own, (z_to - at + Z) % Z]

    def forward(self, at, source, there, way):
        me = self.me
        z_to = me.z_up if way > 0 else me.z_down
        room = me.z < Z - 1 if way > 0 else me.z > 0
        when = room if there is None else there & room
        self.sends.start(
            when, source, self.place(0, at, z_to), self.sems.at[0, at], me.at_z(z_to)
        )

    def begin(self):
        me = self.me
        self.forward(me.z, self.source, None, 1)
        self.forward(me.z, self.source, None, -1)
        self.sends.start(
            True, self.source, self.place(1, me.z, me.z), self.sems.at[1, me.z], me.at_c
        )

    def step(self, k):
        me = self.me
        for at, there, way in (
            (jnp.maximum(me.z - k, 0), me.z - k >= 0, 1),
            (jnp.minimum(me.z + k, Z - 1), me.z + k < Z, -1),
        ):
            place = self.place(0, at, me.z)

            @pl.when(there)
            def _(place=place, at=at):
                arrived(place, self.sems.at[0, at], me.at_c)

            self.forward(at, place, there, way)
            self.sends.start(there, place, self.place(1, at, me.z), self.sems.at[1, at], me.at_c)

    def finish(self):
        me = self.me
        for at in range(Z):
            arrived(self.place(1, at, me.z), self.sems.at[1, at], me.at_c)


def branch_kernel(
    shape, sent, own, tokens, gain, up_held, down_held, group_to, middle, up_to, down_to,
    own_v, c_in, y_out, y_in, low,
    send_sems, local_sems, c_sems, y_sems, group_sems, up_sems, down_sems,
):
    del up_held, down_held
    me = Place(shape)
    inner, outer = shape
    share = up_to.shape[3] // outer
    rows = tokens.shape[0]
    sends = Sends(send_sems)
    load = pltpu.make_async_copy(own, own_v, local_sems.at[0])
    load.start()
    me.greet()
    order = [(me.y + i) % outer for i in list(range(1, outer)) + [0]]
    for at in order:
        sends.start(True, sent.at[at], c_in.at[at], c_sems.at[at], me.at_c)

    def columns(held, x_at, i):
        return held.at[:, x_at, :, i * share : (i + 1) * share]

    for j in range(1, inner):
        for i in range(outer):
            place = columns(up_to, me.x, i)
            sends.start(True, place, place, up_sems.at[j - 1, i], me.at_x(j))
    load.wait()
    for i, at in enumerate(order):
        arrived(c_in.at[at], c_sems.at[at], me.at_c)
        if i < outer - 1:
            each_rows(rows, 16, lambda r, i=i, at=at: y_out.__setitem__(
                (i, r), (own_v[at, r] + c_in[at, r]).astype(BF16)))
            sends.start(True, y_out.at[i], y_in.at[i], y_sems.at[i], me.at_y(i + 1))
    for i in range(outer - 1):
        arrived(y_in.at[i], y_sems.at[i], me.at_c)
    for i in range(1, outer):
        for j in range(inner):
            x_at = (me.x + inner - j) % inner
            sends.start(
                True, columns(down_to, x_at, 0), columns(down_to, x_at, i),
                down_sems.at[i - 1, j], me.at_y(i),
            )

    def work(r):
        total = tokens[r].astype(F32) + own_v[me.y, r] + c_in[me.y, r]
        for i in range(outer - 1):
            total = total + y_in[i, r].astype(F32)
        inverse = lax.rsqrt(jnp.mean(total * total, axis=1, keepdims=True) + EPSILON)
        middle[r] = total
        low[r] = (total * inverse * gain[...]).astype(BF16)

    each_rows(rows, 16, work)
    keep = pltpu.make_async_copy(low, group_to.at[0, 0], local_sems.at[1])
    keep.start()
    group = GroupRows(me, sends, low, group_to, group_sems)
    group.begin()
    for k in range(1, Z):
        group.step(k)
    group.finish()
    for j in range(1, inner):
        for i in range(outer):
            x_at = (me.x + inner - j) % inner
            arrived(columns(up_to, x_at, i), up_sems.at[j - 1, i], me.at_c)
    for i in range(1, outer):
        for j in range(inner):
            x_at = (me.x + inner - j) % inner
            arrived(columns(down_to, x_at, i), down_sems.at[i - 1, j], me.at_c)
    sends.finish()
    keep.wait()


def branch_and_group(sent, own, tokens, gain, up, down):
    inner, outer = sizes()
    rows, width = tokens.shape
    dma = pltpu.SemaphoreType.DMA
    vmem, anywhere = pl.BlockSpec(memory_space=pltpu.VMEM), pl.BlockSpec(memory_space=pl.ANY)
    return pl.pallas_call(
        functools.partial(branch_kernel, (inner, outer)),
        out_shape=(
            jax.ShapeDtypeStruct((C, Z, rows, width), BF16),
            jax.ShapeDtypeStruct((rows, width), F32),
            jax.ShapeDtypeStruct(up.shape, up.dtype),
            jax.ShapeDtypeStruct(down.shape, down.dtype),
        ),
        in_specs=[anywhere, anywhere, vmem, vmem, anywhere, anywhere],
        out_specs=(anywhere, vmem, anywhere, anywhere),
        input_output_aliases={4: 2, 5: 3},
        scratch_shapes=[
            pltpu.VMEM((outer, rows, width), F32),
            pltpu.VMEM((outer, rows, width), F32),
            pltpu.VMEM((outer - 1, rows, width), BF16),
            pltpu.VMEM((outer - 1, rows, width), BF16),
            pltpu.VMEM((rows, width), BF16),
            dma((2 * outer + 3 + 4 * (Z - 1) + (inner - 1) * outer + inner * (outer - 1),)),
            dma((2,)),
            dma((outer,)),
            dma((outer - 1,)),
            dma((C, Z)),
            dma((inner - 1, outer)),
            dma((outer - 1, inner)),
        ],
        compiler_params=pltpu.CompilerParams(
            collective_id=1, has_side_effects=True, vmem_limit_bytes=40 * 1024 * 1024
        ),
        name="branch_and_group",
    )(sent, own, tokens, gain, up, down)


def line_order():
    order = []
    for k in [n for t in range(1, Z) for n in (t, Z - t)] + [0]:
        if k not in order:
            order.append(k)
    return order


def line_sum(me, sends, rows, term, ready, store, held, up, down, between=None):
    z = me.z

    def add(when, target, slot, k, received=None, came=0):
        def body(r):
            value = term(k, r)
            if received is not None:
                value = value + received[came, r].astype(F32)
            target[slot, r] = value.astype(BF16)

        pl.when(when)(lambda: each_rows(rows, 16, body))

    for t in range(1, Z):
        slot = t - 1
        for k, (out, into, sems), out_slot, has, when, to in (
            (t, up, slot, z > 0, (z <= t - 1) & (z < Z - 1), me.z_up),
            (Z - t, down, Z - 1 - t, z < Z - 1, (z >= Z - t) & (z > 0), me.z_down),
        ):
            pl.when(when)(lambda k=k: ready(k))
            if t == 1:
                add(when, out, out_slot, k)
            else:
                pl.when(when & has)(
                    lambda into=into, sems=sems, slot=slot: arrived(
                        into.at[slot - 1], sems.at[slot - 1], me.at_c
                    )
                )
                add(when & has, out, out_slot, k, into, slot - 1)
                add(when & jnp.logical_not(has), out, out_slot, k)
            sends.start(when, out.at[out_slot], into.at[slot], sems.at[slot], me.at_z(to))
        if between is not None:
            between(t)
    ready(0)
    each_rows(rows, 16, lambda r: store(r, term(0, r)))
    for (_, into, sems), has in ((up, z > 0), (down, z < Z - 1)):

        @pl.when(has)
        def _(into=into, sems=sems):
            arrived(into.at[Z - 2], sems.at[Z - 2], me.at_c)
            each_rows(rows, 16, lambda r: store(r, held(r) + into[Z - 2, r].astype(F32)))


class PlaneTerms:
    def __init__(self, me, sends, parts, over_x, blocks, scratch):
        self.me, self.sends, self.parts, self.over_x, self.blocks = me, sends, parts, over_x, blocks
        self.came, self.mine, self.sems, self.local_sems = scratch

    def begin(self):
        me = self.me
        if self.over_x:
            for j in range(1, me.inner):
                for i, part in enumerate(self.parts):
                    self.sends.start(
                        True, part.at[self.blocks, (me.x + j) % me.inner],
                        self.came.at[j - 1, i], self.sems.at[j - 1, i], me.at_x(j),
                    )
            pairs = [(part.at[self.blocks, me.x], self.mine.at[i]) for i, part in enumerate(self.parts)]
        else:
            for i in range(1, me.outer):
                self.sends.start(
                    True, self.parts[i].at[self.blocks], self.came.at[i - 1],
                    self.sems.at[0, i - 1], me.at_y(-i),
                )
            pairs = [(self.parts[0].at[self.blocks], self.mine)]
        self.loads = self.moved(pairs)

    def moved(self, pairs):
        copies = [
            pltpu.make_async_copy(source, target, self.local_sems.at[n])
            for n, (source, target) in enumerate(pairs)
        ]
        for copy in copies:
            copy.start()
        return copies

    def add(self):
        me = self.me
        if self.over_x:
            count, places = me.inner - 1, [(i,) for i in range(me.outer)]
        else:
            count, places = me.outer - 1, [()]
        for n in range(count):
            for place in places:
                sems = self.sems.at[n, place[0]] if place else self.sems.at[0, n]
                arrived(self.came.at[(n, *place)], sems, me.at_c)
        for copy in self.loads:
            copy.wait()
        shape = self.mine.shape[:2]

        def body(r):
            for first in range(shape[0]):
                for second in range(shape[1]):
                    total = self.mine[first, second, r].astype(F32)
                    for n in range(count):
                        total = total + self.came[n, first, second, r].astype(F32)
                    self.mine[first, second, r] = total.astype(BF16)

        each_rows(self.mine.shape[2], 16, body)

    def hand_on(self, kept, sent):
        me = self.me
        if self.over_x:
            pairs = [(self.mine.at[i], kept if i == 0 else sent(i - 1)) for i in range(me.outer)]
        else:
            pairs = [
                (self.mine.at[:, (me.x + j) % me.inner], kept if j == 0 else sent(j - 1))
                for j in range(me.inner)
            ]
        self.loads = self.moved(pairs)

    def second(self, into, sems):
        me = self.me
        for j in range(1, me.inner):
            self.sends.start(
                True, self.mine.at[:, (me.x + j) % me.inner], into.at[j - 1], sems.at[j - 1],
                me.at_x(j),
            )

    def add_second(self, into, sems, kept):
        me = self.me
        for j in range(1, me.inner):
            arrived(into.at[j - 1], sems.at[j - 1], me.at_c)

        def body(r):
            for first in range(self.mine.shape[0]):
                total = self.mine[first, me.x, r].astype(F32)
                for j in range(1, me.inner):
                    total = total + into[j - 1, first, r].astype(F32)
                self.mine[first, me.x, r] = total.astype(BF16)

        each_rows(self.mine.shape[2], 16, body)
        self.loads = self.moved([(self.mine.at[:, me.x], kept)])

    def finish(self):
        for copy in self.loads:
            copy.wait()


def middle_kernel(shape, *refs):
    outer = shape[1]
    sent, own, middle, grads, gain, hidden, down_kernel = refs[:7]
    parts = refs[7 : 7 + 3 * outer]
    rows_to, d_middle, gain_grad, block_out = refs[7 + 3 * outer : 11 + 3 * outer]
    targets = refs[11 + 3 * outer : 14 + 3 * outer]
    scratch = refs[14 + 3 * outer :]
    middle_body(
        shape, sent, own, middle, grads, gain, hidden, down_kernel, parts, targets,
        rows_to, d_middle, gain_grad, block_out, scratch[:8], scratch[8:16],
        [scratch[16 + 4 * n : 20 + 4 * n] for n in range(4)], *scratch[32:],
    )


class PairSum:
    def __init__(self, me, sends, sent, own, scratch):
        self.me, self.sends, self.sent = me, sends, sent
        self.held, self.c_in, out, up_in, down_in, self.c_sems, up_sems, down_sems = scratch
        self.up, self.down = (out, up_in, up_sems), (out, down_in, down_sems)

    def begin(self):
        for k in line_order():
            self.sends.start(
                True, self.sent.at[k], self.c_in.at[k], self.c_sems.at[k], self.me.at_c
            )

    def run(self, between=None):
        def ready(k):
            arrived(self.c_in.at[k], self.c_sems.at[k], self.me.at_c)

        def term(k, r):
            return self.held[k, r] + self.c_in[k, r].astype(F32)

        def store(r, value):
            self.held[0, r] = value

        line_sum(
            self.me, self.sends, self.held.shape[1], term, ready, store,
            lambda r: self.held[0, r], self.up, self.down, between,
        )


def plane_units(me, sends, parts, scratch):
    outer = me.outer
    gate, up, down = (parts[n * outer : (n + 1) * outer] for n in range(3))
    every, low, high = slice(0, Z), slice(0, Z // 2), slice(Z // 2, Z)
    return [
        PlaneTerms(me, sends, gate, True, every, scratch[0]),
        PlaneTerms(me, sends, up, False, every, scratch[1]),
        PlaneTerms(me, sends, down, True, low, scratch[2]),
        PlaneTerms(me, sends, down, False, high, scratch[3]),
    ]


def middle_body(
    shape, sent, own, middle, grads, gain, hidden, down_kernel, parts, targets,
    rows_to, d_middle, gain_grad, block_out, sum_scratch, feed_scratch, unit_scratch, low,
    up_in, hidden_v, feed_sent, down_v, send_sems, local_sems, rows_sems, up_sems, down_sems,
):
    me = Place(shape)
    rows = middle.shape[0]
    sends = Sends(send_sems)
    total = PairSum(me, sends, sent, own, sum_scratch)
    feed = PairSum(me, sends, feed_sent, None, feed_scratch)
    load = pltpu.make_async_copy(own, total.held, local_sems.at[0])
    hidden_load = pltpu.make_async_copy(hidden, hidden_v, local_sems.at[2])
    load.start()
    hidden_load.start()
    me.greet()
    total.begin()
    units = plane_units(me, sends, parts, unit_scratch)
    units_to, units_y, units_x = targets
    for unit in units:
        unit.begin()

    step = down_v.shape[1]
    half_rows = Z * rows

    def down_load(n, slot):
        part = down_kernel.at[pl.ds(pl.multiple_of(n * step, LANES), step)]
        return pltpu.make_async_copy(part, down_v.at[slot], down_sems.at[slot])

    def feed_product(n, carried):
        slot = n % 2
        down_load(n, slot).wait()
        pl.when(n + 1 < down_kernel.shape[0] // step)(lambda: down_load(n + 1, 1 - slot).start())
        across = pl.ds(pl.multiple_of(n * step, LANES), step)
        weight = down_v[slot]
        for k in range(Z):
            kept = hidden_v[k * rows : (k + 1) * rows]
            other = hidden_v[half_rows + k * rows : half_rows + (k + 1) * rows]
            feed.held[k, :, across] = contract_last(kept, weight)
            feed_sent[k, :, across] = contract_last(other, weight).astype(BF16)
        return carried

    down_load(0, 0).start()
    load.wait()
    hidden_load.wait()
    pieces = down_kernel.shape[0] // step
    ends = [pieces * t // (Z - 1) for t in range(Z)]
    total.run(lambda t: lax.fori_loop(ends[t - 1], ends[t], feed_product, 0))
    own_v = total.held
    gain_grad[...] = jnp.zeros_like(gain_grad)

    def work(r):
        values = middle[r]
        inverse = lax.rsqrt(jnp.mean(values * values, axis=1, keepdims=True) + EPSILON)
        normed = values * inverse
        d_normed = own_v[0, r]
        gain_grad[...] += d_normed * normed
        scaled = d_normed * gain[...]
        passed = inverse * (scaled - normed * jnp.mean(scaled * normed, axis=1, keepdims=True))
        total = grads[r].astype(F32) + passed
        d_middle[r] = total
        low[r] = total.astype(BF16)

    each_rows(rows, 16, work)
    keep = pltpu.make_async_copy(low, rows_to.at[me.w], local_sems.at[1])
    keep.start()
    gather = WtRows(me, sends, low, rows_to, rows_sems)
    gather.begin()
    feed.begin()
    half, extra = Z // 2, slice(Z, Z + Z // 2)

    def between(t):
        if t == 1:
            units[0].add()
            units[0].hand_on(units_to.at[0], lambda i: units_y.at[i, 0:Z])
        if t == 2:
            units[1].add()
            units[1].second(up_in, up_sems)
        if t == 3:
            units[2].add()
            units[2].hand_on(units_to.at[2, 0:half], lambda i: units_y.at[i, extra])
            units[3].add()
            units[3].hand_on(units_to.at[2, half:Z], lambda j: units_x.at[j])

    feed.run(between)
    each_rows(rows, 16, lambda r: block_out.__setitem__(
        r, (middle[r] + feed.held[0, r]).astype(BF16)))
    gather.step()
    gather.finish()
    units[1].add_second(up_in, up_sems, units_to.at[1])
    for unit in units:
        unit.finish()
    sends.finish()
    keep.wait()


def middle_and_rows(sent, own, middle, grads, gain, hidden, down_kernel, parts):
    inner, outer = sizes()
    rows, width = middle.shape
    unit_rows, share = parts[0].shape[2:]
    block = (unit_rows, share)
    targets = [
        jax.ShapeDtypeStruct((*shape, *block), BF16)
        for shape in ((3, Z), (outer - 1, Z + Z // 2), (inner - 1, Z // 2))
    ]
    unit_copies = 2 * (inner - 1) * outer + 2 * (outer - 1) + (inner - 1)
    pair_scratch = [pltpu.VMEM((Z, rows, width), F32), pltpu.VMEM((Z, rows, width), BF16)]
    pair_scratch += [pltpu.VMEM((Z - 1, rows, width), BF16)] * 3
    dma = pltpu.SemaphoreType.DMA
    pair_scratch += [dma((Z,)), dma((Z - 1,)), dma((Z - 1,))]
    unit_scratch = []
    for came, mine in (
        ((inner - 1, outer, Z), (outer, Z)),
        ((outer - 1, Z, inner), (Z, inner)),
        ((inner - 1, outer, Z // 2), (outer, Z // 2)),
        ((outer - 1, Z // 2, inner), (Z // 2, inner)),
    ):
        unit_scratch += [pltpu.VMEM((*came, *block), BF16), pltpu.VMEM((*mine, *block), BF16)]
        unit_scratch += [dma((inner - 1, outer)), dma((max(inner, outer),))]
    vmem, anywhere = pl.BlockSpec(memory_space=pltpu.VMEM), pl.BlockSpec(memory_space=pl.ANY)
    return pl.pallas_call(
        functools.partial(middle_kernel, (inner, outer)),
        out_shape=(
            jax.ShapeDtypeStruct((outer * C, rows, width), BF16),
            jax.ShapeDtypeStruct((rows, width), F32),
            jax.ShapeDtypeStruct((16, width), F32),
            jax.ShapeDtypeStruct((rows, width), BF16),
            *targets,
        ),
        in_specs=[anywhere, anywhere, vmem, vmem, vmem] + [anywhere] * (2 + 3 * outer),
        out_specs=(anywhere, vmem, vmem, vmem) + (anywhere,) * 3,
        scratch_shapes=pair_scratch * 2
        + unit_scratch
        + [
            pltpu.VMEM((rows, width), BF16),
            pltpu.VMEM((inner - 1, Z, *block), BF16),
            pltpu.VMEM(hidden.shape, BF16),
            pltpu.VMEM((Z, rows, width), BF16),
            pltpu.VMEM((2, 2 * LANES, hidden.shape[1]), BF16),
            dma((2 * (Z + 2 * (Z - 1)) + 2 * outer + unit_copies,)),
            dma((3,)),
            dma((outer * C,)),
            dma((inner - 1,)),
            dma((2,)),
        ],
        compiler_params=pltpu.CompilerParams(
            collective_id=2, has_side_effects=True, vmem_limit_bytes=60 * 1024 * 1024
        ),
        name="middle_and_rows",
    )(sent, own, middle, grads, gain, hidden, down_kernel, *parts)


class RowsSum:
    def __init__(self, me, sends, terms, total, scratch, sems):
        self.me, self.sends, self.terms, self.total = me, sends, terms, total
        self.own, self.x_in, *ways = scratch
        self.own_sems, self.x_sems, up_sems, down_sems = sems
        self.up, self.down = (*ways[:2], up_sems), (*ways[2:], down_sems)

    def load(self):
        me = self.me
        self.loads = []
        for k in range(Z):
            self.loads.append(
                pltpu.make_async_copy(
                    self.terms.at[(me.z + Z - k) % Z, me.x], self.own.at[k], self.own_sems.at[k]
                )
            )
            self.loads[k].start()

    def begin(self, turns):
        me = self.me
        for turn in turns:
            if turn == Z - 1:
                k = 0
            else:
                k = (jnp.minimum(me.z, Z - 1 - me.z) + turn) % (Z - 1) + 1
                k = jnp.where(me.z < Z // 2, k, Z - k)
            at = (me.z + Z - k) % Z
            for j in range(1, me.inner):
                self.sends.start(
                    True, self.terms.at[at, (me.x + j) % me.inner], self.x_in.at[j - 1, k],
                    self.x_sems.at[j - 1, k], me.at_x(j),
                )

    def run(self, between=None):
        me = self.me

        def ready(k):
            self.loads[k].wait()
            for j in range(1, me.inner):
                arrived(self.x_in.at[j - 1, k], self.x_sems.at[j - 1, k], me.at_c)

        def term(k, r):
            value = self.own[k, r].astype(F32)
            for j in range(1, me.inner):
                value = value + self.x_in[j - 1, k, r].astype(F32)
            return value

        def store(r, value):
            self.total[r] = value

        line_sum(
            me, self.sends, self.total.shape[0], term, ready, store, lambda r: self.total[r],
            self.up, self.down, between,
        )


class ProductsSum(RowsSum):
    def __init__(self, me, sends, factors, total, scratch, sems):
        self.me, self.sends, self.total = me, sends, total
        self.factors = factors
        self.held, self.x_in, out, up_in, down_in, *self.lefts = scratch
        self.own_sems, self.x_sems, up_sems, down_sems = sems
        self.up, self.down = (out, up_in, up_sems), (out, down_in, down_sems)

    def load(self):
        self.loads = []
        for n, (left, _) in enumerate(self.factors):
            copy = pltpu.make_async_copy(left, self.lefts[n], self.own_sems.at[n])
            copy.start()
            self.loads.append(copy)

    def begin(self, turns):
        me = self.me
        while self.loads:
            self.loads.pop().wait()
        rows, span = self.total.shape[0], self.held.shape[1]
        for turn in turns:
            if turn == Z - 1:
                k = 0
            else:
                k = (jnp.minimum(me.z, Z - 1 - me.z) + turn) % (Z - 1) + 1
                k = jnp.where(me.z < Z // 2, k, Z - k)
            at = (me.z + Z - k) % Z

            def tile(i, carried, k=k, at=at):
                first = 0
                down = pl.ds(pl.multiple_of(i * LANES, LANES), LANES)
                across = pl.ds(pl.multiple_of(at * span + i * LANES, LANES), LANES)
                for n, (_, rights) in enumerate(self.factors):
                    left = self.lefts[n][:, across]
                    for right in rights:
                        columns = slice(first, first + right.shape[1])
                        self.held[k, down, columns] = contract_rows(left, right[...]).astype(BF16)
                        first += right.shape[1]
                return carried

            lax.fori_loop(0, span // LANES, tile, 0)
            for j in range(1, me.inner):
                part = pl.ds(pl.multiple_of((me.x + j) % me.inner * rows, 16), rows)
                self.sends.start(
                    True, self.held.at[k, part], self.x_in.at[j - 1, k], self.x_sems.at[j - 1, k],
                    me.at_x(j),
                )

    def run(self, between=None):
        me = self.me
        rows = self.total.shape[0]

        def ready(k):
            for j in range(1, me.inner):
                arrived(self.x_in.at[j - 1, k], self.x_sems.at[j - 1, k], me.at_c)

        def term(k, r):
            mine = pl.ds(pl.multiple_of(me.x * rows + r.start, 16), r.size)
            value = self.held[k, mine].astype(F32)
            for j in range(1, me.inner):
                value = value + self.x_in[j - 1, k, r].astype(F32)
            return value

        def store(r, value):
            self.total[r] = value

        line_sum(
            me, self.sends, rows, term, ready, store, lambda r: self.total[r],
            self.up, self.down, between,
        )


def sums_kernel(shape, *refs):
    inner, outer = shape
    units, units_y, units_x, normed_rows_one, branch_rows, narrow, sent, own = refs[:8]
    d_x, d_y, mixed, tokens, gain, d_middle, gain_two_grad, vectors = refs[8:16]
    units_to, wide_to, narrow_to, tokens_grad, gains, vectors_to = refs[16:22]
    refs = refs[22:]
    wide_scratch, narrow_scratch = refs[:7], refs[7:13]
    (own_v, c_in, y_out, y_in, parts_out, parts_in, gains_v, vec_in) = refs[13:21]
    refs = refs[2:]
    (send_sems, local_sems, c_sems, y_sems, all_sems, vec_sems) = refs[19:25]
    wide_sems, narrow_sems = refs[25:29], refs[29:33]
    units_v, units_y_in, units_x_in, unit_sems, units_y_sems, units_x_sems = refs[33:]
    share = units.shape[3]
    me = Place(shape)
    rows = tokens.shape[0]
    sends = Sends(send_sems)
    load = pltpu.make_async_copy(own, own_v, local_sems.at[0])
    load.start()
    units_load = pltpu.make_async_copy(units, units_v, local_sems.at[1])
    units_load.start()
    me.greet_all()

    order = [(me.y + i) % outer for i in list(range(1, outer)) + [0]]
    for at in order:
        sends.start(True, sent.at[at], c_in.at[at], c_sems.at[at], me.at_c)
    narrow_sum = RowsSum(me, sends, narrow, narrow_to, narrow_scratch, narrow_sems)
    factors = [(normed_rows_one, [d_x, d_y]), (branch_rows, [mixed])]
    wide_sum = ProductsSum(me, sends, factors, wide_to, wide_scratch, wide_sems)
    narrow_sum.load()
    wide_sum.load()
    narrow_sum.begin(range(Z))

    def columns(n, at):
        return units_to.at[n, :, pl.ds(pl.multiple_of(at * share, LANES), share)]

    low, high, extra = slice(0, Z // 2), slice(Z // 2, Z), slice(Z, Z + Z // 2)
    every = slice(0, Z)

    def units_begin_y():
        for n, blocks in enumerate((every, extra)):
            for i in range(1, outer):
                sends.start(
                    True, units_y.at[i - 1, blocks], units_y_in.at[i - 1, blocks],
                    units_y_sems.at[i - 1, n], me.at_y(-i),
                )

    def units_begin_x():
        for j in range(1, inner):
            sends.start(
                True, units_x.at[j - 1], units_x_in.at[j - 1], units_x_sems.at[j - 1], me.at_x(j)
            )

    kept = []

    def unit_add(n, blocks, came, came_blocks, sems, count):
        for i in range(count):
            arrived(came.at[i, came_blocks], sems.at[i], me.at_c)

        def body(r):
            for at in range(blocks.stop - blocks.start):
                total = units_v[n, blocks.start + at, r].astype(F32)
                for i in range(count):
                    total = total + came[i, came_blocks.start + at, r].astype(F32)
                units_v[n, blocks.start + at, r] = total.astype(BF16)

        each_rows(units_v.shape[2], 16, body)

    def unit_pass_on(n):
        copy = pltpu.make_async_copy(units_v.at[n, me.z], columns(n, me.z), local_sems.at[2 + n])
        copy.start()
        kept.append(copy)
        for k in range(1, Z):
            to = (me.z + k) % Z
            sends.start(
                True, units_v.at[n, to], columns(n, me.z), unit_sems.at[n, me.z], me.at_z(to)
            )

    def unit_gate():
        unit_add(0, every, units_y_in, every, units_y_sems.at[:, 0], outer - 1)
        unit_pass_on(0)

    def unit_down():
        unit_add(2, low, units_y_in, extra, units_y_sems.at[:, 1], outer - 1)
        unit_add(2, high, units_x_in, low, units_x_sems, inner - 1)
        unit_pass_on(2)


    def units_finish():
        for n in range(3):
            for k in range(1, Z):
                at = (me.z + Z - k) % Z
                arrived(columns(n, at), unit_sems.at[n, at], me.at_c)
        for copy in kept:
            copy.wait()

    def exchange(held, into, sems, first, devices):
        for n, device in enumerate(devices):
            sends.start(True, held, into.at[first + n], sems.at[first + n], device)

    def gathered(held, into, sems, first, devices):
        for n, _ in enumerate(devices):
            arrived(into.at[first + n], sems.at[first + n], me.at_c)
        total = into[first]
        for n in range(1, len(devices)):
            total = total + into[first + n]
        return held[...] + total

    z_stage = [me.at_z((me.z + k) % Z) for k in range(1, Z)]
    x_stage = [me.at_x(j) for j in range(1, inner)]

    devices = Z * inner * outer * C
    wt = outer * C
    here = me.s * wt + me.w
    width = tokens.shape[1]
    channels = width // devices

    def gains_cut():
        for i in range(devices):
            first = i * channels // LANES * LANES
            first = min(first, width - 2 * LANES)
            window = gains_v[:, first : first + 2 * LANES]
            turn = i * channels - first
            if turn:
                window = pltpu.roll(window, 2 * LANES - turn, 1)
            parts_out[i] = window[:, :LANES]

    def gains_copy(i):
        return pltpu.make_async_remote_copy(
            src_ref=parts_out.at[i], dst_ref=parts_in.at[here],
            send_sem=all_sems.at[0, i], recv_sem=all_sems.at[1, here],
            device_id={"seq": i // wt, "wt": i % wt}, device_id_type=MESH,
        )

    def gains_send(i, carried):
        pl.when(i != here)(lambda: gains_copy(i).start())
        return carried

    def gains_add(i, carried):
        @pl.when(i != here)
        def _():
            gains_copy(i).wait_send()
            arrived(parts_in.at[i], all_sems.at[1, i], me.at_c)
            gains[...] += parts_in[i]

        return carried

    exchange(vectors, vec_in, vec_sems, 0, x_stage)
    units_begin_x()

    units_begin_y()
    units_load.wait()
    unit_pass_on(1)

    load.wait()
    for i, at in enumerate(order):
        arrived(c_in.at[at], c_sems.at[at], me.at_c)
        if i < outer - 1:
            each_rows(rows, 16, lambda r, i=i, at=at: y_out.__setitem__(
                (i, r), (own_v[at, r] + c_in[at, r].astype(F32)).astype(BF16)))
            sends.start(True, y_out.at[i], y_in.at[i], y_sems.at[i], me.at_y(i + 1))
    vectors_to[0] = gathered(vectors, vec_in, vec_sems, 0, x_stage)
    exchange(vectors_to.at[0], vec_in, vec_sems, len(x_stage), z_stage)
    narrow_sum.run()
    vectors_to[1] = gathered(vectors_to.at[0], vec_in, vec_sems, len(x_stage), z_stage)
    wide_sum.begin(range(1))
    unit_gate()
    wide_sum.begin(range(1, 2))
    unit_down()
    wide_sum.begin(range(2, Z))

    def work(r):
        d_normed = own_v[me.y, r] + c_in[me.y, r].astype(F32)
        for i in range(outer - 1):
            d_normed = d_normed + y_in[i, r].astype(F32)
        stream = tokens[r].astype(F32)
        inverse = lax.rsqrt(jnp.mean(stream * stream, axis=1, keepdims=True) + EPSILON)
        normed = stream * inverse
        part = d_normed * normed
        gains_v[0:8] += part[0:8] + part[8:16]
        scaled = d_normed * gain[...]
        passed = inverse * (scaled - normed * jnp.mean(scaled * normed, axis=1, keepdims=True))
        tokens_grad[r] = (d_middle[r] + passed).astype(BF16)

    def between(t):
        if t == 1:
            for i in range(outer - 1):
                arrived(y_in.at[i], y_sems.at[i], me.at_c)
            gains_v[...] = jnp.zeros_like(gains_v)
            each_rows(rows, 16, work)
            gains_v[8:16] = gain_two_grad[0:8] + gain_two_grad[8:16]
            gains_cut()
            lax.fori_loop(0, devices, gains_send, 0)

    wide_sum.run(between)
    gains[...] = parts_out[here]
    lax.fori_loop(0, devices, gains_add, 0)
    units_finish()
    sends.finish()


def last_sums(
    units, units_y, units_x, normed_one, branch_rows, narrow, sent, own,
    d_x, d_y, mixed, tokens, gain, d_middle, gain_two_grad, vectors,
):
    inner, outer = sizes()
    rows, width = tokens.shape
    dma = pltpu.SemaphoreType.DMA
    vmem, anywhere = pl.BlockSpec(memory_space=pltpu.VMEM), pl.BlockSpec(memory_space=pl.ANY)

    def scratch(terms):
        one = terms.shape[2:]
        return [pltpu.VMEM((Z, *one), BF16), pltpu.VMEM((inner - 1, Z, *one), BF16)] + [
            pltpu.VMEM((Z - 1, *one), BF16)
        ] * 4

    devices = Z * inner * outer * C
    copies = 2 * outer - 1 + 2 * (Z * (inner - 1) + 2 * (Z - 1))
    copies += (inner - 1) + (Z - 1) + 2 * (outer - 1) + 2 * (inner - 1) + 3 * (Z - 1)
    _, _, unit_rows, share = units.shape
    block = (unit_rows, d_x.shape[1] + d_y.shape[1] + mixed.shape[1])
    line_sems = [dma((Z,)), dma((inner - 1, Z)), dma((Z - 1,)), dma((Z - 1,))]
    return pl.pallas_call(
        functools.partial(sums_kernel, (inner, outer)),
        out_shape=(
            jax.ShapeDtypeStruct((3, unit_rows, Z * share), BF16),
            jax.ShapeDtypeStruct(block, F32),
            jax.ShapeDtypeStruct(narrow.shape[2:], F32),
            jax.ShapeDtypeStruct((rows, width), BF16),
            jax.ShapeDtypeStruct((16, LANES), F32),
            jax.ShapeDtypeStruct((2, *vectors.shape), F32),
        ),
        in_specs=[anywhere] * 8 + [vmem] * 8,
        out_specs=(anywhere,) + (vmem,) * 5,
        scratch_shapes=[
            pltpu.VMEM((Z, inner * block[0], block[1]), BF16),
            pltpu.VMEM((inner - 1, Z, *block), BF16),
        ]
        + [pltpu.VMEM((Z - 1, *block), BF16)] * 3
        + [pltpu.VMEM(normed_one.shape, BF16), pltpu.VMEM(branch_rows.shape, BF16)]
        + scratch(narrow)
        + [
            pltpu.VMEM((outer, rows, width), F32),
            pltpu.VMEM((outer, rows, width), BF16),
            pltpu.VMEM((outer - 1, rows, width), BF16),
            pltpu.VMEM((outer - 1, rows, width), BF16),
            pltpu.VMEM((devices, 16, LANES), F32),
            pltpu.VMEM((devices, 16, LANES), F32),
            pltpu.VMEM((16, width), F32),
            pltpu.VMEM((inner - 1 + Z - 1, *vectors.shape), F32),
            dma((copies,)),
            dma((5,)),
            dma((outer,)),
            dma((outer - 1,)),
            dma((2, devices)),
            dma((inner - 1 + Z - 1,)),
        ]
        + line_sems * 2
        + [
            pltpu.VMEM(units.shape, BF16),
            pltpu.VMEM(units_y.shape, BF16),
            pltpu.VMEM(units_x.shape, BF16),
            dma((3, Z)),
            dma((outer - 1, 2)),
            dma((inner - 1,)),
        ],
        compiler_params=pltpu.CompilerParams(
            collective_id=5, has_side_effects=True, vmem_limit_bytes=60 * 1024 * 1024
        ),
        name="last_sums",
    )(
        units, units_y, units_x, normed_one, branch_rows, narrow, sent, own,
        d_x, d_y, mixed, tokens, gain, d_middle, gain_two_grad, vectors,
    )


def scan_kernel(backward, factors, inflows, states, entered, products, ends, ends_in, carry, send_sems, arrivals):
    seq = ends_in.shape[0]
    s = lax.axis_index("seq")
    rows, width = factors.shape
    barrier = pltpu.get_barrier_semaphore()

    def device(at):
        return {"seq": at, "wt": lax.axis_index("wt")}

    def greet(i, carried):
        @pl.when(i != s)
        def _():
            pl.semaphore_signal(barrier, inc=1, device_id=device(i), device_id_type=MESH)

        return carried

    lax.fori_loop(0, seq, greet, 0)
    group = 8
    at_row = lax.broadcasted_iota(jnp.int32, (group, width), 0)

    def step(i, carried):
        held, product = carried
        i = rows // group - 1 - i if backward else i
        where = pl.ds(pl.multiple_of(i * group, group), group)
        factor, inflow = factors[where, :], inflows[where, :]
        for by in (1, 2, 4):
            inside = at_row < group - by if backward else at_row >= by
            turn = group - by if backward else by
            inflow = factor * jnp.where(inside, pltpu.roll(inflow, turn, 0), 0.0) + inflow
            factor = factor * jnp.where(inside, pltpu.roll(factor, turn, 0), 1.0)
        inflow = inflow + factor * held
        factor = factor * product
        states[where, :] = inflow
        products[where, :] = factor
        last = slice(0, 1) if backward else slice(group - 1, group)
        return inflow[last], factor[last]

    held, product = lax.fori_loop(
        0, rows // group, step, (jnp.zeros((1, width), F32), jnp.ones((1, width), F32)), unroll=4
    )
    ends[0:1] = product
    ends[1:2] = held
    pl.semaphore_wait(barrier, seq - 1)

    def copy_to(i):
        return pltpu.make_async_remote_copy(
            src_ref=ends, dst_ref=ends_in.at[s], send_sem=send_sems.at[i], recv_sem=arrivals.at[s],
            device_id=device(i), device_id_type=MESH,
        )

    def later(i):
        return i < s if backward else i > s

    def send(i, carried):
        pl.when(later(i))(lambda: copy_to(i).start())
        return carried

    lax.fori_loop(0, seq, send, 0)
    carry[...] = jnp.zeros_like(carry)

    def receive(n, carried):
        i = seq - 1 - n if backward else n

        @pl.when(jnp.logical_not(later(i)) & (i != s))
        def _():
            arrived(ends_in.at[i], arrivals.at[i], device((s + 1) % seq))
            carry[0:1] = ends_in[i, 0:1] * carry[0:1] + ends_in[i, 1:2]

        return carried

    lax.fori_loop(0, seq, receive, 0)
    entering = carry[0:1]
    entered[...] = entering

    def spread(i, carried):
        where = pl.ds(pl.multiple_of(i * group, group), group)
        states[where, :] += products[where, :] * entering
        return carried

    lax.fori_loop(0, rows // group, spread, 0, unroll=8)

    def sent(i, carried):
        pl.when(later(i))(lambda: copy_to(i).wait_send())
        return carried

    lax.fori_loop(0, seq, sent, 0)


def full_scan(factor, inflow, backward):
    seq = lax.axis_size("seq")
    rows, width = factor.shape
    vmem = pl.BlockSpec(memory_space=pltpu.VMEM)
    return pl.pallas_call(
        functools.partial(scan_kernel, backward),
        out_shape=(
            jax.ShapeDtypeStruct((rows, width), F32),
            jax.ShapeDtypeStruct((1, width), F32),
        ),
        in_specs=[vmem, vmem],
        out_specs=(vmem, vmem),
        scratch_shapes=[
            pltpu.VMEM((rows, width), F32),
            pltpu.VMEM((8, width), F32),
            pltpu.VMEM((seq, 8, width), F32),
            pltpu.VMEM((8, width), F32),
            pltpu.SemaphoreType.DMA((seq,)),
            pltpu.SemaphoreType.DMA((seq,)),
        ],
        compiler_params=pltpu.CompilerParams(
            collective_id=4 if backward else 3,
            has_side_effects=True,
            vmem_limit_bytes=32 * 1024 * 1024,
        ),
        name="scan_back" if backward else "scan_ahead",
    )(factor, inflow)


def recurrence_terms(decay_pre, input_pre, decay_log, conv_float):
    log_decay = -DECAY_SCALE * jax.nn.softplus(-decay_log) * jax.nn.sigmoid(decay_pre)
    return (
        jnp.exp(log_decay),
        jnp.sqrt(-jnp.expm1(2.0 * log_decay)) * jax.nn.sigmoid(input_pre) * conv_float,
    )


def per_device(
    tokens,
    norm1_gain,
    x_weight,
    y_weight,
    conv_weight,
    conv_bias,
    decay_gate_weight,
    decay_bias,
    input_gate_weight,
    input_bias,
    decay_param,
    out_weight,
    norm2_gain,
    gate_weight,
    up_weight,
    down_weight,
    out_grad,
):
    seq, wt = lax.axis_size("seq"), lax.axis_size("wt")
    inner, outer = sizes()
    z, x, y, c = places()
    w = lax.axis_index("wt")
    rows_dev, width = tokens.shape
    weight_rows, lru_cols = x_weight.shape
    chunk, block = decay_gate_weight.shape
    half = block // 2
    full = lru_cols - half
    taps_count = conv_weight.shape[1]
    reach = taps_count - 1
    hidden_cols = gate_weight.shape[1]

    def turned(value, axis):
        return jnp.where(c == 0, value, jnp.roll(value, -half, axis))

    def turned_back(value, axis):
        return jnp.where(c == 0, value, jnp.roll(value, half, axis))

    def in_order(own, partner, axis):
        return jnp.where(
            c == 0,
            jnp.concatenate([own, partner], axis),
            jnp.concatenate([partner, own], axis),
        )

    vectors = jnp.stack(
        [v.astype(F32) for v in (norm1_gain, norm2_gain, conv_bias, decay_bias, input_bias)]
        + [decay_param]
        + [conv_weight[:, k].astype(F32) for k in range(taps_count)]
    )
    vectors = jnp.pad(vectors, ((0, -vectors.shape[0] % 8), (0, -chunk % LANES)))

    across = [(i, i % seq * wt + i // seq) for i in range(seq * wt)]
    gates = jnp.concatenate([decay_gate_weight, input_gate_weight], axis=1)

    def padded(weight):
        share = -(-hidden_cols // (Z * LANES)) * LANES
        return jnp.pad(weight, ((0, 0), (0, Z * share - hidden_cols)))

    xy_unit = jnp.concatenate([turned(x_weight, 1), turned(y_weight, 1)], axis=1)
    (
        grad_group, vectors, gate_all, xy_kernel, out_kernel, gate_kernel, up_kernel, down_kernel,
        group_one, xy,
    ) = gather_all(
        tokens, out_grad, vectors, gates, xy_unit, turned(out_weight, 1),
        padded(gate_weight), padded(up_weight), padded(down_weight),
    )
    grad_group = grad_group.reshape(-1, width)
    vectors = jnp.moveaxis(vectors[:, : 6 + taps_count, :chunk], 0, 1).reshape(6 + taps_count, -1)
    gain_one, gain_two = vectors[0], vectors[1]
    own_vectors = turned(
        lax.dynamic_slice(vectors[2:], (0, w * lru_cols), (taps_count + 4, lru_cols)), 1
    )
    tap_bias, decay_shift, input_shift, decay_log = (own_vectors[i] for i in range(4))
    taps = own_vectors[4:]
    xy_kernel = xy_kernel.reshape(width, -1)
    out_kernel = out_kernel.reshape(width, -1)
    gate_kernel = gate_kernel.reshape(width, -1)
    gate_all = turned(gate_all.reshape(lru_cols, 2 * block), 0)
    partner_rows = c_swap(gate_all[full:])
    shared_rows = in_order(gate_all[full:], partner_rows, 0)

    stream = tokens.astype(F32)
    rows = group_one.shape[0]
    x_branch = xy[:, :lru_cols].astype(BF16)
    y_before = xy[:, lru_cols:]
    y_gated, gelu_y_back = jax.vjp(gelu_tanh, y_before)
    rim = lax.ppermute(x_branch[rows - reach :], "seq", [(i, i + 1) for i in range(seq - 1)])
    extended = jnp.concatenate([rim, x_branch], axis=0).astype(F32)
    conv_low = (
        tap_bias
        + sum(taps[k] * extended[reach - k : reach - k + rows] for k in range(taps_count))
    ).astype(BF16)
    shared_conv = in_order(conv_low[:, full:], c_swap(conv_low[:, full:]), 1)
    heads = full // block

    def of_head(value, i):
        return value[:, i * block : (i + 1) * block]

    pre_parts = [
        multiply(of_head(conv_low, i), gate_all[i * block : (i + 1) * block]) for i in range(heads)
    ]
    shared_columns = jnp.where(
        c == 0,
        jnp.concatenate([shared_rows[:, :half], shared_rows[:, block : block + half]], axis=1),
        jnp.concatenate([shared_rows[:, half:block], shared_rows[:, block + half :]], axis=1),
    )
    shared_pre = multiply(shared_conv, shared_columns)
    decay_pre = decay_shift + jnp.concatenate(
        [part[:, :block] for part in pre_parts] + [shared_pre[:, :half]], axis=1
    )
    input_pre = input_shift + jnp.concatenate(
        [part[:, block:] for part in pre_parts] + [shared_pre[:, half:]], axis=1
    )
    (retain, inflow), terms_back = jax.vjp(
        recurrence_terms, decay_pre, input_pre, decay_log, conv_low.astype(F32)
    )
    states, state_in = full_scan(retain, inflow, False)
    before = jnp.concatenate([state_in, states[:-1]])
    lru_low = states.astype(BF16).astype(F32)
    mixed_rows = (lru_low * y_gated).astype(BF16)
    mixed_parts = mixed_rows.reshape(outer, C, rows_dev, lru_cols)

    def branch_of(at):
        part = pick(mixed_parts, at, 1).reshape(outer * rows_dev, lru_cols)
        return contract_last(part, out_kernel).reshape(outer, rows_dev, width)

    group_two, middle, up_kernel, down_kernel = branch_and_group(
        branch_of(1 - c), branch_of(c), tokens, gain_two[None], up_kernel, down_kernel
    )
    up_kernel = up_kernel.reshape(width, -1)
    down_kernel = down_kernel.reshape(width, -1)
    group_two = group_two.reshape(C * Z * rows_dev, width)

    gate_pre = multiply(group_two, gate_kernel)
    up_pre = multiply(group_two, up_kernel)
    active, gelu_gate_back = jax.vjp(gelu_tanh, gate_pre)
    hidden = (active * up_pre).astype(BF16)

    d_hidden = multiply(grad_group, down_kernel)
    d_up = (d_hidden * active).astype(BF16)
    d_gate = gelu_gate_back(d_hidden * up_pre)[0].astype(BF16)
    half_rows = Z * rows_dev

    def d_normed_of(part):
        total = contract_last(d_gate[part], gate_kernel) + contract_last(d_up[part], up_kernel)
        return total.reshape(Z, rows_dev, width)

    def terms_of(left_side, right_side):
        share = right_side.shape[1] // outer
        return [
            contract_rows(left_side, right_side[:, i * share : (i + 1) * share])
            .astype(BF16)
            .reshape(Z, inner, weight_rows, share)
            for i in range(outer)
        ]

    gate_terms = terms_of(group_two, d_gate)
    up_terms = terms_of(group_two, d_up)
    down_terms = terms_of(grad_group, hidden)
    branch_rows, d_middle, gain_two_grad, block_out, units, units_y, units_x = middle_and_rows(
        d_normed_of(slice(half_rows, None)).astype(BF16),
        d_normed_of(slice(0, half_rows)),
        middle,
        out_grad,
        gain_two[None],
        hidden,
        down_kernel,
        gate_terms + up_terms + down_terms,
    )
    branch_rows = branch_rows.reshape(-1, width)

    d_mixed = multiply(branch_rows, out_kernel)
    d_lru = (d_mixed * y_gated).astype(BF16).astype(F32)
    d_y = gelu_y_back(d_mixed * lru_low)[0].astype(BF16)
    passed, passed_in = full_scan(retain, retain * d_lru, True)
    d_total = d_lru + jnp.concatenate([passed[1:], passed_in])
    d_decay_pre, d_input_pre, decay_log_grad, d_conv_direct = terms_back(
        (d_total * before, d_total)
    )
    d_decay_low, d_input_low = d_decay_pre.astype(BF16), d_input_pre.astype(BF16)
    own_low = jnp.concatenate([d_decay_low[:, full:], d_input_low[:, full:]], axis=1)
    partner_low = c_swap(own_low)
    shared_low = jnp.concatenate(
        [
            in_order(own_low[:, :half], partner_low[:, :half], 1),
            in_order(own_low[:, half:], partner_low[:, half:], 1),
        ],
        axis=1,
    )
    lows = [
        jnp.concatenate([of_head(d_decay_low, i), of_head(d_input_low, i)], axis=1)
        for i in range(heads)
    ]
    d_conv = d_conv_direct + jnp.concatenate(
        [contract_last(lows[i], gate_all[i * block : (i + 1) * block]) for i in range(heads)]
        + [contract_last(shared_low, gate_all[full:])],
        axis=1,
    )
    gates_grad = jnp.concatenate(
        [contract_rows(of_head(conv_low, i), lows[i]) for i in range(heads)]
        + [contract_rows(conv_low[:, full:], shared_low)]
    )
    ahead = lax.ppermute(d_conv[:reach], "seq", [(i + 1, i) for i in range(seq - 1)])
    d_extended = jnp.concatenate([d_conv, ahead], axis=0)
    d_x_branch = sum(taps[k] * d_extended[k : k + rows] for k in range(taps_count)).astype(BF16)
    dx_parts = d_x_branch.reshape(outer, C, rows_dev, lru_cols)
    dy_parts = d_y.reshape(outer, C, rows_dev, lru_cols)

    def d_normed_one_of(at):
        dx, dy = (
            pick(parts, at, 1).reshape(outer * rows_dev, lru_cols) for parts in (dx_parts, dy_parts)
        )
        total = contract_last(dx, xy_kernel[:, :lru_cols]) + contract_last(
            dy, xy_kernel[:, lru_cols:]
        )
        return total.reshape(outer, rows_dev, width)

    narrow = turned_back(gates_grad, 0).astype(BF16).reshape(Z, inner, chunk, 2 * block)
    narrow = jnp.pad(narrow, ((0, 0), (0, 0), (0, -chunk % 16), (0, 0)))
    own_sums = jnp.stack(
        [jnp.sum(d_conv, axis=0), jnp.sum(d_decay_pre, axis=0), jnp.sum(d_input_pre, axis=0)]
        + [decay_log_grad]
        + [jnp.sum(d_conv * extended[reach - k : reach - k + rows], axis=0) for k in range(taps_count)],
    )
    own_sums = turned_back(own_sums, 1)
    placed, wide, narrow, tokens_grad, gains, own_sums = last_sums(
        units, units_y, units_x, group_one, branch_rows, narrow,
        d_normed_one_of(1 - c).astype(BF16), d_normed_one_of(c),
        turned_back(d_x_branch, 1), turned_back(d_y, 1), turned_back(mixed_rows, 1),
        tokens, gain_one[None], d_middle, gain_two_grad, own_sums,
    )
    weight_grads = [wide[:, n * lru_cols : (n + 1) * lru_cols] for n in range(3)]
    gate_grad, up_grad, down_grad = (placed[n, :, :hidden_cols].astype(F32) for n in range(3))
    gains = gains.reshape(2, 8, LANES).sum(axis=1)[:, :chunk]
    sums = lax.dynamic_slice(own_sums[1], (0, lax.axis_index("seq") * chunk), (taps_count + 4, chunk))
    own_sums = jnp.concatenate([narrow[:chunk], sums.T], axis=1)
    own_sums = lax.ppermute(own_sums, ("seq", "wt"), [(to, at) for at, to in across])
    sums = own_sums[:, 2 * block :]
    return (
        block_out,
        tokens_grad,
        gains[0],
        weight_grads[0],
        weight_grads[1],
        sums[:, 4:],
        sums[:, 0],
        own_sums[:, :block],
        sums[:, 1],
        own_sums[:, block : 2 * block],
        sums[:, 2],
        sums[:, 3],
        weight_grads[2],
        gains[1],
        gate_grad,
        up_grad,
        down_grad,
    )


def solution(mesh):
    rows, both, lone = P(("seq", "wt"), None), P("seq", "wt"), P(("seq", "wt"))
    in_specs = (
        rows, lone, both, both, rows, lone, rows, lone, rows, lone, lone,
        both, lone, both, both, both, rows,
    )
    out_specs = (
        rows, rows, lone, both, both, rows, lone, rows, lone, rows, lone, lone,
        both, lone, both, both, both,
    )
    return jax.shard_map(
        per_device, mesh=mesh, in_specs=in_specs, out_specs=out_specs, check_vma=False
    )
```
